32 devices in a mesh: groups: 2 (over y), atoms: 4 (over z), pair: 2 (over x), samp: 2 (over core).
Axes of the slice: x: 2, y: 2, z: 4, core: 2. Of those that a mesh axis runs over, the one named last changes fastest.
Arguments:
- atom_single: bfloat16 [24, 2048, 128], P(('groups', 'pair', 'samp'), 'atoms'), parts along dimension 0, may hold values from -6 to 6
- atom_cond: bfloat16 [4096, 128], P(('groups', 'atoms')), parts along dimension 0, may hold values from -6 to 6
- pair_cond: bfloat16 [512, 256, 128], P(('groups', 'pair'), 'atoms'), parts along dimension 0, may hold values from -6 to 6
- atom_counts: int32 [8, 64], P('groups'), parts along dimension 0, may hold values from 1 to 24, 512 in all within a row
- ada_attn_scale: bfloat16 [128, 128], replicated, may hold values from -0.5 to 0.5
- ada_attn_shift: bfloat16 [128, 128], replicated, may hold values from -0.5 to 0.5
- w_query: bfloat16 [128, 128], replicated, may hold values from -4 to 4
- w_key: bfloat16 [128, 128], replicated, may hold values from -4 to 4
- w_value: bfloat16 [128, 128], replicated, may hold values from -0.5 to 0.5
- w_gate: bfloat16 [128, 128], replicated, may hold values from -0.5 to 0.5
- w_out: bfloat16 [128, 128], replicated, may hold values from -0.5 to 0.5
- attn_gate: bfloat16 [128, 128], replicated, may hold values from -0.5 to 0.5
- w_pair: bfloat16 [128, 4], replicated, may hold values from -0.5 to 0.5
- ada_trans_scale: bfloat16 [128, 128], replicated, may hold values from -0.5 to 0.5
- ada_trans_shift: bfloat16 [128, 128], replicated, may hold values from -0.5 to 0.5
- w_swish: bfloat16 [128, 256], replicated, may hold values from -0.5 to 0.5
- w_linear: bfloat16 [128, 256], replicated, may hold values from -0.5 to 0.5
- w_down: bfloat16 [256, 128], replicated, may hold values from -0.375 to 0.375
- trans_gate: bfloat16 [128, 128], replicated, may hold values from -0.5 to 0.5
Outputs:
- updated: bfloat16 [24, 2048, 128], P(('groups', 'pair', 'samp'), 'atoms'), parts along dimension 0
The draws below stay inside these ranges and needn't reach their ends.
There are 2 independent parts, one for each index of `groups`. The reference program is written for one: setup_inputs(seed, part) draws one part's arguments, and reference() takes and returns one part's arrays. A program takes and returns all parts, laid end to end along the dimension named above; an argument that names none is the same for every part. Nothing has to cross between parts.
Inputs may be any that keep to these rules, and one draw needn't show every extreme that they name: Row j of atom_counts gives the atoms of tokens j * 64 to (j + 1) * 64 - 1; every row sums to 512 and holds at least one count equal to 24.
All inputs are finite; a program needn't handle non-finite values.
Results may differ from the reference program's by a relative error of at most 0.0094.
Values may be sent and summed in bfloat16 or wider, within the bound.
No kernel may reach another device: no remote copies, remote signals or barrier semaphores. Data moves between devices by JAX's collectives and lax.ppermute only.
A program may use at most 64 MiB of HBM per device.

```python
import math
import jax
import jax.numpy as jnp
import numpy as np
from jax import lax

C_ATOM = 128
C_PAIR = 128
HEADS = 4
HEAD_DIM = 32
TRANS = 256
Q_WIN = 32
K_WIN = 128
EDGE = 48
TOK_DEV = 64
MOST = 24
ATOM_DEV = 512
SAMPLES = 12
NTOK = 256
NATOM = 2048
N_ATOMS = 4


def draw_w_query(key, part):
    key = jax.random.fold_in(key, 1)
    single = jax.random.truncated_normal(key, -4.0, 4.0, (C_ATOM, C_ATOM), jnp.float32) / math.sqrt(C_ATOM)
    result = single
    return result.astype(jnp.bfloat16)


def draw_w_key(key, part):
    key = jax.random.fold_in(key, 2)
    single = jax.random.truncated_normal(key, -4.0, 4.0, (C_ATOM, C_ATOM), jnp.float32) / math.sqrt(C_ATOM)
    result = single
    return result.astype(jnp.bfloat16)


def levels(key, dims, shards, low, high):
    def one(position, blocks):
        draws = jax.random.uniform(jax.random.fold_in(jax.random.fold_in(key, 6), position), (blocks,), jnp.float32, low / len(shards), high / len(shards))
        return jnp.repeat(jnp.exp(draws), dims[position] // blocks).reshape((-1,) + (1,) * (len(dims) - position - 1))

    level = one(*shards[0])
    for cut in shards[1:]:
        level = level * one(*cut)
    return level


def length_profile(amount, total, most, skew):
    portions = [(1 << 20) // math.isqrt(grade ** skew) + 1 for grade in range(2, amount + 1)]
    surplus, counts = total - most - (amount - 1), [1] * (amount - 1)
    while surplus > 0:
        candidates = [i for i in range(amount - 1) if counts[i] < most]
        whole, budget = sum([portions[i] for i in candidates]), surplus
        for i in candidates:
            more = min(most - counts[i], max(1, budget * portions[i] // whole), surplus)
            counts[i] = counts[i] + more
            surplus = surplus - more
    return np.array([most] + counts)


def uneven(rng, count, total, bound, skew):
    if count == 2:
        one = jax.random.randint(rng, (), max(1, total - bound), min(bound, total - 1) + 1)
        return jnp.stack([one, total - one])
    lengths = jnp.asarray(length_profile(count, total, bound, skew), jnp.int32)
    twos = (count - 1) // 2
    source_of, sink = lengths[1:1 + 2 * twos:2], lengths[2:2 + 2 * twos:2]
    room = jnp.minimum(source_of - 1, bound - sink)
    passed = jax.random.randint(jax.random.fold_in(rng, 1), (twos,), 0, 1 << 20) % (room + 1)
    lengths = lengths.at[1:1 + 2 * twos:2].set(source_of - passed).at[2:2 + 2 * twos:2].set(sink + passed)
    return lengths[jax.random.permutation(jax.random.fold_in(rng, 2), count)]


def noise(key, shape, scale, reach, cuts=(), kind=jnp.bfloat16):
    drawn = jax.random.normal(key, shape, jnp.float32) * scale
    if len(cuts) > 0:
        drawn = levels(key, shape, cuts, -0.22, 0.18) * drawn
    return jnp.clip(drawn, min=-reach, max=reach).astype(kind)


def setup_inputs(seed: int = 0, part: int = 0) -> dict:
    seeds = jax.random.split(jax.random.key(seed), 20)
    own_keys = jax.random.split(jax.random.fold_in(seeds[19], part), 20)
    atom_single = noise(own_keys[0], (SAMPLES, NATOM, C_ATOM), 1.0, 6.0, ((0, 4), (1, 4)))
    atom_cond = noise(own_keys[1], (NATOM, C_ATOM), 1.0, 6.0, ((0, 4),))
    pair_cond = noise(own_keys[2], (NTOK, NTOK, C_PAIR), 1.0, 6.0, ((0, 2), (1, 4)))
    atom_counts = jax.vmap(lambda own: uneven(own, TOK_DEV, ATOM_DEV, MOST, 2))(jax.random.split(own_keys[3], N_ATOMS)).reshape((N_ATOMS, TOK_DEV)).astype(jnp.int32)
    ada_attn_scale = noise(seeds[4], (C_ATOM, C_ATOM), C_ATOM ** -0.5, 0.5)
    ada_attn_shift = noise(seeds[5], (C_ATOM, C_ATOM), C_ATOM ** -0.5, 0.5)
    w_query = draw_w_query(jax.random.fold_in(seeds[19], 71), part)
    w_key = draw_w_key(jax.random.fold_in(seeds[19], 71), part)
    w_value = noise(seeds[8], (C_ATOM, C_ATOM), C_ATOM ** -0.5, 0.5)
    w_gate = noise(seeds[9], (C_ATOM, C_ATOM), C_ATOM ** -0.5, 0.5)
    w_out = noise(seeds[10], (C_ATOM, C_ATOM), C_ATOM ** -0.5, 0.5)
    attn_gate = noise(seeds[11], (C_ATOM, C_ATOM), C_ATOM ** -0.5, 0.5)
    w_pair = noise(seeds[12], (C_PAIR, HEADS), C_PAIR ** -0.5, 0.5)
    ada_trans_scale = noise(seeds[13], (C_ATOM, C_ATOM), C_ATOM ** -0.5, 0.5)
    ada_trans_shift = noise(seeds[14], (C_ATOM, C_ATOM), C_ATOM ** -0.5, 0.5)
    w_swish = noise(seeds[15], (C_ATOM, TRANS), C_ATOM ** -0.5, 0.5)
    w_linear = noise(seeds[16], (C_ATOM, TRANS), C_ATOM ** -0.5, 0.5)
    w_down = noise(seeds[17], (TRANS, C_ATOM), TRANS ** -0.5, 0.375)
    trans_gate = noise(seeds[18], (C_ATOM, C_ATOM), C_ATOM ** -0.5, 0.5)
    return {"atom_single": atom_single, "atom_cond": atom_cond, "pair_cond": pair_cond, "atom_counts": atom_counts, "ada_attn_scale": ada_attn_scale, "ada_attn_shift": ada_attn_shift, "w_query": w_query, "w_key": w_key, "w_value": w_value, "w_gate": w_gate, "w_out": w_out, "attn_gate": attn_gate, "w_pair": w_pair, "ada_trans_scale": ada_trans_scale, "ada_trans_shift": ada_trans_shift, "w_swish": w_swish, "w_linear": w_linear, "w_down": w_down, "trans_gate": trans_gate}


EPSILON = 1e-05
MASKED = -1e+30

def layer_norm(values):
    values = values.astype(jnp.float32)
    centred = values - lax.optimization_barrier(jnp.mean(values, axis=-1, keepdims=True))
    return centred * lax.rsqrt(lax.optimization_barrier(jnp.mean(centred * centred, axis=-1, keepdims=True)) + EPSILON)

def project(matrix_rows, weight):
    flattened = matrix_rows.reshape(-1, matrix_rows.shape[-1])
    mixed = jnp.dot(flattened, weight, preferred_element_type=jnp.float32)
    return mixed.reshape(matrix_rows.shape[:-1] + (weight.shape[1],))

def reference(atom_single, atom_cond, pair_cond, atom_counts, ada_attn_scale, ada_attn_shift, w_query, w_key, w_value, w_gate, w_out, attn_gate, w_pair, ada_trans_scale, ada_trans_shift, w_swish, w_linear, w_down, trans_gate):
    cond_norm = layer_norm(atom_cond).astype(jnp.bfloat16)
    single_norm = layer_norm(atom_single)
    normed = (jax.nn.sigmoid(project(cond_norm, ada_attn_scale)) * single_norm + project(cond_norm, ada_attn_shift)).astype(jnp.bfloat16)
    normed_trans = (jax.nn.sigmoid(project(cond_norm, ada_trans_scale)) * single_norm + project(cond_norm, ada_trans_shift)).astype(jnp.bfloat16)
    hidden = (jax.nn.silu(project(normed_trans, w_swish)) * project(normed_trans, w_linear)).astype(jnp.bfloat16)
    transition = jax.nn.sigmoid(project(cond_norm, trans_gate)) * project(hidden, w_down)

    def token_row(pair_row):
        return jnp.dot(layer_norm(pair_row).astype(jnp.bfloat16), w_pair, preferred_element_type=jnp.float32).astype(jnp.bfloat16)
    token_bias = lax.map(token_row, pair_cond)
    token_of = jnp.repeat(jnp.arange(NTOK, dtype=jnp.int32), atom_counts.reshape(-1), total_repeat_length=NATOM)
    windows = NATOM // Q_WIN
    key_pos = jnp.arange(windows, dtype=jnp.int32)[:, None] * Q_WIN + jnp.arange(K_WIN, dtype=jnp.int32)[None, :] - EDGE
    is_valid = (key_pos >= 0) & (key_pos < NATOM)
    key_clip = jnp.clip(key_pos, 0, NATOM - 1).astype(jnp.int32)
    query_tok = token_of.reshape(windows, Q_WIN)
    key_tok = token_of[key_clip]
    atom_bias = token_bias[query_tok[:, :, None], key_tok[:, None, :]]
    atom_bias = jnp.transpose(atom_bias, (0, 3, 1, 2)).astype(jnp.float32)
    queries = project(normed, w_query).astype(jnp.bfloat16)
    keys_all = project(normed, w_key).astype(jnp.bfloat16)
    values_all = project(normed, w_value).astype(jnp.bfloat16)
    inv_root = 1.0 / math.sqrt(HEAD_DIM)

    def attend(inputs):
        q_one, k_one, v_one = inputs
        q_win = q_one.reshape(windows, Q_WIN, HEADS, HEAD_DIM).astype(jnp.float32)
        k_win = k_one[key_clip].reshape(windows, K_WIN, HEADS, HEAD_DIM).astype(jnp.float32)
        v_win = v_one[key_clip].reshape(windows, K_WIN, HEADS, HEAD_DIM).astype(jnp.float32)
        scores = jnp.einsum('wqhd,wkhd->whqk', q_win, k_win) * inv_root + atom_bias
        scores = jnp.where(is_valid[:, None, None, :], scores, MASKED)
        row_max = lax.optimization_barrier(jnp.max(scores, axis=-1, keepdims=True))
        raised = jnp.exp(scores - row_max)
        probs = (raised / lax.optimization_barrier(jnp.sum(raised, axis=-1, keepdims=True))).astype(jnp.bfloat16)
        mixed = jnp.einsum('whqk,wkhd->wqhd', probs.astype(jnp.float32), v_win)
        return mixed.reshape(NATOM, C_ATOM)
    attended = lax.map(attend, (queries, keys_all, values_all))
    gated_out = (jax.nn.sigmoid(project(normed, w_gate)) * attended).astype(jnp.bfloat16)
    attention = jax.nn.sigmoid(project(cond_norm, attn_gate)) * project(gated_out, w_out)
    return (attention + transition).astype(jnp.bfloat16)
```

```python
import functools
import math

import jax
import jax.numpy as jnp
from jax import lax
from jax.experimental import pallas as pl
from jax.experimental.pallas import tpu as pltpu
from jax.sharding import PartitionSpec as P

Q_WIN = 32
K_WIN = 128
EDGE = 48
GROUP = 32

EPSILON = 1e-05
MASKED = -1e30
LOG2E = math.log2(math.e)
BF16 = jnp.bfloat16
F32 = jnp.float32
LAST = (((1,), (1,)), ((), ()))
VMEM = pl.BlockSpec(memory_space=pltpu.VMEM)


def dot(a, b):
    return jnp.dot(a, b, preferred_element_type=F32)


def iota(shape, dim):
    return lax.broadcasted_iota(jnp.int32, shape, dim)


def centring(width):
    same = iota((width, width), 0) == iota((width, width), 1)
    return jnp.where(same, 1.0 - 1.0 / width, -1.0 / width).astype(BF16)


def averaging(width):
    return jnp.full((width, width), 1.0 / width, BF16)


def layer_norm(rows):
    width = rows.shape[-1]
    centred = dot(rows, centring(width))
    variance = dot((centred * centred).astype(BF16), averaging(width))
    return centred * lax.rsqrt(variance + EPSILON)


def sigmoid(values):
    return 1.0 / (1.0 + jnp.exp2(values * -LOG2E))


def pair_kernel(heads, pair_ref, w_pair_ref, out_ref):
    group, cols, width = pair_ref.shape
    half = group // 2
    lanes = heads * group
    centre = centring(width)
    blank = jnp.zeros((width, width), BF16)
    centre2 = jnp.concatenate(
        [jnp.concatenate([centre, blank], 1), jnp.concatenate([blank, centre], 1)], 0
    )
    spread = (iota((heads, lanes), 1) // group == iota((heads, lanes), 0)).astype(BF16)
    weight = dot(w_pair_ref[...], spread).astype(BF16)
    blank = jnp.zeros((width, lanes), BF16)
    mean = jnp.full((width, lanes), 1.0 / width, BF16)
    mix = jnp.concatenate(
        [jnp.concatenate([weight, blank], 1), jnp.concatenate([blank, mean], 1)], 0
    )
    pair = pair_ref[...]
    both = jnp.concatenate(
        [pair[:half].reshape(half * cols, width), pair[half:].reshape(half * cols, width)], 1
    )
    centred = dot(both, centre2)
    rounded = centred.astype(BF16)
    squares = (centred * centred).astype(BF16)
    slot = iota((cols, 2 * lanes), 1) % group
    total = jnp.zeros((cols, 2 * lanes), F32)
    for part in range(2):
        cut = slice(part * width, (part + 1) * width)
        mixed = dot(jnp.concatenate([rounded[:, cut], squares[:, cut]], 1), mix)
        mixed = mixed.reshape(half, cols, 2 * lanes)
        for index in range(half):
            total = jnp.where(slot == part * half + index, mixed[index], total)
    out_ref[0, 0] = (total[:, :lanes] * lax.rsqrt(total[:, lanes:] + EPSILON)).astype(BF16)


def pair_bias(pair_cond, w_pair, tok_here):
    rows, cols, width = pair_cond.shape
    heads = w_pair.shape[1]
    groups = tok_here // GROUP
    return pl.pallas_call(
        functools.partial(pair_kernel, heads),
        grid=(rows // GROUP,),
        in_specs=[
            pl.BlockSpec((GROUP, cols, width), lambda i: (i, 0, 0)),
            pl.BlockSpec((width, heads), lambda i: (0, 0)),
        ],
        out_specs=pl.BlockSpec(
            (1, 1, cols, heads * GROUP), lambda i: (i // groups, i % groups, 0, 0)
        ),
        out_shape=jax.ShapeDtypeStruct(
            (rows // tok_here, groups, cols, heads * GROUP), BF16
        ),
        compiler_params=pltpu.CompilerParams(vmem_limit_bytes=40 << 20),
        cost_estimate=pl.CostEstimate(
            flops=rows * cols * width * width * 4,
            bytes_accessed=rows * cols * width * 2,
            transcendentals=0,
        ),
    )(pair_cond, w_pair)


def project_kernel(
    single_ref,
    cond_ref,
    edge_prev_ref,
    edge_next_ref,
    ada_attn_scale,
    ada_attn_shift,
    w_query,
    w_key,
    w_value,
    w_gate,
    attn_gate,
    ada_trans_scale,
    ada_trans_shift,
    w_swish,
    w_linear,
    w_down,
    trans_gate,
    query_ref,
    key_ref,
    value_ref,
    gate_ref,
    open_ref,
    trans_ref,
):
    samples, atoms_here, width = single_ref.shape
    hidden_width = w_swish.shape[1]
    step = 128

    def attn_norm(cond, single):
        ada = dot(cond, jnp.concatenate([ada_attn_scale[...], ada_attn_shift[...]], 1))
        scale, shift = sigmoid(ada[:, :width])[None], ada[None, :, width:]
        rows = single.shape[1]
        return (scale * single.reshape(samples, rows, width) + shift).astype(BF16)

    def keys_values(normed):
        both = dot(
            normed.reshape(-1, width), jnp.concatenate([w_key[...], w_value[...]], 1)
        ).astype(BF16)
        both = both.reshape(samples, -1, 2 * width)
        return both[:, :, :width], both[:, :, width:]

    for place, edge_ref in ((0, edge_prev_ref), (EDGE + atoms_here, edge_next_ref)):
        edge = edge_ref[...].reshape(samples + 1, EDGE, width)
        normal = layer_norm(edge.reshape(-1, width)).reshape(samples + 1, EDGE, width)
        keys, values = keys_values(
            attn_norm(normal[samples].astype(BF16), normal[:samples])
        )
        key_ref[:, place : place + EDGE, :] = keys
        value_ref[:, place : place + EDGE, :] = values

    @pl.loop(0, atoms_here // step)
    def _(turn):
        start = pl.multiple_of(turn * step, step)
        at = pl.ds(start, step)
        cond = layer_norm(cond_ref[at, :]).astype(BF16)
        single = layer_norm(single_ref[:, at, :].reshape(-1, width))
        single = single.reshape(samples, step, width)
        normed = attn_norm(cond, single)
        keys, values = keys_values(normed)
        at_ext = pl.ds(pl.multiple_of(start + EDGE, 16), step)
        key_ref[:, at_ext, :] = keys
        value_ref[:, at_ext, :] = values
        both = dot(
            normed.reshape(-1, width), jnp.concatenate([w_query[...], w_gate[...]], 1)
        ).reshape(samples, step, 2 * width)
        query_ref[:, at, :] = both[:, :, :width].astype(BF16)
        gate_ref[:, at, :] = sigmoid(both[:, :, width:])
        gates = dot(cond, jnp.concatenate([attn_gate[...], trans_gate[...]], 1))
        open_ref[at, :] = sigmoid(gates[:, :width])
        ada = dot(cond, jnp.concatenate([ada_trans_scale[...], ada_trans_shift[...]], 1))
        normed_trans = (sigmoid(ada[:, :width])[None] * single + ada[None, :, width:]).astype(BF16)
        flat = normed_trans.reshape(-1, width)
        swish = dot(flat, w_swish[...])
        hidden = (swish * sigmoid(swish) * dot(flat, w_linear[...])).astype(BF16)
        down = dot(hidden, w_down[...]).reshape(samples, step, width)
        trans_ref[:, at, :] = sigmoid(gates[:, width:])[None] * down


def attend_kernel(
    heads,
    blocks,
    at_ref,
    query_ref,
    key_ref,
    value_ref,
    gate_ref,
    open_ref,
    trans_ref,
    counts_ref,
    prev_ref,
    own_ref,
    next_ref,
    w_out_ref,
    out_ref,
    near_ref,
    gated_ref,
):
    samples, atoms_here, width = query_ref.shape
    tok_here = counts_ref.shape[1]
    head_dim = width // heads
    windows = atoms_here // Q_WIN
    lanes = heads * tok_here
    rows = heads * Q_WIN
    device_at = at_ref[0]
    ends = atoms_here * blocks

    def bounds(block, token, reach):
        counts = counts_ref[pl.ds(block, 1), :].astype(F32).astype(BF16)
        counts = jnp.broadcast_to(counts, (8, tok_here))
        before = iota((tok_here, reach), 0)
        first = dot(counts, (before < token).astype(BF16))[:1]
        last = dot(counts, (before <= token).astype(BF16))[:1]
        return first.astype(jnp.int32), last.astype(jnp.int32)

    def expand(block, place, count, offset, tile_ref):
        token = iota((tok_here, tok_here), 1)
        first, last = bounds(block, token, tok_here)
        position = iota((count, tok_here), 0) + offset
        hot = ((first <= position) & (position < last)).astype(F32).astype(BF16)
        tile = tile_ref[...].reshape(tok_here // GROUP, tok_here, heads * GROUP)
        tile = jnp.concatenate([tile[index] for index in range(tok_here // GROUP)], 1)
        near_ref[place : place + count, :] = dot(hot, tile).astype(BF16)

    expand(jnp.maximum(device_at - 1, 0), 0, EDGE, atoms_here - EDGE, prev_ref)
    expand(device_at, EDGE, atoms_here, 0, own_ref)
    expand(jnp.minimum(device_at + 1, blocks - 1), EDGE + atoms_here, EDGE, 0, next_ref)

    lane = iota((tok_here, lanes), 1)
    token = lane // (heads * GROUP) * GROUP + lane % GROUP
    first, last = bounds(device_at, token, lanes)
    lane_head = iota((rows, lanes), 1) // GROUP % heads
    row_head = iota((rows, lanes), 0) // Q_WIN
    same_head = (lane_head == row_head).astype(F32).astype(BF16)
    own_head = (iota((rows, width), 1) // head_dim == iota((rows, width), 0) // Q_WIN)
    own_head = own_head.astype(F32).astype(BF16)
    channel_head = iota((Q_WIN, 2 * width), 1) % width // head_dim
    ones = jnp.ones((K_WIN, width), BF16)
    scaling = LOG2E / math.sqrt(head_dim)

    @pl.loop(0, windows)
    def _(window):
        start = pl.multiple_of(window * Q_WIN, Q_WIN)
        position = iota((Q_WIN, lanes), 0) + start
        hot = ((first <= position) & (position < last)).astype(F32).astype(BF16)
        pick = jnp.concatenate([hot] * heads, 0) * same_head
        bias = lax.dot_general(
            pick, near_ref[pl.ds(start, K_WIN), :], LAST, preferred_element_type=F32
        )
        key_at = iota((rows, K_WIN), 1) + (device_at * atoms_here + start - EDGE)
        bias = jnp.where((key_at >= 0) & (key_at < ends), bias * LOG2E, MASKED)
        for sample in range(samples):
            query = query_ref[sample, pl.ds(start, Q_WIN), :]
            query = jnp.concatenate([query] * heads, 0) * own_head
            keys = key_ref[sample, pl.ds(start, K_WIN), :]
            values = value_ref[sample, pl.ds(start, K_WIN), :]
            scores = lax.dot_general(query, keys, LAST, preferred_element_type=F32)
            scores = scores * scaling + bias
            raised = jnp.exp2(scores - jnp.max(scores, axis=-1, keepdims=True)).astype(BF16)
            mixed = dot(raised, jnp.concatenate([values, ones], 1))
            picked = mixed[:Q_WIN]
            for head in range(1, heads):
                picked = jnp.where(
                    channel_head == head, mixed[head * Q_WIN : (head + 1) * Q_WIN], picked
                )
            attended = picked[:, :width] / picked[:, width:]
            gate = gate_ref[sample, pl.ds(start, Q_WIN), :]
            gated_ref[sample, pl.ds(start, Q_WIN), :] = (gate * attended).astype(BF16)

    for sample in range(samples):
        mixed = dot(gated_ref[sample], w_out_ref[...])
        out_ref[sample] = (open_ref[...] * mixed + trans_ref[sample]).astype(BF16)


def shards(
    atom_single,
    atom_cond,
    pair_cond,
    atom_counts,
    ada_attn_scale,
    ada_attn_shift,
    w_query,
    w_key,
    w_value,
    w_gate,
    w_out,
    attn_gate,
    w_pair,
    ada_trans_scale,
    ada_trans_shift,
    w_swish,
    w_linear,
    w_down,
    trans_gate,
):
    device_at = lax.axis_index("atoms")
    blocks = lax.axis_size("atoms")
    samples, atoms_here, width = atom_single.shape
    tok_here = atom_counts.shape[1]
    heads = w_pair.shape[1]
    groups = tok_here // GROUP
    rows_pair = pair_cond.shape[0] // tok_here
    at = device_at.astype(jnp.int32).reshape(1)

    def edge(cut):
        return jnp.concatenate([atom_single[:, cut], atom_cond[None, cut]], 0)

    edges = jnp.stack([edge(slice(0, EDGE)), edge(slice(atoms_here - EDGE, atoms_here))])
    edges = lax.all_gather(edges, "atoms")
    tiles = pair_bias(pair_cond, w_pair, tok_here)
    tiles = lax.all_gather(tiles, ("pair", "atoms"))

    weights = (
        ada_attn_scale,
        ada_attn_shift,
        w_query,
        w_key,
        w_value,
        w_gate,
        attn_gate,
        ada_trans_scale,
        ada_trans_shift,
        w_swish,
        w_linear,
        w_down,
        trans_gate,
    )
    whole = lambda array: pl.BlockSpec(array.shape, lambda i, at: (0,) * array.ndim)
    spot = (1, 1, samples + 1, EDGE, width)
    ext = atoms_here + 2 * EDGE
    shapes = [
        jax.ShapeDtypeStruct((samples, atoms_here, width), BF16),
        jax.ShapeDtypeStruct((samples, ext, width), BF16),
        jax.ShapeDtypeStruct((samples, ext, width), BF16),
        jax.ShapeDtypeStruct((samples, atoms_here, width), F32),
        jax.ShapeDtypeStruct((atoms_here, width), F32),
        jax.ShapeDtypeStruct((samples, atoms_here, width), F32),
    ]
    projected = pl.pallas_call(
        project_kernel_at,
        grid_spec=pltpu.PrefetchScalarGridSpec(
            num_scalar_prefetch=1,
            grid=(1,),
            in_specs=[
                whole(atom_single),
                whole(atom_cond),
                pl.BlockSpec(spot, lambda i, at: (jnp.maximum(at[0] - 1, 0), 1, 0, 0, 0)),
                pl.BlockSpec(spot, lambda i, at: (jnp.minimum(at[0] + 1, blocks - 1), 0, 0, 0, 0)),
            ]
            + [whole(weight) for weight in weights],
            out_specs=[whole(shape) for shape in shapes],
        ),
        out_shape=shapes,
        compiler_params=pltpu.CompilerParams(vmem_limit_bytes=40 << 20),
        cost_estimate=pl.CostEstimate(
            flops=samples * atoms_here * width * width * 24,
            bytes_accessed=4 << 20,
            transcendentals=0,
        ),
    )(at, atom_single, atom_cond, edges, edges, *weights)

    tile_spot = (1, 1, groups, tok_here, heads * GROUP)

    def tile_at(shift):
        def index(i, at):
            column = jnp.clip(at[0] + shift, 0, blocks - 1)
            return at[0] // rows_pair * blocks + column, at[0] % rows_pair, 0, 0, 0

        return pl.BlockSpec(tile_spot, index)

    return pl.pallas_call(
        functools.partial(attend_kernel, heads, blocks),
        grid_spec=pltpu.PrefetchScalarGridSpec(
            num_scalar_prefetch=1,
            grid=(1,),
            in_specs=[whole(shape) for shape in shapes]
            + [whole(atom_counts), tile_at(-1), tile_at(0), tile_at(1), whole(w_out)],
            out_specs=whole(shapes[0]),
            scratch_shapes=[
                pltpu.VMEM((ext, heads * tok_here), BF16),
                pltpu.VMEM((samples, atoms_here, width), BF16),
            ],
        ),
        out_shape=shapes[0],
        compiler_params=pltpu.CompilerParams(vmem_limit_bytes=40 << 20),
        cost_estimate=pl.CostEstimate(
            flops=samples * atoms_here * width * width * 12,
            bytes_accessed=4 << 20,
            transcendentals=0,
        ),
    )(at, *projected, atom_counts, tiles, tiles, tiles, w_out)


def project_kernel_at(at_ref, *refs):
    project_kernel(*refs)


def solution(mesh):
    return jax.shard_map(
        shards,
        mesh=mesh,
        in_specs=(
            P(("groups", "pair", "samp"), "atoms", None),
            P(("groups", "atoms"), None),
            P(("groups", "pair"), "atoms", None),
            P("groups", None),
        )
        + (P(),) * 15,
        out_specs=P(("groups", "pair", "samp"), "atoms", None),
        check_vma=False,
    )
```

```python
import functools
import math

import jax
import jax.numpy as jnp
from jax import lax
from jax.experimental import pallas as pl
from jax.experimental.pallas import tpu as pltpu
from jax.sharding import PartitionSpec as P

Q_WIN = 32
K_WIN = 128
EDGE = 48
GROUP = 32

EPSILON = 1e-05
MASKED = -1e30
LOG2E = math.log2(math.e)
BF16 = jnp.bfloat16
F32 = jnp.float32
LAST = (((1,), (1,)), ((), ()))
VMEM_LIMIT = 62 << 20


def dot(a, b):
    return jnp.dot(a, b, preferred_element_type=F32)


def iota(shape, dim):
    return lax.broadcasted_iota(jnp.int32, shape, dim)


def centring(width):
    same = iota((width, width), 0) == iota((width, width), 1)
    return jnp.where(same, 1.0 - 1.0 / width, -1.0 / width).astype(BF16)


def averaging(width):
    return jnp.full((width, width), 1.0 / width, BF16)


def layer_norm(rows):
    width = rows.shape[-1]
    centred = dot(rows, centring(width))
    variance = dot((centred * centred).astype(BF16), averaging(width))
    return centred * lax.rsqrt(variance + EPSILON)


def sigmoid(values):
    return 1.0 / (1.0 + jnp.exp2(values * -LOG2E))


def pair_kernel(heads, pair_ref, w_pair_ref, out_ref):
    group, cols, width = pair_ref.shape
    half = group // 2
    lanes = heads * group
    centre = centring(width)
    blank = jnp.zeros((width, width), BF16)
    centre2 = jnp.concatenate(
        [jnp.concatenate([centre, blank], 1), jnp.concatenate([blank, centre], 1)], 0
    )
    spread = (iota((heads, lanes), 1) // group == iota((heads, lanes), 0)).astype(BF16)
    weight = dot(w_pair_ref[...], spread).astype(BF16)
    blank = jnp.zeros((width, lanes), BF16)
    mean = jnp.full((width, lanes), 1.0 / width, BF16)
    mix = jnp.concatenate(
        [jnp.concatenate([weight, blank], 1), jnp.concatenate([blank, mean], 1)], 0
    )
    pair = pair_ref[...]
    both = jnp.concatenate(
        [pair[:half].reshape(half * cols, width), pair[half:].reshape(half * cols, width)], 1
    )
    centred = dot(both, centre2)
    rounded = centred.astype(BF16)
    squares = (centred * centred).astype(BF16)
    slot = iota((cols, 2 * lanes), 1) % group
    total = jnp.zeros((cols, 2 * lanes), F32)
    for part in range(2):
        cut = slice(part * width, (part + 1) * width)
        mixed = dot(jnp.concatenate([rounded[:, cut], squares[:, cut]], 1), mix)
        mixed = mixed.reshape(half, cols, 2 * lanes)
        for index in range(half):
            total = jnp.where(slot == part * half + index, mixed[index], total)
    out_ref[0, 0] = (total[:, :lanes] * lax.rsqrt(total[:, lanes:] + EPSILON)).astype(BF16)


def pair_bias(pair_cond, w_pair, tok_here):
    rows, cols, width = pair_cond.shape
    heads = w_pair.shape[1]
    groups = tok_here // GROUP
    return pl.pallas_call(
        functools.partial(pair_kernel, heads),
        grid=(rows // GROUP,),
        in_specs=[
            pl.BlockSpec((GROUP, cols, width), lambda i: (i, 0, 0)),
            pl.BlockSpec((width, heads), lambda i: (0, 0)),
        ],
        out_specs=pl.BlockSpec(
            (1, 1, cols, heads * GROUP), lambda i: (i // groups, i % groups, 0, 0)
        ),
        out_shape=jax.ShapeDtypeStruct(
            (rows // tok_here, groups, cols, heads * GROUP), BF16
        ),
        compiler_params=pltpu.CompilerParams(vmem_limit_bytes=VMEM_LIMIT),
        cost_estimate=pl.CostEstimate(
            flops=rows * cols * width * width * 4,
            bytes_accessed=rows * cols * width * 2,
            transcendentals=0,
        ),
    )(pair_cond, w_pair)


def project_kernel(
    single_ref,
    cond_ref,
    edge_prev_ref,
    edge_next_ref,
    ada_attn_scale,
    ada_attn_shift,
    w_query,
    w_key,
    w_value,
    w_gate,
    attn_gate,
    ada_trans_scale,
    ada_trans_shift,
    w_swish,
    w_linear,
    w_down,
    trans_gate,
    query_ref,
    key_ref,
    value_ref,
    gate_ref,
    open_ref,
    trans_ref,
):
    samples, atoms_here, width = single_ref.shape
    hidden_width = w_swish.shape[1]
    step = 128

    def attn_norm(cond, single):
        ada = dot(cond, jnp.concatenate([ada_attn_scale[...], ada_attn_shift[...]], 1))
        scale, shift = sigmoid(ada[:, :width])[None], ada[None, :, width:]
        rows = single.shape[1]
        return (scale * single.reshape(samples, rows, width) + shift).astype(BF16)

    def keys_values(normed):
        both = dot(
            normed.reshape(-1, width), jnp.concatenate([w_key[...], w_value[...]], 1)
        ).astype(BF16)
        both = both.reshape(samples, -1, 2 * width)
        return both[:, :, :width], both[:, :, width:]

    for place, edge_ref in ((0, edge_prev_ref), (EDGE + atoms_here, edge_next_ref)):
        edge = edge_ref[...].reshape(samples + 1, EDGE, width)
        normal = layer_norm(edge.reshape(-1, width)).reshape(samples + 1, EDGE, width)
        keys, values = keys_values(
            attn_norm(normal[samples].astype(BF16), normal[:samples])
        )
        key_ref[:, place : place + EDGE, :] = keys
        value_ref[:, place : place + EDGE, :] = values

    @pl.loop(0, atoms_here // step)
    def _(turn):
        start = pl.multiple_of(turn * step, step)
        at = pl.ds(start, step)
        cond = layer_norm(cond_ref[at, :]).astype(BF16)
        single = layer_norm(single_ref[:, at, :].reshape(-1, width))
        single = single.reshape(samples, step, width)
        normed = attn_norm(cond, single)
        keys, values = keys_values(normed)
        at_ext = pl.ds(pl.multiple_of(start + EDGE, 16), step)
        key_ref[:, at_ext, :] = keys
        value_ref[:, at_ext, :] = values
        both = dot(
            normed.reshape(-1, width), jnp.concatenate([w_query[...], w_gate[...]], 1)
        ).reshape(samples, step, 2 * width)
        query_ref[:, at, :] = both[:, :, :width].astype(BF16)
        gate_ref[:, at, :] = sigmoid(both[:, :, width:])
        gates = dot(cond, jnp.concatenate([attn_gate[...], trans_gate[...]], 1))
        open_ref[at, :] = sigmoid(gates[:, :width])
        ada = dot(cond, jnp.concatenate([ada_trans_scale[...], ada_trans_shift[...]], 1))
        normed_trans = (sigmoid(ada[:, :width])[None] * single + ada[None, :, width:]).astype(BF16)
        flat = normed_trans.reshape(-1, width)
        swish = dot(flat, w_swish[...])
        hidden = (swish * sigmoid(swish) * dot(flat, w_linear[...])).astype(BF16)
        down = dot(hidden, w_down[...]).reshape(samples, step, width)
        trans_ref[:, at, :] = sigmoid(gates[:, width:])[None] * down


def attend_kernel(
    heads,
    blocks,
    at_ref,
    query_ref,
    key_ref,
    value_ref,
    gate_ref,
    open_ref,
    trans_ref,
    counts_ref,
    prev_ref,
    own_ref,
    next_ref,
    w_out_ref,
    out_ref,
    near_ref,
    gated_ref,
):
    samples, atoms_here, width = query_ref.shape
    tok_here = counts_ref.shape[1]
    head_dim = width // heads
    windows = atoms_here // Q_WIN
    lanes = heads * tok_here
    rows = heads * Q_WIN
    device_at = at_ref[0]
    ends = atoms_here * blocks

    def bounds(block, token, reach):
        counts = counts_ref[pl.ds(block, 1), :].astype(F32).astype(BF16)
        counts = jnp.broadcast_to(counts, (8, tok_here))
        before = iota((tok_here, reach), 0)
        first = dot(counts, (before < token).astype(BF16))[:1]
        last = dot(counts, (before <= token).astype(BF16))[:1]
        return first.astype(jnp.int32), last.astype(jnp.int32)

    def expand(block, place, count, offset, tile_ref):
        token = iota((tok_here, tok_here), 1)
        first, last = bounds(block, token, tok_here)
        position = iota((count, tok_here), 0) + offset
        hot = ((first <= position) & (position < last)).astype(F32).astype(BF16)
        tile = tile_ref[...].reshape(tok_here // GROUP, tok_here, heads * GROUP)
        tile = jnp.concatenate([tile[index] for index in range(tok_here // GROUP)], 1)
        near_ref[place : place + count, :] = dot(hot, tile).astype(BF16)

    expand(jnp.maximum(device_at - 1, 0), 0, EDGE, atoms_here - EDGE, prev_ref)
    expand(device_at, EDGE, atoms_here, 0, own_ref)
    expand(jnp.minimum(device_at + 1, blocks - 1), EDGE + atoms_here, EDGE, 0, next_ref)

    lane = iota((tok_here, lanes), 1)
    token = lane // (heads * GROUP) * GROUP + lane % GROUP
    first, last = bounds(device_at, token, lanes)
    lane_head = iota((rows, lanes), 1) // GROUP % heads
    row_head = iota((rows, lanes), 0) // Q_WIN
    same_head = (lane_head == row_head).astype(F32).astype(BF16)
    own_head = (iota((rows, width), 1) // head_dim == iota((rows, width), 0) // Q_WIN)
    own_head = own_head.astype(F32).astype(BF16)
    channel_head = iota((Q_WIN, 2 * width), 1) % width // head_dim
    ones = jnp.ones((K_WIN, width), BF16)
    scaling = LOG2E / math.sqrt(head_dim)

    batch = math.gcd(windows, 4)

    @pl.loop(0, windows // batch)
    def _(turn):
        starts = [pl.multiple_of((turn * batch + i) * Q_WIN, Q_WIN) for i in range(batch)]
        biases = []
        for start in starts:
            position = iota((Q_WIN, lanes), 0) + start
            hot = ((first <= position) & (position < last)).astype(F32).astype(BF16)
            pick = jnp.concatenate([hot] * heads, 0) * same_head
            bias = lax.dot_general(
                pick, near_ref[pl.ds(start, K_WIN), :], LAST, preferred_element_type=F32
            )
            key_at = iota((rows, K_WIN), 1) + (device_at * atoms_here + start - EDGE)
            biases.append(jnp.where((key_at >= 0) & (key_at < ends), bias * LOG2E, MASKED))
        units = [(sample, i) for i in range(batch) for sample in range(samples)]
        scores = []
        for sample, i in units:
            query = query_ref[sample, pl.ds(starts[i], Q_WIN), :]
            query = jnp.concatenate([query] * heads, 0) * own_head
            keys = key_ref[sample, pl.ds(starts[i], K_WIN), :]
            product = lax.dot_general(query, keys, LAST, preferred_element_type=F32)
            scores.append(product * scaling + biases[i])
        tops = [jnp.max(score, axis=-1, keepdims=True) for score in scores]
        raised = [jnp.exp2(score - top).astype(BF16) for score, top in zip(scores, tops)]
        for (sample, i), weight in zip(units, raised):
            values = value_ref[sample, pl.ds(starts[i], K_WIN), :]
            mixed = dot(weight, jnp.concatenate([values, ones], 1))
            picked = mixed[:Q_WIN]
            for head in range(1, heads):
                picked = jnp.where(
                    channel_head == head, mixed[head * Q_WIN : (head + 1) * Q_WIN], picked
                )
            attended = picked[:, :width] / picked[:, width:]
            gate = gate_ref[sample, pl.ds(starts[i], Q_WIN), :]
            gated_ref[sample, pl.ds(starts[i], Q_WIN), :] = (gate * attended).astype(BF16)

    for sample in range(samples):
        mixed = dot(gated_ref[sample], w_out_ref[...])
        out_ref[sample] = (open_ref[...] * mixed + trans_ref[sample]).astype(BF16)


def shards(
    atom_single,
    atom_cond,
    pair_cond,
    atom_counts,
    ada_attn_scale,
    ada_attn_shift,
    w_query,
    w_key,
    w_value,
    w_gate,
    w_out,
    attn_gate,
    w_pair,
    ada_trans_scale,
    ada_trans_shift,
    w_swish,
    w_linear,
    w_down,
    trans_gate,
):
    device_at = lax.axis_index("atoms")
    blocks = lax.axis_size("atoms")
    samples, atoms_here, width = atom_single.shape
    tok_here = atom_counts.shape[1]
    heads = w_pair.shape[1]
    groups = tok_here // GROUP
    rows_pair = pair_cond.shape[0] // tok_here
    at = device_at.astype(jnp.int32).reshape(1)

    def edge(cut):
        return jnp.concatenate([atom_single[:, cut], atom_cond[None, cut]], 0)

    head, tail = edge(slice(0, EDGE)), edge(slice(atoms_here - EDGE, atoms_here))
    above = (jnp.arange(blocks) < device_at)[:, None, None, None]
    edges = lax.all_to_all(jnp.where(above, head[None], tail[None]), "atoms", 0, 0)
    tiles = pair_bias(pair_cond, w_pair, tok_here)
    tiles = jnp.tile(tiles, (lax.axis_size("pair") * blocks // rows_pair, 1, 1, 1))
    tiles = lax.all_to_all(tiles, ("pair", "atoms"), 0, 0)

    weights = (
        ada_attn_scale,
        ada_attn_shift,
        w_query,
        w_key,
        w_value,
        w_gate,
        attn_gate,
        ada_trans_scale,
        ada_trans_shift,
        w_swish,
        w_linear,
        w_down,
        trans_gate,
    )
    whole = lambda array: pl.BlockSpec(array.shape, lambda i, at: (0,) * array.ndim)
    spot = (1, samples + 1, EDGE, width)
    ext = atoms_here + 2 * EDGE
    shapes = [
        jax.ShapeDtypeStruct((samples, atoms_here, width), BF16),
        jax.ShapeDtypeStruct((samples, ext, width), BF16),
        jax.ShapeDtypeStruct((samples, ext, width), BF16),
        jax.ShapeDtypeStruct((samples, atoms_here, width), F32),
        jax.ShapeDtypeStruct((atoms_here, width), F32),
        jax.ShapeDtypeStruct((samples, atoms_here, width), F32),
    ]
    projected = pl.pallas_call(
        project_kernel_at,
        grid_spec=pltpu.PrefetchScalarGridSpec(
            num_scalar_prefetch=1,
            grid=(1,),
            in_specs=[
                whole(atom_single),
                whole(atom_cond),
                pl.BlockSpec(spot, lambda i, at: (jnp.maximum(at[0] - 1, 0), 0, 0, 0)),
                pl.BlockSpec(spot, lambda i, at: (jnp.minimum(at[0] + 1, blocks - 1), 0, 0, 0)),
            ]
            + [whole(weight) for weight in weights],
            out_specs=[whole(shape) for shape in shapes],
        ),
        out_shape=shapes,
        compiler_params=pltpu.CompilerParams(vmem_limit_bytes=VMEM_LIMIT),
        cost_estimate=pl.CostEstimate(
            flops=samples * atoms_here * width * width * 24,
            bytes_accessed=4 << 20,
            transcendentals=0,
        ),
    )(at, atom_single, atom_cond, edges, edges, *weights)

    tile_spot = (1, groups, tok_here, heads * GROUP)

    def tile_at(shift):
        def index(i, at):
            column = jnp.clip(at[0] + shift, 0, blocks - 1)
            return at[0] // rows_pair * blocks + column, 0, 0, 0

        return pl.BlockSpec(tile_spot, index)

    return pl.pallas_call(
        functools.partial(attend_kernel, heads, blocks),
        grid_spec=pltpu.PrefetchScalarGridSpec(
            num_scalar_prefetch=1,
            grid=(1,),
            in_specs=[whole(shape) for shape in shapes]
            + [whole(atom_counts), tile_at(-1), tile_at(0), tile_at(1), whole(w_out)],
            out_specs=whole(shapes[0]),
            scratch_shapes=[
                pltpu.VMEM((ext, heads * tok_here), BF16),
                pltpu.VMEM((samples, atoms_here, width), BF16),
            ],
        ),
        out_shape=shapes[0],
        compiler_params=pltpu.CompilerParams(vmem_limit_bytes=VMEM_LIMIT),
        cost_estimate=pl.CostEstimate(
            flops=samples * atoms_here * width * width * 12,
            bytes_accessed=4 << 20,
            transcendentals=0,
        ),
    )(at, *projected, atom_counts, tiles, tiles, tiles, w_out)


def project_kernel_at(at_ref, *refs):
    project_kernel(*refs)


def solution(mesh):
    return jax.shard_map(
        shards,
        mesh=mesh,
        in_specs=(
            P(("groups", "pair", "samp"), "atoms", None),
            P(("groups", "atoms"), None),
            P(("groups", "pair"), "atoms", None),
            P("groups", None),
        )
        + (P(),) * 15,
        out_specs=P(("groups", "pair", "samp"), "atoms", None),
        check_vma=False,
    )
```

```python
import functools
import math

import jax
import jax.numpy as jnp
from jax import lax
from jax.experimental import pallas as pl
from jax.experimental.pallas import tpu as pltpu
from jax.sharding import PartitionSpec as P

Q_WIN = 32
K_WIN = 128
EDGE = 48
GROUP = 32

EPSILON = 1e-05
MASKED = -1e30
LOG2E = math.log2(math.e)
BF16 = jnp.bfloat16
F32 = jnp.float32
LAST = (((1,), (1,)), ((), ()))
VMEM_LIMIT = 32 << 20
IN_VMEM = pl.BlockSpec(memory_space=pltpu.VMEM)
IN_HBM = pl.BlockSpec(memory_space=pltpu.HBM)
IN_SMEM = pl.BlockSpec(memory_space=pltpu.SMEM)


def dot(a, b):
    return jnp.dot(a, b, preferred_element_type=F32)


def iota(shape, dim):
    return lax.broadcasted_iota(jnp.int32, shape, dim)


def twice(matrix):
    blank = jnp.zeros_like(matrix)
    return jnp.concatenate(
        [jnp.concatenate([matrix, blank], 1), jnp.concatenate([blank, matrix], 1)], 0
    )


def side_by_side(rows):
    half = rows.shape[0] // 2
    return jnp.concatenate([rows[:half], rows[half:]], 1)


def centring(width):
    same = iota((width, width), 0) == iota((width, width), 1)
    return jnp.where(same, 1.0 - 1.0 / width, -1.0 / width).astype(BF16)


def averaging(width):
    return jnp.full((width, width), 1.0 / width, BF16)


def layer_norm(rows):
    width = rows.shape[1]
    centred = dot(side_by_side(rows), twice(centring(width)))
    variance = dot((centred * centred).astype(BF16), twice(averaging(width)))
    normal = centred * lax.rsqrt(variance + EPSILON)
    return jnp.concatenate([normal[:, :width], normal[:, width:]], 0)


def sigmoid(values):
    return pl.reciprocal(1.0 + jnp.exp2(values * -LOG2E), approx=True)


def attn_norm(cond, single, ada):
    width = single.shape[-1]
    mixed = dot(cond, ada)
    return (sigmoid(mixed[:, :width])[None] * single + mixed[None, :, width:]).astype(BF16)


def pair_kernel(
    tok_here,
    blocks,
    packing,
    at_ref,
    w_pair_ref,
    pair_hbm,
    single_hbm,
    cond_hbm,
    *refs,
):
    count = sum(len(names) for names in packing)
    weights_hbm, refs = refs[:count], refs[count:]
    tiles_ref, edges_hbm, single_ref, cond_ref = refs[:4]
    packed_refs, refs = refs[4 : 4 + len(packing)], refs[4 + len(packing) :]
    pair_ref, pair_sem, sem = refs
    rows, cols, width = pair_ref.shape
    heads = w_pair_ref.shape[0]
    samples, atoms_here, _ = single_ref.shape
    group = GROUP
    chunks = rows // group
    half = group // 2
    lanes = heads * group
    device_at = at_ref[0]

    pair_copies = [
        pltpu.make_async_copy(
            pair_hbm.at[pl.ds(i * group, group)],
            pair_ref.at[pl.ds(i * group, group)],
            pair_sem.at[i],
        )
        for i in range(chunks)
    ]
    for copy in pair_copies:
        copy.start()
    moves = [(single_hbm, single_ref), (cond_hbm, cond_ref)]
    for place, cut in (
        (jnp.maximum(device_at - 1, 0), pl.ds(0, EDGE)),
        (jnp.minimum(device_at + 1, blocks - 1), pl.ds(atoms_here - EDGE, EDGE)),
    ):
        moves.append((single_hbm.at[:, cut], edges_hbm.at[place, pl.ds(0, samples)]))
        moves.append((cond_hbm.at[cut], edges_hbm.at[place, samples]))
    index = 0
    for names, packed in zip(packing, packed_refs):
        offset = 0
        for _ in names:
            source = weights_hbm[index]
            span = source.shape[1]
            moves.append((source, packed.at[:, pl.ds(offset, span)]))
            offset += span
            index += 1
    copies = [
        pltpu.make_async_copy(source, target, sem.at[i])
        for i, (source, target) in enumerate(moves)
    ]
    for copy in copies:
        copy.start()

    centre = twice(centring(width))
    w_pair = w_pair_ref[...].astype(F32)
    spread = jnp.concatenate(
        [jnp.broadcast_to(w_pair[h : h + 1], (group, width)) for h in range(heads)], 0
    )
    weight = spread.T.astype(BF16)
    mean = jnp.full((width, lanes), 1.0 / width, BF16)
    blank = jnp.zeros((width, lanes), BF16)
    mix = jnp.concatenate(
        [jnp.concatenate([weight, blank], 1), jnp.concatenate([blank, mean], 1)], 0
    )
    slot = iota((cols, 2 * lanes), 1) % group
    per_block = tok_here // group
    owners = rows // tok_here
    for chunk in range(chunks):
        pair_copies[chunk].wait()
        pair = pair_ref[chunk * group : (chunk + 1) * group].reshape(group * cols, width)
        centred = dot(side_by_side(pair), centre)
        rounded = centred.astype(BF16)
        squares = (centred * centred).astype(BF16)
        total = jnp.zeros((cols, 2 * lanes), F32)
        for part in range(2):
            cut = slice(part * width, (part + 1) * width)
            mixed = dot(jnp.concatenate([rounded[:, cut], squares[:, cut]], 1), mix)
            mixed = mixed.reshape(half, cols, 2 * lanes)
            for i in range(half):
                total = jnp.where(slot == part * half + i, mixed[i], total)
        bias = (total[:, :lanes] * lax.rsqrt(total[:, lanes:] + EPSILON)).astype(BF16)
        owner, part = divmod(chunk, per_block)
        for target in range(owner, tiles_ref.shape[0], owners):
            tiles_ref[target, part] = bias
    for copy in copies:
        copy.wait()


def project_kernel(
    single_ref,
    cond_ref,
    ada_attn,
    ada_trans,
    gates_ref,
    w_kv,
    w_qg,
    w_up,
    w_down,
    query_ref,
    key_ref,
    value_ref,
    gate_ref,
    open_ref,
    trans_ref,
):
    samples, atoms_here, width = single_ref.shape
    hidden_width = w_down.shape[0]
    step = math.gcd(atoms_here, 256)
    for start in range(0, atoms_here, step):
        at = slice(start, start + step)
        cond = layer_norm(cond_ref[at, :]).astype(BF16)
        single = layer_norm(single_ref[:, at, :].reshape(-1, width))
        single = single.reshape(samples, step, width)
        normed = attn_norm(cond, single, ada_attn[...]).reshape(-1, width)
        both = dot(normed, w_kv[...]).astype(BF16).reshape(samples, step, 2 * width)
        key_ref[:, at, :] = both[:, :, :width]
        value_ref[:, at, :] = both[:, :, width:]
        both = dot(normed, w_qg[...]).reshape(samples, step, 2 * width)
        query_ref[:, at, :] = both[:, :, :width].astype(BF16)
        gate_ref[:, at, :] = sigmoid(both[:, :, width:])
        gates = dot(cond, gates_ref[...])
        open_ref[at, :] = sigmoid(gates[:, :width])
        normed = attn_norm(cond, single, ada_trans[...]).reshape(-1, width)
        swish = dot(normed, w_up[:, :hidden_width])
        hidden = (swish * sigmoid(swish) * dot(normed, w_up[:, hidden_width:])).astype(BF16)
        down = dot(hidden, w_down[...]).reshape(samples, step, width)
        trans_ref[:, at, :] = sigmoid(gates[:, width:])[None] * down


def attend_kernel(
    heads,
    blocks,
    owners,
    at_ref,
    counts_ref,
    query_ref,
    own_key_ref,
    own_value_ref,
    gate_ref,
    open_ref,
    trans_ref,
    ada_attn,
    w_kv,
    w_out_ref,
    edges_hbm,
    tiles_hbm,
    out_ref,
    key_ref,
    value_ref,
    near_ref,
    gated_ref,
    edges_ref,
    tiles_ref,
    sem,
):
    samples, atoms_here, width = query_ref.shape
    tok_here = counts_ref.shape[1]
    head_dim = width // heads
    windows = atoms_here // Q_WIN
    lanes = heads * tok_here
    rows = heads * Q_WIN
    device_at = at_ref[0]
    ends = atoms_here * blocks
    around = [jnp.maximum(device_at - 1, 0), device_at, jnp.minimum(device_at + 1, blocks - 1)]

    copies = [
        pltpu.make_async_copy(edges_hbm.at[place], edges_ref.at[side], sem.at[side])
        for side, place in enumerate((around[0], around[2]))
    ]
    for i, place in enumerate(around):
        source = tiles_hbm.at[device_at // owners * blocks + place]
        copies.append(pltpu.make_async_copy(source, tiles_ref.at[i], sem.at[2 + i]))
    for copy in copies:
        copy.start()

    key_ref[:, EDGE : EDGE + atoms_here, :] = own_key_ref[...]
    value_ref[:, EDGE : EDGE + atoms_here, :] = own_value_ref[...]

    def bounds(block, token, reach):
        counts = counts_ref[pl.ds(block, 1), :].astype(F32).astype(BF16)
        counts = jnp.broadcast_to(counts, (8, tok_here))
        before = iota((tok_here, reach), 0)
        first = dot(counts, (before < token).astype(BF16))[:1]
        last = dot(counts, (before <= token).astype(BF16))[:1]
        return first.astype(jnp.int32), last.astype(jnp.int32)

    def hot_rows(block, count, offset):
        token = iota((tok_here, tok_here), 1)
        first, last = bounds(block, token, tok_here)
        position = iota((count, tok_here), 0) + offset
        return ((first <= position) & (position < last)).astype(F32).astype(BF16)

    spans = ((0, EDGE, atoms_here - EDGE), (EDGE, atoms_here, 0), (EDGE + atoms_here, EDGE, 0))
    hots = [hot_rows(block, span[1], span[2]) for block, span in zip(around, spans)]

    copies[0].wait()
    copies[1].wait()
    normal = layer_norm(edges_ref[...].reshape(-1, width))
    normal = normal.reshape(2, samples + 1, EDGE, width)
    for side, place in enumerate((0, EDGE + atoms_here)):
        cond = normal[side, samples].astype(BF16)
        normed = attn_norm(cond, normal[side, :samples], ada_attn[...])
        both = dot(normed.reshape(-1, width), w_kv[...]).astype(BF16)
        both = both.reshape(samples, EDGE, 2 * width)
        key_ref[:, place : place + EDGE, :] = both[:, :, :width]
        value_ref[:, place : place + EDGE, :] = both[:, :, width:]

    for i, (place, count, _) in enumerate(spans):
        copies[2 + i].wait()
        tile = jnp.concatenate([tiles_ref[i, part] for part in range(tok_here // GROUP)], 1)
        near_ref[place : place + count, :] = dot(hots[i], tile).astype(BF16)

    lane = iota((tok_here, lanes), 1)
    token = lane // (heads * GROUP) * GROUP + lane % GROUP
    first, last = bounds(device_at, token, lanes)
    lane_head = iota((rows, lanes), 1) // GROUP % heads
    row_head = iota((rows, lanes), 0) // Q_WIN
    same_head = (lane_head == row_head).astype(F32).astype(BF16)
    own_head = (iota((rows, width), 1) // head_dim == iota((rows, width), 0) // Q_WIN)
    own_head = own_head.astype(F32).astype(BF16)
    channel_head = iota((Q_WIN, 2 * width), 1) % width // head_dim
    ones = jnp.ones((K_WIN, width), BF16)
    scaling = LOG2E / math.sqrt(head_dim)

    batch = math.gcd(windows, 4)

    @pl.loop(0, windows // batch)
    def _(turn):
        starts = [pl.multiple_of((turn * batch + i) * Q_WIN, Q_WIN) for i in range(batch)]
        biases = []
        for start in starts:
            position = iota((Q_WIN, lanes), 0) + start
            hot = ((first <= position) & (position < last)).astype(F32).astype(BF16)
            pick = jnp.concatenate([hot] * heads, 0) * same_head
            bias = lax.dot_general(
                pick, near_ref[pl.ds(start, K_WIN), :], LAST, preferred_element_type=F32
            )
            key_at = iota((rows, K_WIN), 1) + (device_at * atoms_here + start - EDGE)
            biases.append(jnp.where((key_at >= 0) & (key_at < ends), bias * LOG2E, MASKED))
        units = [(sample, i) for i in range(batch) for sample in range(samples)]
        scores = []
        for sample, i in units:
            query = query_ref[sample, pl.ds(starts[i], Q_WIN), :]
            query = jnp.concatenate([query] * heads, 0) * own_head
            keys = key_ref[sample, pl.ds(starts[i], K_WIN), :]
            product = lax.dot_general(query, keys, LAST, preferred_element_type=F32)
            scores.append(product * scaling + biases[i])
        tops = [jnp.max(score, axis=-1, keepdims=True) for score in scores]
        raised = [jnp.exp2(score - top).astype(BF16) for score, top in zip(scores, tops)]
        for (sample, i), weight in zip(units, raised):
            values = value_ref[sample, pl.ds(starts[i], K_WIN), :]
            mixed = dot(weight, jnp.concatenate([values, ones], 1))
            picked = mixed[:Q_WIN]
            for head in range(1, heads):
                picked = jnp.where(
                    channel_head == head, mixed[head * Q_WIN : (head + 1) * Q_WIN], picked
                )
            attended = picked[:, :width] * pl.reciprocal(picked[:, width:], approx=True)
            gate = gate_ref[sample, pl.ds(starts[i], Q_WIN), :]
            gated_ref[sample, pl.ds(starts[i], Q_WIN), :] = (gate * attended).astype(BF16)

    for sample in range(samples):
        mixed = dot(gated_ref[sample], w_out_ref[...])
        out_ref[sample] = (open_ref[...] * mixed + trans_ref[sample]).astype(BF16)


def shards(
    atom_single,
    atom_cond,
    pair_cond,
    atom_counts,
    ada_attn_scale,
    ada_attn_shift,
    w_query,
    w_key,
    w_value,
    w_gate,
    w_out,
    attn_gate,
    w_pair,
    ada_trans_scale,
    ada_trans_shift,
    w_swish,
    w_linear,
    w_down,
    trans_gate,
):
    device_at = lax.axis_index("atoms")
    blocks = lax.axis_size("atoms")
    samples, atoms_here, width = atom_single.shape
    tok_here = atom_counts.shape[1]
    heads = w_pair.shape[1]
    groups = tok_here // GROUP
    pairs = lax.axis_size("pair")
    rows_pair = pair_cond.shape[0] // tok_here
    at = device_at.astype(jnp.int32).reshape(1)
    in_hbm = lambda array: pltpu.with_memory_space_constraint(array, pltpu.HBM)
    in_vmem = lambda array: pltpu.with_memory_space_constraint(array, pltpu.VMEM)

    packing = (
        (ada_attn_scale, ada_attn_shift),
        (ada_trans_scale, ada_trans_shift),
        (attn_gate, trans_gate),
        (w_key, w_value),
        (w_query, w_gate),
        (w_swish, w_linear),
        (w_down,),
        (w_out,),
    )
    flat = [array for arrays in packing for array in arrays]
    rows, cols, _ = pair_cond.shape
    lanes = heads * GROUP
    shapes = [
        jax.ShapeDtypeStruct((pairs * blocks, groups, cols, lanes), BF16),
        pltpu.HBM((blocks, samples + 1, EDGE, width), BF16),
        pltpu.VMEM(atom_single.shape, BF16),
        pltpu.VMEM(atom_cond.shape, BF16),
    ] + [
        pltpu.VMEM((arrays[0].shape[0], sum(a.shape[1] for a in arrays)), BF16)
        for arrays in packing
    ]
    made = pl.pallas_call(
        functools.partial(pair_kernel, tok_here, blocks, [(0,) * len(a) for a in packing]),
        in_specs=[IN_SMEM, IN_VMEM] + [IN_HBM] * (3 + len(flat)),
        out_specs=[IN_VMEM, IN_HBM] + [IN_VMEM] * (2 + len(packing)),
        out_shape=shapes,
        scratch_shapes=[
            pltpu.VMEM(pair_cond.shape, BF16),
            pltpu.SemaphoreType.DMA((rows // GROUP,)),
            pltpu.SemaphoreType.DMA((6 + len(flat),)),
        ],
        compiler_params=pltpu.CompilerParams(vmem_limit_bytes=VMEM_LIMIT),
        cost_estimate=pl.CostEstimate(
            flops=rows * cols * width * width * 4,
            bytes_accessed=rows * cols * width * 2,
            transcendentals=0,
        ),
    )(at, w_pair.T, *map(in_hbm, (pair_cond, atom_single, atom_cond, *flat)))
    tiles, edges, single, cond, *packed = made
    ada_attn, ada_trans, gates, w_kv, w_qg, w_up, w_down, w_out = packed
    tiles = lax.all_to_all(tiles, ("pair", "atoms"), 0, 0)
    edges = lax.all_to_all(edges, "atoms", 0, 0)

    wide = (samples, atoms_here, width)
    shapes = [pltpu.VMEM(wide, BF16)] * 3 + [
        pltpu.VMEM(wide, F32),
        pltpu.VMEM((atoms_here, width), F32),
        pltpu.VMEM(wide, F32),
    ]
    operands = (single, cond, ada_attn, ada_trans, gates, w_kv, w_qg, w_up, w_down)
    projected = pl.pallas_call(
        project_kernel,
        in_specs=[IN_VMEM] * len(operands),
        out_specs=[IN_VMEM] * len(shapes),
        out_shape=shapes,
        compiler_params=pltpu.CompilerParams(vmem_limit_bytes=VMEM_LIMIT),
        cost_estimate=pl.CostEstimate(
            flops=samples * atoms_here * width * width * 24,
            bytes_accessed=4 << 20,
            transcendentals=0,
        ),
    )(*map(in_vmem, operands))

    ext = atoms_here + 2 * EDGE
    operands = (*projected, ada_attn, w_kv, w_out)
    return pl.pallas_call(
        functools.partial(attend_kernel, heads, blocks, rows_pair),
        in_specs=[IN_SMEM, IN_VMEM] + [IN_VMEM] * len(operands) + [IN_HBM] * 2,
        out_specs=IN_VMEM,
        out_shape=jax.ShapeDtypeStruct(wide, BF16),
        scratch_shapes=[
            pltpu.VMEM((samples, ext, width), BF16),
            pltpu.VMEM((samples, ext, width), BF16),
            pltpu.VMEM((ext, heads * tok_here), BF16),
            pltpu.VMEM(wide, BF16),
            pltpu.VMEM((2, samples + 1, EDGE, width), BF16),
            pltpu.VMEM((3, groups, cols, lanes), BF16),
            pltpu.SemaphoreType.DMA((5,)),
        ],
        compiler_params=pltpu.CompilerParams(vmem_limit_bytes=VMEM_LIMIT),
        cost_estimate=pl.CostEstimate(
            flops=samples * atoms_here * width * width * 12,
            bytes_accessed=4 << 20,
            transcendentals=0,
        ),
    )(at, atom_counts, *map(in_vmem, operands), in_hbm(edges), in_hbm(tiles))


def solution(mesh):
    return jax.shard_map(
        shards,
        mesh=mesh,
        in_specs=(
            P(("groups", "pair", "samp"), "atoms", None),
            P(("groups", "atoms"), None),
            P(("groups", "pair"), "atoms", None),
            P("groups", None),
        )
        + (P(),) * 15,
        out_specs=P(("groups", "pair", "samp"), "atoms", None),
        check_vma=False,
    )
```

```python
import functools
import math

import jax
import jax.numpy as jnp
from jax import lax
from jax.experimental import pallas as pl
from jax.experimental.pallas import tpu as pltpu
from jax.sharding import PartitionSpec as P

Q_WIN = 32
K_WIN = 128
EDGE = 48
GROUP = 32

EPSILON = 1e-05
MASKED = -1e30
LOG2E = math.log2(math.e)
BF16 = jnp.bfloat16
F32 = jnp.float32
LAST = (((1,), (1,)), ((), ()))
VMEM_LIMIT = 32 << 20
IN_VMEM = pl.BlockSpec(memory_space=pltpu.VMEM)
IN_HBM = pl.BlockSpec(memory_space=pltpu.HBM)
IN_SMEM = pl.BlockSpec(memory_space=pltpu.SMEM)


def dot(a, b):
    return jnp.dot(a, b, preferred_element_type=F32)


def iota(shape, dim):
    return lax.broadcasted_iota(jnp.int32, shape, dim)


def twice(matrix):
    blank = jnp.zeros_like(matrix)
    return jnp.concatenate(
        [jnp.concatenate([matrix, blank], 1), jnp.concatenate([blank, matrix], 1)], 0
    )


def side_by_side(rows):
    half = rows.shape[0] // 2
    return jnp.concatenate([rows[:half], rows[half:]], 1)


def centring(width):
    same = iota((width, width), 0) == iota((width, width), 1)
    return jnp.where(same, 1.0 - 1.0 / width, -1.0 / width).astype(BF16)


def averaging(width):
    return jnp.full((width, width), 1.0 / width, BF16)


def layer_norm(rows):
    width = rows.shape[1]
    centred = dot(side_by_side(rows), twice(centring(width)))
    variance = dot((centred * centred).astype(BF16), twice(averaging(width)))
    normal = centred * lax.rsqrt(variance + EPSILON)
    return jnp.concatenate([normal[:, :width], normal[:, width:]], 0)


def sigmoid(values):
    return pl.reciprocal(1.0 + jnp.exp2(values * -LOG2E), approx=True)


def attn_norm(cond, single, ada):
    width = single.shape[-1]
    mixed = dot(cond, ada)
    return (sigmoid(mixed[:, :width])[None] * single + mixed[None, :, width:]).astype(BF16)


def edge_kernel(
    blocks, at_ref, single_hbm, cond_hbm, w_pair_hbm, edges_hbm, mix_ref, w_pair_ref, sem
):
    samples, atoms_here, width = single_hbm.shape
    device_at = at_ref[0]
    copies = []
    for place, cut in (
        (jnp.maximum(device_at - 1, 0), pl.ds(0, EDGE)),
        (jnp.minimum(device_at + 1, blocks - 1), pl.ds(atoms_here - EDGE, EDGE)),
    ):
        for source, target in (
            (single_hbm.at[:, cut], edges_hbm.at[place, pl.ds(0, samples)]),
            (cond_hbm.at[cut], edges_hbm.at[place, samples]),
        ):
            copies.append(pltpu.make_async_copy(source, target, sem.at[len(copies)]))
    copies.append(pltpu.make_async_copy(w_pair_hbm, w_pair_ref, sem.at[len(copies)]))
    for copy in copies:
        copy.start()
    copies.pop().wait()
    heads = w_pair_ref.shape[0]
    w_pair = w_pair_ref[...].astype(F32)
    spread = jnp.concatenate(
        [jnp.broadcast_to(w_pair[h : h + 1], (GROUP, width)) for h in range(heads)], 0
    )
    weight = spread.T.astype(BF16)
    mean = jnp.full((width, heads * GROUP), 1.0 / width, BF16)
    blank = jnp.zeros((width, heads * GROUP), BF16)
    mix_ref[...] = jnp.concatenate(
        [jnp.concatenate([weight, blank], 1), jnp.concatenate([blank, mean], 1)], 0
    )
    for copy in copies:
        copy.wait()


def pair_kernel(
    tok_here,
    packing,
    mix_ref,
    pair_hbm,
    single_hbm,
    cond_hbm,
    *refs,
):
    count = sum(len(names) for names in packing)
    weights_hbm, refs = refs[:count], refs[count:]
    tiles_ref, single_ref, cond_ref = refs[:3]
    packed_refs, refs = refs[3 : 3 + len(packing)], refs[3 + len(packing) :]
    pair_ref, pair_sem, sem = refs
    rows, cols, width = pair_ref.shape
    group = GROUP
    chunks = rows // group
    half = group // 2
    lanes = mix_ref.shape[1] // 2

    def pair_copy(i):
        at = pl.ds(i * group, group)
        return pltpu.make_async_copy(pair_hbm.at[at], pair_ref.at[at], pair_sem.at[i])

    for i in range(chunks):
        pair_copy(i).start()
    moves = [(single_hbm, single_ref), (cond_hbm, cond_ref)]
    index = 0
    for names, packed in zip(packing, packed_refs):
        offset = 0
        for _ in names:
            source = weights_hbm[index]
            span = source.shape[1]
            moves.append((source, packed.at[:, pl.ds(offset, span)]))
            offset += span
            index += 1
    copies = [
        pltpu.make_async_copy(source, target, sem.at[i])
        for i, (source, target) in enumerate(moves)
    ]
    for copy in copies:
        copy.start()

    centre = twice(centring(width))
    slot = iota((cols, 2 * lanes), 1) % group
    per_block = tok_here // group
    owners = rows // tok_here

    @pl.loop(0, chunks)
    def _(chunk):
        pair_copy(chunk).wait()
        pair = pair_ref[pl.ds(chunk * group, group)].reshape(group * cols, width)
        centred = dot(side_by_side(pair), centre)
        rounded = centred.astype(BF16)
        squares = (centred * centred).astype(BF16)
        total = jnp.zeros((cols, 2 * lanes), F32)
        for part in range(2):
            cut = slice(part * width, (part + 1) * width)
            mixed = dot(jnp.concatenate([rounded[:, cut], squares[:, cut]], 1), mix_ref[...])
            mixed = mixed.reshape(half, cols, 2 * lanes)
            for i in range(half):
                total = jnp.where(slot == part * half + i, mixed[i], total)
        bias = (total[:, :lanes] * lax.rsqrt(total[:, lanes:] + EPSILON)).astype(BF16)
        for target in range(0, tiles_ref.shape[0], owners):
            tiles_ref[target + chunk // per_block, chunk % per_block] = bias

    for copy in copies:
        copy.wait()


def project_kernel(
    single_ref,
    cond_ref,
    ada_attn,
    ada_trans,
    gates_ref,
    w_kv,
    w_qg,
    w_up,
    w_down,
    query_ref,
    key_ref,
    value_ref,
    gate_ref,
    open_ref,
    trans_ref,
):
    samples, atoms_here, width = single_ref.shape
    hidden_width = w_down.shape[0]
    step = math.gcd(atoms_here, 256)
    for start in range(0, atoms_here, step):
        at = slice(start, start + step)
        cond = layer_norm(cond_ref[at, :]).astype(BF16)
        single = layer_norm(single_ref[:, at, :].reshape(-1, width))
        single = single.reshape(samples, step, width)
        normed = attn_norm(cond, single, ada_attn[...]).reshape(-1, width)
        both = dot(normed, w_kv[...]).astype(BF16).reshape(samples, step, 2 * width)
        key_ref[:, at, :] = both[:, :, :width]
        value_ref[:, at, :] = both[:, :, width:]
        both = dot(normed, w_qg[...]).reshape(samples, step, 2 * width)
        query_ref[:, at, :] = both[:, :, :width].astype(BF16)
        gate_ref[:, at, :] = sigmoid(both[:, :, width:]).astype(BF16)
        gates = dot(cond, gates_ref[...])
        open_ref[at, :] = sigmoid(gates[:, :width]).astype(BF16)
        normed = attn_norm(cond, single, ada_trans[...]).reshape(-1, width)
        swish = dot(normed, w_up[:, :hidden_width])
        hidden = (swish * sigmoid(swish) * dot(normed, w_up[:, hidden_width:])).astype(BF16)
        down = dot(hidden, w_down[...]).reshape(samples, step, width)
        trans_ref[:, at, :] = (sigmoid(gates[:, width:])[None] * down).astype(BF16)


def attend_kernel(
    heads,
    blocks,
    owners,
    at_ref,
    counts_ref,
    query_ref,
    own_key_ref,
    own_value_ref,
    gate_ref,
    open_ref,
    trans_ref,
    ada_attn,
    w_kv,
    w_out_ref,
    edges_ref,
    tiles_ref,
    out_ref,
    key_ref,
    value_ref,
    near_ref,
    gated_ref,
):
    samples, atoms_here, width = query_ref.shape
    tok_here = counts_ref.shape[1]
    head_dim = width // heads
    windows = atoms_here // Q_WIN
    lanes = heads * tok_here
    rows = heads * Q_WIN
    device_at = at_ref[0]
    ends = atoms_here * blocks
    around = [jnp.maximum(device_at - 1, 0), device_at, jnp.minimum(device_at + 1, blocks - 1)]

    key_ref[:, EDGE : EDGE + atoms_here, :] = own_key_ref[...]
    value_ref[:, EDGE : EDGE + atoms_here, :] = own_value_ref[...]

    def bounds(block, token, reach):
        counts = counts_ref[pl.ds(block, 1), :].astype(F32).astype(BF16)
        counts = jnp.broadcast_to(counts, (8, tok_here))
        before = iota((tok_here, reach), 0)
        first = dot(counts, (before < token).astype(BF16))[:1]
        last = dot(counts, (before <= token).astype(BF16))[:1]
        return first.astype(jnp.int32), last.astype(jnp.int32)

    def hot_rows(block, count, offset):
        token = iota((tok_here, tok_here), 1)
        first, last = bounds(block, token, tok_here)
        position = iota((count, tok_here), 0) + offset
        return ((first <= position) & (position < last)).astype(F32).astype(BF16)

    spans = ((0, EDGE, atoms_here - EDGE), (EDGE, atoms_here, 0), (EDGE + atoms_here, EDGE, 0))
    hots = [hot_rows(block, span[1], span[2]) for block, span in zip(around, spans)]

    edges = jnp.concatenate([edges_ref[around[0]], edges_ref[around[2]]], 0)
    normal = layer_norm(edges.reshape(-1, width))
    normal = normal.reshape(2, samples + 1, EDGE, width)
    for side, place in enumerate((0, EDGE + atoms_here)):
        cond = normal[side, samples].astype(BF16)
        normed = attn_norm(cond, normal[side, :samples], ada_attn[...])
        both = dot(normed.reshape(-1, width), w_kv[...]).astype(BF16)
        both = both.reshape(samples, EDGE, 2 * width)
        key_ref[:, place : place + EDGE, :] = both[:, :, :width]
        value_ref[:, place : place + EDGE, :] = both[:, :, width:]

    for i, (place, count, _) in enumerate(spans):
        place_from = device_at // owners * blocks + around[i]
        tile = jnp.concatenate(
            [tiles_ref[place_from, part] for part in range(tok_here // GROUP)], 1
        )
        near_ref[place : place + count, :] = dot(hots[i], tile).astype(BF16)

    lane = iota((tok_here, lanes), 1)
    token = lane // (heads * GROUP) * GROUP + lane % GROUP
    first, last = bounds(device_at, token, lanes)
    lane_head = iota((rows, lanes), 1) // GROUP % heads
    row_head = iota((rows, lanes), 0) // Q_WIN
    same_head = (lane_head == row_head).astype(F32).astype(BF16)
    own_head = (iota((rows, width), 1) // head_dim == iota((rows, width), 0) // Q_WIN)
    own_head = own_head.astype(F32).astype(BF16)
    channel_head = iota((Q_WIN, 2 * width), 1) % width // head_dim
    ones = jnp.ones((K_WIN, width), BF16)
    scaling = LOG2E / math.sqrt(head_dim)

    batch = math.gcd(windows, 4)

    @pl.loop(0, windows // batch)
    def _(turn):
        starts = [pl.multiple_of((turn * batch + i) * Q_WIN, Q_WIN) for i in range(batch)]
        biases = []
        for start in starts:
            position = iota((Q_WIN, lanes), 0) + start
            hot = ((first <= position) & (position < last)).astype(F32).astype(BF16)
            pick = jnp.concatenate([hot] * heads, 0) * same_head
            bias = lax.dot_general(
                pick, near_ref[pl.ds(start, K_WIN), :], LAST, preferred_element_type=F32
            )
            key_at = iota((rows, K_WIN), 1) + (device_at * atoms_here + start - EDGE)
            biases.append(jnp.where((key_at >= 0) & (key_at < ends), bias * LOG2E, MASKED))
        units = [(sample, i) for i in range(batch) for sample in range(samples)]
        scores = []
        for sample, i in units:
            query = query_ref[sample, pl.ds(starts[i], Q_WIN), :]
            query = jnp.concatenate([query] * heads, 0) * own_head
            keys = key_ref[sample, pl.ds(starts[i], K_WIN), :]
            product = lax.dot_general(query, keys, LAST, preferred_element_type=F32)
            scores.append(product * scaling + biases[i])
        tops = [jnp.max(score, axis=-1, keepdims=True) for score in scores]
        raised = [jnp.exp2(score - top).astype(BF16) for score, top in zip(scores, tops)]
        for (sample, i), weight in zip(units, raised):
            values = value_ref[sample, pl.ds(starts[i], K_WIN), :]
            mixed = dot(weight, jnp.concatenate([values, ones], 1))
            picked = mixed[:Q_WIN]
            for head in range(1, heads):
                picked = jnp.where(
                    channel_head == head, mixed[head * Q_WIN : (head + 1) * Q_WIN], picked
                )
            attended = picked[:, :width] * pl.reciprocal(picked[:, width:], approx=True)
            gate = gate_ref[sample, pl.ds(starts[i], Q_WIN), :].astype(F32)
            gated_ref[sample, pl.ds(starts[i], Q_WIN), :] = (gate * attended).astype(BF16)

    for sample in range(samples):
        mixed = dot(gated_ref[sample], w_out_ref[...])
        out_ref[sample] = (open_ref[...].astype(F32) * mixed + trans_ref[sample].astype(F32)).astype(BF16)


def shards(
    atom_single,
    atom_cond,
    pair_cond,
    atom_counts,
    ada_attn_scale,
    ada_attn_shift,
    w_query,
    w_key,
    w_value,
    w_gate,
    w_out,
    attn_gate,
    w_pair,
    ada_trans_scale,
    ada_trans_shift,
    w_swish,
    w_linear,
    w_down,
    trans_gate,
):
    device_at = lax.axis_index("atoms")
    blocks = lax.axis_size("atoms")
    samples, atoms_here, width = atom_single.shape
    tok_here = atom_counts.shape[1]
    heads = w_pair.shape[1]
    groups = tok_here // GROUP
    pairs = lax.axis_size("pair")
    rows_pair = pair_cond.shape[0] // tok_here
    at = device_at.astype(jnp.int32).reshape(1)
    in_hbm = lambda array: pltpu.with_memory_space_constraint(array, pltpu.HBM)
    in_vmem = lambda array: pltpu.with_memory_space_constraint(array, pltpu.VMEM)

    packing = (
        (ada_attn_scale, ada_attn_shift),
        (ada_trans_scale, ada_trans_shift),
        (attn_gate, trans_gate),
        (w_key, w_value),
        (w_query, w_gate),
        (w_swish, w_linear),
        (w_down,),
        (w_out,),
    )
    flat = [array for arrays in packing for array in arrays]
    rows, cols, _ = pair_cond.shape
    lanes = heads * GROUP
    shapes = [
        pltpu.VMEM((pairs * blocks, groups, cols, lanes), BF16),
        pltpu.VMEM(atom_single.shape, BF16),
        pltpu.VMEM(atom_cond.shape, BF16),
    ] + [
        pltpu.VMEM((arrays[0].shape[0], sum(a.shape[1] for a in arrays)), BF16)
        for arrays in packing
    ]
    edges, mix = pl.pallas_call(
        functools.partial(edge_kernel, blocks),
        in_specs=[IN_SMEM] + [IN_HBM] * 3,
        out_specs=[IN_HBM, IN_VMEM],
        out_shape=[
            pltpu.HBM((blocks, samples + 1, EDGE, width), BF16),
            pltpu.VMEM((2 * width, 2 * lanes), BF16),
        ],
        scratch_shapes=[pltpu.VMEM((heads, width), BF16), pltpu.SemaphoreType.DMA((5,))],
    )(at, *map(in_hbm, (atom_single, atom_cond, w_pair.T)))
    edges = lax.all_to_all(edges, "atoms", 0, 0)
    made = pl.pallas_call(
        functools.partial(pair_kernel, tok_here, [(0,) * len(a) for a in packing]),
        in_specs=[IN_VMEM] + [IN_HBM] * (3 + len(flat)),
        out_specs=[IN_VMEM] * (3 + len(packing)),
        out_shape=shapes,
        scratch_shapes=[
            pltpu.VMEM(pair_cond.shape, BF16),
            pltpu.SemaphoreType.DMA((rows // GROUP,)),
            pltpu.SemaphoreType.DMA((2 + len(flat),)),
        ],
        compiler_params=pltpu.CompilerParams(vmem_limit_bytes=VMEM_LIMIT),
        cost_estimate=pl.CostEstimate(
            flops=rows * cols * width * width * 4,
            bytes_accessed=rows * cols * width * 2,
            transcendentals=0,
        ),
    )(in_vmem(mix), *map(in_hbm, (pair_cond, atom_single, atom_cond, *flat)))
    tiles, single, cond, *packed = made
    ada_attn, ada_trans, gates, w_kv, w_qg, w_up, w_down, w_out = packed
    tiles = lax.all_to_all(tiles, ("pair", "atoms"), 0, 0)

    wide = (samples, atoms_here, width)
    shapes = [pltpu.VMEM(wide, BF16)] * 4 + [
        pltpu.VMEM((atoms_here, width), BF16),
        pltpu.VMEM(wide, BF16),
    ]
    operands = (single, cond, ada_attn, ada_trans, gates, w_kv, w_qg, w_up, w_down)
    projected = pl.pallas_call(
        project_kernel,
        in_specs=[IN_VMEM] * len(operands),
        out_specs=[IN_VMEM] * len(shapes),
        out_shape=shapes,
        input_output_aliases={0: 0, 1: 4},
        compiler_params=pltpu.CompilerParams(vmem_limit_bytes=VMEM_LIMIT),
        cost_estimate=pl.CostEstimate(
            flops=samples * atoms_here * width * width * 24,
            bytes_accessed=4 << 20,
            transcendentals=0,
        ),
    )(*map(in_vmem, operands))

    ext = atoms_here + 2 * EDGE
    operands = (*projected, ada_attn, w_kv, w_out, edges, tiles)
    return pl.pallas_call(
        functools.partial(attend_kernel, heads, blocks, rows_pair),
        in_specs=[IN_SMEM] + [IN_VMEM] * (1 + len(operands)),
        out_specs=IN_VMEM,
        out_shape=jax.ShapeDtypeStruct(wide, BF16),
        scratch_shapes=[
            pltpu.VMEM((samples, ext, width), BF16),
            pltpu.VMEM((samples, ext, width), BF16),
            pltpu.VMEM((ext, heads * tok_here), BF16),
            pltpu.VMEM(wide, BF16),
        ],
        compiler_params=pltpu.CompilerParams(vmem_limit_bytes=VMEM_LIMIT),
        cost_estimate=pl.CostEstimate(
            flops=samples * atoms_here * width * width * 12,
            bytes_accessed=4 << 20,
            transcendentals=0,
        ),
    )(at, atom_counts, *map(in_vmem, operands))


def solution(mesh):
    return jax.shard_map(
        shards,
        mesh=mesh,
        in_specs=(
            P(("groups", "pair", "samp"), "atoms", None),
            P(("groups", "atoms"), None),
            P(("groups", "pair"), "atoms", None),
            P("groups", None),
        )
        + (P(),) * 15,
        out_specs=P(("groups", "pair", "samp"), "atoms", None),
        check_vma=False,
    )
```

```python
import functools
import math

import jax
import jax.numpy as jnp
from jax import lax
from jax.experimental import pallas as pl
from jax.experimental.pallas import tpu as pltpu
from jax.sharding import PartitionSpec as P

Q_WIN = 32
K_WIN = 128
EDGE = 48
GROUP = 32

EPSILON = 1e-05
MASKED = -1e30
LOG2E = math.log2(math.e)
BF16 = jnp.bfloat16
F32 = jnp.float32
LAST = (((1,), (1,)), ((), ()))
VMEM_LIMIT = 32 << 20
IN_VMEM = pl.BlockSpec(memory_space=pltpu.VMEM)
IN_HBM = pl.BlockSpec(memory_space=pltpu.HBM)
IN_SMEM = pl.BlockSpec(memory_space=pltpu.SMEM)


def dot(a, b):
    return jnp.dot(a, b, preferred_element_type=F32)


def iota(shape, dim):
    return lax.broadcasted_iota(jnp.int32, shape, dim)


def twice(matrix):
    blank = jnp.zeros_like(matrix)
    return jnp.concatenate(
        [jnp.concatenate([matrix, blank], 1), jnp.concatenate([blank, matrix], 1)], 0
    )


def side_by_side(rows):
    half = rows.shape[0] // 2
    return jnp.concatenate([rows[:half], rows[half:]], 1)


def centring(width):
    same = iota((width, width), 0) == iota((width, width), 1)
    return jnp.where(same, 1.0 - 1.0 / width, -1.0 / width).astype(BF16)


def averaging(width):
    return jnp.full((width, width), 1.0 / width, BF16)


def layer_norm(rows):
    width = rows.shape[1]
    centred = dot(side_by_side(rows), twice(centring(width)))
    variance = dot((centred * centred).astype(BF16), twice(averaging(width)))
    normal = centred * lax.rsqrt(variance + EPSILON)
    return jnp.concatenate([normal[:, :width], normal[:, width:]], 0)


def sigmoid(values):
    return pl.reciprocal(1.0 + jnp.exp2(values * -LOG2E), approx=True)


def attn_norm(cond, single, ada):
    width = single.shape[-1]
    mixed = dot(cond, ada)
    return (sigmoid(mixed[:, :width])[None] * single + mixed[None, :, width:]).astype(BF16)


def pair_kernel(tok_here, packing, w_pair_hbm, pair_hbm, single_hbm, cond_hbm, *refs):
    count = sum(packing)
    weights_hbm, refs = refs[:count], refs[count:]
    tiles_ref, down_ref, up_ref, single_ref, cond_ref = refs[:5]
    packed_refs, refs = refs[5 : 5 + len(packing)], refs[5 + len(packing) :]
    w_pair_ref, pair_ref, pair_sem, sem = refs
    rows, cols, width = pair_ref.shape
    heads = w_pair_ref.shape[0]
    samples, atoms_here, _ = single_ref.shape
    group = GROUP
    lanes = heads * group
    half = group // 2
    pieces = rows // half

    def pair_copy(i):
        at = pl.ds(i * half, half)
        return pltpu.make_async_copy(pair_hbm.at[at], pair_ref.at[at], pair_sem.at[i])

    moves = [(w_pair_hbm, w_pair_ref), (single_hbm, single_ref), (cond_hbm, cond_ref)]
    for send_ref, start in ((down_ref, 0), (up_ref, atoms_here - EDGE)):
        cut = pl.ds(start, EDGE)
        for sample in range(samples):
            moves.append((single_hbm.at[sample, cut], send_ref.at[pl.ds(sample * EDGE, EDGE)]))
        moves.append((cond_hbm.at[cut], send_ref.at[pl.ds(samples * EDGE, EDGE)]))
    index = 0
    for number, packed in zip(packing, packed_refs):
        offset = 0
        for _ in range(number):
            source = weights_hbm[index]
            span = source.shape[1]
            moves.append((source, packed.at[:, pl.ds(offset, span)]))
            offset += span
            index += 1
    copies = [
        pltpu.make_async_copy(source, target, sem.at[i])
        for i, (source, target) in enumerate(moves)
    ]
    copies[0].start()
    for i in range(4):
        pair_copy(i).start()

    centre = twice(centring(width))
    copies[0].wait()
    w_pair = w_pair_ref[...].astype(F32)
    spread = jnp.concatenate(
        [jnp.broadcast_to(w_pair[h : h + 1], (group, width)) for h in range(heads)], 0
    )
    weight = spread.T.astype(BF16)
    mean = jnp.full((width, lanes), 1.0 / width, BF16)
    blank = jnp.zeros((width, lanes), BF16)
    mix = jnp.concatenate(
        [jnp.concatenate([weight, blank], 1), jnp.concatenate([blank, mean], 1)], 0
    )
    slot = iota((cols, 2 * lanes), 1) % group
    per_block = tok_here // group

    @pl.loop(0, rows // group)
    def _(chunk):
        for part in range(2):
            piece = chunk * 2 + part
            pair_copy(piece).wait()

            @pl.when(piece + 4 < pieces)
            def _():
                pair_copy(piece + 4).start()

        @pl.when(chunk == 0)
        def _():
            for copy in copies[1:]:
                copy.start()

        pair = pair_ref[pl.ds(chunk * group, group)].reshape(group * cols, width)
        centred = dot(side_by_side(pair), centre)
        rounded = centred.astype(BF16)
        squares = (centred * centred).astype(BF16)
        total = jnp.zeros((cols, 2 * lanes), F32)
        for part in range(2):
            cut = slice(part * width, (part + 1) * width)
            mixed = dot(jnp.concatenate([rounded[:, cut], squares[:, cut]], 1), mix)
            mixed = mixed.reshape(half, cols, 2 * lanes)
            for i in range(half):
                total = jnp.where(slot == part * half + i, mixed[i], total)
        bias = (total[:, :lanes] * lax.rsqrt(total[:, lanes:] + EPSILON)).astype(BF16)
        tiles_ref[chunk // per_block, chunk % per_block] = bias

    for copy in copies[1:]:
        copy.wait()


def transition_kernel(
    single_ref,
    cond_ref,
    ada_attn,
    ada_trans,
    gates_ref,
    w_up,
    w_down,
    normed_ref,
    open_ref,
    trans_ref,
):
    samples, atoms_here, width = single_ref.shape
    hidden_width = w_down.shape[0]
    step = math.gcd(atoms_here, 256)
    for start in range(0, atoms_here, step):
        at = slice(start, start + step)
        cond = layer_norm(cond_ref[at, :]).astype(BF16)
        single = layer_norm(single_ref[:, at, :].reshape(-1, width))
        single = single.reshape(samples, step, width)
        normed_ref[:, at, :] = attn_norm(cond, single, ada_attn[...])
        gates = dot(cond, gates_ref[...])
        open_ref[at, :] = sigmoid(gates[:, :width]).astype(BF16)
        normed = attn_norm(cond, single, ada_trans[...]).reshape(-1, width)
        swish = dot(normed, w_up[:, :hidden_width])
        hidden = (swish * sigmoid(swish) * dot(normed, w_up[:, hidden_width:])).astype(BF16)
        down = dot(hidden, w_down[...]).reshape(samples, step, width)
        trans_ref[:, at, :] = (sigmoid(gates[:, width:])[None] * down).astype(BF16)


def tile_of(own_ref, other_ref, pair_at, row_block):
    owners, groups, cols, lanes = own_ref.shape
    place, part = row_block // owners, row_block % owners
    other = other_ref[0, part] if other_ref.shape[0] == 1 else other_ref[place, part]
    return jnp.where(place == pair_at, own_ref[part], other)


def select_kernel(blocks, at_ref, pair_ref, own_ref, other_ref, down_in, up_in, _, down_ref, up_ref, __):
    del down_in, up_in
    _, groups, cols, lanes = own_ref.shape
    rows = groups * cols
    for send_ref, row_block in (
        (down_ref, jnp.maximum(at_ref[0] - 1, 0)),
        (up_ref, jnp.minimum(at_ref[0] + 1, blocks - 1)),
    ):
        tile = tile_of(own_ref, other_ref, pair_ref[0], row_block)
        send_ref[send_ref.shape[0] - rows :, :] = tile.reshape(rows, lanes)


def project_kernel(normed_ref, w_kv, w_qg, query_ref, key_ref, value_ref, gate_ref):
    samples, atoms_here, width = normed_ref.shape
    step = math.gcd(atoms_here, 256)
    for start in range(0, atoms_here, step):
        at = slice(start, start + step)
        normed = normed_ref[:, at, :].reshape(-1, width)
        both = dot(normed, w_kv[...]).astype(BF16).reshape(samples, step, 2 * width)
        key_ref[:, at, :] = both[:, :, :width]
        value_ref[:, at, :] = both[:, :, width:]
        both = dot(normed, w_qg[...]).reshape(samples, step, 2 * width)
        query_ref[:, at, :] = both[:, :, :width].astype(BF16)
        gate_ref[:, at, :] = sigmoid(both[:, :, width:]).astype(BF16)


def attend_kernel(
    heads,
    blocks,
    at_ref,
    pair_ref,
    counts_ref,
    query_ref,
    own_key_ref,
    own_value_ref,
    gate_ref,
    open_ref,
    trans_ref,
    ada_attn,
    w_kv,
    w_out_ref,
    own_ref,
    other_ref,
    prev_ref,
    next_ref,
    out_ref,
    key_ref,
    value_ref,
    near_ref,
    gated_ref,
):
    samples, atoms_here, width = query_ref.shape
    tok_here = counts_ref.shape[1]
    head_dim = width // heads
    windows = atoms_here // Q_WIN
    lanes = heads * tok_here
    rows = heads * Q_WIN
    device_at = at_ref[0]
    ends = atoms_here * blocks
    around = [jnp.maximum(device_at - 1, 0), device_at, jnp.minimum(device_at + 1, blocks - 1)]

    key_ref[:, EDGE : EDGE + atoms_here, :] = own_key_ref[...]
    value_ref[:, EDGE : EDGE + atoms_here, :] = own_value_ref[...]

    def bounds(block, token, reach):
        counts = counts_ref[pl.ds(block, 1), :].astype(F32).astype(BF16)
        counts = jnp.broadcast_to(counts, (8, tok_here))
        before = iota((tok_here, reach), 0)
        first = dot(counts, (before < token).astype(BF16))[:1]
        last = dot(counts, (before <= token).astype(BF16))[:1]
        return first.astype(jnp.int32), last.astype(jnp.int32)

    def hot_rows(block, count, offset):
        token = iota((tok_here, tok_here), 1)
        first, last = bounds(block, token, tok_here)
        position = iota((count, tok_here), 0) + offset
        return ((first <= position) & (position < last)).astype(F32).astype(BF16)

    spans = ((0, EDGE, atoms_here - EDGE), (EDGE, atoms_here, 0), (EDGE + atoms_here, EDGE, 0))
    hots = [hot_rows(block, span[1], span[2]) for block, span in zip(around, spans)]

    count = (samples + 1) * EDGE
    normal = layer_norm(jnp.concatenate([prev_ref[:count], next_ref[:count]], 0))
    normal = normal.reshape(2, samples + 1, EDGE, width)
    for side, place in enumerate((0, EDGE + atoms_here)):
        cond = normal[side, samples].astype(BF16)
        normed = attn_norm(cond, normal[side, :samples], ada_attn[...])
        both = dot(normed.reshape(-1, width), w_kv[...]).astype(BF16)
        both = both.reshape(samples, EDGE, 2 * width)
        key_ref[:, place : place + EDGE, :] = both[:, :, :width]
        value_ref[:, place : place + EDGE, :] = both[:, :, width:]

    held = tile_of(own_ref, other_ref, pair_ref[0], device_at)
    tiles = [prev_ref[count:], held, next_ref[count:]]
    for i, (place, count, _) in enumerate(spans):
        tile = tiles[i].reshape(tok_here // GROUP, tok_here, heads * GROUP)
        tile = jnp.concatenate([tile[part] for part in range(tok_here // GROUP)], 1)
        near_ref[place : place + count, :] = dot(hots[i], tile).astype(BF16)

    lane = iota((tok_here, lanes), 1)
    token = lane // (heads * GROUP) * GROUP + lane % GROUP
    first, last = bounds(device_at, token, lanes)
    lane_head = iota((rows, lanes), 1) // GROUP % heads
    row_head = iota((rows, lanes), 0) // Q_WIN
    same_head = (lane_head == row_head).astype(F32).astype(BF16)
    own_head = (iota((rows, width), 1) // head_dim == iota((rows, width), 0) // Q_WIN)
    own_head = own_head.astype(F32).astype(BF16)
    channel_head = iota((Q_WIN, 2 * width), 1) % width // head_dim
    ones = jnp.ones((K_WIN, width), BF16)
    scaling = LOG2E / math.sqrt(head_dim)

    batch = math.gcd(windows, 4)

    @pl.loop(0, windows // batch)
    def _(turn):
        starts = [pl.multiple_of((turn * batch + i) * Q_WIN, Q_WIN) for i in range(batch)]
        biases = []
        for start in starts:
            position = iota((Q_WIN, lanes), 0) + start
            hot = ((first <= position) & (position < last)).astype(F32).astype(BF16)
            pick = jnp.concatenate([hot] * heads, 0) * same_head
            bias = lax.dot_general(
                pick, near_ref[pl.ds(start, K_WIN), :], LAST, preferred_element_type=F32
            )
            key_at = iota((rows, K_WIN), 1) + (device_at * atoms_here + start - EDGE)
            biases.append(jnp.where((key_at >= 0) & (key_at < ends), bias * LOG2E, MASKED))
        units = [(sample, i) for i in range(batch) for sample in range(samples)]
        scores = []
        for sample, i in units:
            query = query_ref[sample, pl.ds(starts[i], Q_WIN), :]
            query = jnp.concatenate([query] * heads, 0) * own_head
            keys = key_ref[sample, pl.ds(starts[i], K_WIN), :]
            product = lax.dot_general(query, keys, LAST, preferred_element_type=F32)
            scores.append(product * scaling + biases[i])
        tops = [jnp.max(score, axis=-1, keepdims=True) for score in scores]
        raised = [jnp.exp2(score - top).astype(BF16) for score, top in zip(scores, tops)]
        for (sample, i), weight in zip(units, raised):
            values = value_ref[sample, pl.ds(starts[i], K_WIN), :]
            mixed = dot(weight, jnp.concatenate([values, ones], 1))
            picked = mixed[:Q_WIN]
            for head in range(1, heads):
                picked = jnp.where(
                    channel_head == head, mixed[head * Q_WIN : (head + 1) * Q_WIN], picked
                )
            attended = picked[:, :width] * pl.reciprocal(picked[:, width:], approx=True)
            gate = gate_ref[sample, pl.ds(starts[i], Q_WIN), :].astype(F32)
            gated_ref[sample, pl.ds(starts[i], Q_WIN), :] = (gate * attended).astype(BF16)

    for sample in range(samples):
        mixed = dot(gated_ref[sample], w_out_ref[...])
        out_ref[sample] = (open_ref[...].astype(F32) * mixed + trans_ref[sample].astype(F32)).astype(BF16)


def shards(
    atom_single,
    atom_cond,
    pair_cond,
    atom_counts,
    ada_attn_scale,
    ada_attn_shift,
    w_query,
    w_key,
    w_value,
    w_gate,
    w_out,
    attn_gate,
    w_pair,
    ada_trans_scale,
    ada_trans_shift,
    w_swish,
    w_linear,
    w_down,
    trans_gate,
):
    device_at = lax.axis_index("atoms")
    blocks = lax.axis_size("atoms")
    samples, atoms_here, width = atom_single.shape
    tok_here = atom_counts.shape[1]
    heads = w_pair.shape[1]
    groups = tok_here // GROUP
    pairs = lax.axis_size("pair")
    owners = pair_cond.shape[0] // tok_here
    at = device_at.astype(jnp.int32).reshape(1)
    pair_at = lax.axis_index("pair").astype(jnp.int32).reshape(1)
    in_hbm = lambda array: pltpu.with_memory_space_constraint(array, pltpu.HBM)
    in_vmem = lambda array: pltpu.with_memory_space_constraint(array, pltpu.VMEM)

    packing = (
        (ada_attn_scale, ada_attn_shift),
        (ada_trans_scale, ada_trans_shift),
        (attn_gate, trans_gate),
        (w_key, w_value),
        (w_query, w_gate),
        (w_swish, w_linear),
        (w_down,),
        (w_out,),
    )
    flat = [array for arrays in packing for array in arrays]
    rows, cols, _ = pair_cond.shape
    lanes = heads * GROUP
    wide = (samples, atoms_here, width)
    params = pltpu.CompilerParams(vmem_limit_bytes=VMEM_LIMIT)

    def cost(products):
        return pl.CostEstimate(flops=2 * products, bytes_accessed=4 << 20, transcendentals=0)

    sent = pltpu.VMEM(((samples + 1) * EDGE + groups * cols, lanes), BF16)
    shapes = [
        pltpu.VMEM((owners, groups, cols, lanes), BF16),
        sent,
        sent,
        pltpu.VMEM(wide, BF16),
        pltpu.VMEM(atom_cond.shape, BF16),
    ] + [
        pltpu.VMEM((arrays[0].shape[0], sum(a.shape[1] for a in arrays)), BF16)
        for arrays in packing
    ]
    made = pl.pallas_call(
        functools.partial(pair_kernel, tok_here, [len(arrays) for arrays in packing]),
        in_specs=[IN_HBM] * (4 + len(flat)),
        out_specs=[IN_VMEM] * len(shapes),
        out_shape=shapes,
        scratch_shapes=[
            pltpu.VMEM((heads, width), BF16),
            pltpu.VMEM(pair_cond.shape, BF16),
            pltpu.SemaphoreType.DMA((2 * rows // GROUP,)),
            pltpu.SemaphoreType.DMA((3 + 2 * (samples + 1) + len(flat),)),
        ],
        compiler_params=params,
        cost_estimate=cost(rows * cols * width * width * 2),
    )(*map(in_hbm, (w_pair.T, pair_cond, atom_single, atom_cond, *flat)))
    own, down, up, single, cond, *packed = made
    ada_attn, ada_trans, gates, w_kv, w_qg, w_up, w_down, w_out = packed
    if pairs == 2:
        other = lax.ppermute(own, "pair", [(0, 1), (1, 0)])[None]
    else:
        other = lax.all_gather(own, "pair")

    operands = (single, cond, ada_attn, ada_trans, gates, w_up, w_down)
    normed, opened, trans = pl.pallas_call(
        transition_kernel,
        in_specs=[IN_VMEM] * len(operands),
        out_specs=[IN_VMEM] * 3,
        out_shape=[
            pltpu.VMEM(wide, BF16),
            pltpu.VMEM((atoms_here, width), BF16),
            pltpu.VMEM(wide, BF16),
        ],
        compiler_params=params,
        cost_estimate=cost(samples * atoms_here * width * width * 10),
    )(*map(in_vmem, operands))

    operands = (own, other, down, up, normed)
    down, up, normed = pl.pallas_call(
        functools.partial(select_kernel, blocks),
        in_specs=[IN_SMEM] * 2 + [IN_VMEM] * len(operands),
        out_specs=[IN_VMEM] * 3,
        out_shape=[sent, sent, pltpu.VMEM(wide, BF16)],
        input_output_aliases={4: 0, 5: 1, 6: 2},
        compiler_params=params,
    )(at, pair_at, *map(in_vmem, operands))
    steps = range(blocks - 1)
    from_prev = lax.ppermute(up, "atoms", [(i, i + 1) for i in steps])
    from_next = lax.ppermute(down, "atoms", [(i + 1, i) for i in steps])

    operands = (normed, w_kv, w_qg)
    projected = pl.pallas_call(
        project_kernel,
        in_specs=[IN_VMEM] * len(operands),
        out_specs=[IN_VMEM] * 4,
        out_shape=[pltpu.VMEM(wide, BF16)] * 4,
        compiler_params=params,
        cost_estimate=cost(samples * atoms_here * width * width * 10),
    )(*map(in_vmem, operands))

    ext = atoms_here + 2 * EDGE
    operands = (*projected, opened, trans, ada_attn, w_kv, w_out, own, other, from_prev, from_next)
    return pl.pallas_call(
        functools.partial(attend_kernel, heads, blocks),
        in_specs=[IN_SMEM] * 2 + [IN_VMEM] * (1 + len(operands)),
        out_specs=IN_VMEM,
        out_shape=jax.ShapeDtypeStruct(wide, BF16),
        scratch_shapes=[
            pltpu.VMEM((samples, ext, width), BF16),
            pltpu.VMEM((samples, ext, width), BF16),
            pltpu.VMEM((ext, heads * tok_here), BF16),
            pltpu.VMEM(wide, BF16),
        ],
        compiler_params=params,
        cost_estimate=cost(samples * atoms_here * width * width * 12),
    )(at, pair_at, atom_counts, *map(in_vmem, operands))


def solution(mesh):
    return jax.shard_map(
        shards,
        mesh=mesh,
        in_specs=(
            P(("groups", "pair", "samp"), "atoms", None),
            P(("groups", "atoms"), None),
            P(("groups", "pair"), "atoms", None),
            P("groups", None),
        )
        + (P(),) * 15,
        out_specs=P(("groups", "pair", "samp"), "atoms", None),
        check_vma=False,
    )
```

```python
import functools
import math

import jax
import jax.numpy as jnp
from jax import lax
from jax.experimental import pallas as pl
from jax.experimental.pallas import tpu as pltpu
from jax.sharding import PartitionSpec as P

Q_WIN = 32
K_WIN = 128
EDGE = 48
GROUP = 32

EPSILON = 1e-05
MASKED = -1e30
LOG2E = math.log2(math.e)
BF16 = jnp.bfloat16
F32 = jnp.float32
LAST = (((1,), (1,)), ((), ()))
VMEM_LIMIT = 32 << 20
IN_VMEM = pl.BlockSpec(memory_space=pltpu.VMEM)
IN_HBM = pl.BlockSpec(memory_space=pltpu.HBM)
IN_SMEM = pl.BlockSpec(memory_space=pltpu.SMEM)


def dot(a, b):
    return jnp.dot(a, b, preferred_element_type=F32)


def iota(shape, dim):
    return lax.broadcasted_iota(jnp.int32, shape, dim)


def twice(matrix):
    blank = jnp.zeros_like(matrix)
    return jnp.concatenate(
        [jnp.concatenate([matrix, blank], 1), jnp.concatenate([blank, matrix], 1)], 0
    )


def side_by_side(rows):
    half = rows.shape[0] // 2
    return jnp.concatenate([rows[:half], rows[half:]], 1)


def centring(width):
    same = iota((width, width), 0) == iota((width, width), 1)
    return jnp.where(same, 1.0 - 1.0 / width, -1.0 / width).astype(BF16)


def averaging(width):
    return jnp.full((width, width), 1.0 / width, BF16)


def layer_norm(rows):
    width = rows.shape[1]
    centred = dot(side_by_side(rows), twice(centring(width)))
    variance = dot((centred * centred).astype(BF16), twice(averaging(width)))
    normal = centred * lax.rsqrt(variance + EPSILON)
    return jnp.concatenate([normal[:, :width], normal[:, width:]], 0)


def sigmoid(values):
    return pl.reciprocal(1.0 + jnp.exp2(values * -LOG2E), approx=True)


def attn_norm(cond, single, ada):
    width = single.shape[-1]
    mixed = dot(cond, ada)
    return (sigmoid(mixed[:, :width])[None] * single + mixed[None, :, width:]).astype(BF16)


def pair_kernel(tok_here, packing, at_ref, w_pair_hbm, pair_hbm, single_hbm, cond_hbm, *refs):
    count = sum(packing)
    weights_hbm, refs = refs[:count], refs[count:]
    tiles_ref, near_ref, far_ref, single_ref, cond_ref = refs[:5]
    packed_refs, refs = refs[5 : 5 + len(packing)], refs[5 + len(packing) :]
    w_pair_ref, pair_ref, pair_sem, sem = refs
    rows, cols, width = pair_ref.shape
    heads = w_pair_ref.shape[0]
    samples, atoms_here, _ = single_ref.shape
    group = GROUP
    lanes = heads * group
    half = group // 2
    pieces = rows // half

    def pair_copy(i):
        at = pl.ds(i * half, half)
        return pltpu.make_async_copy(pair_hbm.at[at], pair_ref.at[at], pair_sem.at[i])

    moves = [(w_pair_hbm, w_pair_ref), (single_hbm, single_ref), (cond_hbm, cond_ref)]
    for send_ref, parity in ((near_ref, 1), (far_ref, 0)):
        start = jnp.where(at_ref[0] % 2 == parity, 0, atoms_here - EDGE)
        cut = pl.ds(pl.multiple_of(start, 16), EDGE)
        for sample in range(samples):
            moves.append((single_hbm.at[sample, cut], send_ref.at[pl.ds(sample * EDGE, EDGE)]))
        moves.append((cond_hbm.at[cut], send_ref.at[pl.ds(samples * EDGE, EDGE)]))
    index = 0
    for number, packed in zip(packing, packed_refs):
        offset = 0
        for _ in range(number):
            source = weights_hbm[index]
            span = source.shape[1]
            moves.append((source, packed.at[:, pl.ds(offset, span)]))
            offset += span
            index += 1
    copies = [
        pltpu.make_async_copy(source, target, sem.at[i])
        for i, (source, target) in enumerate(moves)
    ]
    copies[0].start()
    for i in range(4):
        pair_copy(i).start()

    centre = twice(centring(width))
    copies[0].wait()
    w_pair = w_pair_ref[...].astype(F32)
    spread = jnp.concatenate(
        [jnp.broadcast_to(w_pair[h : h + 1], (group, width)) for h in range(heads)], 0
    )
    weight = spread.T.astype(BF16)
    mean = jnp.full((width, lanes), 1.0 / width, BF16)
    blank = jnp.zeros((width, lanes), BF16)
    mix = jnp.concatenate(
        [jnp.concatenate([weight, blank], 1), jnp.concatenate([blank, mean], 1)], 0
    )
    slot = iota((cols, 2 * lanes), 1) % group
    per_block = tok_here // group

    @pl.loop(0, rows // group)
    def _(chunk):
        for part in range(2):
            piece = chunk * 2 + part
            pair_copy(piece).wait()

            @pl.when(piece + 4 < pieces)
            def _():
                pair_copy(piece + 4).start()

        @pl.when(chunk == 0)
        def _():
            for copy in copies[1:]:
                copy.start()

        pair = pair_ref[pl.ds(chunk * group, group)].reshape(group * cols, width)
        centred = dot(side_by_side(pair), centre)
        rounded = centred.astype(BF16)
        squares = (centred * centred).astype(BF16)
        total = jnp.zeros((cols, 2 * lanes), F32)
        for part in range(2):
            cut = slice(part * width, (part + 1) * width)
            mixed = dot(jnp.concatenate([rounded[:, cut], squares[:, cut]], 1), mix)
            mixed = mixed.reshape(half, cols, 2 * lanes)
            for i in range(half):
                total = jnp.where(slot == part * half + i, mixed[i], total)
        bias = (total[:, :lanes] * lax.rsqrt(total[:, lanes:] + EPSILON)).astype(BF16)
        tiles_ref[chunk // per_block, chunk % per_block] = bias

    for copy in copies[1:]:
        copy.wait()


def project_kernel(
    single_ref,
    cond_ref,
    ada_attn,
    ada_trans,
    gates_ref,
    w_kv,
    w_qg,
    w_up,
    w_down,
    query_ref,
    key_ref,
    value_ref,
    gate_ref,
    open_ref,
    trans_ref,
):
    samples, atoms_here, width = single_ref.shape
    hidden_width = w_down.shape[0]
    step = math.gcd(atoms_here, 256)
    for start in range(0, atoms_here, step):
        at = slice(start, start + step)
        cond = layer_norm(cond_ref[at, :]).astype(BF16)
        single = layer_norm(single_ref[:, at, :].reshape(-1, width))
        single = single.reshape(samples, step, width)
        normed = attn_norm(cond, single, ada_attn[...]).reshape(-1, width)
        both = dot(normed, w_kv[...]).astype(BF16).reshape(samples, step, 2 * width)
        key_ref[:, at, :] = both[:, :, :width]
        value_ref[:, at, :] = both[:, :, width:]
        both = dot(normed, w_qg[...]).reshape(samples, step, 2 * width)
        query_ref[:, at, :] = both[:, :, :width].astype(BF16)
        gate_ref[:, at, :] = sigmoid(both[:, :, width:]).astype(BF16)
        gates = dot(cond, gates_ref[...])
        open_ref[at, :] = sigmoid(gates[:, :width]).astype(BF16)
        normed = attn_norm(cond, single, ada_trans[...]).reshape(-1, width)
        swish = dot(normed, w_up[:, :hidden_width])
        hidden = (swish * sigmoid(swish) * dot(normed, w_up[:, hidden_width:])).astype(BF16)
        down = dot(hidden, w_down[...]).reshape(samples, step, width)
        trans_ref[:, at, :] = (sigmoid(gates[:, width:])[None] * down).astype(BF16)


def tile_of(own_ref, other_ref, pair_at, row_block):
    owners, groups, cols, lanes = own_ref.shape
    place, part = row_block // owners, row_block % owners
    other = other_ref[0, part] if other_ref.shape[0] == 1 else other_ref[place, part]
    return jnp.where(place == pair_at, own_ref[part], other)


def select_kernel(blocks, at_ref, pair_ref, own_ref, other_ref, *refs):
    near_ref, far_ref, _, held_ref = refs[3:]
    groups, cols, lanes = own_ref.shape[1:]
    rows = groups * cols
    device_at, pair_at = at_ref[0], pair_ref[0]
    for send_ref, parity in ((near_ref, 0), (far_ref, 1)):
        beside = jnp.where(device_at % 2 == parity, device_at + 1, device_at - 1)
        tile = tile_of(own_ref, other_ref, pair_at, jnp.clip(beside, 0, blocks - 1))
        send_ref[send_ref.shape[0] - rows :, :] = tile.reshape(rows, lanes)
    held_ref[...] = tile_of(own_ref, other_ref, pair_at, device_at).reshape(rows, lanes)


def bounds(counts_ref, block, token):
    tok_here = counts_ref.shape[1]
    counts = counts_ref[pl.ds(block, 1), :].astype(F32).astype(BF16)
    counts = jnp.broadcast_to(counts, (8, tok_here))
    before = iota((tok_here, token.shape[1]), 0)
    first = dot(counts, (before < token).astype(BF16))[:1]
    last = dot(counts, (before <= token).astype(BF16))[:1]
    return first.astype(jnp.int32), last.astype(jnp.int32)


def one_hot(reach, offset, count):
    first, last = reach
    position = iota((count, first.shape[1]), 0) + offset
    return ((first <= position) & (position < last)).astype(F32).astype(BF16)


def expand(hot, tile, tok_here):
    tile = tile.reshape(tok_here // GROUP, tok_here, tile.shape[-1])
    tile = jnp.concatenate([tile[part] for part in range(tok_here // GROUP)], 1)
    return dot(hot, tile).astype(BF16)


def attend(heads, reach, windows, query_ref, gate_ref, gated_ref):
    samples, _, width = query_ref.shape
    head_dim = width // heads
    lanes = reach[0].shape[1]
    rows = heads * Q_WIN
    lane_head = iota((rows, lanes), 1) // GROUP % heads
    row_head = iota((rows, lanes), 0) // Q_WIN
    same_head = (lane_head == row_head).astype(F32).astype(BF16)
    own_head = iota((rows, width), 1) // head_dim == iota((rows, width), 0) // Q_WIN
    own_head = own_head.astype(F32).astype(BF16)
    channel_head = iota((Q_WIN, 2 * width), 1) % width // head_dim
    ones = jnp.ones((K_WIN, width), BF16)
    scaling = LOG2E / math.sqrt(head_dim)

    biases = []
    for start, _, near, mask in windows:
        pick = jnp.concatenate([one_hot(reach, start, Q_WIN)] * heads, 0) * same_head
        bias = lax.dot_general(pick, near, LAST, preferred_element_type=F32) * LOG2E
        biases.append(bias if mask is None else jnp.where(mask, bias, MASKED))
    units = [(sample, i) for i in range(len(windows)) for sample in range(samples)]
    scores = []
    for sample, i in units:
        query = query_ref[sample, pl.ds(windows[i][0], Q_WIN), :]
        query = jnp.concatenate([query] * heads, 0) * own_head
        keys = windows[i][1](sample)[0]
        product = lax.dot_general(query, keys, LAST, preferred_element_type=F32)
        scores.append(product * scaling + biases[i])
    tops = [jnp.max(score, axis=-1, keepdims=True) for score in scores]
    raised = [jnp.exp2(score - top).astype(BF16) for score, top in zip(scores, tops)]
    for (sample, i), weight in zip(units, raised):
        values = windows[i][1](sample)[1]
        mixed = dot(weight, jnp.concatenate([values, ones], 1))
        picked = mixed[:Q_WIN]
        for head in range(1, heads):
            picked = jnp.where(
                channel_head == head, mixed[head * Q_WIN : (head + 1) * Q_WIN], picked
            )
        attended = picked[:, :width] * pl.reciprocal(picked[:, width:], approx=True)
        at = pl.ds(windows[i][0], Q_WIN)
        gate = gate_ref[sample, at, :].astype(F32)
        gated_ref[sample, at, :] = (gate * attended).astype(BF16)


def close(sample, cut, gated_ref, open_ref, trans_ref, w_out_ref):
    mixed = dot(gated_ref[sample, cut, :], w_out_ref[...])
    opened, trans = open_ref[cut, :].astype(F32), trans_ref[sample, cut, :].astype(F32)
    return (opened * mixed + trans).astype(BF16)


def row_tokens(heads, tok_here):
    lane = iota((tok_here, heads * tok_here), 1)
    return lane // (heads * GROUP) * GROUP + lane % GROUP


def inner_kernel(
    heads,
    at_ref,
    counts_ref,
    query_ref,
    key_ref,
    value_ref,
    gate_ref,
    open_ref,
    trans_ref,
    w_out_ref,
    held_ref,
    out_ref,
    near_ref,
    gated_ref,
):
    samples, atoms_here, width = query_ref.shape
    tok_here = counts_ref.shape[1]
    device_at = at_ref[0]
    hot = one_hot(
        bounds(counts_ref, device_at, iota((tok_here, tok_here), 1)), 0, atoms_here
    )
    near_ref[...] = expand(hot, held_ref[...], tok_here)
    reach = bounds(counts_ref, device_at, row_tokens(heads, tok_here))
    skip = -(-EDGE // Q_WIN)
    inner = atoms_here // Q_WIN - 2 * skip
    batch = math.gcd(inner, 4)

    @pl.loop(0, inner // batch)
    def _(turn):
        windows = []
        for i in range(batch):
            start = pl.multiple_of((turn * batch + i + skip) * Q_WIN, Q_WIN)
            cut = pl.ds(pl.multiple_of(start - EDGE, 16), K_WIN)
            parts = lambda sample, cut=cut: (key_ref[sample, cut, :], value_ref[sample, cut, :])
            windows.append((start, parts, near_ref[cut, :], None))
        attend(heads, reach, windows, query_ref, gate_ref, gated_ref)

    cut = slice(skip * Q_WIN, atoms_here - skip * Q_WIN)
    for sample in range(samples):
        out_ref[sample] = close(sample, cut, gated_ref, open_ref, trans_ref, w_out_ref)


def outer_kernel(
    heads,
    blocks,
    at_ref,
    counts_ref,
    query_ref,
    own_key_ref,
    own_value_ref,
    gate_ref,
    open_ref,
    trans_ref,
    w_out_ref,
    held_ref,
    inner_ref,
    ada_attn,
    w_kv,
    first_ref,
    second_ref,
    out_hbm,
    key_ref,
    value_ref,
    near_ref,
    gated_ref,
    out_ref,
    sem,
):
    samples, atoms_here, width = query_ref.shape
    tok_here = counts_ref.shape[1]
    device_at = at_ref[0]
    ends = atoms_here * blocks
    skip = -(-EDGE // Q_WIN)
    margin = skip * Q_WIN
    reach_keys = key_ref.shape[2]
    inside = reach_keys - EDGE

    whole = pltpu.make_async_copy(
        inner_ref, out_hbm.at[:, pl.ds(margin, atoms_here - 2 * margin)], sem.at[0]
    )
    whole.start()

    even = device_at % 2 == 0
    first, second = first_ref[...], second_ref[...]
    arrived = (jnp.where(even, second, first), jnp.where(even, first, second))
    count = (samples + 1) * EDGE
    normal = layer_norm(jnp.concatenate([rows[:count] for rows in arrived], 0))
    normal = normal.reshape(2, samples + 1, EDGE, width)
    token = iota((tok_here, tok_here), 1)
    own_reach = bounds(counts_ref, device_at, token)
    sides = (
        (jnp.maximum(device_at - 1, 0), atoms_here - EDGE, 0, EDGE, 0),
        (jnp.minimum(device_at + 1, blocks - 1), 0, inside, 0, atoms_here - inside),
    )
    for side, (block, offset, place, own_place, own_start) in enumerate(sides):
        cond = normal[side, samples].astype(BF16)
        normed = attn_norm(cond, normal[side, :samples], ada_attn[...])
        both = dot(normed.reshape(-1, width), w_kv[...]).astype(BF16)
        both = both.reshape(samples, EDGE, 2 * width)
        for ref, own_ref, edge in (
            (key_ref, own_key_ref, both[:, :, :width]),
            (value_ref, own_value_ref, both[:, :, width:]),
        ):
            ref[side, :, place : place + EDGE, :] = edge
            ref[side, :, own_place : own_place + inside, :] = own_ref[
                :, own_start : own_start + inside, :
            ]
        hot = one_hot(bounds(counts_ref, block, token), offset, EDGE)
        near_ref[side, place : place + EDGE, :] = expand(hot, arrived[side][count:], tok_here)
        hot = one_hot(own_reach, own_start, inside)
        near_ref[side, own_place : own_place + inside, :] = expand(hot, held_ref[...], tok_here)

    reach = bounds(counts_ref, device_at, row_tokens(heads, tok_here))
    windows = []
    for side in range(2):
        for i in range(skip):
            start = i * Q_WIN + side * (atoms_here - margin)
            cut = slice(i * Q_WIN, i * Q_WIN + K_WIN)
            parts = lambda sample, side=side, cut=cut: (
                key_ref[side, sample, cut, :],
                value_ref[side, sample, cut, :],
            )
            key_at = iota((heads * Q_WIN, K_WIN), 1) + (device_at * atoms_here + start - EDGE)
            mask = (key_at >= 0) & (key_at < ends)
            windows.append((start, parts, near_ref[side, cut, :], mask))
    attend(heads, reach, windows, query_ref, gate_ref, gated_ref)
    copies = []
    for side in range(2):
        cut = slice(side * (atoms_here - margin), side * (atoms_here - margin) + margin)
        for sample in range(samples):
            out_ref[side, sample] = close(sample, cut, gated_ref, open_ref, trans_ref, w_out_ref)
        target = out_hbm.at[:, pl.ds(side * (atoms_here - margin), margin)]
        copies.append(pltpu.make_async_copy(out_ref.at[side], target, sem.at[1 + side]))
        copies[-1].start()
    for copy in copies:
        copy.wait()
    whole.wait()


def shards(
    atom_single,
    atom_cond,
    pair_cond,
    atom_counts,
    ada_attn_scale,
    ada_attn_shift,
    w_query,
    w_key,
    w_value,
    w_gate,
    w_out,
    attn_gate,
    w_pair,
    ada_trans_scale,
    ada_trans_shift,
    w_swish,
    w_linear,
    w_down,
    trans_gate,
):
    device_at = lax.axis_index("atoms")
    blocks = lax.axis_size("atoms")
    samples, atoms_here, width = atom_single.shape
    tok_here = atom_counts.shape[1]
    heads = w_pair.shape[1]
    groups = tok_here // GROUP
    pairs = lax.axis_size("pair")
    owners = pair_cond.shape[0] // tok_here
    at = device_at.astype(jnp.int32).reshape(1)
    pair_at = lax.axis_index("pair").astype(jnp.int32).reshape(1)
    in_hbm = lambda array: pltpu.with_memory_space_constraint(array, pltpu.HBM)
    in_vmem = lambda array: pltpu.with_memory_space_constraint(array, pltpu.VMEM)

    packing = (
        (ada_attn_scale, ada_attn_shift),
        (ada_trans_scale, ada_trans_shift),
        (attn_gate, trans_gate),
        (w_key, w_value),
        (w_query, w_gate),
        (w_swish, w_linear),
        (w_down,),
        (w_out,),
    )
    flat = [array for arrays in packing for array in arrays]
    rows, cols, _ = pair_cond.shape
    lanes = heads * GROUP
    wide = (samples, atoms_here, width)
    params = pltpu.CompilerParams(vmem_limit_bytes=VMEM_LIMIT)

    def cost(products):
        return pl.CostEstimate(flops=2 * products, bytes_accessed=4 << 20, transcendentals=0)

    sent = pltpu.VMEM(((samples + 1) * EDGE + groups * cols, lanes), BF16)
    shapes = [
        pltpu.VMEM((owners, groups, cols, lanes), BF16),
        sent,
        sent,
        pltpu.VMEM(wide, BF16),
        pltpu.VMEM(atom_cond.shape, BF16),
    ] + [
        pltpu.VMEM((arrays[0].shape[0], sum(a.shape[1] for a in arrays)), BF16)
        for arrays in packing
    ]
    made = pl.pallas_call(
        functools.partial(pair_kernel, tok_here, [len(arrays) for arrays in packing]),
        in_specs=[IN_SMEM] + [IN_HBM] * (4 + len(flat)),
        out_specs=[IN_VMEM] * len(shapes),
        out_shape=shapes,
        scratch_shapes=[
            pltpu.VMEM((heads, width), BF16),
            pltpu.VMEM(pair_cond.shape, BF16),
            pltpu.SemaphoreType.DMA((2 * rows // GROUP,)),
            pltpu.SemaphoreType.DMA((3 + 2 * (samples + 1) + len(flat),)),
        ],
        compiler_params=params,
        cost_estimate=cost(rows * cols * width * width * 2),
    )(at, *map(in_hbm, (w_pair.T, pair_cond, atom_single, atom_cond, *flat)))
    own, near, far, single, cond, *packed = made
    ada_attn, ada_trans, gates, w_kv, w_qg, w_up, w_down, w_out = packed
    if pairs == 2:
        other = lax.ppermute(own, "pair", [(0, 1), (1, 0)])[None]
    else:
        other = lax.all_gather(own, "pair")

    operands = (single, cond, ada_attn, ada_trans, gates, w_kv, w_qg, w_up, w_down)
    query, keys, values, gate, opened, trans = pl.pallas_call(
        project_kernel,
        in_specs=[IN_VMEM] * len(operands),
        out_specs=[IN_VMEM] * 6,
        out_shape=[pltpu.VMEM(wide, BF16)] * 4
        + [pltpu.VMEM((atoms_here, width), BF16), pltpu.VMEM(wide, BF16)],
        compiler_params=params,
        cost_estimate=cost(samples * atoms_here * width * width * 20),
    )(*map(in_vmem, operands))

    operands = (own, other, near, far, opened)
    near, far, opened, held = pl.pallas_call(
        functools.partial(select_kernel, blocks),
        in_specs=[IN_SMEM] * 2 + [IN_VMEM] * len(operands),
        out_specs=[IN_VMEM] * 4,
        out_shape=[
            sent,
            sent,
            pltpu.VMEM((atoms_here, width), BF16),
            pltpu.VMEM((groups * cols, lanes), BF16),
        ],
        input_output_aliases={4: 0, 5: 1, 6: 2},
        compiler_params=params,
    )(at, pair_at, *map(in_vmem, operands))

    def swap(value, start):
        sides = [(i, i + 1) for i in range(start, blocks - 1, 2)]
        return lax.ppermute(value, "atoms", sides + [(j, i) for i, j in sides])

    first, second = swap(near, 0), swap(far, 1)

    margin = -(-EDGE // Q_WIN) * Q_WIN
    operands = (query, keys, values, gate, opened, trans, w_out, held)
    inner = pl.pallas_call(
        functools.partial(inner_kernel, heads),
        in_specs=[IN_SMEM] + [IN_VMEM] * (1 + len(operands)),
        out_specs=IN_VMEM,
        out_shape=pltpu.VMEM((samples, atoms_here - 2 * margin, width), BF16),
        scratch_shapes=[
            pltpu.VMEM((atoms_here, heads * tok_here), BF16),
            pltpu.VMEM(wide, BF16),
        ],
        compiler_params=params,
        cost_estimate=cost(samples * atoms_here * width * width * 12),
    )(at, atom_counts, *map(in_vmem, operands))

    reach = margin - Q_WIN + K_WIN
    operands += (inner, ada_attn, w_kv, first, second)
    return pl.pallas_call(
        functools.partial(outer_kernel, heads, blocks),
        in_specs=[IN_SMEM] + [IN_VMEM] * (1 + len(operands)),
        out_specs=IN_HBM,
        out_shape=pltpu.HBM(wide, BF16),
        scratch_shapes=[
            pltpu.VMEM((2, samples, reach, width), BF16),
            pltpu.VMEM((2, samples, reach, width), BF16),
            pltpu.VMEM((2, reach, heads * tok_here), BF16),
            pltpu.VMEM(wide, BF16),
            pltpu.VMEM((2, samples, margin, width), BF16),
            pltpu.SemaphoreType.DMA((3,)),
        ],
        compiler_params=params,
        cost_estimate=cost(samples * atoms_here * width * width * 4),
    )(at, atom_counts, *map(in_vmem, operands))


def solution(mesh):
    return jax.shard_map(
        shards,
        mesh=mesh,
        in_specs=(
            P(("groups", "pair", "samp"), "atoms", None),
            P(("groups", "atoms"), None),
            P(("groups", "pair"), "atoms", None),
            P("groups", None),
        )
        + (P(),) * 15,
        out_specs=P(("groups", "pair", "samp"), "atoms", None),
        check_vma=False,
    )
```

```python
import functools
import math

import jax
import jax.numpy as jnp
from jax import lax
from jax.experimental import pallas as pl
from jax.experimental.pallas import tpu as pltpu
from jax.sharding import PartitionSpec as P

Q_WIN = 32
K_WIN = 128
EDGE = 48
GROUP = 32

EPSILON = 1e-05
MASKED = -1e30
LOG2E = math.log2(math.e)
BF16 = jnp.bfloat16
F32 = jnp.float32
LAST = (((1,), (1,)), ((), ()))
VMEM_LIMIT = 32 << 20
IN_VMEM = pl.BlockSpec(memory_space=pltpu.VMEM)
IN_HBM = pl.BlockSpec(memory_space=pltpu.HBM)
IN_SMEM = pl.BlockSpec(memory_space=pltpu.SMEM)


def dot(a, b):
    return jnp.dot(a, b, preferred_element_type=F32)


def iota(shape, dim):
    return lax.broadcasted_iota(jnp.int32, shape, dim)


def twice(matrix):
    blank = jnp.zeros_like(matrix)
    return jnp.concatenate(
        [jnp.concatenate([matrix, blank], 1), jnp.concatenate([blank, matrix], 1)], 0
    )


def side_by_side(rows):
    half = rows.shape[0] // 2
    return jnp.concatenate([rows[:half], rows[half:]], 1)


def centring(width):
    same = iota((width, width), 0) == iota((width, width), 1)
    return jnp.where(same, 1.0 - 1.0 / width, -1.0 / width).astype(BF16)


def averaging(width):
    return jnp.full((width, width), 1.0 / width, BF16)


def layer_norm(rows):
    width = rows.shape[1]
    centred = dot(side_by_side(rows), twice(centring(width)))
    variance = dot((centred * centred).astype(BF16), twice(averaging(width)))
    normal = centred * lax.rsqrt(variance + EPSILON)
    return jnp.concatenate([normal[:, :width], normal[:, width:]], 0)


def sigmoid(values):
    return pl.reciprocal(1.0 + jnp.exp2(values * -LOG2E), approx=True)


def attn_norm(cond, single, ada):
    width = single.shape[-1]
    mixed = dot(cond, ada)
    return (sigmoid(mixed[:, :width])[None] * single + mixed[None, :, width:]).astype(BF16)


def pair_kernel(packing, core_ref, w_pair_hbm, pair_hbm, single_hbm, cond_hbm, *refs):
    count = sum(packing)
    weights_hbm, refs = refs[:count], refs[count:]
    tile_ref, single_ref, cond_ref = refs[:3]
    packed_refs, refs = refs[3 : 3 + len(packing)], refs[3 + len(packing) :]
    w_pair_ref, pair_ref, pair_sem, sem = refs
    rows, cols, width = pair_ref.shape
    heads = w_pair_ref.shape[0]
    group = GROUP
    lanes = heads * group
    half = group // 2
    pieces = rows // half
    row_start = core_ref[0] * rows

    def pair_copy(i):
        source = pair_hbm.at[pl.ds(row_start + i * half, half)]
        return pltpu.make_async_copy(source, pair_ref.at[pl.ds(i * half, half)], pair_sem.at[i])

    moves = [(w_pair_hbm, w_pair_ref), (single_hbm, single_ref), (cond_hbm, cond_ref)]
    index = 0
    for number, packed in zip(packing, packed_refs):
        offset = 0
        for _ in range(number):
            source = weights_hbm[index]
            span = source.shape[1]
            moves.append((source, packed.at[:, pl.ds(offset, span)]))
            offset += span
            index += 1
    copies = [
        pltpu.make_async_copy(source, target, sem.at[i])
        for i, (source, target) in enumerate(moves)
    ]
    copies[0].start()
    for i in range(pieces):
        pair_copy(i).start()

    centre = twice(centring(width))
    copies[0].wait()
    w_pair = w_pair_ref[...].astype(F32)
    spread = jnp.concatenate(
        [jnp.broadcast_to(w_pair[h : h + 1], (group, width)) for h in range(heads)], 0
    )
    weight = spread.T.astype(BF16)
    mean = jnp.full((width, lanes), 1.0 / width, BF16)
    blank = jnp.zeros((width, lanes), BF16)
    mix = jnp.concatenate(
        [jnp.concatenate([weight, blank], 1), jnp.concatenate([blank, mean], 1)], 0
    )
    slot = iota((cols, 2 * lanes), 1) % group

    @pl.loop(0, rows // group)
    def _(chunk):
        for part in range(2):
            pair_copy(chunk * 2 + part).wait()

        @pl.when(chunk == 0)
        def _():
            for copy in copies[1:]:
                copy.start()

        pair = pair_ref[pl.ds(chunk * group, group)].reshape(group * cols, width)
        centred = dot(side_by_side(pair), centre)
        rounded = centred.astype(BF16)
        squares = (centred * centred).astype(BF16)
        total = jnp.zeros((cols, 2 * lanes), F32)
        for part in range(2):
            cut = slice(part * width, (part + 1) * width)
            mixed = dot(jnp.concatenate([rounded[:, cut], squares[:, cut]], 1), mix)
            mixed = mixed.reshape(half, cols, 2 * lanes)
            for i in range(half):
                total = jnp.where(slot == part * half + i, mixed[i], total)
        bias = (total[:, :lanes] * lax.rsqrt(total[:, lanes:] + EPSILON)).astype(BF16)
        tile_ref[chunk] = bias

    for copy in copies[1:]:
        copy.wait()


def project_kernel(
    at_ref,
    single_ref,
    cond_ref,
    ada_attn,
    ada_trans,
    gates_ref,
    w_kv,
    w_qg,
    w_up,
    w_down,
    query_ref,
    key_ref,
    value_ref,
    gate_ref,
    open_ref,
    trans_ref,
    near_ref,
    far_ref,
):
    samples, atoms_here, width = single_ref.shape
    hidden_width = w_down.shape[0]
    step = math.gcd(atoms_here, 256)
    for start in range(0, atoms_here, step):
        at = slice(start, start + step)
        cond = layer_norm(cond_ref[at, :]).astype(BF16)
        single = layer_norm(single_ref[:, at, :].reshape(-1, width))
        single = single.reshape(samples, step, width)
        normed = attn_norm(cond, single, ada_attn[...]).reshape(-1, width)
        both = dot(normed, w_kv[...]).astype(BF16).reshape(samples, step, 2 * width)
        key_ref[:, at, :] = both[:, :, :width]
        value_ref[:, at, :] = both[:, :, width:]
        both = dot(normed, w_qg[...]).reshape(samples, step, 2 * width)
        query_ref[:, at, :] = both[:, :, :width].astype(BF16)
        gate_ref[:, at, :] = sigmoid(both[:, :, width:]).astype(BF16)
        gates = dot(cond, gates_ref[...])
        open_ref[at, :] = sigmoid(gates[:, :width]).astype(BF16)
        normed = attn_norm(cond, single, ada_trans[...]).reshape(-1, width)
        swish = dot(normed, w_up[:, :hidden_width])
        hidden = (swish * sigmoid(swish) * dot(normed, w_up[:, hidden_width:])).astype(BF16)
        down = dot(hidden, w_down[...]).reshape(samples, step, width)
        trans_ref[:, at, :] = (sigmoid(gates[:, width:])[None] * down).astype(BF16)
    even = at_ref[0] % 2 == 0
    for i, ref in enumerate((key_ref, value_ref)):
        for sample in range(samples):
            head, tail = ref[sample, :EDGE, :], ref[sample, atoms_here - EDGE :, :]
            place = (2 * sample + i) * EDGE
            near_ref[place : place + EDGE, :] = jnp.where(even, tail, head)
            far_ref[place : place + EDGE, :] = jnp.where(even, head, tail)


def tile_of(refs, place, row_block):
    if len(refs) == 1:
        return refs[0][row_block]
    pair_at, core_at = place
    owners = 2
    mine, theirs, across, diagonal = [ref[...] for ref in refs]
    near = jnp.where(row_block % owners == core_at, mine, theirs)
    far = jnp.where(row_block % owners == core_at, across, diagonal)
    return jnp.where(row_block // owners == pair_at, near, far)


def select_kernel(blocks, at_ref, pair_ref, core_ref, *refs):
    *tile_refs, _, __, ___, near_ref, far_ref, ____, held_ref = refs
    groups, cols, lanes = tile_refs[0].shape[-3:]
    rows = groups * cols
    device_at, place = at_ref[0], (pair_ref[0], core_ref[0])
    for send_ref, parity in ((near_ref, 0), (far_ref, 1)):
        beside = jnp.where(device_at % 2 == parity, device_at + 1, device_at - 1)
        tile = tile_of(tile_refs, place, jnp.clip(beside, 0, blocks - 1))
        send_ref[send_ref.shape[0] - rows :, :] = tile.reshape(rows, lanes)
    held_ref[...] = tile_of(tile_refs, place, device_at).reshape(rows, lanes)


def bounds(counts_ref, block, token):
    tok_here = counts_ref.shape[1]
    counts = counts_ref[pl.ds(block, 1), :].astype(F32).astype(BF16)
    counts = jnp.broadcast_to(counts, (8, tok_here))
    before = iota((tok_here, token.shape[1]), 0)
    first = dot(counts, (before < token).astype(BF16))[:1]
    last = dot(counts, (before <= token).astype(BF16))[:1]
    return first.astype(jnp.int32), last.astype(jnp.int32)


def one_hot(reach, offset, count):
    first, last = reach
    position = iota((count, first.shape[1]), 0) + offset
    return ((first <= position) & (position < last)).astype(F32).astype(BF16)


def expand(hot, tile, tok_here):
    tile = tile.reshape(tok_here // GROUP, tok_here, tile.shape[-1])
    tile = jnp.concatenate([tile[part] for part in range(tok_here // GROUP)], 1)
    return dot(hot, tile).astype(BF16)


def attend(heads, reach, windows, query_ref, gate_ref, gated_ref):
    samples, _, width = query_ref.shape
    head_dim = width // heads
    lanes = reach[0].shape[1]
    rows = heads * Q_WIN
    lane_head = iota((rows, lanes), 1) // GROUP % heads
    row_head = iota((rows, lanes), 0) // Q_WIN
    same_head = (lane_head == row_head).astype(F32).astype(BF16)
    own_head = iota((rows, width), 1) // head_dim == iota((rows, width), 0) // Q_WIN
    own_head = own_head.astype(F32).astype(BF16)
    channel_head = iota((Q_WIN, 2 * width), 1) % width // head_dim
    ones = jnp.ones((K_WIN, width), BF16)
    scaling = LOG2E / math.sqrt(head_dim)

    biases = []
    for start, _, near, mask in windows:
        pick = jnp.concatenate([one_hot(reach, start, Q_WIN)] * heads, 0) * same_head
        bias = lax.dot_general(pick, near, LAST, preferred_element_type=F32) * LOG2E
        biases.append(bias if mask is None else jnp.where(mask, bias, MASKED))
    units = [(sample, i) for i in range(len(windows)) for sample in range(samples)]
    scores = []
    for sample, i in units:
        query = query_ref[sample, pl.ds(windows[i][0], Q_WIN), :]
        query = jnp.concatenate([query] * heads, 0) * own_head
        keys = windows[i][1](sample)[0]
        product = lax.dot_general(query, keys, LAST, preferred_element_type=F32)
        scores.append(product * scaling + biases[i])
    tops = [jnp.max(score, axis=-1, keepdims=True) for score in scores]
    raised = [jnp.exp2(score - top).astype(BF16) for score, top in zip(scores, tops)]
    for (sample, i), weight in zip(units, raised):
        values = windows[i][1](sample)[1]
        mixed = dot(weight, jnp.concatenate([values, ones], 1))
        picked = mixed[:Q_WIN]
        for head in range(1, heads):
            picked = jnp.where(
                channel_head == head, mixed[head * Q_WIN : (head + 1) * Q_WIN], picked
            )
        attended = picked[:, :width] * pl.reciprocal(picked[:, width:], approx=True)
        at = pl.ds(windows[i][0], Q_WIN)
        gate = gate_ref[sample, at, :].astype(F32)
        gated_ref[sample, at, :] = (gate * attended).astype(BF16)


def close(sample, cut, gated_ref, open_ref, trans_ref, w_out_ref):
    mixed = dot(gated_ref[sample, cut, :], w_out_ref[...])
    opened, trans = open_ref[cut, :].astype(F32), trans_ref[sample, cut, :].astype(F32)
    return (opened * mixed + trans).astype(BF16)


def row_tokens(heads, tok_here):
    lane = iota((tok_here, heads * tok_here), 1)
    return lane // (heads * GROUP) * GROUP + lane % GROUP


def inner_kernel(
    heads,
    at_ref,
    counts_ref,
    query_ref,
    key_ref,
    value_ref,
    gate_ref,
    open_ref,
    trans_ref,
    w_out_ref,
    held_ref,
    out_ref,
    near_ref,
    gated_ref,
):
    samples, atoms_here, width = query_ref.shape
    tok_here = counts_ref.shape[1]
    device_at = at_ref[0]
    hot = one_hot(
        bounds(counts_ref, device_at, iota((tok_here, tok_here), 1)), 0, atoms_here
    )
    near_ref[...] = expand(hot, held_ref[...], tok_here)
    reach = bounds(counts_ref, device_at, row_tokens(heads, tok_here))
    skip = -(-EDGE // Q_WIN)
    inner = atoms_here // Q_WIN - 2 * skip
    batch = math.gcd(inner, 4)

    @pl.loop(0, inner // batch)
    def _(turn):
        windows = []
        for i in range(batch):
            start = pl.multiple_of((turn * batch + i + skip) * Q_WIN, Q_WIN)
            cut = pl.ds(pl.multiple_of(start - EDGE, 16), K_WIN)
            parts = lambda sample, cut=cut: (key_ref[sample, cut, :], value_ref[sample, cut, :])
            windows.append((start, parts, near_ref[cut, :], None))
        attend(heads, reach, windows, query_ref, gate_ref, gated_ref)

    cut = slice(skip * Q_WIN, atoms_here - skip * Q_WIN)
    for sample in range(samples):
        out_ref[sample] = close(sample, cut, gated_ref, open_ref, trans_ref, w_out_ref)


def outer_kernel(
    heads,
    blocks,
    at_ref,
    counts_ref,
    query_ref,
    own_key_ref,
    own_value_ref,
    gate_ref,
    open_ref,
    trans_ref,
    w_out_ref,
    held_ref,
    inner_ref,
    first_ref,
    second_ref,
    out_hbm,
    key_ref,
    value_ref,
    near_ref,
    gated_ref,
    out_ref,
    sem,
):
    samples, atoms_here, width = query_ref.shape
    tok_here = counts_ref.shape[1]
    device_at = at_ref[0]
    ends = atoms_here * blocks
    skip = -(-EDGE // Q_WIN)
    margin = skip * Q_WIN
    reach_keys = key_ref.shape[2]
    inside = reach_keys - EDGE

    whole = pltpu.make_async_copy(
        inner_ref, out_hbm.at[:, pl.ds(margin, atoms_here - 2 * margin)], sem.at[0]
    )
    whole.start()

    even = device_at % 2 == 0
    first, second = first_ref[...], second_ref[...]
    arrived = (jnp.where(even, second, first), jnp.where(even, first, second))
    count = 2 * samples * EDGE
    token = iota((tok_here, tok_here), 1)
    own_reach = bounds(counts_ref, device_at, token)
    sides = (
        (jnp.maximum(device_at - 1, 0), atoms_here - EDGE, 0, EDGE, 0),
        (jnp.minimum(device_at + 1, blocks - 1), 0, inside, 0, atoms_here - inside),
    )
    for side, (block, offset, place, own_place, own_start) in enumerate(sides):
        edges = arrived[side][:count].reshape(samples, 2, EDGE, width)
        for i, (ref, own_ref) in enumerate(((key_ref, own_key_ref), (value_ref, own_value_ref))):
            ref[side, :, place : place + EDGE, :] = edges[:, i]
            ref[side, :, own_place : own_place + inside, :] = own_ref[
                :, own_start : own_start + inside, :
            ]
        hot = one_hot(bounds(counts_ref, block, token), offset, EDGE)
        near_ref[side, place : place + EDGE, :] = expand(hot, arrived[side][count:], tok_here)
        hot = one_hot(own_reach, own_start, inside)
        near_ref[side, own_place : own_place + inside, :] = expand(hot, held_ref[...], tok_here)

    reach = bounds(counts_ref, device_at, row_tokens(heads, tok_here))
    windows = []
    for side in range(2):
        for i in range(skip):
            start = i * Q_WIN + side * (atoms_here - margin)
            cut = slice(i * Q_WIN, i * Q_WIN + K_WIN)
            parts = lambda sample, side=side, cut=cut: (
                key_ref[side, sample, cut, :],
                value_ref[side, sample, cut, :],
            )
            key_at = iota((heads * Q_WIN, K_WIN), 1) + (device_at * atoms_here + start - EDGE)
            mask = (key_at >= 0) & (key_at < ends)
            windows.append((start, parts, near_ref[side, cut, :], mask))
    attend(heads, reach, windows, query_ref, gate_ref, gated_ref)
    copies = []
    for side in range(2):
        cut = slice(side * (atoms_here - margin), side * (atoms_here - margin) + margin)
        for sample in range(samples):
            out_ref[side, sample] = close(sample, cut, gated_ref, open_ref, trans_ref, w_out_ref)
        target = out_hbm.at[:, pl.ds(side * (atoms_here - margin), margin)]
        copies.append(pltpu.make_async_copy(out_ref.at[side], target, sem.at[1 + side]))
        copies[-1].start()
    for copy in copies:
        copy.wait()
    whole.wait()


def shards(
    atom_single,
    atom_cond,
    pair_cond,
    atom_counts,
    ada_attn_scale,
    ada_attn_shift,
    w_query,
    w_key,
    w_value,
    w_gate,
    w_out,
    attn_gate,
    w_pair,
    ada_trans_scale,
    ada_trans_shift,
    w_swish,
    w_linear,
    w_down,
    trans_gate,
):
    device_at = lax.axis_index("atoms")
    blocks = lax.axis_size("atoms")
    samples, atoms_here, width = atom_single.shape
    tok_here = atom_counts.shape[1]
    heads = w_pair.shape[1]
    groups = tok_here // GROUP
    pairs = lax.axis_size("pair")
    assert pair_cond.shape[0] == lax.axis_size("samp") * tok_here
    at = device_at.astype(jnp.int32).reshape(1)
    pair_at = lax.axis_index("pair").astype(jnp.int32).reshape(1)
    core_at = lax.axis_index("samp").astype(jnp.int32).reshape(1)
    in_hbm = lambda array: pltpu.with_memory_space_constraint(array, pltpu.HBM)
    in_vmem = lambda array: pltpu.with_memory_space_constraint(array, pltpu.VMEM)

    packing = (
        (ada_attn_scale, ada_attn_shift),
        (ada_trans_scale, ada_trans_shift),
        (attn_gate, trans_gate),
        (w_key, w_value),
        (w_query, w_gate),
        (w_swish, w_linear),
        (w_down,),
        (w_out,),
    )
    flat = [array for arrays in packing for array in arrays]
    cols = pair_cond.shape[1]
    lanes = heads * GROUP
    wide = (samples, atoms_here, width)
    params = pltpu.CompilerParams(vmem_limit_bytes=VMEM_LIMIT)

    def cost(products):
        return pl.CostEstimate(flops=2 * products, bytes_accessed=4 << 20, transcendentals=0)

    sent = pltpu.VMEM((2 * samples * EDGE + groups * cols, lanes), BF16)
    shapes = [
        pltpu.VMEM((groups, cols, lanes), BF16),
        pltpu.VMEM(wide, BF16),
        pltpu.VMEM(atom_cond.shape, BF16),
    ] + [
        pltpu.VMEM((arrays[0].shape[0], sum(a.shape[1] for a in arrays)), BF16)
        for arrays in packing
    ]
    made = pl.pallas_call(
        functools.partial(pair_kernel, [len(arrays) for arrays in packing]),
        in_specs=[IN_SMEM] + [IN_HBM] * (4 + len(flat)),
        out_specs=[IN_VMEM] * len(shapes),
        out_shape=shapes,
        scratch_shapes=[
            pltpu.VMEM((heads, width), BF16),
            pltpu.VMEM((tok_here, cols, width), BF16),
            pltpu.SemaphoreType.DMA((2 * groups,)),
            pltpu.SemaphoreType.DMA((3 + len(flat),)),
        ],
        compiler_params=params,
        cost_estimate=cost(tok_here * cols * width * width * 2),
    )(core_at, *map(in_hbm, (w_pair.T, pair_cond, atom_single, atom_cond, *flat)))
    own, single, cond, *packed = made
    ada_attn, ada_trans, gates, w_kv, w_qg, w_up, w_down, w_out = packed
    if pairs == 2:
        swapped = [(0, 1), (1, 0)]
        across = lax.ppermute(own, "pair", swapped)
        diagonal = lax.ppermute(own, ("pair", "samp"), [(0, 3), (1, 2), (2, 1), (3, 0)])
        tiles = (own, lax.ppermute(own, "samp", swapped), across, diagonal)
    else:
        tiles = (lax.all_gather(own, ("pair", "samp")),)

    operands = (single, cond, ada_attn, ada_trans, gates, w_kv, w_qg, w_up, w_down)
    query, keys, values, gate, opened, trans, near, far = pl.pallas_call(
        project_kernel,
        in_specs=[IN_SMEM] + [IN_VMEM] * len(operands),
        out_specs=[IN_VMEM] * 8,
        out_shape=[pltpu.VMEM(wide, BF16)] * 4
        + [pltpu.VMEM((atoms_here, width), BF16), pltpu.VMEM(wide, BF16), sent, sent],
        compiler_params=params,
        cost_estimate=cost(samples * atoms_here * width * width * 20),
    )(at, *map(in_vmem, operands))

    operands = (*tiles, near, far, opened)
    first = 3 + len(tiles)
    near, far, opened, held = pl.pallas_call(
        functools.partial(select_kernel, blocks),
        in_specs=[IN_SMEM] * 3 + [IN_VMEM] * len(operands),
        out_specs=[IN_VMEM] * 4,
        out_shape=[
            sent,
            sent,
            pltpu.VMEM((atoms_here, width), BF16),
            pltpu.VMEM((groups * cols, lanes), BF16),
        ],
        input_output_aliases={first: 0, first + 1: 1, first + 2: 2},
        compiler_params=params,
    )(at, pair_at, core_at, *map(in_vmem, operands))

    def swap(value, start):
        sides = [(i, i + 1) for i in range(start, blocks - 1, 2)]
        return lax.ppermute(value, "atoms", sides + [(j, i) for i, j in sides])

    first, second = swap(near, 0), swap(far, 1)

    margin = -(-EDGE // Q_WIN) * Q_WIN
    operands = (query, keys, values, gate, opened, trans, w_out, held)
    inner = pl.pallas_call(
        functools.partial(inner_kernel, heads),
        in_specs=[IN_SMEM] + [IN_VMEM] * (1 + len(operands)),
        out_specs=IN_VMEM,
        out_shape=pltpu.VMEM((samples, atoms_here - 2 * margin, width), BF16),
        scratch_shapes=[
            pltpu.VMEM((atoms_here, heads * tok_here), BF16),
            pltpu.VMEM(wide, BF16),
        ],
        compiler_params=params,
        cost_estimate=cost(samples * atoms_here * width * width * 12),
    )(at, atom_counts, *map(in_vmem, operands))

    reach = margin - Q_WIN + K_WIN
    operands += (inner, first, second)
    return pl.pallas_call(
        functools.partial(outer_kernel, heads, blocks),
        in_specs=[IN_SMEM] + [IN_VMEM] * (1 + len(operands)),
        out_specs=IN_HBM,
        out_shape=pltpu.HBM(wide, BF16),
        scratch_shapes=[
            pltpu.VMEM((2, samples, reach, width), BF16),
            pltpu.VMEM((2, samples, reach, width), BF16),
            pltpu.VMEM((2, reach, heads * tok_here), BF16),
            pltpu.VMEM(wide, BF16),
            pltpu.VMEM((2, samples, margin, width), BF16),
            pltpu.SemaphoreType.DMA((3,)),
        ],
        compiler_params=params,
        cost_estimate=cost(samples * atoms_here * width * width * 4),
    )(at, atom_counts, *map(in_vmem, operands))


def solution(mesh):
    return jax.shard_map(
        shards,
        mesh=mesh,
        in_specs=(
            P(("groups", "pair", "samp"), "atoms", None),
            P(("groups", "atoms"), None),
            P(("groups", "pair"), "atoms", None),
            P("groups", None),
        )
        + (P(),) * 15,
        out_specs=P(("groups", "pair", "samp"), "atoms", None),
        check_vma=False,
    )
```

```python
import functools
import math

import jax
import jax.numpy as jnp
from jax import lax
from jax.experimental import pallas as pl
from jax.experimental.pallas import tpu as pltpu
from jax.sharding import PartitionSpec as P

Q_WIN = 32
K_WIN = 128
EDGE = 48
GROUP = 32

EPSILON = 1e-05
MASKED = -1e30
LOG2E = math.log2(math.e)
BF16 = jnp.bfloat16
F32 = jnp.float32
LAST = (((1,), (1,)), ((), ()))
VMEM_LIMIT = 32 << 20
IN_VMEM = pl.BlockSpec(memory_space=pltpu.VMEM)
IN_HBM = pl.BlockSpec(memory_space=pltpu.HBM)
IN_SMEM = pl.BlockSpec(memory_space=pltpu.SMEM)


def dot(a, b):
    return jnp.dot(a, b, preferred_element_type=F32)


def iota(shape, dim):
    return lax.broadcasted_iota(jnp.int32, shape, dim)


def twice(matrix):
    blank = jnp.zeros_like(matrix)
    return jnp.concatenate(
        [jnp.concatenate([matrix, blank], 1), jnp.concatenate([blank, matrix], 1)], 0
    )


def side_by_side(rows):
    half = rows.shape[0] // 2
    return jnp.concatenate([rows[:half], rows[half:]], 1)


def centring(width):
    same = iota((width, width), 0) == iota((width, width), 1)
    return jnp.where(same, 1.0 - 1.0 / width, -1.0 / width).astype(BF16)


def averaging(width):
    return jnp.full((width, width), 1.0 / width, BF16)


def layer_norm(rows):
    width = rows.shape[1]
    centred = dot(side_by_side(rows), twice(centring(width)))
    variance = dot((centred * centred).astype(BF16), twice(averaging(width)))
    normal = centred * lax.rsqrt(variance + EPSILON)
    return jnp.concatenate([normal[:, :width], normal[:, width:]], 0)


def sigmoid(values):
    return pl.reciprocal(1.0 + jnp.exp2(values * -LOG2E), approx=True)


def attn_norm(cond, single, ada):
    width = single.shape[-1]
    mixed = dot(cond, ada)
    return (sigmoid(mixed[:, :width])[None] * single + mixed[None, :, width:]).astype(BF16)


def pair_kernel(packing, core_ref, w_pair_hbm, pair_hbm, single_hbm, cond_hbm, *refs):
    count = sum(packing)
    weights_hbm, refs = refs[:count], refs[count:]
    tile_ref, single_ref, cond_ref = refs[:3]
    packed_refs, refs = refs[3 : 3 + len(packing)], refs[3 + len(packing) :]
    w_pair_ref, pair_ref, pair_sem, sem = refs
    rows, cols, width = pair_ref.shape
    heads = w_pair_ref.shape[0]
    group = GROUP
    lanes = heads * group
    half = group // 2
    pieces = rows // half
    row_start = core_ref[0] * rows

    def pair_copy(i):
        source = pair_hbm.at[pl.ds(row_start + i * half, half)]
        return pltpu.make_async_copy(source, pair_ref.at[pl.ds(i * half, half)], pair_sem.at[i])

    moves = [(w_pair_hbm, w_pair_ref), (single_hbm, single_ref), (cond_hbm, cond_ref)]
    index = 0
    for number, packed in zip(packing, packed_refs):
        offset = 0
        for _ in range(number):
            source = weights_hbm[index]
            span = source.shape[1]
            moves.append((source, packed.at[:, pl.ds(offset, span)]))
            offset += span
            index += 1
    copies = [
        pltpu.make_async_copy(source, target, sem.at[i])
        for i, (source, target) in enumerate(moves)
    ]
    copies[0].start()
    for i in range(pieces):
        pair_copy(i).start()

    centre = twice(centring(width))
    copies[0].wait()
    w_pair = w_pair_ref[...].astype(F32)
    spread = jnp.concatenate(
        [jnp.broadcast_to(w_pair[h : h + 1], (group, width)) for h in range(heads)], 0
    )
    weight = spread.T.astype(BF16)
    mean = jnp.full((width, lanes), 1.0 / width, BF16)
    blank = jnp.zeros((width, lanes), BF16)
    mix = jnp.concatenate(
        [jnp.concatenate([weight, blank], 1), jnp.concatenate([blank, mean], 1)], 0
    )
    slot = iota((cols, 2 * lanes), 1) % group

    @pl.loop(0, rows // group)
    def _(chunk):
        for part in range(2):
            pair_copy(chunk * 2 + part).wait()

        @pl.when(chunk == 0)
        def _():
            for copy in copies[1:]:
                copy.start()

        pair = pair_ref[pl.ds(chunk * group, group)].reshape(group * cols, width)
        centred = dot(side_by_side(pair), centre)
        rounded = centred.astype(BF16)
        squares = (centred * centred).astype(BF16)
        total = jnp.zeros((cols, 2 * lanes), F32)
        for part in range(2):
            cut = slice(part * width, (part + 1) * width)
            mixed = dot(jnp.concatenate([rounded[:, cut], squares[:, cut]], 1), mix)
            mixed = mixed.reshape(half, cols, 2 * lanes)
            for i in range(half):
                total = jnp.where(slot == part * half + i, mixed[i], total)
        bias = (total[:, :lanes] * lax.rsqrt(total[:, lanes:] + EPSILON)).astype(BF16)
        tile_ref[chunk] = bias

    for copy in copies[1:]:
        copy.wait()


def project_kernel(
    at_ref,
    single_ref,
    cond_ref,
    ada_attn,
    ada_trans,
    gates_ref,
    w_kv,
    w_qg,
    w_up,
    w_down,
    query_ref,
    key_ref,
    value_ref,
    gate_ref,
    open_ref,
    trans_ref,
    near_ref,
    far_ref,
):
    samples, atoms_here, width = single_ref.shape
    hidden_width = w_down.shape[0]
    step = math.gcd(atoms_here, 256)
    for start in range(0, atoms_here, step):
        at = slice(start, start + step)
        cond = layer_norm(cond_ref[at, :]).astype(BF16)
        single = layer_norm(single_ref[:, at, :].reshape(-1, width))
        single = single.reshape(samples, step, width)
        normed = attn_norm(cond, single, ada_attn[...])
        if start == 0:
            heads_of = [normed[sample, :EDGE] for sample in range(samples)]
        if start + step == atoms_here:
            tails_of = [normed[sample, step - EDGE :] for sample in range(samples)]
        normed = normed.reshape(-1, width)
        both = dot(normed, w_kv[...]).astype(BF16).reshape(samples, step, 2 * width)
        key_ref[:, at, :] = both[:, :, :width]
        value_ref[:, at, :] = both[:, :, width:]
        both = dot(normed, w_qg[...]).reshape(samples, step, 2 * width)
        query_ref[:, at, :] = both[:, :, :width].astype(BF16)
        gate_ref[:, at, :] = sigmoid(both[:, :, width:]).astype(BF16)
        gates = dot(cond, gates_ref[...])
        open_ref[at, :] = sigmoid(gates[:, :width]).astype(BF16)
        normed = attn_norm(cond, single, ada_trans[...]).reshape(-1, width)
        swish = dot(normed, w_up[:, :hidden_width])
        hidden = (swish * sigmoid(swish) * dot(normed, w_up[:, hidden_width:])).astype(BF16)
        down = dot(hidden, w_down[...]).reshape(samples, step, width)
        trans_ref[:, at, :] = (sigmoid(gates[:, width:])[None] * down).astype(BF16)
    even = at_ref[0] % 2 == 0
    for sample, (head, tail) in enumerate(zip(heads_of, tails_of)):
        cut = slice(sample * EDGE, (sample + 1) * EDGE)
        near_ref[cut, :] = jnp.where(even, tail, head)
        far_ref[cut, :] = jnp.where(even, head, tail)


def tile_of(refs, place, row_block):
    if len(refs) == 1:
        return refs[0][row_block]
    pair_at, core_at = place
    owners = 2
    mine, theirs, across, diagonal = [ref[...] for ref in refs]
    near = jnp.where(row_block % owners == core_at, mine, theirs)
    far = jnp.where(row_block % owners == core_at, across, diagonal)
    return jnp.where(row_block // owners == pair_at, near, far)


def select_kernel(blocks, at_ref, pair_ref, core_ref, *refs):
    *tile_refs, _, __, ___, near_ref, far_ref, ____, held_ref = refs
    groups, cols, lanes = tile_refs[0].shape[-3:]
    rows = groups * cols
    device_at, place = at_ref[0], (pair_ref[0], core_ref[0])
    for send_ref, parity in ((near_ref, 0), (far_ref, 1)):
        beside = jnp.where(device_at % 2 == parity, device_at + 1, device_at - 1)
        tile = tile_of(tile_refs, place, jnp.clip(beside, 0, blocks - 1))
        send_ref[send_ref.shape[0] - rows :, :] = tile.reshape(rows, lanes)
    held_ref[...] = tile_of(tile_refs, place, device_at).reshape(rows, lanes)


def bounds(counts_ref, block, token):
    tok_here = counts_ref.shape[1]
    counts = counts_ref[pl.ds(block, 1), :].astype(F32).astype(BF16)
    counts = jnp.broadcast_to(counts, (8, tok_here))
    before = iota((tok_here, token.shape[1]), 0)
    first = dot(counts, (before < token).astype(BF16))[:1]
    last = dot(counts, (before <= token).astype(BF16))[:1]
    return first.astype(jnp.int32), last.astype(jnp.int32)


def one_hot(reach, offset, count):
    first, last = reach
    position = iota((count, first.shape[1]), 0) + offset
    return ((first <= position) & (position < last)).astype(F32).astype(BF16)


def expand(hot, tile, tok_here):
    tile = tile.reshape(tok_here // GROUP, tok_here, tile.shape[-1])
    tile = jnp.concatenate([tile[part] for part in range(tok_here // GROUP)], 1)
    return dot(hot, tile).astype(BF16)


def attend(heads, reach, windows, query_ref, gate_ref, gated_ref):
    samples, _, width = query_ref.shape
    head_dim = width // heads
    lanes = reach[0].shape[1]
    rows = heads * Q_WIN
    lane_head = iota((rows, lanes), 1) // GROUP % heads
    row_head = iota((rows, lanes), 0) // Q_WIN
    same_head = (lane_head == row_head).astype(F32).astype(BF16)
    own_head = iota((rows, width), 1) // head_dim == iota((rows, width), 0) // Q_WIN
    own_head = own_head.astype(F32).astype(BF16)
    channel_head = iota((Q_WIN, 2 * width), 1) % width // head_dim
    ones = jnp.ones((K_WIN, width), BF16)
    scaling = LOG2E / math.sqrt(head_dim)

    biases = []
    for start, _, near, mask in windows:
        pick = jnp.concatenate([one_hot(reach, start, Q_WIN)] * heads, 0) * same_head
        bias = lax.dot_general(pick, near, LAST, preferred_element_type=F32) * LOG2E
        biases.append(bias if mask is None else jnp.where(mask, bias, MASKED))
    units = [(sample, i) for i in range(len(windows)) for sample in range(samples)]
    scores = []
    for sample, i in units:
        query = query_ref[sample, pl.ds(windows[i][0], Q_WIN), :]
        query = jnp.concatenate([query] * heads, 0) * own_head
        keys = windows[i][1](sample)[0]
        product = lax.dot_general(query, keys, LAST, preferred_element_type=F32)
        scores.append(product * scaling + biases[i])
    tops = [jnp.max(score, axis=-1, keepdims=True) for score in scores]
    raised = [jnp.exp2(score - top).astype(BF16) for score, top in zip(scores, tops)]
    for (sample, i), weight in zip(units, raised):
        values = windows[i][1](sample)[1]
        mixed = dot(weight, jnp.concatenate([values, ones], 1))
        picked = mixed[:Q_WIN]
        for head in range(1, heads):
            picked = jnp.where(
                channel_head == head, mixed[head * Q_WIN : (head + 1) * Q_WIN], picked
            )
        attended = picked[:, :width] * pl.reciprocal(picked[:, width:], approx=True)
        at = pl.ds(windows[i][0], Q_WIN)
        gate = gate_ref[sample, at, :].astype(F32)
        gated_ref[sample, at, :] = (gate * attended).astype(BF16)


def close(sample, cut, gated_ref, open_ref, trans_ref, w_out_ref):
    mixed = dot(gated_ref[sample, cut, :], w_out_ref[...])
    opened, trans = open_ref[cut, :].astype(F32), trans_ref[sample, cut, :].astype(F32)
    return (opened * mixed + trans).astype(BF16)


def row_tokens(heads, tok_here):
    lane = iota((tok_here, heads * tok_here), 1)
    return lane // (heads * GROUP) * GROUP + lane % GROUP


def inner_kernel(
    heads,
    at_ref,
    counts_ref,
    query_ref,
    key_ref,
    value_ref,
    gate_ref,
    open_ref,
    trans_ref,
    w_out_ref,
    held_ref,
    out_ref,
    near_ref,
    gated_ref,
):
    samples, atoms_here, width = query_ref.shape
    tok_here = counts_ref.shape[1]
    device_at = at_ref[0]
    hot = one_hot(
        bounds(counts_ref, device_at, iota((tok_here, tok_here), 1)), 0, atoms_here
    )
    near_ref[...] = expand(hot, held_ref[...], tok_here)
    reach = bounds(counts_ref, device_at, row_tokens(heads, tok_here))
    skip = -(-EDGE // Q_WIN)
    inner = atoms_here // Q_WIN - 2 * skip
    batch = math.gcd(inner, 4)

    @pl.loop(0, inner // batch)
    def _(turn):
        windows = []
        for i in range(batch):
            start = pl.multiple_of((turn * batch + i + skip) * Q_WIN, Q_WIN)
            cut = pl.ds(pl.multiple_of(start - EDGE, 16), K_WIN)
            parts = lambda sample, cut=cut: (key_ref[sample, cut, :], value_ref[sample, cut, :])
            windows.append((start, parts, near_ref[cut, :], None))
        attend(heads, reach, windows, query_ref, gate_ref, gated_ref)

    cut = slice(skip * Q_WIN, atoms_here - skip * Q_WIN)
    for sample in range(samples):
        out_ref[sample] = close(sample, cut, gated_ref, open_ref, trans_ref, w_out_ref)


def outer_kernel(
    heads,
    blocks,
    at_ref,
    counts_ref,
    query_ref,
    own_key_ref,
    own_value_ref,
    gate_ref,
    open_ref,
    trans_ref,
    w_out_ref,
    held_ref,
    inner_ref,
    w_kv,
    first_ref,
    second_ref,
    out_hbm,
    key_ref,
    value_ref,
    near_ref,
    gated_ref,
    out_ref,
    sem,
):
    samples, atoms_here, width = query_ref.shape
    tok_here = counts_ref.shape[1]
    device_at = at_ref[0]
    ends = atoms_here * blocks
    skip = -(-EDGE // Q_WIN)
    margin = skip * Q_WIN
    reach_keys = key_ref.shape[2]
    inside = reach_keys - EDGE

    whole = pltpu.make_async_copy(
        inner_ref, out_hbm.at[:, pl.ds(margin, atoms_here - 2 * margin)], sem.at[0]
    )
    whole.start()

    even = device_at % 2 == 0
    first, second = first_ref[...], second_ref[...]
    arrived = (jnp.where(even, second, first), jnp.where(even, first, second))
    count = samples * EDGE
    edges = jnp.concatenate([rows[:count] for rows in arrived], 0)
    edges = dot(edges, w_kv[...]).astype(BF16).reshape(2, samples, EDGE, 2 * width)
    token = iota((tok_here, tok_here), 1)
    own_reach = bounds(counts_ref, device_at, token)
    sides = (
        (jnp.maximum(device_at - 1, 0), atoms_here - EDGE, 0, EDGE, 0),
        (jnp.minimum(device_at + 1, blocks - 1), 0, inside, 0, atoms_here - inside),
    )
    for side, (block, offset, place, own_place, own_start) in enumerate(sides):
        for i, (ref, own_ref) in enumerate(((key_ref, own_key_ref), (value_ref, own_value_ref))):
            ref[side, :, place : place + EDGE, :] = edges[side, :, :, i * width : (i + 1) * width]
            ref[side, :, own_place : own_place + inside, :] = own_ref[
                :, own_start : own_start + inside, :
            ]
        hot = one_hot(bounds(counts_ref, block, token), offset, EDGE)
        near_ref[side, place : place + EDGE, :] = expand(hot, arrived[side][count:], tok_here)
        hot = one_hot(own_reach, own_start, inside)
        near_ref[side, own_place : own_place + inside, :] = expand(hot, held_ref[...], tok_here)

    reach = bounds(counts_ref, device_at, row_tokens(heads, tok_here))
    windows = []
    for side in range(2):
        for i in range(skip):
            start = i * Q_WIN + side * (atoms_here - margin)
            cut = slice(i * Q_WIN, i * Q_WIN + K_WIN)
            parts = lambda sample, side=side, cut=cut: (
                key_ref[side, sample, cut, :],
                value_ref[side, sample, cut, :],
            )
            key_at = iota((heads * Q_WIN, K_WIN), 1) + (device_at * atoms_here + start - EDGE)
            mask = (key_at >= 0) & (key_at < ends)
            windows.append((start, parts, near_ref[side, cut, :], mask))
    attend(heads, reach, windows, query_ref, gate_ref, gated_ref)
    copies = []
    for side in range(2):
        cut = slice(side * (atoms_here - margin), side * (atoms_here - margin) + margin)
        for sample in range(samples):
            out_ref[side, sample] = close(sample, cut, gated_ref, open_ref, trans_ref, w_out_ref)
        target = out_hbm.at[:, pl.ds(side * (atoms_here - margin), margin)]
        copies.append(pltpu.make_async_copy(out_ref.at[side], target, sem.at[1 + side]))
        copies[-1].start()
    for copy in copies:
        copy.wait()
    whole.wait()


def shards(
    atom_single,
    atom_cond,
    pair_cond,
    atom_counts,
    ada_attn_scale,
    ada_attn_shift,
    w_query,
    w_key,
    w_value,
    w_gate,
    w_out,
    attn_gate,
    w_pair,
    ada_trans_scale,
    ada_trans_shift,
    w_swish,
    w_linear,
    w_down,
    trans_gate,
):
    device_at = lax.axis_index("atoms")
    blocks = lax.axis_size("atoms")
    samples, atoms_here, width = atom_single.shape
    tok_here = atom_counts.shape[1]
    heads = w_pair.shape[1]
    groups = tok_here // GROUP
    pairs = lax.axis_size("pair")
    assert pair_cond.shape[0] == lax.axis_size("samp") * tok_here
    at = device_at.astype(jnp.int32).reshape(1)
    pair_at = lax.axis_index("pair").astype(jnp.int32).reshape(1)
    core_at = lax.axis_index("samp").astype(jnp.int32).reshape(1)
    in_hbm = lambda array: pltpu.with_memory_space_constraint(array, pltpu.HBM)
    in_vmem = lambda array: pltpu.with_memory_space_constraint(array, pltpu.VMEM)

    packing = (
        (ada_attn_scale, ada_attn_shift),
        (ada_trans_scale, ada_trans_shift),
        (attn_gate, trans_gate),
        (w_key, w_value),
        (w_query, w_gate),
        (w_swish, w_linear),
        (w_down,),
        (w_out,),
    )
    flat = [array for arrays in packing for array in arrays]
    cols = pair_cond.shape[1]
    lanes = heads * GROUP
    wide = (samples, atoms_here, width)
    params = pltpu.CompilerParams(vmem_limit_bytes=VMEM_LIMIT)

    def cost(products):
        return pl.CostEstimate(flops=2 * products, bytes_accessed=4 << 20, transcendentals=0)

    sent = pltpu.VMEM((samples * EDGE + groups * cols, lanes), BF16)
    shapes = [
        pltpu.VMEM((groups, cols, lanes), BF16),
        pltpu.VMEM(wide, BF16),
        pltpu.VMEM(atom_cond.shape, BF16),
    ] + [
        pltpu.VMEM((arrays[0].shape[0], sum(a.shape[1] for a in arrays)), BF16)
        for arrays in packing
    ]
    made = pl.pallas_call(
        functools.partial(pair_kernel, [len(arrays) for arrays in packing]),
        in_specs=[IN_SMEM] + [IN_HBM] * (4 + len(flat)),
        out_specs=[IN_VMEM] * len(shapes),
        out_shape=shapes,
        scratch_shapes=[
            pltpu.VMEM((heads, width), BF16),
            pltpu.VMEM((tok_here, cols, width), BF16),
            pltpu.SemaphoreType.DMA((2 * groups,)),
            pltpu.SemaphoreType.DMA((3 + len(flat),)),
        ],
        compiler_params=params,
        cost_estimate=cost(tok_here * cols * width * width * 2),
    )(core_at, *map(in_hbm, (w_pair.T, pair_cond, atom_single, atom_cond, *flat)))
    own, single, cond, *packed = made
    ada_attn, ada_trans, gates, w_kv, w_qg, w_up, w_down, w_out = packed
    if pairs == 2:
        swapped = [(0, 1), (1, 0)]
        across = lax.ppermute(own, "pair", swapped)
        diagonal = lax.ppermute(own, ("pair", "samp"), [(0, 3), (1, 2), (2, 1), (3, 0)])
        tiles = (own, lax.ppermute(own, "samp", swapped), across, diagonal)
    else:
        tiles = (lax.all_gather(own, ("pair", "samp")),)

    operands = (single, cond, ada_attn, ada_trans, gates, w_kv, w_qg, w_up, w_down)
    query, keys, values, gate, opened, trans, near, far = pl.pallas_call(
        project_kernel,
        in_specs=[IN_SMEM] + [IN_VMEM] * len(operands),
        out_specs=[IN_VMEM] * 8,
        out_shape=[pltpu.VMEM(wide, BF16)] * 4
        + [pltpu.VMEM((atoms_here, width), BF16), pltpu.VMEM(wide, BF16), sent, sent],
        compiler_params=params,
        cost_estimate=cost(samples * atoms_here * width * width * 20),
    )(at, *map(in_vmem, operands))

    operands = (*tiles, near, far, opened)
    first = 3 + len(tiles)
    near, far, opened, held = pl.pallas_call(
        functools.partial(select_kernel, blocks),
        in_specs=[IN_SMEM] * 3 + [IN_VMEM] * len(operands),
        out_specs=[IN_VMEM] * 4,
        out_shape=[
            sent,
            sent,
            pltpu.VMEM((atoms_here, width), BF16),
            pltpu.VMEM((groups * cols, lanes), BF16),
        ],
        input_output_aliases={first: 0, first + 1: 1, first + 2: 2},
        compiler_params=params,
    )(at, pair_at, core_at, *map(in_vmem, operands))

    def swap(value, start):
        sides = [(i, i + 1) for i in range(start, blocks - 1, 2)]
        alone = set(range(blocks)) - {i for side in sides for i in side}
        pairs_of = sides + [(j, i) for i, j in sides] + [(i, i) for i in sorted(alone)]
        return lax.ppermute(value, "atoms", pairs_of)

    first, second = swap(near, 0), swap(far, 1)

    margin = -(-EDGE // Q_WIN) * Q_WIN
    operands = (query, keys, values, gate, opened, trans, w_out, held)
    inner = pl.pallas_call(
        functools.partial(inner_kernel, heads),
        in_specs=[IN_SMEM] + [IN_VMEM] * (1 + len(operands)),
        out_specs=IN_VMEM,
        out_shape=pltpu.VMEM((samples, atoms_here - 2 * margin, width), BF16),
        scratch_shapes=[
            pltpu.VMEM((atoms_here, heads * tok_here), BF16),
            pltpu.VMEM(wide, BF16),
        ],
        compiler_params=params,
        cost_estimate=cost(samples * atoms_here * width * width * 12),
    )(at, atom_counts, *map(in_vmem, operands))

    reach = margin - Q_WIN + K_WIN
    operands += (inner, w_kv, first, second)
    return pl.pallas_call(
        functools.partial(outer_kernel, heads, blocks),
        in_specs=[IN_SMEM] + [IN_VMEM] * (1 + len(operands)),
        out_specs=IN_HBM,
        out_shape=pltpu.HBM(wide, BF16),
        scratch_shapes=[
            pltpu.VMEM((2, samples, reach, width), BF16),
            pltpu.VMEM((2, samples, reach, width), BF16),
            pltpu.VMEM((2, reach, heads * tok_here), BF16),
            pltpu.VMEM(wide, BF16),
            pltpu.VMEM((2, samples, margin, width), BF16),
            pltpu.SemaphoreType.DMA((3,)),
        ],
        compiler_params=params,
        cost_estimate=cost(samples * atoms_here * width * width * 4),
    )(at, atom_counts, *map(in_vmem, operands))


def solution(mesh):
    return jax.shard_map(
        shards,
        mesh=mesh,
        in_specs=(
            P(("groups", "pair", "samp"), "atoms", None),
            P(("groups", "atoms"), None),
            P(("groups", "pair"), "atoms", None),
            P("groups", None),
        )
        + (P(),) * 15,
        out_specs=P(("groups", "pair", "samp"), "atoms", None),
        check_vma=False,
    )
```

```python
import functools
import math

import jax
import jax.numpy as jnp
from jax import lax
from jax.experimental import pallas as pl
from jax.experimental.pallas import tpu as pltpu
from jax.sharding import PartitionSpec as P

Q_WIN = 32
K_WIN = 128
EDGE = 48
GROUP = 32

EPSILON = 1e-05
MASKED = -1e30
LOG2E = math.log2(math.e)
BF16 = jnp.bfloat16
F32 = jnp.float32
LAST = (((1,), (1,)), ((), ()))
VMEM_LIMIT = 32 << 20
IN_VMEM = pl.BlockSpec(memory_space=pltpu.VMEM)
IN_HBM = pl.BlockSpec(memory_space=pltpu.HBM)
IN_SMEM = pl.BlockSpec(memory_space=pltpu.SMEM)


def dot(a, b):
    return jnp.dot(a, b, preferred_element_type=F32)


def iota(shape, dim):
    return lax.broadcasted_iota(jnp.int32, shape, dim)


def twice(matrix):
    blank = jnp.zeros_like(matrix)
    return jnp.concatenate(
        [jnp.concatenate([matrix, blank], 1), jnp.concatenate([blank, matrix], 1)], 0
    )


def side_by_side(rows):
    half = rows.shape[0] // 2
    return jnp.concatenate([rows[:half], rows[half:]], 1)


def centring(width):
    same = iota((width, width), 0) == iota((width, width), 1)
    return jnp.where(same, 1.0 - 1.0 / width, -1.0 / width).astype(BF16)


def averaging(width):
    return jnp.full((width, width), 1.0 / width, BF16)


def layer_norm(rows):
    width = rows.shape[1]
    centred = dot(side_by_side(rows), twice(centring(width)))
    variance = dot((centred * centred).astype(BF16), twice(averaging(width)))
    normal = centred * lax.rsqrt(variance + EPSILON)
    return jnp.concatenate([normal[:, :width], normal[:, width:]], 0)


def sigmoid(values):
    return pl.reciprocal(1.0 + jnp.exp2(values * -LOG2E), approx=True)


def attn_norm(cond, single, ada):
    width = single.shape[-1]
    mixed = dot(cond, ada)
    return (sigmoid(mixed[:, :width])[None] * single + mixed[None, :, width:]).astype(BF16)


def pair_kernel(packing, core_ref, w_pair_hbm, pair_hbm, single_hbm, cond_hbm, *refs):
    count = sum(packing)
    weights_hbm, refs = refs[:count], refs[count:]
    tile_ref, single_ref, cond_ref = refs[:3]
    packed_refs, refs = refs[3 : 3 + len(packing)], refs[3 + len(packing) :]
    w_pair_ref, pair_ref, pair_sem, sem = refs
    rows, cols, width = pair_ref.shape
    heads = w_pair_ref.shape[0]
    group = GROUP
    lanes = heads * group
    half = group // 2
    pieces = rows // half
    row_start = core_ref[0] * rows

    def pair_copy(i):
        source = pair_hbm.at[pl.ds(row_start + i * half, half)]
        return pltpu.make_async_copy(source, pair_ref.at[pl.ds(i * half, half)], pair_sem.at[i])

    moves = [(w_pair_hbm, w_pair_ref), (single_hbm, single_ref), (cond_hbm, cond_ref)]
    index = 0
    for number, packed in zip(packing, packed_refs):
        offset = 0
        for _ in range(number):
            source = weights_hbm[index]
            span = source.shape[1]
            moves.append((source, packed.at[:, pl.ds(offset, span)]))
            offset += span
            index += 1
    copies = [
        pltpu.make_async_copy(source, target, sem.at[i])
        for i, (source, target) in enumerate(moves)
    ]
    copies[0].start()
    for i in range(pieces):
        pair_copy(i).start()

    centre = twice(centring(width))
    copies[0].wait()
    w_pair = w_pair_ref[...].astype(F32)
    spread = jnp.concatenate(
        [jnp.broadcast_to(w_pair[h : h + 1], (group, width)) for h in range(heads)], 0
    )
    weight = spread.T.astype(BF16)
    mean = jnp.full((width, lanes), 1.0 / width, BF16)
    blank = jnp.zeros((width, lanes), BF16)
    mix = jnp.concatenate(
        [jnp.concatenate([weight, blank], 1), jnp.concatenate([blank, mean], 1)], 0
    )
    slot = iota((cols, 2 * lanes), 1) % group

    @pl.loop(0, rows // group)
    def _(chunk):
        for part in range(2):
            pair_copy(chunk * 2 + part).wait()

        @pl.when(chunk == 0)
        def _():
            for copy in copies[1:]:
                copy.start()

        pair = pair_ref[pl.ds(chunk * group, group)].reshape(group * cols, width)
        centred = dot(side_by_side(pair), centre)
        rounded = centred.astype(BF16)
        squares = (centred * centred).astype(BF16)
        total = jnp.zeros((cols, 2 * lanes), F32)
        for part in range(2):
            cut = slice(part * width, (part + 1) * width)
            mixed = dot(jnp.concatenate([rounded[:, cut], squares[:, cut]], 1), mix)
            mixed = mixed.reshape(half, cols, 2 * lanes)
            for i in range(half):
                total = jnp.where(slot == part * half + i, mixed[i], total)
        bias = (total[:, :lanes] * lax.rsqrt(total[:, lanes:] + EPSILON)).astype(BF16)
        tile_ref[chunk] = bias

    for copy in copies[1:]:
        copy.wait()


def project_kernel(
    at_ref,
    single_ref,
    cond_ref,
    ada_attn,
    ada_trans,
    gates_ref,
    w_kv,
    w_qg,
    w_up,
    w_down,
    query_ref,
    key_ref,
    value_ref,
    gate_ref,
    open_ref,
    trans_ref,
    near_ref,
    far_ref,
):
    samples, atoms_here, width = single_ref.shape
    hidden_width = w_down.shape[0]
    step = math.gcd(atoms_here, 256)
    for start in range(0, atoms_here, step):
        at = slice(start, start + step)
        cond = layer_norm(cond_ref[at, :]).astype(BF16)
        single = layer_norm(single_ref[:, at, :].reshape(-1, width))
        single = single.reshape(samples, step, width)
        normed = attn_norm(cond, single, ada_attn[...])
        if start == 0:
            heads_of = [normed[sample, :EDGE] for sample in range(samples)]
        if start + step == atoms_here:
            tails_of = [normed[sample, step - EDGE :] for sample in range(samples)]
        normed = normed.reshape(-1, width)
        both = dot(normed, w_kv[...]).astype(BF16).reshape(samples, step, 2 * width)
        key_ref[:, at, :] = both[:, :, :width]
        value_ref[:, at, :] = both[:, :, width:]
        both = dot(normed, w_qg[...]).reshape(samples, step, 2 * width)
        query_ref[:, at, :] = both[:, :, :width].astype(BF16)
        gate_ref[:, at, :] = sigmoid(both[:, :, width:]).astype(BF16)
        gates = dot(cond, gates_ref[...])
        open_ref[at, :] = sigmoid(gates[:, :width]).astype(BF16)
        normed = attn_norm(cond, single, ada_trans[...]).reshape(-1, width)
        swish = dot(normed, w_up[:, :hidden_width])
        hidden = (swish * sigmoid(swish) * dot(normed, w_up[:, hidden_width:])).astype(BF16)
        down = dot(hidden, w_down[...]).reshape(samples, step, width)
        trans_ref[:, at, :] = (sigmoid(gates[:, width:])[None] * down).astype(BF16)
    even = at_ref[0] % 2 == 0
    for sample, (head, tail) in enumerate(zip(heads_of, tails_of)):
        cut = slice(sample * EDGE, (sample + 1) * EDGE)
        near_ref[cut, :] = jnp.where(even, tail, head)
        far_ref[cut, :] = jnp.where(even, head, tail)


def tile_of(refs, place, row_block):
    if len(refs) == 1:
        return refs[0][row_block]
    pair_at, core_at = place
    owners = 2
    mine, theirs, across, diagonal = [ref[...] for ref in refs]
    near = jnp.where(row_block % owners == core_at, mine, theirs)
    far = jnp.where(row_block % owners == core_at, across, diagonal)
    return jnp.where(row_block // owners == pair_at, near, far)


def select_kernel(blocks, at_ref, pair_ref, core_ref, *refs):
    *tile_refs, _, __, ___, near_ref, far_ref, ____, held_ref = refs
    groups, cols, lanes = tile_refs[0].shape[-3:]
    rows = groups * cols
    device_at, place = at_ref[0], (pair_ref[0], core_ref[0])
    for send_ref, parity in ((near_ref, 0), (far_ref, 1)):
        beside = jnp.where(device_at % 2 == parity, device_at + 1, device_at - 1)
        tile = tile_of(tile_refs, place, jnp.clip(beside, 0, blocks - 1))
        send_ref[send_ref.shape[0] - rows :, :] = tile.reshape(rows, lanes)
    held_ref[...] = tile_of(tile_refs, place, device_at).reshape(rows, lanes)


def bounds(counts_ref, block, token):
    tok_here = counts_ref.shape[1]
    counts = counts_ref[pl.ds(block, 1), :].astype(F32).astype(BF16)
    counts = jnp.broadcast_to(counts, (8, tok_here))
    before = iota((tok_here, token.shape[1]), 0)
    first = dot(counts, (before < token).astype(BF16))[:1]
    last = dot(counts, (before <= token).astype(BF16))[:1]
    return first.astype(jnp.int32), last.astype(jnp.int32)


def one_hot(reach, offset, count):
    first, last = reach
    position = iota((count, first.shape[1]), 0) + offset
    return ((first <= position) & (position < last)).astype(F32).astype(BF16)


def expand(hot, tile, tok_here):
    tile = tile.reshape(tok_here // GROUP, tok_here, tile.shape[-1])
    tile = jnp.concatenate([tile[part] for part in range(tok_here // GROUP)], 1)
    return dot(hot, tile).astype(BF16)


def attend(heads, reach, windows, query_ref, gate_ref, gated_ref):
    samples, _, width = query_ref.shape
    head_dim = width // heads
    lanes = reach[0].shape[1]
    rows = heads * Q_WIN
    lane_head = iota((rows, lanes), 1) // GROUP % heads
    row_head = iota((rows, lanes), 0) // Q_WIN
    same_head = (lane_head == row_head).astype(F32).astype(BF16)
    own_head = iota((rows, width), 1) // head_dim == iota((rows, width), 0) // Q_WIN
    own_head = own_head.astype(F32).astype(BF16)
    channel_head = iota((Q_WIN, 2 * width), 1) % width // head_dim
    ones = jnp.ones((K_WIN, width), BF16)
    scaling = LOG2E / math.sqrt(head_dim)

    biases = []
    for start, _, near, mask in windows:
        pick = jnp.concatenate([one_hot(reach, start, Q_WIN)] * heads, 0) * same_head
        bias = lax.dot_general(pick, near, LAST, preferred_element_type=F32) * LOG2E
        biases.append(bias if mask is None else jnp.where(mask, bias, MASKED))
    units = [(sample, i) for i in range(len(windows)) for sample in range(samples)]
    scores = []
    for sample, i in units:
        query = query_ref[sample, pl.ds(windows[i][0], Q_WIN), :]
        query = jnp.concatenate([query] * heads, 0) * own_head
        keys = windows[i][1](sample)[0]
        product = lax.dot_general(query, keys, LAST, preferred_element_type=F32)
        scores.append(product * scaling + biases[i])
    tops = [jnp.max(score, axis=-1, keepdims=True) for score in scores]
    raised = [jnp.exp2(score - top).astype(BF16) for score, top in zip(scores, tops)]
    for (sample, i), weight in zip(units, raised):
        values = windows[i][1](sample)[1]
        mixed = dot(weight, jnp.concatenate([values, ones], 1))
        picked = mixed[:Q_WIN]
        for head in range(1, heads):
            picked = jnp.where(
                channel_head == head, mixed[head * Q_WIN : (head + 1) * Q_WIN], picked
            )
        attended = picked[:, :width] * pl.reciprocal(picked[:, width:], approx=True)
        at = pl.ds(windows[i][0], Q_WIN)
        gate = gate_ref[sample, at, :].astype(F32)
        gated_ref[sample, at, :] = (gate * attended).astype(BF16)


def close(sample, cut, gated_ref, open_ref, trans_ref, w_out_ref):
    mixed = dot(gated_ref[sample, cut, :], w_out_ref[...])
    opened, trans = open_ref[cut, :].astype(F32), trans_ref[sample, cut, :].astype(F32)
    return (opened * mixed + trans).astype(BF16)


def row_tokens(heads, tok_here):
    lane = iota((tok_here, heads * tok_here), 1)
    return lane // (heads * GROUP) * GROUP + lane % GROUP


def inner_kernel(
    heads,
    at_ref,
    counts_ref,
    query_ref,
    key_ref,
    value_ref,
    gate_ref,
    open_ref,
    trans_ref,
    w_out_ref,
    held_ref,
    out_ref,
    near_ref,
    gated_ref,
):
    samples, atoms_here, width = query_ref.shape
    tok_here = counts_ref.shape[1]
    device_at = at_ref[0]
    hot = one_hot(
        bounds(counts_ref, device_at, iota((tok_here, tok_here), 1)), 0, atoms_here
    )
    near_ref[...] = expand(hot, held_ref[...], tok_here)
    reach = bounds(counts_ref, device_at, row_tokens(heads, tok_here))
    skip = -(-EDGE // Q_WIN)
    inner = atoms_here // Q_WIN - 2 * skip
    batch = math.gcd(inner, 4)

    @pl.loop(0, inner // batch)
    def _(turn):
        windows = []
        for i in range(batch):
            start = pl.multiple_of((turn * batch + i + skip) * Q_WIN, Q_WIN)
            cut = pl.ds(pl.multiple_of(start - EDGE, 16), K_WIN)
            parts = lambda sample, cut=cut: (key_ref[sample, cut, :], value_ref[sample, cut, :])
            windows.append((start, parts, near_ref[cut, :], None))
        attend(heads, reach, windows, query_ref, gate_ref, gated_ref)

    cut = slice(skip * Q_WIN, atoms_here - skip * Q_WIN)
    for sample in range(samples):
        out_ref[sample] = close(sample, cut, gated_ref, open_ref, trans_ref, w_out_ref)


def outer_kernel(
    heads,
    blocks,
    at_ref,
    counts_ref,
    query_ref,
    own_key_ref,
    own_value_ref,
    gate_ref,
    open_ref,
    trans_ref,
    w_out_ref,
    held_ref,
    inner_ref,
    w_kv,
    second_ref,
    first_ref,
    out_hbm,
    key_ref,
    value_ref,
    near_ref,
    gated_ref,
    out_ref,
    sem,
):
    samples, atoms_here, width = query_ref.shape
    tok_here = counts_ref.shape[1]
    device_at = at_ref[0]
    ends = atoms_here * blocks
    skip = -(-EDGE // Q_WIN)
    margin = skip * Q_WIN
    reach_keys = key_ref.shape[2]
    inside = reach_keys - EDGE

    whole = pltpu.make_async_copy(
        inner_ref, out_hbm.at[:, pl.ds(margin, atoms_here - 2 * margin)], sem.at[0]
    )
    whole.start()

    even = device_at % 2 == 0
    first, second = first_ref[...], second_ref[...]
    arrived = (jnp.where(even, second, first), jnp.where(even, first, second))
    count = samples * EDGE
    edges = jnp.concatenate([rows[:count] for rows in arrived], 0)
    edges = dot(edges, w_kv[...]).astype(BF16).reshape(2, samples, EDGE, 2 * width)
    token = iota((tok_here, tok_here), 1)
    own_reach = bounds(counts_ref, device_at, token)
    sides = (
        (jnp.maximum(device_at - 1, 0), atoms_here - EDGE, 0, EDGE, 0),
        (jnp.minimum(device_at + 1, blocks - 1), 0, inside, 0, atoms_here - inside),
    )
    for side, (block, offset, place, own_place, own_start) in enumerate(sides):
        for i, (ref, own_ref) in enumerate(((key_ref, own_key_ref), (value_ref, own_value_ref))):
            ref[side, :, place : place + EDGE, :] = edges[side, :, :, i * width : (i + 1) * width]
            ref[side, :, own_place : own_place + inside, :] = own_ref[
                :, own_start : own_start + inside, :
            ]
        hot = one_hot(bounds(counts_ref, block, token), offset, EDGE)
        near_ref[side, place : place + EDGE, :] = expand(hot, arrived[side][count:], tok_here)
        hot = one_hot(own_reach, own_start, inside)
        near_ref[side, own_place : own_place + inside, :] = expand(hot, held_ref[...], tok_here)

    reach = bounds(counts_ref, device_at, row_tokens(heads, tok_here))
    windows = []
    for side in range(2):
        for i in range(skip):
            start = i * Q_WIN + side * (atoms_here - margin)
            cut = slice(i * Q_WIN, i * Q_WIN + K_WIN)
            parts = lambda sample, side=side, cut=cut: (
                key_ref[side, sample, cut, :],
                value_ref[side, sample, cut, :],
            )
            key_at = iota((heads * Q_WIN, K_WIN), 1) + (device_at * atoms_here + start - EDGE)
            mask = (key_at >= 0) & (key_at < ends)
            windows.append((start, parts, near_ref[side, cut, :], mask))
    attend(heads, reach, windows, query_ref, gate_ref, gated_ref)
    copies = []
    for side in range(2):
        cut = slice(side * (atoms_here - margin), side * (atoms_here - margin) + margin)
        for sample in range(samples):
            out_ref[side, sample] = close(sample, cut, gated_ref, open_ref, trans_ref, w_out_ref)
        target = out_hbm.at[:, pl.ds(side * (atoms_here - margin), margin)]
        copies.append(pltpu.make_async_copy(out_ref.at[side], target, sem.at[1 + side]))
        copies[-1].start()
    for copy in copies:
        copy.wait()
    whole.wait()


def shards(
    atom_single,
    atom_cond,
    pair_cond,
    atom_counts,
    ada_attn_scale,
    ada_attn_shift,
    w_query,
    w_key,
    w_value,
    w_gate,
    w_out,
    attn_gate,
    w_pair,
    ada_trans_scale,
    ada_trans_shift,
    w_swish,
    w_linear,
    w_down,
    trans_gate,
):
    device_at = lax.axis_index("atoms")
    blocks = lax.axis_size("atoms")
    samples, atoms_here, width = atom_single.shape
    tok_here = atom_counts.shape[1]
    heads = w_pair.shape[1]
    groups = tok_here // GROUP
    pairs = lax.axis_size("pair")
    assert pair_cond.shape[0] == lax.axis_size("samp") * tok_here
    at = device_at.astype(jnp.int32).reshape(1)
    pair_at = lax.axis_index("pair").astype(jnp.int32).reshape(1)
    core_at = lax.axis_index("samp").astype(jnp.int32).reshape(1)
    in_hbm = lambda array: pltpu.with_memory_space_constraint(array, pltpu.HBM)
    in_vmem = lambda array: pltpu.with_memory_space_constraint(array, pltpu.VMEM)

    packing = (
        (ada_attn_scale, ada_attn_shift),
        (ada_trans_scale, ada_trans_shift),
        (attn_gate, trans_gate),
        (w_key, w_value),
        (w_query, w_gate),
        (w_swish, w_linear),
        (w_down,),
        (w_out,),
    )
    flat = [array for arrays in packing for array in arrays]
    cols = pair_cond.shape[1]
    lanes = heads * GROUP
    wide = (samples, atoms_here, width)
    params = pltpu.CompilerParams(vmem_limit_bytes=VMEM_LIMIT)

    def cost(products):
        return pl.CostEstimate(flops=2 * products, bytes_accessed=4 << 20, transcendentals=0)

    sent = pltpu.VMEM((samples * EDGE + groups * cols, lanes), BF16)
    shapes = [
        pltpu.VMEM((groups, cols, lanes), BF16),
        pltpu.VMEM(wide, BF16),
        pltpu.VMEM(atom_cond.shape, BF16),
    ] + [
        pltpu.VMEM((arrays[0].shape[0], sum(a.shape[1] for a in arrays)), BF16)
        for arrays in packing
    ]
    made = pl.pallas_call(
        functools.partial(pair_kernel, [len(arrays) for arrays in packing]),
        in_specs=[IN_SMEM] + [IN_HBM] * (4 + len(flat)),
        out_specs=[IN_VMEM] * len(shapes),
        out_shape=shapes,
        scratch_shapes=[
            pltpu.VMEM((heads, width), BF16),
            pltpu.VMEM((tok_here, cols, width), BF16),
            pltpu.SemaphoreType.DMA((2 * groups,)),
            pltpu.SemaphoreType.DMA((3 + len(flat),)),
        ],
        compiler_params=params,
        cost_estimate=cost(tok_here * cols * width * width * 2),
    )(core_at, *map(in_hbm, (w_pair.T, pair_cond, atom_single, atom_cond, *flat)))
    own, single, cond, *packed = made
    ada_attn, ada_trans, gates, w_kv, w_qg, w_up, w_down, w_out = packed
    if pairs == 2:
        swapped = [(0, 1), (1, 0)]
        across = lax.ppermute(own, "pair", swapped)
        diagonal = lax.ppermute(own, ("pair", "samp"), [(0, 3), (1, 2), (2, 1), (3, 0)])
        tiles = (own, lax.ppermute(own, "samp", swapped), across, diagonal)
    else:
        tiles = (lax.all_gather(own, ("pair", "samp")),)

    operands = (single, cond, ada_attn, ada_trans, gates, w_kv, w_qg, w_up, w_down)
    query, keys, values, gate, opened, trans, near, far = pl.pallas_call(
        project_kernel,
        in_specs=[IN_SMEM] + [IN_VMEM] * len(operands),
        out_specs=[IN_VMEM] * 8,
        out_shape=[pltpu.VMEM(wide, BF16)] * 4
        + [pltpu.VMEM((atoms_here, width), BF16), pltpu.VMEM(wide, BF16), sent, sent],
        compiler_params=params,
        cost_estimate=cost(samples * atoms_here * width * width * 20),
    )(at, *map(in_vmem, operands))

    operands = (*tiles, near, far, opened)
    first = 3 + len(tiles)
    near, far, opened, held = pl.pallas_call(
        functools.partial(select_kernel, blocks),
        in_specs=[IN_SMEM] * 3 + [IN_VMEM] * len(operands),
        out_specs=[IN_VMEM] * 4,
        out_shape=[
            sent,
            sent,
            pltpu.VMEM((atoms_here, width), BF16),
            pltpu.VMEM((groups * cols, lanes), BF16),
        ],
        input_output_aliases={first: 0, first + 1: 1, first + 2: 2},
        compiler_params=params,
    )(at, pair_at, core_at, *map(in_vmem, operands))

    def swap(value, start):
        sides = [(i, i + 1) for i in range(start, blocks - 1, 2)]
        alone = set(range(blocks)) - {i for side in sides for i in side}
        pairs_of = sides + [(j, i) for i, j in sides] + [(i, i) for i in sorted(alone)]
        return lax.ppermute(value, "atoms", pairs_of)

    second = swap(far, 1)
    first = swap(near, 0)

    margin = -(-EDGE // Q_WIN) * Q_WIN
    operands = (query, keys, values, gate, opened, trans, w_out, held)
    inner = pl.pallas_call(
        functools.partial(inner_kernel, heads),
        in_specs=[IN_SMEM] + [IN_VMEM] * (1 + len(operands)),
        out_specs=IN_VMEM,
        out_shape=pltpu.VMEM((samples, atoms_here - 2 * margin, width), BF16),
        scratch_shapes=[
            pltpu.VMEM((atoms_here, heads * tok_here), BF16),
            pltpu.VMEM(wide, BF16),
        ],
        compiler_params=params,
        cost_estimate=cost(samples * atoms_here * width * width * 12),
    )(at, atom_counts, *map(in_vmem, operands))

    reach = margin - Q_WIN + K_WIN
    operands += (inner, w_kv, second, first)
    return pl.pallas_call(
        functools.partial(outer_kernel, heads, blocks),
        in_specs=[IN_SMEM] + [IN_VMEM] * (1 + len(operands)),
        out_specs=IN_HBM,
        out_shape=pltpu.HBM(wide, BF16),
        scratch_shapes=[
            pltpu.VMEM((2, samples, reach, width), BF16),
            pltpu.VMEM((2, samples, reach, width), BF16),
            pltpu.VMEM((2, reach, heads * tok_here), BF16),
            pltpu.VMEM(wide, BF16),
            pltpu.VMEM((2, samples, margin, width), BF16),
            pltpu.SemaphoreType.DMA((3,)),
        ],
        compiler_params=params,
        cost_estimate=cost(samples * atoms_here * width * width * 4),
    )(at, atom_counts, *map(in_vmem, operands))


def solution(mesh):
    return jax.shard_map(
        shards,
        mesh=mesh,
        in_specs=(
            P(("groups", "pair", "samp"), "atoms", None),
            P(("groups", "atoms"), None),
            P(("groups", "pair"), "atoms", None),
            P("groups", None),
        )
        + (P(),) * 15,
        out_specs=P(("groups", "pair", "samp"), "atoms", None),
        check_vma=False,
    )
```

```python
import functools
import math

import jax
import jax.numpy as jnp
from jax import lax
from jax.experimental import pallas as pl
from jax.experimental.pallas import tpu as pltpu
from jax.sharding import PartitionSpec as P

Q_WIN = 32
K_WIN = 128
EDGE = 48
GROUP = 32

EPSILON = 1e-05
MASKED = -1e30
LOG2E = math.log2(math.e)
BF16 = jnp.bfloat16
F32 = jnp.float32
LAST = (((1,), (1,)), ((), ()))
VMEM_LIMIT = 32 << 20
IN_VMEM = pl.BlockSpec(memory_space=pltpu.VMEM)
IN_HBM = pl.BlockSpec(memory_space=pltpu.HBM)
IN_SMEM = pl.BlockSpec(memory_space=pltpu.SMEM)


def dot(a, b):
    return jnp.dot(a, b, preferred_element_type=F32)


def iota(shape, dim):
    return lax.broadcasted_iota(jnp.int32, shape, dim)


def twice(matrix):
    blank = jnp.zeros_like(matrix)
    return jnp.concatenate(
        [jnp.concatenate([matrix, blank], 1), jnp.concatenate([blank, matrix], 1)], 0
    )


def side_by_side(rows):
    half = rows.shape[0] // 2
    return jnp.concatenate([rows[:half], rows[half:]], 1)


def centre(rows):
    values = rows.astype(F32)
    centred = values - jnp.mean(values, axis=-1, keepdims=True)
    return centred, jnp.mean(centred * centred, axis=-1, keepdims=True)


def layer_norm(rows):
    centred, variance = centre(rows)
    return centred * lax.rsqrt(variance + EPSILON)


def sigmoid(values):
    return pl.reciprocal(1.0 + jnp.exp2(values * -LOG2E), approx=True)


def attn_norm(cond, single, ada):
    width = single.shape[-1]
    mixed = dot(cond, ada)
    return (sigmoid(mixed[:, :width])[None] * single + mixed[None, :, width:]).astype(BF16)


def pair_kernel(packing, core_ref, w_pair_hbm, pair_hbm, single_hbm, cond_hbm, *refs):
    count = sum(packing)
    weights_hbm, refs = refs[:count], refs[count:]
    tile_ref, single_ref, cond_ref = refs[:3]
    packed_refs, refs = refs[3 : 3 + len(packing)], refs[3 + len(packing) :]
    w_pair_ref, pair_ref, pair_sem, sem = refs
    rows, cols, width = pair_ref.shape
    heads = w_pair_ref.shape[0]
    group = GROUP
    lanes = heads * group
    half = group // 2
    pieces = rows // half
    row_start = core_ref[0] * rows

    def pair_copy(i):
        source = pair_hbm.at[pl.ds(row_start + i * half, half)]
        return pltpu.make_async_copy(source, pair_ref.at[pl.ds(i * half, half)], pair_sem.at[i])

    moves = [(w_pair_hbm, w_pair_ref), (single_hbm, single_ref), (cond_hbm, cond_ref)]
    index = 0
    for number, packed in zip(packing, packed_refs):
        offset = 0
        for _ in range(number):
            source = weights_hbm[index]
            span = source.shape[1]
            moves.append((source, packed.at[:, pl.ds(offset, span)]))
            offset += span
            index += 1
    copies = [
        pltpu.make_async_copy(source, target, sem.at[i])
        for i, (source, target) in enumerate(moves)
    ]
    copies[0].start()
    for i in range(pieces):
        pair_copy(i).start()

    copies[0].wait()
    w_pair = w_pair_ref[...].astype(F32)
    spread = jnp.concatenate(
        [jnp.broadcast_to(w_pair[h : h + 1], (group, width)) for h in range(heads)], 0
    )
    mix = twice(spread.T.astype(BF16))
    slot = iota((cols, lanes), 1) % group

    @pl.loop(0, rows // group)
    def _(chunk):
        for part in range(2):
            pair_copy(chunk * 2 + part).wait()

        @pl.when(chunk == 0)
        def _():
            for copy in copies[1:]:
                copy.start()

        pair = pair_ref[pl.ds(chunk * group, group)].reshape(group * cols, width)
        centred, variance = centre(pair)
        variance = variance.reshape(group, cols, 1)
        mixed = dot(side_by_side(centred.astype(BF16)), mix).reshape(half, cols, 2 * lanes)
        total = jnp.zeros((cols, lanes), F32)
        spread_out = jnp.zeros((cols, lanes), F32)
        for i in range(group):
            side = slice(i // half * lanes, (i // half + 1) * lanes)
            total = jnp.where(slot == i, mixed[i % half, :, side], total)
            spread_out = jnp.where(slot == i, variance[i], spread_out)
        bias = (total * lax.rsqrt(spread_out + EPSILON)).astype(BF16)
        tile_ref[chunk] = bias

    for copy in copies[1:]:
        copy.wait()


def project_kernel(
    at_ref,
    single_ref,
    cond_ref,
    ada_attn,
    ada_trans,
    gates_ref,
    w_kv,
    w_qg,
    w_up,
    w_down,
    query_ref,
    key_ref,
    value_ref,
    gate_ref,
    open_ref,
    trans_ref,
    near_ref,
    far_ref,
):
    samples, atoms_here, width = single_ref.shape
    hidden_width = w_down.shape[0]
    step = math.gcd(atoms_here, 256)
    for start in range(0, atoms_here, step):
        at = slice(start, start + step)
        cond = layer_norm(cond_ref[at, :]).astype(BF16)
        single = layer_norm(single_ref[:, at, :].reshape(-1, width))
        single = single.reshape(samples, step, width)
        normed = attn_norm(cond, single, ada_attn[...])
        if start == 0:
            heads_of = [normed[sample, :EDGE] for sample in range(samples)]
        if start + step == atoms_here:
            tails_of = [normed[sample, step - EDGE :] for sample in range(samples)]
        normed = normed.reshape(-1, width)
        both = dot(normed, w_kv[...]).astype(BF16).reshape(samples, step, 2 * width)
        key_ref[:, at, :] = both[:, :, :width]
        value_ref[:, at, :] = both[:, :, width:]
        both = dot(normed, w_qg[...]).reshape(samples, step, 2 * width)
        query_ref[:, at, :] = both[:, :, :width].astype(BF16)
        gate_ref[:, at, :] = sigmoid(both[:, :, width:]).astype(BF16)
        gates = dot(cond, gates_ref[...])
        open_ref[at, :] = sigmoid(gates[:, :width]).astype(BF16)
        normed = attn_norm(cond, single, ada_trans[...]).reshape(-1, width)
        swish = dot(normed, w_up[:, :hidden_width])
        hidden = (swish * sigmoid(swish) * dot(normed, w_up[:, hidden_width:])).astype(BF16)
        down = dot(hidden, w_down[...]).reshape(samples, step, width)
        trans_ref[:, at, :] = (sigmoid(gates[:, width:])[None] * down).astype(BF16)
    even = at_ref[0] % 2 == 0
    for sample, (head, tail) in enumerate(zip(heads_of, tails_of)):
        cut = slice(sample * EDGE, (sample + 1) * EDGE)
        near_ref[cut, :] = jnp.where(even, tail, head)
        far_ref[cut, :] = jnp.where(even, head, tail)


def tile_of(refs, place, row_block):
    if len(refs) == 1:
        return refs[0][row_block]
    pair_at, core_at = place
    owners = 2
    mine, theirs, across, diagonal = [ref[...] for ref in refs]
    near = jnp.where(row_block % owners == core_at, mine, theirs)
    far = jnp.where(row_block % owners == core_at, across, diagonal)
    return jnp.where(row_block // owners == pair_at, near, far)


def select_kernel(blocks, at_ref, pair_ref, core_ref, *refs):
    *tile_refs, _, __, ___, near_ref, far_ref, ____, held_ref = refs
    groups, cols, lanes = tile_refs[0].shape[-3:]
    rows = groups * cols
    device_at, place = at_ref[0], (pair_ref[0], core_ref[0])
    for send_ref, parity in ((near_ref, 0), (far_ref, 1)):
        beside = jnp.where(device_at % 2 == parity, device_at + 1, device_at - 1)
        tile = tile_of(tile_refs, place, jnp.clip(beside, 0, blocks - 1))
        send_ref[send_ref.shape[0] - rows :, :] = tile.reshape(rows, lanes)
    held_ref[...] = tile_of(tile_refs, place, device_at).reshape(rows, lanes)


def bounds(counts_ref, block, token):
    tok_here = counts_ref.shape[1]
    counts = counts_ref[pl.ds(block, 1), :].astype(F32).astype(BF16)
    counts = jnp.broadcast_to(counts, (8, tok_here))
    before = iota((tok_here, token.shape[1]), 0)
    first = dot(counts, (before < token).astype(BF16))[:1]
    last = dot(counts, (before <= token).astype(BF16))[:1]
    return first.astype(jnp.int32), last.astype(jnp.int32)


def one_hot(reach, offset, count):
    first, last = reach
    position = iota((count, first.shape[1]), 0) + offset
    return ((first <= position) & (position < last)).astype(F32).astype(BF16)


def expand(hot, tile, tok_here):
    tile = tile.reshape(tok_here // GROUP, tok_here, tile.shape[-1])
    tile = jnp.concatenate([tile[part] for part in range(tok_here // GROUP)], 1)
    return dot(hot, tile).astype(BF16)


def attend(heads, reach, windows, query_ref, gate_ref, gated_ref):
    samples, _, width = query_ref.shape
    head_dim = width // heads
    lanes = reach[0].shape[1]
    rows = heads * Q_WIN
    lane_head = iota((rows, lanes), 1) // GROUP % heads
    row_head = iota((rows, lanes), 0) // Q_WIN
    same_head = (lane_head == row_head).astype(F32).astype(BF16)
    own_head = iota((rows, width), 1) // head_dim == iota((rows, width), 0) // Q_WIN
    own_head = own_head.astype(F32).astype(BF16)
    channel_head = iota((Q_WIN, width), 1) // head_dim
    scaling = LOG2E / math.sqrt(head_dim)

    biases = []
    for start, _, near, mask in windows:
        pick = jnp.concatenate([one_hot(reach, start, Q_WIN)] * heads, 0) * same_head
        bias = lax.dot_general(pick, near, LAST, preferred_element_type=F32) * LOG2E
        biases.append(bias if mask is None else jnp.where(mask, bias, MASKED))
    units = [(sample, i) for i in range(len(windows)) for sample in range(samples)]

    def diagonal(parts):
        if len(parts) == 1:
            return parts[0]
        blank = jnp.zeros_like(parts[0])
        return jnp.concatenate(
            [jnp.concatenate([parts[0], blank], 1), jnp.concatenate([blank, parts[1]], 1)], 0
        )

    scores = []
    for first in range(0, len(units), 2):
        couple = units[first : first + 2]
        queries, keys = [], []
        for sample, i in couple:
            query = query_ref[sample, pl.ds(windows[i][0], Q_WIN), :]
            queries.append(jnp.concatenate([query] * heads, 0) * own_head)
            keys.append(windows[i][1](sample)[0])
        product = lax.dot_general(
            jnp.concatenate(queries, 1), diagonal(keys), LAST, preferred_element_type=F32
        )
        for j, (_, i) in enumerate(couple):
            cut = slice(j * K_WIN, (j + 1) * K_WIN)
            scores.append(product[:, cut] * scaling + biases[i])
    tops = [jnp.max(score, axis=-1, keepdims=True) for score in scores]
    raised = [jnp.exp2(score - top) for score, top in zip(scores, tops)]
    sums = [jnp.sum(weight, axis=-1, keepdims=True) for weight in raised]
    raised = [weight.astype(BF16) for weight in raised]
    for first in range(0, len(units), 2):
        couple = units[first : first + 2]
        values = [windows[i][1](sample)[1] for sample, i in couple]
        mixed = dot(jnp.concatenate(raised[first : first + 2], 1), diagonal(values))
        for j, (sample, i) in enumerate(couple):
            cut = slice(j * width, (j + 1) * width)
            picked, total = mixed[:Q_WIN, cut], sums[first + j][:Q_WIN]
            total = jnp.broadcast_to(total, picked.shape)
            for head in range(1, heads):
                rows_of = slice(head * Q_WIN, (head + 1) * Q_WIN)
                picked = jnp.where(channel_head == head, mixed[rows_of, cut], picked)
                total = jnp.where(channel_head == head, sums[first + j][rows_of], total)
            attended = picked * pl.reciprocal(total, approx=True)
            at = pl.ds(windows[i][0], Q_WIN)
            gate = gate_ref[sample, at, :].astype(F32)
            gated_ref[sample, at, :] = (gate * attended).astype(BF16)


def close(sample, cut, gated_ref, open_ref, trans_ref, w_out_ref):
    mixed = dot(gated_ref[sample, cut, :], w_out_ref[...])
    opened, trans = open_ref[cut, :].astype(F32), trans_ref[sample, cut, :].astype(F32)
    return (opened * mixed + trans).astype(BF16)


def row_tokens(heads, tok_here):
    lane = iota((tok_here, heads * tok_here), 1)
    return lane // (heads * GROUP) * GROUP + lane % GROUP


def inner_kernel(
    heads,
    at_ref,
    counts_ref,
    query_ref,
    key_ref,
    value_ref,
    gate_ref,
    open_ref,
    trans_ref,
    w_out_ref,
    held_ref,
    out_ref,
    near_ref,
    gated_ref,
):
    samples, atoms_here, width = query_ref.shape
    tok_here = counts_ref.shape[1]
    device_at = at_ref[0]
    hot = one_hot(
        bounds(counts_ref, device_at, iota((tok_here, tok_here), 1)), 0, atoms_here
    )
    near_ref[...] = expand(hot, held_ref[...], tok_here)
    reach = bounds(counts_ref, device_at, row_tokens(heads, tok_here))
    skip = -(-EDGE // Q_WIN)
    inner = atoms_here // Q_WIN - 2 * skip
    batch = math.gcd(inner, 4)

    @pl.loop(0, inner // batch)
    def _(turn):
        windows = []
        for i in range(batch):
            start = pl.multiple_of((turn * batch + i + skip) * Q_WIN, Q_WIN)
            cut = pl.ds(pl.multiple_of(start - EDGE, 16), K_WIN)
            parts = lambda sample, cut=cut: (key_ref[sample, cut, :], value_ref[sample, cut, :])
            windows.append((start, parts, near_ref[cut, :], None))
        attend(heads, reach, windows, query_ref, gate_ref, gated_ref)

    cut = slice(skip * Q_WIN, atoms_here - skip * Q_WIN)
    for sample in range(samples):
        out_ref[sample] = close(sample, cut, gated_ref, open_ref, trans_ref, w_out_ref)


def outer_kernel(
    heads,
    blocks,
    at_ref,
    counts_ref,
    query_ref,
    own_key_ref,
    own_value_ref,
    gate_ref,
    open_ref,
    trans_ref,
    w_out_ref,
    held_ref,
    inner_ref,
    w_kv,
    first_ref,
    second_ref,
    out_hbm,
    key_ref,
    value_ref,
    near_ref,
    gated_ref,
    out_ref,
    sem,
):
    samples, atoms_here, width = query_ref.shape
    tok_here = counts_ref.shape[1]
    device_at = at_ref[0]
    ends = atoms_here * blocks
    skip = -(-EDGE // Q_WIN)
    margin = skip * Q_WIN
    reach_keys = key_ref.shape[2]
    inside = reach_keys - EDGE

    whole = pltpu.make_async_copy(
        inner_ref, out_hbm.at[:, pl.ds(margin, atoms_here - 2 * margin)], sem.at[0]
    )
    whole.start()

    even = device_at % 2 == 0
    first, second = first_ref[...], second_ref[...]
    arrived = (jnp.where(even, second, first), jnp.where(even, first, second))
    count = samples * EDGE
    edges = jnp.concatenate([rows[:count] for rows in arrived], 0)
    edges = dot(edges, w_kv[...]).astype(BF16).reshape(2, samples, EDGE, 2 * width)
    token = iota((tok_here, tok_here), 1)
    own_reach = bounds(counts_ref, device_at, token)
    sides = (
        (jnp.maximum(device_at - 1, 0), atoms_here - EDGE, 0, EDGE, 0),
        (jnp.minimum(device_at + 1, blocks - 1), 0, inside, 0, atoms_here - inside),
    )
    for side, (block, offset, place, own_place, own_start) in enumerate(sides):
        for i, (ref, own_ref) in enumerate(((key_ref, own_key_ref), (value_ref, own_value_ref))):
            ref[side, :, place : place + EDGE, :] = edges[side, :, :, i * width : (i + 1) * width]
            ref[side, :, own_place : own_place + inside, :] = own_ref[
                :, own_start : own_start + inside, :
            ]
        hot = one_hot(bounds(counts_ref, block, token), offset, EDGE)
        near_ref[side, place : place + EDGE, :] = expand(hot, arrived[side][count:], tok_here)
        hot = one_hot(own_reach, own_start, inside)
        near_ref[side, own_place : own_place + inside, :] = expand(hot, held_ref[...], tok_here)

    reach = bounds(counts_ref, device_at, row_tokens(heads, tok_here))
    windows = []
    for side in range(2):
        for i in range(skip):
            start = i * Q_WIN + side * (atoms_here - margin)
            cut = slice(i * Q_WIN, i * Q_WIN + K_WIN)
            parts = lambda sample, side=side, cut=cut: (
                key_ref[side, sample, cut, :],
                value_ref[side, sample, cut, :],
            )
            key_at = iota((heads * Q_WIN, K_WIN), 1) + (device_at * atoms_here + start - EDGE)
            mask = (key_at >= 0) & (key_at < ends)
            windows.append((start, parts, near_ref[side, cut, :], mask))
    attend(heads, reach, windows, query_ref, gate_ref, gated_ref)
    copies = []
    for side in range(2):
        cut = slice(side * (atoms_here - margin), side * (atoms_here - margin) + margin)
        for sample in range(samples):
            out_ref[side, sample] = close(sample, cut, gated_ref, open_ref, trans_ref, w_out_ref)
        target = out_hbm.at[:, pl.ds(side * (atoms_here - margin), margin)]
        copies.append(pltpu.make_async_copy(out_ref.at[side], target, sem.at[1 + side]))
        copies[-1].start()
    for copy in copies:
        copy.wait()
    whole.wait()


def shards(
    atom_single,
    atom_cond,
    pair_cond,
    atom_counts,
    ada_attn_scale,
    ada_attn_shift,
    w_query,
    w_key,
    w_value,
    w_gate,
    w_out,
    attn_gate,
    w_pair,
    ada_trans_scale,
    ada_trans_shift,
    w_swish,
    w_linear,
    w_down,
    trans_gate,
):
    device_at = lax.axis_index("atoms")
    blocks = lax.axis_size("atoms")
    samples, atoms_here, width = atom_single.shape
    tok_here = atom_counts.shape[1]
    heads = w_pair.shape[1]
    groups = tok_here // GROUP
    pairs = lax.axis_size("pair")
    assert pair_cond.shape[0] == lax.axis_size("samp") * tok_here
    at = device_at.astype(jnp.int32).reshape(1)
    pair_at = lax.axis_index("pair").astype(jnp.int32).reshape(1)
    core_at = lax.axis_index("samp").astype(jnp.int32).reshape(1)
    in_hbm = lambda array: pltpu.with_memory_space_constraint(array, pltpu.HBM)
    in_vmem = lambda array: pltpu.with_memory_space_constraint(array, pltpu.VMEM)

    packing = (
        (ada_attn_scale, ada_attn_shift),
        (ada_trans_scale, ada_trans_shift),
        (attn_gate, trans_gate),
        (w_key, w_value),
        (w_query, w_gate),
        (w_swish, w_linear),
        (w_down,),
        (w_out,),
    )
    flat = [array for arrays in packing for array in arrays]
    cols = pair_cond.shape[1]
    lanes = heads * GROUP
    wide = (samples, atoms_here, width)
    params = pltpu.CompilerParams(vmem_limit_bytes=VMEM_LIMIT)

    def cost(products):
        return pl.CostEstimate(flops=2 * products, bytes_accessed=4 << 20, transcendentals=0)

    sent = pltpu.VMEM((samples * EDGE + groups * cols, lanes), BF16)
    shapes = [
        pltpu.VMEM((groups, cols, lanes), BF16),
        pltpu.VMEM(wide, BF16),
        pltpu.VMEM(atom_cond.shape, BF16),
    ] + [
        pltpu.VMEM((arrays[0].shape[0], sum(a.shape[1] for a in arrays)), BF16)
        for arrays in packing
    ]
    made = pl.pallas_call(
        functools.partial(pair_kernel, [len(arrays) for arrays in packing]),
        in_specs=[IN_SMEM] + [IN_HBM] * (4 + len(flat)),
        out_specs=[IN_VMEM] * len(shapes),
        out_shape=shapes,
        scratch_shapes=[
            pltpu.VMEM((heads, width), BF16),
            pltpu.VMEM((tok_here, cols, width), BF16),
            pltpu.SemaphoreType.DMA((2 * groups,)),
            pltpu.SemaphoreType.DMA((3 + len(flat),)),
        ],
        compiler_params=params,
        cost_estimate=cost(tok_here * cols * width * width * 2),
    )(core_at, *map(in_hbm, (w_pair.T, pair_cond, atom_single, atom_cond, *flat)))
    own, single, cond, *packed = made
    ada_attn, ada_trans, gates, w_kv, w_qg, w_up, w_down, w_out = packed
    if pairs == 2:
        swapped = [(0, 1), (1, 0)]
        across = lax.ppermute(own, "pair", swapped)
        diagonal = lax.ppermute(own, ("pair", "samp"), [(0, 3), (1, 2), (2, 1), (3, 0)])
        tiles = (own, lax.ppermute(own, "samp", swapped), across, diagonal)
    else:
        tiles = (lax.all_gather(own, ("pair", "samp")),)

    operands = (single, cond, ada_attn, ada_trans, gates, w_kv, w_qg, w_up, w_down)
    query, keys, values, gate, opened, trans, near, far = pl.pallas_call(
        project_kernel,
        in_specs=[IN_SMEM] + [IN_VMEM] * len(operands),
        out_specs=[IN_VMEM] * 8,
        out_shape=[pltpu.VMEM(wide, BF16)] * 4
        + [pltpu.VMEM((atoms_here, width), BF16), pltpu.VMEM(wide, BF16), sent, sent],
        compiler_params=params,
        cost_estimate=cost(samples * atoms_here * width * width * 20),
    )(at, *map(in_vmem, operands))

    operands = (*tiles, near, far, opened)
    first = 3 + len(tiles)
    near, far, opened, held = pl.pallas_call(
        functools.partial(select_kernel, blocks),
        in_specs=[IN_SMEM] * 3 + [IN_VMEM] * len(operands),
        out_specs=[IN_VMEM] * 4,
        out_shape=[
            sent,
            sent,
            pltpu.VMEM((atoms_here, width), BF16),
            pltpu.VMEM((groups * cols, lanes), BF16),
        ],
        input_output_aliases={first: 0, first + 1: 1, first + 2: 2},
        compiler_params=params,
    )(at, pair_at, core_at, *map(in_vmem, operands))

    def swap(value, start):
        sides = [(i, i + 1) for i in range(start, blocks - 1, 2)]
        alone = set(range(blocks)) - {i for side in sides for i in side}
        pairs_of = sides + [(j, i) for i, j in sides] + [(i, i) for i in sorted(alone)]
        return lax.ppermute(value, "atoms", pairs_of)

    first, second = swap(near, 0), swap(far, 1)

    margin = -(-EDGE // Q_WIN) * Q_WIN
    operands = (query, keys, values, gate, opened, trans, w_out, held)
    inner = pl.pallas_call(
        functools.partial(inner_kernel, heads),
        in_specs=[IN_SMEM] + [IN_VMEM] * (1 + len(operands)),
        out_specs=IN_VMEM,
        out_shape=pltpu.VMEM((samples, atoms_here - 2 * margin, width), BF16),
        scratch_shapes=[
            pltpu.VMEM((atoms_here, heads * tok_here), BF16),
            pltpu.VMEM(wide, BF16),
        ],
        compiler_params=params,
        cost_estimate=cost(samples * atoms_here * width * width * 12),
    )(at, atom_counts, *map(in_vmem, operands))

    reach = margin - Q_WIN + K_WIN
    operands += (inner, w_kv, first, second)
    return pl.pallas_call(
        functools.partial(outer_kernel, heads, blocks),
        in_specs=[IN_SMEM] + [IN_VMEM] * (1 + len(operands)),
        out_specs=IN_HBM,
        out_shape=pltpu.HBM(wide, BF16),
        scratch_shapes=[
            pltpu.VMEM((2, samples, reach, width), BF16),
            pltpu.VMEM((2, samples, reach, width), BF16),
            pltpu.VMEM((2, reach, heads * tok_here), BF16),
            pltpu.VMEM(wide, BF16),
            pltpu.VMEM((2, samples, margin, width), BF16),
            pltpu.SemaphoreType.DMA((3,)),
        ],
        compiler_params=params,
        cost_estimate=cost(samples * atoms_here * width * width * 4),
    )(at, atom_counts, *map(in_vmem, operands))


def solution(mesh):
    return jax.shard_map(
        shards,
        mesh=mesh,
        in_specs=(
            P(("groups", "pair", "samp"), "atoms", None),
            P(("groups", "atoms"), None),
            P(("groups", "pair"), "atoms", None),
            P("groups", None),
        )
        + (P(),) * 15,
        out_specs=P(("groups", "pair", "samp"), "atoms", None),
        check_vma=False,
    )
```

```python
import functools
import math

import jax
import jax.numpy as jnp
from jax import lax
from jax.experimental import pallas as pl
from jax.experimental.pallas import tpu as pltpu
from jax.sharding import PartitionSpec as P

Q_WIN = 32
K_WIN = 128
EDGE = 48
GROUP = 32

EPSILON = 1e-05
MASKED = -1e30
LOG2E = math.log2(math.e)
BF16 = jnp.bfloat16
F32 = jnp.float32
LAST = (((1,), (1,)), ((), ()))
VMEM_LIMIT = 32 << 20
IN_VMEM = pl.BlockSpec(memory_space=pltpu.VMEM)
IN_HBM = pl.BlockSpec(memory_space=pltpu.HBM)
IN_SMEM = pl.BlockSpec(memory_space=pltpu.SMEM)


def dot(a, b):
    return jnp.dot(a, b, preferred_element_type=F32)


def iota(shape, dim):
    return lax.broadcasted_iota(jnp.int32, shape, dim)


def twice(matrix):
    blank = jnp.zeros_like(matrix)
    return jnp.concatenate(
        [jnp.concatenate([matrix, blank], 1), jnp.concatenate([blank, matrix], 1)], 0
    )


def side_by_side(rows):
    half = rows.shape[0] // 2
    return jnp.concatenate([rows[:half], rows[half:]], 1)


def centre(rows):
    values = rows.astype(F32)
    centred = values - jnp.mean(values, axis=-1, keepdims=True)
    return centred, jnp.mean(centred * centred, axis=-1, keepdims=True)


def layer_norm(rows):
    centred, variance = centre(rows)
    return centred * lax.rsqrt(variance + EPSILON)


def sigmoid(values):
    return 0.5 * jnp.tanh(0.5 * values) + 0.5


def attn_norm(cond, single, ada):
    width = single.shape[-1]
    mixed = dot(cond, ada)
    return (sigmoid(mixed[:, :width])[None] * single + mixed[None, :, width:]).astype(BF16)


def pair_kernel(packing, core_ref, w_pair_hbm, pair_hbm, single_hbm, cond_hbm, *refs):
    count = sum(packing)
    weights_hbm, refs = refs[:count], refs[count:]
    tile_ref, single_ref, cond_ref = refs[:3]
    packed_refs, refs = refs[3 : 3 + len(packing)], refs[3 + len(packing) :]
    w_pair_ref, pair_ref, pair_sem, sem = refs
    rows, cols, width = pair_ref.shape
    heads = w_pair_ref.shape[0]
    group = GROUP
    lanes = heads * group
    half = group // 2
    pieces = rows // half
    row_start = core_ref[0] * rows

    def pair_copy(i):
        source = pair_hbm.at[pl.ds(row_start + i * half, half)]
        return pltpu.make_async_copy(source, pair_ref.at[pl.ds(i * half, half)], pair_sem.at[i])

    moves = [(w_pair_hbm, w_pair_ref), (single_hbm, single_ref), (cond_hbm, cond_ref)]
    index = 0
    for number, packed in zip(packing, packed_refs):
        offset = 0
        for _ in range(number):
            source = weights_hbm[index]
            span = source.shape[1]
            moves.append((source, packed.at[:, pl.ds(offset, span)]))
            offset += span
            index += 1
    copies = [
        pltpu.make_async_copy(source, target, sem.at[i])
        for i, (source, target) in enumerate(moves)
    ]
    copies[0].start()
    for i in range(pieces):
        pair_copy(i).start()
    for copy in copies[1:]:
        copy.start()

    copies[0].wait()
    w_pair = w_pair_ref[...].astype(F32)
    spread = jnp.concatenate(
        [jnp.broadcast_to(w_pair[h : h + 1], (group, width)) for h in range(heads)], 0
    )
    mix = twice(spread.T.astype(BF16))
    slot = iota((cols, lanes), 1) % group

    @pl.loop(0, rows // group)
    def _(chunk):
        for part in range(2):
            pair_copy(chunk * 2 + part).wait()

        pair = pair_ref[pl.ds(chunk * group, group)].reshape(group * cols, width)
        centred, variance = centre(pair)
        variance = variance.reshape(group, cols, 1)
        mixed = dot(side_by_side(centred.astype(BF16)), mix).reshape(half, cols, 2 * lanes)
        total = jnp.zeros((cols, lanes), F32)
        spread_out = jnp.zeros((cols, lanes), F32)
        for i in range(group):
            side = slice(i // half * lanes, (i // half + 1) * lanes)
            total = jnp.where(slot == i, mixed[i % half, :, side], total)
            spread_out = jnp.where(slot == i, variance[i], spread_out)
        bias = (total * lax.rsqrt(spread_out + EPSILON)).astype(BF16)
        tile_ref[chunk] = bias

    for copy in copies[1:]:
        copy.wait()


def project_kernel(
    at_ref,
    single_ref,
    cond_ref,
    ada_attn,
    ada_trans,
    gates_ref,
    w_kv,
    w_qg,
    w_up,
    w_down,
    query_ref,
    key_ref,
    value_ref,
    gate_ref,
    open_ref,
    trans_ref,
    near_ref,
    far_ref,
):
    samples, atoms_here, width = single_ref.shape
    hidden_width = w_down.shape[0]
    step = math.gcd(atoms_here, 256)
    for start in range(0, atoms_here, step):
        at = slice(start, start + step)
        cond = layer_norm(cond_ref[at, :]).astype(BF16)
        single = layer_norm(single_ref[:, at, :].reshape(-1, width))
        single = single.reshape(samples, step, width)
        normed = attn_norm(cond, single, ada_attn[...])
        if start == 0:
            heads_of = [normed[sample, :EDGE] for sample in range(samples)]
        if start + step == atoms_here:
            tails_of = [normed[sample, step - EDGE :] for sample in range(samples)]
        normed = normed.reshape(-1, width)
        both = dot(normed, w_kv[...]).astype(BF16).reshape(samples, step, 2 * width)
        key_ref[:, at, :] = both[:, :, :width]
        value_ref[:, at, :] = both[:, :, width:]
        both = dot(normed, w_qg[...]).reshape(samples, step, 2 * width)
        query_ref[:, at, :] = both[:, :, :width].astype(BF16)
        gate_ref[:, at, :] = sigmoid(both[:, :, width:]).astype(BF16)
        gates = dot(cond, gates_ref[...])
        open_ref[at, :] = sigmoid(gates[:, :width]).astype(BF16)
        normed = attn_norm(cond, single, ada_trans[...]).reshape(-1, width)
        swish = dot(normed, w_up[:, :hidden_width])
        hidden = (swish * sigmoid(swish) * dot(normed, w_up[:, hidden_width:])).astype(BF16)
        down = dot(hidden, w_down[...]).reshape(samples, step, width)
        trans_ref[:, at, :] = (sigmoid(gates[:, width:])[None] * down).astype(BF16)
    even = at_ref[0] % 2 == 0
    for sample, (head, tail) in enumerate(zip(heads_of, tails_of)):
        cut = slice(sample * EDGE, (sample + 1) * EDGE)
        near_ref[cut, :] = jnp.where(even, tail, head)
        far_ref[cut, :] = jnp.where(even, head, tail)


def tile_of(refs, place, row_block):
    if len(refs) == 1:
        return refs[0][row_block]
    pair_at, core_at = place
    owners = 2
    mine, theirs, across, diagonal = [ref[...] for ref in refs]
    near = jnp.where(row_block % owners == core_at, mine, theirs)
    far = jnp.where(row_block % owners == core_at, across, diagonal)
    return jnp.where(row_block // owners == pair_at, near, far)


def select_kernel(blocks, at_ref, pair_ref, core_ref, *refs):
    *tile_refs, _, __, ___, near_ref, far_ref, ____, held_ref = refs
    groups, cols, lanes = tile_refs[0].shape[-3:]
    rows = groups * cols
    device_at, place = at_ref[0], (pair_ref[0], core_ref[0])
    for send_ref, parity in ((near_ref, 0), (far_ref, 1)):
        beside = jnp.where(device_at % 2 == parity, device_at + 1, device_at - 1)
        tile = tile_of(tile_refs, place, jnp.clip(beside, 0, blocks - 1))
        send_ref[send_ref.shape[0] - rows :, :] = tile.reshape(rows, lanes)
    held_ref[...] = tile_of(tile_refs, place, device_at).reshape(rows, lanes)


def bounds(counts_ref, block, token):
    tok_here = counts_ref.shape[1]
    counts = counts_ref[pl.ds(block, 1), :].astype(F32).astype(BF16)
    counts = jnp.broadcast_to(counts, (8, tok_here))
    before = iota((tok_here, token.shape[1]), 0)
    first = dot(counts, (before < token).astype(BF16))[:1]
    last = dot(counts, (before <= token).astype(BF16))[:1]
    return first.astype(jnp.int32), last.astype(jnp.int32)


def one_hot(reach, offset, count):
    first, last = reach
    position = iota((count, first.shape[1]), 0) + offset
    return ((first <= position) & (position < last)).astype(F32).astype(BF16)


def expand(hot, tile, tok_here):
    tile = tile.reshape(tok_here // GROUP, tok_here, tile.shape[-1])
    tile = jnp.concatenate([tile[part] for part in range(tok_here // GROUP)], 1)
    return dot(hot, tile).astype(BF16)


def attend(heads, reach, windows, query_ref, gate_ref, gated_ref):
    samples, _, width = query_ref.shape
    head_dim = width // heads
    lanes = reach[0].shape[1]
    rows = heads * Q_WIN
    lane_head = iota((rows, lanes), 1) // GROUP % heads
    row_head = iota((rows, lanes), 0) // Q_WIN
    same_head = (lane_head == row_head).astype(F32).astype(BF16)
    own_head = iota((rows, width), 1) // head_dim == iota((rows, width), 0) // Q_WIN
    own_head = own_head.astype(F32).astype(BF16)
    channel_head = iota((Q_WIN, 2 * width), 1) % width // head_dim
    ones = jnp.ones((K_WIN, width), BF16)
    scaling = LOG2E / math.sqrt(head_dim)

    biases = []
    for start, _, near, mask in windows:
        pick = jnp.concatenate([one_hot(reach, start, Q_WIN)] * heads, 0) * same_head
        bias = lax.dot_general(pick, near, LAST, preferred_element_type=F32) * LOG2E
        biases.append(bias if mask is None else jnp.where(mask, bias, MASKED))
    units = [(sample, i) for i in range(len(windows)) for sample in range(samples)]
    scores = []
    for sample, i in units:
        query = query_ref[sample, pl.ds(windows[i][0], Q_WIN), :]
        query = jnp.concatenate([query] * heads, 0) * own_head
        keys = windows[i][1](sample)[0]
        product = lax.dot_general(query, keys, LAST, preferred_element_type=F32)
        scores.append(product * scaling + biases[i])
    tops = [jnp.max(score, axis=-1, keepdims=True) for score in scores]
    raised = [jnp.exp2(score - top).astype(BF16) for score, top in zip(scores, tops)]
    for (sample, i), weight in zip(units, raised):
        values = windows[i][1](sample)[1]
        mixed = dot(weight, jnp.concatenate([values, ones], 1))
        picked = mixed[:Q_WIN]
        for head in range(1, heads):
            picked = jnp.where(
                channel_head == head, mixed[head * Q_WIN : (head + 1) * Q_WIN], picked
            )
        attended = picked[:, :width] * pl.reciprocal(picked[:, width:], approx=True)
        at = pl.ds(windows[i][0], Q_WIN)
        gate = gate_ref[sample, at, :].astype(F32)
        gated_ref[sample, at, :] = (gate * attended).astype(BF16)


def close(sample, cut, gated_ref, open_ref, trans_ref, w_out_ref):
    mixed = dot(gated_ref[sample, cut, :], w_out_ref[...])
    opened, trans = open_ref[cut, :].astype(F32), trans_ref[sample, cut, :].astype(F32)
    return (opened * mixed + trans).astype(BF16)


def row_tokens(heads, tok_here):
    lane = iota((tok_here, heads * tok_here), 1)
    return lane // (heads * GROUP) * GROUP + lane % GROUP


def inner_kernel(
    heads,
    at_ref,
    counts_ref,
    query_ref,
    key_ref,
    value_ref,
    gate_ref,
    open_ref,
    trans_ref,
    w_out_ref,
    held_ref,
    out_ref,
    near_ref,
    gated_ref,
):
    samples, atoms_here, width = query_ref.shape
    tok_here = counts_ref.shape[1]
    device_at = at_ref[0]
    hot = one_hot(
        bounds(counts_ref, device_at, iota((tok_here, tok_here), 1)), 0, atoms_here
    )
    near_ref[...] = expand(hot, held_ref[...], tok_here)
    reach = bounds(counts_ref, device_at, row_tokens(heads, tok_here))
    skip = -(-EDGE // Q_WIN)
    inner = atoms_here // Q_WIN - 2 * skip
    batch = math.gcd(inner, 12)

    @pl.loop(0, inner // batch)
    def _(turn):
        windows = []
        for i in range(batch):
            start = pl.multiple_of((turn * batch + i + skip) * Q_WIN, Q_WIN)
            cut = pl.ds(pl.multiple_of(start - EDGE, 16), K_WIN)
            parts = lambda sample, cut=cut: (key_ref[sample, cut, :], value_ref[sample, cut, :])
            windows.append((start, parts, near_ref[cut, :], None))
        attend(heads, reach, windows, query_ref, gate_ref, gated_ref)

    cut = slice(skip * Q_WIN, atoms_here - skip * Q_WIN)
    for sample in range(samples):
        out_ref[sample] = close(sample, cut, gated_ref, open_ref, trans_ref, w_out_ref)


def outer_kernel(
    heads,
    blocks,
    at_ref,
    counts_ref,
    query_ref,
    own_key_ref,
    own_value_ref,
    gate_ref,
    open_ref,
    trans_ref,
    w_out_ref,
    held_ref,
    inner_ref,
    w_kv,
    first_ref,
    second_ref,
    out_hbm,
    key_ref,
    value_ref,
    near_ref,
    gated_ref,
    out_ref,
    sem,
):
    samples, atoms_here, width = query_ref.shape
    tok_here = counts_ref.shape[1]
    device_at = at_ref[0]
    ends = atoms_here * blocks
    skip = -(-EDGE // Q_WIN)
    margin = skip * Q_WIN
    reach_keys = key_ref.shape[2]
    inside = reach_keys - EDGE

    whole = pltpu.make_async_copy(
        inner_ref, out_hbm.at[:, pl.ds(margin, atoms_here - 2 * margin)], sem.at[0]
    )
    whole.start()

    even = device_at % 2 == 0
    first, second = first_ref[...], second_ref[...]
    arrived = (jnp.where(even, second, first), jnp.where(even, first, second))
    count = samples * EDGE
    edges = jnp.concatenate([rows[:count] for rows in arrived], 0)
    edges = dot(edges, w_kv[...]).astype(BF16).reshape(2, samples, EDGE, 2 * width)
    token = iota((tok_here, tok_here), 1)
    own_reach = bounds(counts_ref, device_at, token)
    sides = (
        (jnp.maximum(device_at - 1, 0), atoms_here - EDGE, 0, EDGE, 0),
        (jnp.minimum(device_at + 1, blocks - 1), 0, inside, 0, atoms_here - inside),
    )
    for side, (block, offset, place, own_place, own_start) in enumerate(sides):
        for i, (ref, own_ref) in enumerate(((key_ref, own_key_ref), (value_ref, own_value_ref))):
            ref[side, :, place : place + EDGE, :] = edges[side, :, :, i * width : (i + 1) * width]
            ref[side, :, own_place : own_place + inside, :] = own_ref[
                :, own_start : own_start + inside, :
            ]
        hot = one_hot(bounds(counts_ref, block, token), offset, EDGE)
        near_ref[side, place : place + EDGE, :] = expand(hot, arrived[side][count:], tok_here)
        hot = one_hot(own_reach, own_start, inside)
        near_ref[side, own_place : own_place + inside, :] = expand(hot, held_ref[...], tok_here)

    reach = bounds(counts_ref, device_at, row_tokens(heads, tok_here))
    windows = []
    for side in range(2):
        for i in range(skip):
            start = i * Q_WIN + side * (atoms_here - margin)
            cut = slice(i * Q_WIN, i * Q_WIN + K_WIN)
            parts = lambda sample, side=side, cut=cut: (
                key_ref[side, sample, cut, :],
                value_ref[side, sample, cut, :],
            )
            key_at = iota((heads * Q_WIN, K_WIN), 1) + (device_at * atoms_here + start - EDGE)
            mask = (key_at >= 0) & (key_at < ends)
            windows.append((start, parts, near_ref[side, cut, :], mask))
    attend(heads, reach, windows, query_ref, gate_ref, gated_ref)
    copies = []
    for side in range(2):
        cut = slice(side * (atoms_here - margin), side * (atoms_here - margin) + margin)
        for sample in range(samples):
            out_ref[side, sample] = close(sample, cut, gated_ref, open_ref, trans_ref, w_out_ref)
        target = out_hbm.at[:, pl.ds(side * (atoms_here - margin), margin)]
        copies.append(pltpu.make_async_copy(out_ref.at[side], target, sem.at[1 + side]))
        copies[-1].start()
    for copy in copies:
        copy.wait()
    whole.wait()


def shards(
    atom_single,
    atom_cond,
    pair_cond,
    atom_counts,
    ada_attn_scale,
    ada_attn_shift,
    w_query,
    w_key,
    w_value,
    w_gate,
    w_out,
    attn_gate,
    w_pair,
    ada_trans_scale,
    ada_trans_shift,
    w_swish,
    w_linear,
    w_down,
    trans_gate,
):
    device_at = lax.axis_index("atoms")
    blocks = lax.axis_size("atoms")
    samples, atoms_here, width = atom_single.shape
    tok_here = atom_counts.shape[1]
    heads = w_pair.shape[1]
    groups = tok_here // GROUP
    pairs = lax.axis_size("pair")
    assert pair_cond.shape[0] == lax.axis_size("samp") * tok_here
    at = device_at.astype(jnp.int32).reshape(1)
    pair_at = lax.axis_index("pair").astype(jnp.int32).reshape(1)
    core_at = lax.axis_index("samp").astype(jnp.int32).reshape(1)
    in_hbm = lambda array: pltpu.with_memory_space_constraint(array, pltpu.HBM)
    in_vmem = lambda array: pltpu.with_memory_space_constraint(array, pltpu.VMEM)

    packing = (
        (ada_attn_scale, ada_attn_shift),
        (ada_trans_scale, ada_trans_shift),
        (attn_gate, trans_gate),
        (w_key, w_value),
        (w_query, w_gate),
        (w_swish, w_linear),
        (w_down,),
        (w_out,),
    )
    flat = [array for arrays in packing for array in arrays]
    cols = pair_cond.shape[1]
    lanes = heads * GROUP
    wide = (samples, atoms_here, width)
    params = pltpu.CompilerParams(vmem_limit_bytes=VMEM_LIMIT)

    def cost(products):
        return pl.CostEstimate(flops=2 * products, bytes_accessed=4 << 20, transcendentals=0)

    sent = pltpu.VMEM((samples * EDGE + groups * cols, lanes), BF16)
    shapes = [
        pltpu.VMEM((groups, cols, lanes), BF16),
        pltpu.VMEM(wide, BF16),
        pltpu.VMEM(atom_cond.shape, BF16),
    ] + [
        pltpu.VMEM((arrays[0].shape[0], sum(a.shape[1] for a in arrays)), BF16)
        for arrays in packing
    ]
    made = pl.pallas_call(
        functools.partial(pair_kernel, [len(arrays) for arrays in packing]),
        in_specs=[IN_SMEM] + [IN_HBM] * (4 + len(flat)),
        out_specs=[IN_VMEM] * len(shapes),
        out_shape=shapes,
        scratch_shapes=[
            pltpu.VMEM((heads, width), BF16),
            pltpu.VMEM((tok_here, cols, width), BF16),
            pltpu.SemaphoreType.DMA((2 * groups,)),
            pltpu.SemaphoreType.DMA((3 + len(flat),)),
        ],
        compiler_params=params,
        cost_estimate=cost(tok_here * cols * width * width * 2),
    )(core_at, *map(in_hbm, (w_pair.T, pair_cond, atom_single, atom_cond, *flat)))
    own, single, cond, *packed = made
    ada_attn, ada_trans, gates, w_kv, w_qg, w_up, w_down, w_out = packed
    if pairs == 2:
        swapped = [(0, 1), (1, 0)]
        across = lax.ppermute(own, "pair", swapped)
        diagonal = lax.ppermute(own, ("pair", "samp"), [(0, 3), (1, 2), (2, 1), (3, 0)])
        tiles = (own, lax.ppermute(own, "samp", swapped), across, diagonal)
    else:
        tiles = (lax.all_gather(own, ("pair", "samp")),)

    operands = (single, cond, ada_attn, ada_trans, gates, w_kv, w_qg, w_up, w_down)
    query, keys, values, gate, opened, trans, near, far = pl.pallas_call(
        project_kernel,
        in_specs=[IN_SMEM] + [IN_VMEM] * len(operands),
        out_specs=[IN_VMEM] * 8,
        out_shape=[pltpu.VMEM(wide, BF16)] * 4
        + [pltpu.VMEM((atoms_here, width), BF16), pltpu.VMEM(wide, BF16), sent, sent],
        compiler_params=params,
        cost_estimate=cost(samples * atoms_here * width * width * 20),
    )(at, *map(in_vmem, operands))

    operands = (*tiles, near, far, opened)
    first = 3 + len(tiles)
    near, far, opened, held = pl.pallas_call(
        functools.partial(select_kernel, blocks),
        in_specs=[IN_SMEM] * 3 + [IN_VMEM] * len(operands),
        out_specs=[IN_VMEM] * 4,
        out_shape=[
            sent,
            sent,
            pltpu.VMEM((atoms_here, width), BF16),
            pltpu.VMEM((groups * cols, lanes), BF16),
        ],
        input_output_aliases={first: 0, first + 1: 1, first + 2: 2},
        compiler_params=params,
    )(at, pair_at, core_at, *map(in_vmem, operands))

    def swap(value, start):
        sides = [(i, i + 1) for i in range(start, blocks - 1, 2)]
        alone = set(range(blocks)) - {i for side in sides for i in side}
        pairs_of = sides + [(j, i) for i, j in sides] + [(i, i) for i in sorted(alone)]
        return lax.ppermute(value, "atoms", pairs_of)

    first, second = swap(near, 0), swap(far, 1)

    margin = -(-EDGE // Q_WIN) * Q_WIN
    operands = (query, keys, values, gate, opened, trans, w_out, held)
    inner = pl.pallas_call(
        functools.partial(inner_kernel, heads),
        in_specs=[IN_SMEM] + [IN_VMEM] * (1 + len(operands)),
        out_specs=IN_VMEM,
        out_shape=pltpu.VMEM((samples, atoms_here - 2 * margin, width), BF16),
        scratch_shapes=[
            pltpu.VMEM((atoms_here, heads * tok_here), BF16),
            pltpu.VMEM(wide, BF16),
        ],
        compiler_params=params,
        cost_estimate=cost(samples * atoms_here * width * width * 12),
    )(at, atom_counts, *map(in_vmem, operands))

    reach = margin - Q_WIN + K_WIN
    operands += (inner, w_kv, first, second)
    return pl.pallas_call(
        functools.partial(outer_kernel, heads, blocks),
        in_specs=[IN_SMEM] + [IN_VMEM] * (1 + len(operands)),
        out_specs=IN_HBM,
        out_shape=pltpu.HBM(wide, BF16),
        scratch_shapes=[
            pltpu.VMEM((2, samples, reach, width), BF16),
            pltpu.VMEM((2, samples, reach, width), BF16),
            pltpu.VMEM((2, reach, heads * tok_here), BF16),
            pltpu.VMEM(wide, BF16),
            pltpu.VMEM((2, samples, margin, width), BF16),
            pltpu.SemaphoreType.DMA((3,)),
        ],
        compiler_params=params,
        cost_estimate=cost(samples * atoms_here * width * width * 4),
    )(at, atom_counts, *map(in_vmem, operands))


def solution(mesh):
    return jax.shard_map(
        shards,
        mesh=mesh,
        in_specs=(
            P(("groups", "pair", "samp"), "atoms", None),
            P(("groups", "atoms"), None),
            P(("groups", "pair"), "atoms", None),
            P("groups", None),
        )
        + (P(),) * 15,
        out_specs=P(("groups", "pair", "samp"), "atoms", None),
        check_vma=False,
    )
```

```python
import functools
import math

import jax
import jax.numpy as jnp
from jax import lax
from jax.experimental import pallas as pl
from jax.experimental.pallas import tpu as pltpu
from jax.sharding import PartitionSpec as P

Q_WIN = 32
K_WIN = 128
EDGE = 48
GROUP = 32

EPSILON = 1e-05
MASKED = -1e30
LOG2E = math.log2(math.e)
BF16 = jnp.bfloat16
F32 = jnp.float32
LAST = (((1,), (1,)), ((), ()))
VMEM_LIMIT = 32 << 20
IN_VMEM = pl.BlockSpec(memory_space=pltpu.VMEM)
IN_HBM = pl.BlockSpec(memory_space=pltpu.HBM)
IN_SMEM = pl.BlockSpec(memory_space=pltpu.SMEM)


def dot(a, b):
    return jnp.dot(a, b, preferred_element_type=F32)


def iota(shape, dim):
    return lax.broadcasted_iota(jnp.int32, shape, dim)


def twice(matrix):
    blank = jnp.zeros_like(matrix)
    return jnp.concatenate(
        [jnp.concatenate([matrix, blank], 1), jnp.concatenate([blank, matrix], 1)], 0
    )


def side_by_side(rows):
    half = rows.shape[0] // 2
    return jnp.concatenate([rows[:half], rows[half:]], 1)


def centre(rows):
    values = rows.astype(F32)
    centred = values - jnp.mean(values, axis=-1, keepdims=True)
    return centred, jnp.mean(centred * centred, axis=-1, keepdims=True)


def layer_norm(rows):
    centred, variance = centre(rows)
    return centred * lax.rsqrt(variance + EPSILON)


def sigmoid(values):
    return 0.5 * jnp.tanh(0.5 * values) + 0.5


def attn_norm(cond, single, ada):
    width = single.shape[-1]
    mixed = dot(cond, ada)
    return (sigmoid(mixed[:, :width])[None] * single + mixed[None, :, width:]).astype(BF16)


def pair_kernel(packing, w_pair_hbm, pair_hbm, single_hbm, cond_hbm, *refs):
    count = sum(packing)
    weights_hbm, refs = refs[:count], refs[count:]
    tile_ref, single_ref, cond_ref = refs[:3]
    packed_refs, refs = refs[3 : 3 + len(packing)], refs[3 + len(packing) :]
    w_pair_ref, pair_ref, pair_sem, sem = refs
    rows, cols, width = pair_ref.shape
    heads = w_pair_ref.shape[0]
    group = GROUP
    lanes = heads * group
    half = group // 2
    pieces = rows // half

    def pair_copy(i):
        at = pl.ds(i * half, half)
        return pltpu.make_async_copy(pair_hbm.at[at], pair_ref.at[at], pair_sem.at[i])

    moves = [(w_pair_hbm, w_pair_ref), (single_hbm, single_ref), (cond_hbm, cond_ref)]
    index = 0
    for number, packed in zip(packing, packed_refs):
        offset = 0
        for _ in range(number):
            source = weights_hbm[index]
            span = source.shape[1]
            moves.append((source, packed.at[:, pl.ds(offset, span)]))
            offset += span
            index += 1
    copies = [
        pltpu.make_async_copy(source, target, sem.at[i])
        for i, (source, target) in enumerate(moves)
    ]
    copies[0].start()
    for i in range(pieces):
        pair_copy(i).start()
    copies[0].wait()
    w_pair = w_pair_ref[...].astype(F32)
    spread = jnp.concatenate(
        [jnp.broadcast_to(w_pair[h : h + 1], (group, width)) for h in range(heads)], 0
    )
    mix = twice(spread.T.astype(BF16))
    slot = iota((cols, lanes), 1) % group
    per_block = tile_ref.shape[1]

    @pl.loop(0, rows // group)
    def _(chunk):
        for part in range(2):
            pair_copy(chunk * 2 + part).wait()

        @pl.when(chunk == 1)
        def _():
            for copy in copies[1:]:
                copy.start()

        pair = pair_ref[pl.ds(chunk * group, group)].reshape(group * cols, width)
        centred, variance = centre(pair)
        variance = variance.reshape(group, cols, 1)
        mixed = dot(side_by_side(centred.astype(BF16)), mix).reshape(half, cols, 2 * lanes)
        total = jnp.zeros((cols, lanes), F32)
        spread_out = jnp.zeros((cols, lanes), F32)
        for i in range(group):
            side = slice(i // half * lanes, (i // half + 1) * lanes)
            total = jnp.where(slot == i, mixed[i % half, :, side], total)
            spread_out = jnp.where(slot == i, variance[i], spread_out)
        bias = (total * lax.rsqrt(spread_out + EPSILON)).astype(BF16)
        tile_ref[chunk // per_block, chunk % per_block] = bias

    for copy in copies[1:]:
        copy.wait()


def project_kernel(
    at_ref,
    single_ref,
    cond_ref,
    ada_attn,
    w_kv,
    w_qg,
    *refs,
):
    late_hbm, refs = refs[:8], refs[8:]
    query_ref, key_ref, value_ref, gate_ref, open_ref, trans_ref, near_ref, far_ref, w_out = refs[:9]
    ada_trans, gates_ref, w_up, w_down, sem = refs[9:]
    samples, atoms_here, width = single_ref.shape
    hidden_width = w_down.shape[0]
    targets = [w_out, w_down]
    for ref in (ada_trans, gates_ref, w_up):
        middle = ref.shape[1] // 2
        targets += [ref.at[:, pl.ds(0, middle)], ref.at[:, pl.ds(middle, middle)]]
    copies = [
        pltpu.make_async_copy(source, target, sem.at[i])
        for i, (source, target) in enumerate(zip(late_hbm, targets))
    ]
    for copy in copies:
        copy.start()
    transitions = []
    step = math.gcd(atoms_here, 256)
    for start in range(0, atoms_here, step):
        at = slice(start, start + step)
        cond = layer_norm(cond_ref[at, :]).astype(BF16)
        single = layer_norm(single_ref[:, at, :].reshape(-1, width))
        single = single.reshape(samples, step, width)
        normed = attn_norm(cond, single, ada_attn[...])
        if start == 0:
            heads_of = [normed[sample, :EDGE] for sample in range(samples)]
        if start + step == atoms_here:
            tails_of = [normed[sample, step - EDGE :] for sample in range(samples)]
        normed = normed.reshape(-1, width)
        both = dot(normed, w_kv[...]).astype(BF16).reshape(samples, step, 2 * width)
        key_ref[:, at, :] = both[:, :, :width]
        value_ref[:, at, :] = both[:, :, width:]
        both = dot(normed, w_qg[...]).reshape(samples, step, 2 * width)
        query_ref[:, at, :] = both[:, :, :width].astype(BF16)
        gate_ref[:, at, :] = sigmoid(both[:, :, width:]).astype(BF16)
        transitions.append((at, cond, single))

    for copy in copies:
        copy.wait()
    for at, cond, single in transitions:
        gates = dot(cond, gates_ref[...])
        open_ref[at, :] = sigmoid(gates[:, :width]).astype(BF16)
        normed = attn_norm(cond, single, ada_trans[...]).reshape(-1, width)
        swish = dot(normed, w_up[:, :hidden_width])
        hidden = (swish * sigmoid(swish) * dot(normed, w_up[:, hidden_width:])).astype(BF16)
        down = dot(hidden, w_down[...]).reshape(samples, step, width)
        trans_ref[:, at, :] = (sigmoid(gates[:, width:])[None] * down).astype(BF16)
    even = at_ref[0] % 2 == 0
    for sample, (head, tail) in enumerate(zip(heads_of, tails_of)):
        cut = slice(sample * EDGE, (sample + 1) * EDGE)
        near_ref[cut, :] = jnp.where(even, tail, head)
        far_ref[cut, :] = jnp.where(even, head, tail)


def tile_of(own_ref, other_ref, pair_at, row_block):
    owners, groups, cols, lanes = own_ref.shape
    place, part = row_block // owners, row_block % owners
    other = other_ref[0, part] if other_ref.shape[0] == 1 else other_ref[place, part]
    return jnp.where(place == pair_at, own_ref[part], other)


def select_kernel(blocks, at_ref, pair_ref, own_ref, other_ref, *refs):
    near_ref, far_ref, _, held_ref, again_ref = refs[3:]
    groups, cols, lanes = own_ref.shape[1:]
    rows = groups * cols
    device_at, pair_at = at_ref[0], pair_ref[0]
    for send_ref, parity in ((near_ref, 0), (far_ref, 1)):
        beside = jnp.where(device_at % 2 == parity, device_at + 1, device_at - 1)
        tile = tile_of(own_ref, other_ref, pair_at, jnp.clip(beside, 0, blocks - 1))
        send_ref[send_ref.shape[0] - rows :, :] = tile.reshape(rows, lanes)
    held_ref[...] = tile_of(own_ref, other_ref, pair_at, device_at).reshape(rows, lanes)
    again_ref[...] = near_ref[...]


def bounds(counts_ref, block, token):
    tok_here = counts_ref.shape[1]
    counts = counts_ref[pl.ds(block, 1), :].astype(F32).astype(BF16)
    counts = jnp.broadcast_to(counts, (8, tok_here))
    before = iota((tok_here, token.shape[1]), 0)
    first = dot(counts, (before < token).astype(BF16))[:1]
    last = dot(counts, (before <= token).astype(BF16))[:1]
    return first.astype(jnp.int32), last.astype(jnp.int32)


def one_hot(reach, offset, count):
    first, last = reach
    position = iota((count, first.shape[1]), 0) + offset
    return ((first <= position) & (position < last)).astype(F32).astype(BF16)


def expand(hot, tile, tok_here):
    tile = tile.reshape(tok_here // GROUP, tok_here, tile.shape[-1])
    tile = jnp.concatenate([tile[part] for part in range(tok_here // GROUP)], 1)
    return dot(hot, tile).astype(BF16)


def attend(heads, reach, windows, query_ref, gate_ref, gated_ref):
    samples, _, width = query_ref.shape
    head_dim = width // heads
    lanes = reach[0].shape[1]
    rows = heads * Q_WIN
    lane_head = iota((rows, lanes), 1) // GROUP % heads
    row_head = iota((rows, lanes), 0) // Q_WIN
    same_head = (lane_head == row_head).astype(F32).astype(BF16)
    own_head = iota((rows, width), 1) // head_dim == iota((rows, width), 0) // Q_WIN
    own_head = own_head.astype(F32).astype(BF16)
    channel_head = iota((Q_WIN, 2 * width), 1) % width // head_dim
    ones = jnp.ones((K_WIN, width), BF16)
    scaling = LOG2E / math.sqrt(head_dim)

    biases = []
    for start, _, near, mask in windows:
        pick = jnp.concatenate([one_hot(reach, start, Q_WIN)] * heads, 0) * same_head
        bias = lax.dot_general(pick, near, LAST, preferred_element_type=F32) * LOG2E
        biases.append(bias if mask is None else jnp.where(mask, bias, MASKED))
    units = [(sample, i) for i in range(len(windows)) for sample in range(samples)]
    scores = []
    for sample, i in units:
        query = query_ref[sample, pl.ds(windows[i][0], Q_WIN), :]
        query = jnp.concatenate([query] * heads, 0) * own_head
        keys = windows[i][1](sample)[0]
        product = lax.dot_general(query, keys, LAST, preferred_element_type=F32)
        scores.append(product * scaling + biases[i])
    tops = [jnp.max(score, axis=-1, keepdims=True) for score in scores]
    raised = [jnp.exp2(score - top).astype(BF16) for score, top in zip(scores, tops)]
    for (sample, i), weight in zip(units, raised):
        values = windows[i][1](sample)[1]
        mixed = dot(weight, jnp.concatenate([values, ones], 1))
        picked = mixed[:Q_WIN]
        for head in range(1, heads):
            picked = jnp.where(
                channel_head == head, mixed[head * Q_WIN : (head + 1) * Q_WIN], picked
            )
        attended = picked[:, :width] * pl.reciprocal(picked[:, width:], approx=True)
        at = pl.ds(windows[i][0], Q_WIN)
        gate = gate_ref[sample, at, :].astype(F32)
        gated_ref[sample, at, :] = (gate * attended).astype(BF16)


def close(sample, cut, gated_ref, open_ref, trans_ref, w_out_ref):
    mixed = dot(gated_ref[sample, cut, :], w_out_ref[...])
    opened, trans = open_ref[cut, :].astype(F32), trans_ref[sample, cut, :].astype(F32)
    return (opened * mixed + trans).astype(BF16)


def row_tokens(heads, tok_here):
    lane = iota((tok_here, heads * tok_here), 1)
    return lane // (heads * GROUP) * GROUP + lane % GROUP


def inner_kernel(
    heads,
    at_ref,
    counts_ref,
    query_ref,
    key_ref,
    value_ref,
    gate_ref,
    open_ref,
    trans_ref,
    w_out_ref,
    held_ref,
    out_ref,
    near_ref,
    gated_ref,
):
    samples, atoms_here, width = query_ref.shape
    tok_here = counts_ref.shape[1]
    device_at = at_ref[0]
    hot = one_hot(
        bounds(counts_ref, device_at, iota((tok_here, tok_here), 1)), 0, atoms_here
    )
    near_ref[...] = expand(hot, held_ref[...], tok_here)
    reach = bounds(counts_ref, device_at, row_tokens(heads, tok_here))
    skip = -(-EDGE // Q_WIN)
    inner = atoms_here // Q_WIN - 2 * skip
    batch = math.gcd(inner, 12)

    @pl.loop(0, inner // batch)
    def _(turn):
        windows = []
        for i in range(batch):
            start = pl.multiple_of((turn * batch + i + skip) * Q_WIN, Q_WIN)
            cut = pl.ds(pl.multiple_of(start - EDGE, 16), K_WIN)
            parts = lambda sample, cut=cut: (key_ref[sample, cut, :], value_ref[sample, cut, :])
            windows.append((start, parts, near_ref[cut, :], None))
        attend(heads, reach, windows, query_ref, gate_ref, gated_ref)

    cut = slice(skip * Q_WIN, atoms_here - skip * Q_WIN)
    for sample in range(samples):
        out_ref[sample] = close(sample, cut, gated_ref, open_ref, trans_ref, w_out_ref)


def outer_kernel(
    heads,
    blocks,
    at_ref,
    counts_ref,
    query_ref,
    own_key_ref,
    own_value_ref,
    gate_ref,
    open_ref,
    trans_ref,
    w_out_ref,
    held_ref,
    inner_ref,
    w_kv,
    early_ref,
    second_ref,
    late_ref,
    out_hbm,
    key_ref,
    value_ref,
    near_ref,
    gated_ref,
    out_ref,
    sem,
):
    samples, atoms_here, width = query_ref.shape
    tok_here = counts_ref.shape[1]
    device_at = at_ref[0]
    ends = atoms_here * blocks
    skip = -(-EDGE // Q_WIN)
    margin = skip * Q_WIN
    reach_keys = key_ref.shape[2]
    inside = reach_keys - EDGE

    whole = pltpu.make_async_copy(
        inner_ref, out_hbm.at[:, pl.ds(margin, atoms_here - 2 * margin)], sem.at[0]
    )
    whole.start()

    even = device_at % 2 == 0
    first = jnp.where(device_at % 4 < 2, early_ref[...], late_ref[...])
    second = second_ref[...]
    arrived = (jnp.where(even, second, first), jnp.where(even, first, second))
    count = samples * EDGE
    edges = jnp.concatenate([rows[:count] for rows in arrived], 0)
    edges = dot(edges, w_kv[...]).astype(BF16).reshape(2, samples, EDGE, 2 * width)
    token = iota((tok_here, tok_here), 1)
    own_reach = bounds(counts_ref, device_at, token)
    sides = (
        (jnp.maximum(device_at - 1, 0), atoms_here - EDGE, 0, EDGE, 0),
        (jnp.minimum(device_at + 1, blocks - 1), 0, inside, 0, atoms_here - inside),
    )
    for side, (block, offset, place, own_place, own_start) in enumerate(sides):
        for i, (ref, own_ref) in enumerate(((key_ref, own_key_ref), (value_ref, own_value_ref))):
            ref[side, :, place : place + EDGE, :] = edges[side, :, :, i * width : (i + 1) * width]
            ref[side, :, own_place : own_place + inside, :] = own_ref[
                :, own_start : own_start + inside, :
            ]
        hot = one_hot(bounds(counts_ref, block, token), offset, EDGE)
        near_ref[side, place : place + EDGE, :] = expand(hot, arrived[side][count:], tok_here)
        hot = one_hot(own_reach, own_start, inside)
        near_ref[side, own_place : own_place + inside, :] = expand(hot, held_ref[...], tok_here)

    reach = bounds(counts_ref, device_at, row_tokens(heads, tok_here))
    windows = []
    for side in range(2):
        for i in range(skip):
            start = i * Q_WIN + side * (atoms_here - margin)
            cut = slice(i * Q_WIN, i * Q_WIN + K_WIN)
            parts = lambda sample, side=side, cut=cut: (
                key_ref[side, sample, cut, :],
                value_ref[side, sample, cut, :],
            )
            key_at = iota((heads * Q_WIN, K_WIN), 1) + (device_at * atoms_here + start - EDGE)
            mask = (key_at >= 0) & (key_at < ends)
            windows.append((start, parts, near_ref[side, cut, :], mask))
    attend(heads, reach, windows, query_ref, gate_ref, gated_ref)
    copies = []
    for side in range(2):
        cut = slice(side * (atoms_here - margin), side * (atoms_here - margin) + margin)
        for sample in range(samples):
            out_ref[side, sample] = close(sample, cut, gated_ref, open_ref, trans_ref, w_out_ref)
        target = out_hbm.at[:, pl.ds(side * (atoms_here - margin), margin)]
        copies.append(pltpu.make_async_copy(out_ref.at[side], target, sem.at[1 + side]))
        copies[-1].start()
    for copy in copies:
        copy.wait()
    whole.wait()


def shards(
    atom_single,
    atom_cond,
    pair_cond,
    atom_counts,
    ada_attn_scale,
    ada_attn_shift,
    w_query,
    w_key,
    w_value,
    w_gate,
    w_out,
    attn_gate,
    w_pair,
    ada_trans_scale,
    ada_trans_shift,
    w_swish,
    w_linear,
    w_down,
    trans_gate,
):
    device_at = lax.axis_index("atoms")
    blocks = lax.axis_size("atoms")
    samples, atoms_here, width = atom_single.shape
    tok_here = atom_counts.shape[1]
    heads = w_pair.shape[1]
    groups = tok_here // GROUP
    pairs = lax.axis_size("pair")
    owners = pair_cond.shape[0] // tok_here
    at = device_at.astype(jnp.int32).reshape(1)
    pair_at = lax.axis_index("pair").astype(jnp.int32).reshape(1)
    in_hbm = lambda array: pltpu.with_memory_space_constraint(array, pltpu.HBM)
    in_vmem = lambda array: pltpu.with_memory_space_constraint(array, pltpu.VMEM)

    packing = ((ada_attn_scale, ada_attn_shift), (w_key, w_value), (w_query, w_gate))
    late = (w_out, w_down, ada_trans_scale, ada_trans_shift, attn_gate, trans_gate, w_swish, w_linear)
    flat = [array for arrays in packing for array in arrays]
    rows, cols, _ = pair_cond.shape
    lanes = heads * GROUP
    wide = (samples, atoms_here, width)
    params = pltpu.CompilerParams(vmem_limit_bytes=VMEM_LIMIT)

    def cost(products):
        return pl.CostEstimate(flops=2 * products, bytes_accessed=4 << 20, transcendentals=0)

    sent = pltpu.VMEM((samples * EDGE + groups * cols, lanes), BF16)
    shapes = [
        pltpu.VMEM((owners, groups, cols, lanes), BF16),
        pltpu.VMEM(wide, BF16),
        pltpu.VMEM(atom_cond.shape, BF16),
    ] + [
        pltpu.VMEM((arrays[0].shape[0], sum(a.shape[1] for a in arrays)), BF16)
        for arrays in packing
    ]
    made = pl.pallas_call(
        functools.partial(pair_kernel, [len(arrays) for arrays in packing]),
        in_specs=[IN_HBM] * (4 + len(flat)),
        out_specs=[IN_VMEM] * len(shapes),
        out_shape=shapes,
        scratch_shapes=[
            pltpu.VMEM((heads, width), BF16),
            pltpu.VMEM(pair_cond.shape, BF16),
            pltpu.SemaphoreType.DMA((2 * rows // GROUP,)),
            pltpu.SemaphoreType.DMA((3 + len(flat),)),
        ],
        compiler_params=params,
        cost_estimate=cost(rows * cols * width * width * 2),
    )(*map(in_hbm, (w_pair.T, pair_cond, atom_single, atom_cond, *flat)))
    own, single, cond, *packed = made
    ada_attn, w_kv, w_qg = packed
    if pairs == 2:
        other = lax.ppermute(own, "pair", [(0, 1), (1, 0)])[None]
    else:
        other = lax.all_gather(own, "pair")

    operands = (single, cond, ada_attn, w_kv, w_qg)
    query, keys, values, gate, opened, trans, near, far, w_out = pl.pallas_call(
        project_kernel,
        in_specs=[IN_SMEM] + [IN_VMEM] * len(operands) + [IN_HBM] * len(late),
        out_specs=[IN_VMEM] * 9,
        out_shape=[pltpu.VMEM(wide, BF16)] * 4
        + [pltpu.VMEM((atoms_here, width), BF16), pltpu.VMEM(wide, BF16), sent, sent]
        + [pltpu.VMEM(w_out.shape, BF16)],
        scratch_shapes=[
            pltpu.VMEM((width, 2 * width), BF16),
            pltpu.VMEM((width, 2 * width), BF16),
            pltpu.VMEM((width, 2 * w_swish.shape[1]), BF16),
            pltpu.VMEM(w_down.shape, BF16),
            pltpu.SemaphoreType.DMA((len(late),)),
        ],
        compiler_params=params,
        cost_estimate=cost(samples * atoms_here * width * width * 20),
    )(at, *map(in_vmem, operands), *map(in_hbm, late))

    operands = (own, other, near, far, opened)
    near, far, opened, held, again = pl.pallas_call(
        functools.partial(select_kernel, blocks),
        in_specs=[IN_SMEM] * 2 + [IN_VMEM] * len(operands),
        out_specs=[IN_VMEM] * 5,
        out_shape=[
            sent,
            sent,
            pltpu.VMEM((atoms_here, width), BF16),
            pltpu.VMEM((groups * cols, lanes), BF16),
            sent,
        ],
        input_output_aliases={4: 0, 5: 1, 6: 2},
        compiler_params=params,
    )(at, pair_at, *map(in_vmem, operands))

    def swap(value, start, step):
        sides = [(i, i + 1) for i in range(start, blocks - 1, step)]
        return lax.ppermute(value, "atoms", sides + [(j, i) for i, j in sides])

    early, second, later = swap(near, 0, 4), swap(far, 1, 2), swap(again, 2, 4)

    margin = -(-EDGE // Q_WIN) * Q_WIN
    operands = (query, keys, values, gate, opened, trans, w_out, held)
    inner = pl.pallas_call(
        functools.partial(inner_kernel, heads),
        in_specs=[IN_SMEM] + [IN_VMEM] * (1 + len(operands)),
        out_specs=IN_VMEM,
        out_shape=pltpu.VMEM((samples, atoms_here - 2 * margin, width), BF16),
        scratch_shapes=[
            pltpu.VMEM((atoms_here, heads * tok_here), BF16),
            pltpu.VMEM(wide, BF16),
        ],
        compiler_params=params,
        cost_estimate=cost(samples * atoms_here * width * width * 12),
    )(at, atom_counts, *map(in_vmem, operands))

    reach = margin - Q_WIN + K_WIN
    operands += (inner, w_kv, early, second, later)
    return pl.pallas_call(
        functools.partial(outer_kernel, heads, blocks),
        in_specs=[IN_SMEM] + [IN_VMEM] * (1 + len(operands)),
        out_specs=IN_HBM,
        out_shape=pltpu.HBM(wide, BF16),
        scratch_shapes=[
            pltpu.VMEM((2, samples, reach, width), BF16),
            pltpu.VMEM((2, samples, reach, width), BF16),
            pltpu.VMEM((2, reach, heads * tok_here), BF16),
            pltpu.VMEM(wide, BF16),
            pltpu.VMEM((2, samples, margin, width), BF16),
            pltpu.SemaphoreType.DMA((3,)),
        ],
        compiler_params=params,
        cost_estimate=cost(samples * atoms_here * width * width * 4),
    )(at, atom_counts, *map(in_vmem, operands))


def solution(mesh):
    return jax.shard_map(
        shards,
        mesh=mesh,
        in_specs=(
            P(("groups", "pair", "samp"), "atoms", None),
            P(("groups", "atoms"), None),
            P(("groups", "pair"), "atoms", None),
            P("groups", None),
        )
        + (P(),) * 15,
        out_specs=P(("groups", "pair", "samp"), "atoms", None),
        check_vma=False,
    )
```

```python
import functools
import math

import jax
import jax.numpy as jnp
from jax import lax
from jax.experimental import pallas as pl
from jax.experimental.pallas import tpu as pltpu
from jax.sharding import PartitionSpec as P

Q_WIN = 32
K_WIN = 128
EDGE = 48
GROUP = 32

EPSILON = 1e-05
MASKED = -1e30
LOG2E = math.log2(math.e)
BF16 = jnp.bfloat16
F32 = jnp.float32
LAST = (((1,), (1,)), ((), ()))
VMEM_LIMIT = 32 << 20
IN_VMEM = pl.BlockSpec(memory_space=pltpu.VMEM)
IN_HBM = pl.BlockSpec(memory_space=pltpu.HBM)
IN_SMEM = pl.BlockSpec(memory_space=pltpu.SMEM)


def dot(a, b):
    return jnp.dot(a, b, preferred_element_type=F32)


def iota(shape, dim):
    return lax.broadcasted_iota(jnp.int32, shape, dim)


def twice(matrix):
    blank = jnp.zeros_like(matrix)
    return jnp.concatenate(
        [jnp.concatenate([matrix, blank], 1), jnp.concatenate([blank, matrix], 1)], 0
    )


def side_by_side(rows):
    half = rows.shape[0] // 2
    return jnp.concatenate([rows[:half], rows[half:]], 1)


def centre(rows):
    values = rows.astype(F32)
    centred = values - jnp.mean(values, axis=-1, keepdims=True)
    return centred, jnp.mean(centred * centred, axis=-1, keepdims=True)


def layer_norm(rows):
    centred, variance = centre(rows)
    return centred * lax.rsqrt(variance + EPSILON)


def sigmoid(values):
    return 0.5 * jnp.tanh(0.5 * values) + 0.5


def attn_norm(cond, single, ada):
    width = single.shape[-1]
    mixed = dot(cond, ada)
    return (sigmoid(mixed[:, :width])[None] * single + mixed[None, :, width:]).astype(BF16)


def pair_kernel(packing, core_ref, w_pair_hbm, pair_hbm, single_hbm, cond_hbm, *refs):
    count = sum(packing)
    weights_hbm, refs = refs[:count], refs[count:]
    tile_ref, single_ref, cond_ref = refs[:3]
    packed_refs, refs = refs[3 : 3 + len(packing)], refs[3 + len(packing) :]
    w_pair_ref, pair_ref, pair_sem, sem = refs
    rows, cols, width = pair_ref.shape
    heads = w_pair_ref.shape[0]
    group = GROUP
    lanes = heads * group
    half = group // 2
    pieces = rows // half
    row_start = core_ref[0] * rows

    def pair_copy(i):
        source = pair_hbm.at[pl.ds(row_start + i * half, half)]
        return pltpu.make_async_copy(source, pair_ref.at[pl.ds(i * half, half)], pair_sem.at[i])

    moves = [(w_pair_hbm, w_pair_ref), (single_hbm, single_ref), (cond_hbm, cond_ref)]
    index = 0
    for number, packed in zip(packing, packed_refs):
        offset = 0
        for _ in range(number):
            source = weights_hbm[index]
            span = source.shape[1]
            moves.append((source, packed.at[:, pl.ds(offset, span)]))
            offset += span
            index += 1
    copies = [
        pltpu.make_async_copy(source, target, sem.at[i])
        for i, (source, target) in enumerate(moves)
    ]
    copies[0].start()
    for i in range(pieces):
        pair_copy(i).start()
    copies[0].wait()
    w_pair = w_pair_ref[...].astype(F32)
    spread = jnp.concatenate(
        [jnp.broadcast_to(w_pair[h : h + 1], (group, width)) for h in range(heads)], 0
    )
    mix = twice(spread.T.astype(BF16))
    slot = iota((cols, lanes), 1) % group

    @pl.loop(0, rows // group)
    def _(chunk):
        for part in range(2):
            pair_copy(chunk * 2 + part).wait()

        @pl.when(chunk == 0)
        def _():
            for copy in copies[1:]:
                copy.start()

        pair = pair_ref[pl.ds(chunk * group, group)].reshape(group * cols, width)
        centred, variance = centre(pair)
        variance = variance.reshape(group, cols, 1)
        mixed = dot(side_by_side(centred.astype(BF16)), mix).reshape(half, cols, 2 * lanes)
        total = jnp.zeros((cols, lanes), F32)
        spread_out = jnp.zeros((cols, lanes), F32)
        for i in range(group):
            side = slice(i // half * lanes, (i // half + 1) * lanes)
            total = jnp.where(slot == i, mixed[i % half, :, side], total)
            spread_out = jnp.where(slot == i, variance[i], spread_out)
        bias = (total * lax.rsqrt(spread_out + EPSILON)).astype(BF16)
        tile_ref[chunk] = bias

    for copy in copies[1:]:
        copy.wait()


def project_kernel(
    at_ref,
    single_ref,
    cond_ref,
    ada_attn,
    ada_trans,
    gates_ref,
    w_kv,
    w_qg,
    w_up,
    w_down,
    query_ref,
    key_ref,
    value_ref,
    gate_ref,
    open_ref,
    trans_ref,
    near_ref,
    far_ref,
):
    samples, atoms_here, width = single_ref.shape
    hidden_width = w_down.shape[0]
    step = math.gcd(atoms_here, 256)
    for start in range(0, atoms_here, step):
        at = slice(start, start + step)
        cond = layer_norm(cond_ref[at, :]).astype(BF16)
        single = layer_norm(single_ref[:, at, :].reshape(-1, width))
        single = single.reshape(samples, step, width)
        normed = attn_norm(cond, single, ada_attn[...])
        if start == 0:
            heads_of = [normed[sample, :EDGE] for sample in range(samples)]
        if start + step == atoms_here:
            tails_of = [normed[sample, step - EDGE :] for sample in range(samples)]
        normed = normed.reshape(-1, width)
        both = dot(normed, w_kv[...]).astype(BF16).reshape(samples, step, 2 * width)
        key_ref[:, at, :] = both[:, :, :width]
        value_ref[:, at, :] = both[:, :, width:]
        both = dot(normed, w_qg[...]).reshape(samples, step, 2 * width)
        query_ref[:, at, :] = both[:, :, :width].astype(BF16)
        gate_ref[:, at, :] = sigmoid(both[:, :, width:]).astype(BF16)
        gates = dot(cond, gates_ref[...])
        open_ref[at, :] = sigmoid(gates[:, :width]).astype(BF16)
        normed = attn_norm(cond, single, ada_trans[...]).reshape(-1, width)
        swish = dot(normed, w_up[:, :hidden_width])
        hidden = (swish * sigmoid(swish) * dot(normed, w_up[:, hidden_width:])).astype(BF16)
        down = dot(hidden, w_down[...]).reshape(samples, step, width)
        trans_ref[:, at, :] = (sigmoid(gates[:, width:])[None] * down).astype(BF16)
    even = at_ref[0] % 2 == 0
    for sample, (head, tail) in enumerate(zip(heads_of, tails_of)):
        cut = slice(sample * EDGE, (sample + 1) * EDGE)
        near_ref[cut, :] = jnp.where(even, tail, head)
        far_ref[cut, :] = jnp.where(even, head, tail)


def tile_of(refs, place, row_block):
    if len(refs) == 1:
        return refs[0][row_block]
    pair_at, core_at = place
    owners = 2
    mine, theirs, across, diagonal = [ref[...] for ref in refs]
    near = jnp.where(row_block % owners == core_at, mine, theirs)
    far = jnp.where(row_block % owners == core_at, across, diagonal)
    return jnp.where(row_block // owners == pair_at, near, far)


def select_kernel(blocks, at_ref, pair_ref, core_ref, *refs):
    *tile_refs, _, __, ___, near_ref, far_ref, ____, held_ref = refs
    groups, cols, lanes = tile_refs[0].shape[-3:]
    rows = groups * cols
    device_at, place = at_ref[0], (pair_ref[0], core_ref[0])
    for send_ref, parity in ((near_ref, 0), (far_ref, 1)):
        beside = jnp.where(device_at % 2 == parity, device_at + 1, device_at - 1)
        tile = tile_of(tile_refs, place, jnp.clip(beside, 0, blocks - 1))
        send_ref[send_ref.shape[0] - rows :, :] = tile.reshape(rows, lanes)
    held_ref[...] = tile_of(tile_refs, place, device_at).reshape(rows, lanes)


def bounds(counts_ref, block, token):
    tok_here = counts_ref.shape[1]
    counts = counts_ref[pl.ds(block, 1), :].astype(F32).astype(BF16)
    counts = jnp.broadcast_to(counts, (8, tok_here))
    before = iota((tok_here, token.shape[1]), 0)
    first = dot(counts, (before < token).astype(BF16))[:1]
    last = dot(counts, (before <= token).astype(BF16))[:1]
    return first.astype(jnp.int32), last.astype(jnp.int32)


def one_hot(reach, offset, count):
    first, last = reach
    position = iota((count, first.shape[1]), 0) + offset
    return ((first <= position) & (position < last)).astype(F32).astype(BF16)


def expand(hot, tile, tok_here):
    tile = tile.reshape(tok_here // GROUP, tok_here, tile.shape[-1])
    tile = jnp.concatenate([tile[part] for part in range(tok_here // GROUP)], 1)
    return dot(hot, tile).astype(BF16)


def attend(heads, reach, windows, query_ref, gate_ref, gated_ref):
    samples, _, width = query_ref.shape
    head_dim = width // heads
    lanes = reach[0].shape[1]
    rows = heads * Q_WIN
    lane_head = iota((rows, lanes), 1) // GROUP % heads
    row_head = iota((rows, lanes), 0) // Q_WIN
    same_head = (lane_head == row_head).astype(F32).astype(BF16)
    own_head = iota((rows, width), 1) // head_dim == iota((rows, width), 0) // Q_WIN
    own_head = own_head.astype(F32).astype(BF16)
    channel_head = iota((Q_WIN, 2 * width), 1) % width // head_dim
    ones = jnp.ones((K_WIN, width), BF16)
    scaling = LOG2E / math.sqrt(head_dim)

    biases = []
    for start, _, near, mask in windows:
        pick = jnp.concatenate([one_hot(reach, start, Q_WIN)] * heads, 0) * same_head
        bias = lax.dot_general(pick, near, LAST, preferred_element_type=F32) * LOG2E
        biases.append(bias if mask is None else jnp.where(mask, bias, MASKED))
    units = [(sample, i) for i in range(len(windows)) for sample in range(samples)]
    scores = []
    for sample, i in units:
        query = query_ref[sample, pl.ds(windows[i][0], Q_WIN), :]
        query = jnp.concatenate([query] * heads, 0) * own_head
        keys = windows[i][1](sample)[0]
        product = lax.dot_general(query, keys, LAST, preferred_element_type=F32)
        scores.append(product * scaling + biases[i])
    tops = [jnp.max(score, axis=-1, keepdims=True) for score in scores]
    raised = [jnp.exp2(score - top).astype(BF16) for score, top in zip(scores, tops)]
    for (sample, i), weight in zip(units, raised):
        values = windows[i][1](sample)[1]
        mixed = dot(weight, jnp.concatenate([values, ones], 1))
        picked = mixed[:Q_WIN]
        for head in range(1, heads):
            picked = jnp.where(
                channel_head == head, mixed[head * Q_WIN : (head + 1) * Q_WIN], picked
            )
        attended = picked[:, :width] * pl.reciprocal(picked[:, width:], approx=True)
        at = pl.ds(windows[i][0], Q_WIN)
        gate = gate_ref[sample, at, :].astype(F32)
        gated_ref[sample, at, :] = (gate * attended).astype(BF16)


def close(sample, cut, gated_ref, open_ref, trans_ref, w_out_ref):
    mixed = dot(gated_ref[sample, cut, :], w_out_ref[...])
    opened, trans = open_ref[cut, :].astype(F32), trans_ref[sample, cut, :].astype(F32)
    return (opened * mixed + trans).astype(BF16)


def row_tokens(heads, tok_here):
    lane = iota((tok_here, heads * tok_here), 1)
    return lane // (heads * GROUP) * GROUP + lane % GROUP


def inner_kernel(
    heads,
    at_ref,
    counts_ref,
    query_ref,
    key_ref,
    value_ref,
    gate_ref,
    open_ref,
    trans_ref,
    w_out_ref,
    held_ref,
    out_ref,
    near_ref,
    gated_ref,
):
    samples, atoms_here, width = query_ref.shape
    tok_here = counts_ref.shape[1]
    device_at = at_ref[0]
    hot = one_hot(
        bounds(counts_ref, device_at, iota((tok_here, tok_here), 1)), 0, atoms_here
    )
    near_ref[...] = expand(hot, held_ref[...], tok_here)
    reach = bounds(counts_ref, device_at, row_tokens(heads, tok_here))
    skip = -(-EDGE // Q_WIN)
    inner = atoms_here // Q_WIN - 2 * skip
    batch = math.gcd(inner, 12)

    @pl.loop(0, inner // batch)
    def _(turn):
        windows = []
        for i in range(batch):
            start = pl.multiple_of((turn * batch + i + skip) * Q_WIN, Q_WIN)
            cut = pl.ds(pl.multiple_of(start - EDGE, 16), K_WIN)
            parts = lambda sample, cut=cut: (key_ref[sample, cut, :], value_ref[sample, cut, :])
            windows.append((start, parts, near_ref[cut, :], None))
        attend(heads, reach, windows, query_ref, gate_ref, gated_ref)

    cut = slice(skip * Q_WIN, atoms_here - skip * Q_WIN)
    for sample in range(samples):
        out_ref[sample] = close(sample, cut, gated_ref, open_ref, trans_ref, w_out_ref)


def outer_kernel(
    heads,
    blocks,
    at_ref,
    counts_ref,
    query_ref,
    own_key_ref,
    own_value_ref,
    gate_ref,
    open_ref,
    trans_ref,
    w_out_ref,
    held_ref,
    inner_ref,
    w_kv,
    first_ref,
    second_ref,
    out_hbm,
    key_ref,
    value_ref,
    near_ref,
    gated_ref,
    out_ref,
    sem,
):
    samples, atoms_here, width = query_ref.shape
    tok_here = counts_ref.shape[1]
    device_at = at_ref[0]
    ends = atoms_here * blocks
    skip = -(-EDGE // Q_WIN)
    margin = skip * Q_WIN
    reach_keys = key_ref.shape[2]
    inside = reach_keys - EDGE

    whole = pltpu.make_async_copy(
        inner_ref, out_hbm.at[:, pl.ds(margin, atoms_here - 2 * margin)], sem.at[0]
    )
    whole.start()

    even = device_at % 2 == 0
    first, second = first_ref[...], second_ref[...]
    arrived = (jnp.where(even, second, first), jnp.where(even, first, second))
    count = samples * EDGE
    edges = jnp.concatenate([rows[:count] for rows in arrived], 0)
    edges = dot(edges, w_kv[...]).astype(BF16).reshape(2, samples, EDGE, 2 * width)
    token = iota((tok_here, tok_here), 1)
    own_reach = bounds(counts_ref, device_at, token)
    sides = (
        (jnp.maximum(device_at - 1, 0), atoms_here - EDGE, 0, EDGE, 0),
        (jnp.minimum(device_at + 1, blocks - 1), 0, inside, 0, atoms_here - inside),
    )
    for side, (block, offset, place, own_place, own_start) in enumerate(sides):
        for i, (ref, own_ref) in enumerate(((key_ref, own_key_ref), (value_ref, own_value_ref))):
            ref[side, :, place : place + EDGE, :] = edges[side, :, :, i * width : (i + 1) * width]
            ref[side, :, own_place : own_place + inside, :] = own_ref[
                :, own_start : own_start + inside, :
            ]
        hot = one_hot(bounds(counts_ref, block, token), offset, EDGE)
        near_ref[side, place : place + EDGE, :] = expand(hot, arrived[side][count:], tok_here)
        hot = one_hot(own_reach, own_start, inside)
        near_ref[side, own_place : own_place + inside, :] = expand(hot, held_ref[...], tok_here)

    reach = bounds(counts_ref, device_at, row_tokens(heads, tok_here))
    windows = []
    for side in range(2):
        for i in range(skip):
            start = i * Q_WIN + side * (atoms_here - margin)
            cut = slice(i * Q_WIN, i * Q_WIN + K_WIN)
            parts = lambda sample, side=side, cut=cut: (
                key_ref[side, sample, cut, :],
                value_ref[side, sample, cut, :],
            )
            key_at = iota((heads * Q_WIN, K_WIN), 1) + (device_at * atoms_here + start - EDGE)
            mask = (key_at >= 0) & (key_at < ends)
            windows.append((start, parts, near_ref[side, cut, :], mask))
    attend(heads, reach, windows, query_ref, gate_ref, gated_ref)
    copies = []
    for side in range(2):
        cut = slice(side * (atoms_here - margin), side * (atoms_here - margin) + margin)
        for sample in range(samples):
            out_ref[side, sample] = close(sample, cut, gated_ref, open_ref, trans_ref, w_out_ref)
        target = out_hbm.at[:, pl.ds(side * (atoms_here - margin), margin)]
        copies.append(pltpu.make_async_copy(out_ref.at[side], target, sem.at[1 + side]))
        copies[-1].start()
    for copy in copies:
        copy.wait()
    whole.wait()


def shards(
    atom_single,
    atom_cond,
    pair_cond,
    atom_counts,
    ada_attn_scale,
    ada_attn_shift,
    w_query,
    w_key,
    w_value,
    w_gate,
    w_out,
    attn_gate,
    w_pair,
    ada_trans_scale,
    ada_trans_shift,
    w_swish,
    w_linear,
    w_down,
    trans_gate,
):
    device_at = lax.axis_index("atoms")
    blocks = lax.axis_size("atoms")
    samples, atoms_here, width = atom_single.shape
    tok_here = atom_counts.shape[1]
    heads = w_pair.shape[1]
    groups = tok_here // GROUP
    pairs = lax.axis_size("pair")
    assert pair_cond.shape[0] == lax.axis_size("samp") * tok_here
    at = device_at.astype(jnp.int32).reshape(1)
    pair_at = lax.axis_index("pair").astype(jnp.int32).reshape(1)
    core_at = lax.axis_index("samp").astype(jnp.int32).reshape(1)
    in_hbm = lambda array: pltpu.with_memory_space_constraint(array, pltpu.HBM)
    in_vmem = lambda array: pltpu.with_memory_space_constraint(array, pltpu.VMEM)

    packing = (
        (ada_attn_scale, ada_attn_shift),
        (ada_trans_scale, ada_trans_shift),
        (attn_gate, trans_gate),
        (w_key, w_value),
        (w_query, w_gate),
        (w_swish, w_linear),
        (w_down,),
        (w_out,),
    )
    flat = [array for arrays in packing for array in arrays]
    cols = pair_cond.shape[1]
    lanes = heads * GROUP
    wide = (samples, atoms_here, width)
    params = pltpu.CompilerParams(vmem_limit_bytes=VMEM_LIMIT)

    def cost(products):
        return pl.CostEstimate(flops=2 * products, bytes_accessed=4 << 20, transcendentals=0)

    sent = pltpu.VMEM((samples * EDGE + groups * cols, lanes), BF16)
    shapes = [
        pltpu.VMEM((groups, cols, lanes), BF16),
        pltpu.VMEM(wide, BF16),
        pltpu.VMEM(atom_cond.shape, BF16),
    ] + [
        pltpu.VMEM((arrays[0].shape[0], sum(a.shape[1] for a in arrays)), BF16)
        for arrays in packing
    ]
    made = pl.pallas_call(
        functools.partial(pair_kernel, [len(arrays) for arrays in packing]),
        in_specs=[IN_SMEM] + [IN_HBM] * (4 + len(flat)),
        out_specs=[IN_VMEM] * len(shapes),
        out_shape=shapes,
        scratch_shapes=[
            pltpu.VMEM((heads, width), BF16),
            pltpu.VMEM((tok_here, cols, width), BF16),
            pltpu.SemaphoreType.DMA((2 * groups,)),
            pltpu.SemaphoreType.DMA((3 + len(flat),)),
        ],
        compiler_params=params,
        cost_estimate=cost(tok_here * cols * width * width * 2),
    )(core_at, *map(in_hbm, (w_pair.T, pair_cond, atom_single, atom_cond, *flat)))
    own, single, cond, *packed = made
    ada_attn, ada_trans, gates, w_kv, w_qg, w_up, w_down, w_out = packed
    if pairs == 2:
        swapped = [(0, 1), (1, 0)]
        across = lax.ppermute(own, "pair", swapped)
        diagonal = lax.ppermute(own, ("pair", "samp"), [(0, 3), (1, 2), (2, 1), (3, 0)])
        tiles = (own, lax.ppermute(own, "samp", swapped), across, diagonal)
    else:
        tiles = (lax.all_gather(own, ("pair", "samp")),)

    operands = (single, cond, ada_attn, ada_trans, gates, w_kv, w_qg, w_up, w_down)
    query, keys, values, gate, opened, trans, near, far = pl.pallas_call(
        project_kernel,
        in_specs=[IN_SMEM] + [IN_VMEM] * len(operands),
        out_specs=[IN_VMEM] * 8,
        out_shape=[pltpu.VMEM(wide, BF16)] * 4
        + [pltpu.VMEM((atoms_here, width), BF16), pltpu.VMEM(wide, BF16), sent, sent],
        compiler_params=params,
        cost_estimate=cost(samples * atoms_here * width * width * 20),
    )(at, *map(in_vmem, operands))

    operands = (*tiles, near, far, opened)
    first = 3 + len(tiles)
    near, far, opened, held = pl.pallas_call(
        functools.partial(select_kernel, blocks),
        in_specs=[IN_SMEM] * 3 + [IN_VMEM] * len(operands),
        out_specs=[IN_VMEM] * 4,
        out_shape=[
            sent,
            sent,
            pltpu.VMEM((atoms_here, width), BF16),
            pltpu.VMEM((groups * cols, lanes), BF16),
        ],
        input_output_aliases={first: 0, first + 1: 1, first + 2: 2},
        compiler_params=params,
    )(at, pair_at, core_at, *map(in_vmem, operands))

    def swap(value, start):
        cores = lax.axis_size("samp")
        other_of = {}
        for i in range(start, blocks - 1, 2):
            other_of[i], other_of[i + 1] = i + 1, i
        sides = []
        for i in range(blocks):
            for core in range(cores):
                target = (other_of[i], core) if i in other_of else (i, (core + 1) % cores)
                sides.append((i * cores + core, target[0] * cores + target[1]))
        return lax.ppermute(value, ("atoms", "samp"), sides)

    first, second = swap(near, 0), swap(far, 1)

    margin = -(-EDGE // Q_WIN) * Q_WIN
    operands = (query, keys, values, gate, opened, trans, w_out, held)
    inner = pl.pallas_call(
        functools.partial(inner_kernel, heads),
        in_specs=[IN_SMEM] + [IN_VMEM] * (1 + len(operands)),
        out_specs=IN_VMEM,
        out_shape=pltpu.VMEM((samples, atoms_here - 2 * margin, width), BF16),
        scratch_shapes=[
            pltpu.VMEM((atoms_here, heads * tok_here), BF16),
            pltpu.VMEM(wide, BF16),
        ],
        compiler_params=params,
        cost_estimate=cost(samples * atoms_here * width * width * 12),
    )(at, atom_counts, *map(in_vmem, operands))

    reach = margin - Q_WIN + K_WIN
    operands += (inner, w_kv, first, second)
    return pl.pallas_call(
        functools.partial(outer_kernel, heads, blocks),
        in_specs=[IN_SMEM] + [IN_VMEM] * (1 + len(operands)),
        out_specs=IN_HBM,
        out_shape=pltpu.HBM(wide, BF16),
        scratch_shapes=[
            pltpu.VMEM((2, samples, reach, width), BF16),
            pltpu.VMEM((2, samples, reach, width), BF16),
            pltpu.VMEM((2, reach, heads * tok_here), BF16),
            pltpu.VMEM(wide, BF16),
            pltpu.VMEM((2, samples, margin, width), BF16),
            pltpu.SemaphoreType.DMA((3,)),
        ],
        compiler_params=params,
        cost_estimate=cost(samples * atoms_here * width * width * 4),
    )(at, atom_counts, *map(in_vmem, operands))


def solution(mesh):
    return jax.shard_map(
        shards,
        mesh=mesh,
        in_specs=(
            P(("groups", "pair", "samp"), "atoms", None),
            P(("groups", "atoms"), None),
            P(("groups", "pair"), "atoms", None),
            P("groups", None),
        )
        + (P(),) * 15,
        out_specs=P(("groups", "pair", "samp"), "atoms", None),
        check_vma=False,
    )
```

```python
import functools
import math

import jax
import jax.numpy as jnp
from jax import lax
from jax.experimental import pallas as pl
from jax.experimental.pallas import tpu as pltpu
from jax.sharding import PartitionSpec as P

Q_WIN = 32
K_WIN = 128
EDGE = 48
GROUP = 32

EPSILON = 1e-05
MASKED = -1e30
LOG2E = math.log2(math.e)
BF16 = jnp.bfloat16
F32 = jnp.float32
LAST = (((1,), (1,)), ((), ()))
VMEM_LIMIT = 32 << 20
IN_VMEM = pl.BlockSpec(memory_space=pltpu.VMEM)
IN_HBM = pl.BlockSpec(memory_space=pltpu.HBM)
IN_SMEM = pl.BlockSpec(memory_space=pltpu.SMEM)


def dot(a, b):
    return jnp.dot(a, b, preferred_element_type=F32)


def iota(shape, dim):
    return lax.broadcasted_iota(jnp.int32, shape, dim)


def twice(matrix):
    blank = jnp.zeros_like(matrix)
    return jnp.concatenate(
        [jnp.concatenate([matrix, blank], 1), jnp.concatenate([blank, matrix], 1)], 0
    )


def side_by_side(rows):
    half = rows.shape[0] // 2
    return jnp.concatenate([rows[:half], rows[half:]], 1)


def centre(rows):
    values = rows.astype(F32)
    centred = values - jnp.mean(values, axis=-1, keepdims=True)
    return centred, jnp.mean(centred * centred, axis=-1, keepdims=True)


def layer_norm(rows):
    centred, variance = centre(rows)
    return centred * lax.rsqrt(variance + EPSILON)


def sigmoid(values):
    return 0.5 * jnp.tanh(0.5 * values) + 0.5


def attn_norm(cond, single, ada):
    width = single.shape[-1]
    mixed = dot(cond, ada)
    return (sigmoid(mixed[:, :width])[None] * single + mixed[None, :, width:]).astype(BF16)


def pair_kernel(packing, core_ref, w_pair_hbm, pair_hbm, single_hbm, cond_hbm, *refs):
    count = sum(packing)
    weights_hbm, refs = refs[:count], refs[count:]
    tile_ref, single_ref, cond_ref = refs[:3]
    packed_refs, refs = refs[3 : 3 + len(packing)], refs[3 + len(packing) :]
    w_pair_ref, pair_ref, pair_sem, sem = refs
    rows, cols, width = pair_ref.shape
    heads = w_pair_ref.shape[0]
    group = GROUP
    lanes = heads * group
    half = group // 2
    pieces = rows // half
    row_start = core_ref[0] * rows

    def pair_copy(i):
        source = pair_hbm.at[pl.ds(row_start + i * half, half)]
        return pltpu.make_async_copy(source, pair_ref.at[pl.ds(i * half, half)], pair_sem.at[i])

    moves = [(w_pair_hbm, w_pair_ref), (single_hbm, single_ref), (cond_hbm, cond_ref)]
    index = 0
    for number, packed in zip(packing, packed_refs):
        offset = 0
        for _ in range(number):
            source = weights_hbm[index]
            span = source.shape[1]
            moves.append((source, packed.at[:, pl.ds(offset, span)]))
            offset += span
            index += 1
    copies = [
        pltpu.make_async_copy(source, target, sem.at[i])
        for i, (source, target) in enumerate(moves)
    ]
    copies[0].start()
    for i in range(pieces):
        pair_copy(i).start()
    copies[0].wait()
    w_pair = w_pair_ref[...].astype(F32)
    spread = jnp.concatenate(
        [jnp.broadcast_to(w_pair[h : h + 1], (group, width)) for h in range(heads)], 0
    )
    mix = twice(spread.T.astype(BF16))
    slot = iota((cols, lanes), 1) % group

    @pl.loop(0, rows // group)
    def _(chunk):
        for part in range(2):
            pair_copy(chunk * 2 + part).wait()

        @pl.when(chunk == 0)
        def _():
            for copy in copies[1:]:
                copy.start()

        pair = pair_ref[pl.ds(chunk * group, group)].reshape(group * cols, width)
        centred, variance = centre(pair)
        variance = variance.reshape(group, cols, 1)
        mixed = dot(side_by_side(centred.astype(BF16)), mix).reshape(half, cols, 2 * lanes)
        total = jnp.zeros((cols, lanes), F32)
        spread_out = jnp.zeros((cols, lanes), F32)
        for i in range(group):
            side = slice(i // half * lanes, (i // half + 1) * lanes)
            total = jnp.where(slot == i, mixed[i % half, :, side], total)
            spread_out = jnp.where(slot == i, variance[i], spread_out)
        bias = (total * lax.rsqrt(spread_out + EPSILON)).astype(BF16)
        tile_ref[chunk] = bias

    for copy in copies[1:]:
        copy.wait()


def project_kernel(
    at_ref,
    single_ref,
    cond_ref,
    ada_attn,
    ada_trans,
    gates_ref,
    w_kv,
    w_qg,
    w_up,
    w_down,
    query_ref,
    key_ref,
    value_ref,
    gate_ref,
    open_ref,
    trans_ref,
    near_ref,
    far_ref,
):
    samples, atoms_here, width = single_ref.shape
    hidden_width = w_down.shape[0]
    step = math.gcd(atoms_here, 256)
    for start in range(0, atoms_here, step):
        at = slice(start, start + step)
        cond = layer_norm(cond_ref[at, :]).astype(BF16)
        single = layer_norm(single_ref[:, at, :].reshape(-1, width))
        single = single.reshape(samples, step, width)
        normed = attn_norm(cond, single, ada_attn[...])
        if start == 0:
            heads_of = [normed[sample, :EDGE] for sample in range(samples)]
        if start + step == atoms_here:
            tails_of = [normed[sample, step - EDGE :] for sample in range(samples)]
        normed = normed.reshape(-1, width)
        both = dot(normed, w_kv[...]).astype(BF16).reshape(samples, step, 2 * width)
        key_ref[:, at, :] = both[:, :, :width]
        value_ref[:, at, :] = both[:, :, width:]
        both = dot(normed, w_qg[...]).reshape(samples, step, 2 * width)
        query_ref[:, at, :] = both[:, :, :width].astype(BF16)
        gate_ref[:, at, :] = sigmoid(both[:, :, width:]).astype(BF16)
        gates = dot(cond, gates_ref[...])
        open_ref[at, :] = sigmoid(gates[:, :width]).astype(BF16)
        normed = attn_norm(cond, single, ada_trans[...]).reshape(-1, width)
        swish = dot(normed, w_up[:, :hidden_width])
        hidden = (swish * sigmoid(swish) * dot(normed, w_up[:, hidden_width:])).astype(BF16)
        down = dot(hidden, w_down[...]).reshape(samples, step, width)
        trans_ref[:, at, :] = (sigmoid(gates[:, width:])[None] * down).astype(BF16)
    even = at_ref[0] % 2 == 0
    for sample, (head, tail) in enumerate(zip(heads_of, tails_of)):
        cut = slice(sample * EDGE, (sample + 1) * EDGE)
        near_ref[cut, :] = jnp.where(even, tail, head)
        far_ref[cut, :] = jnp.where(even, head, tail)


def tile_of(refs, place, row_block):
    if len(refs) == 1:
        return refs[0][row_block]
    pair_at, core_at = place
    owners = 2
    mine, theirs, across, diagonal = [ref[...] for ref in refs]
    near = jnp.where(row_block % owners == core_at, mine, theirs)
    far = jnp.where(row_block % owners == core_at, across, diagonal)
    return jnp.where(row_block // owners == pair_at, near, far)


def select_kernel(blocks, at_ref, pair_ref, core_ref, *refs):
    *tile_refs, _, __, ___, near_ref, far_ref, ____, held_ref, again_ref = refs
    groups, cols, lanes = tile_refs[0].shape[-3:]
    rows = groups * EDGE
    device_at, place = at_ref[0], (pair_ref[0], core_ref[0])
    for send_ref, parity in ((near_ref, 0), (far_ref, 1)):
        above = device_at % 2 == parity
        beside = jnp.where(above, device_at + 1, device_at - 1)
        tile = tile_of(tile_refs, place, jnp.clip(beside, 0, blocks - 1))
        tile = jnp.where(above, tile[:, cols - EDGE :], tile[:, :EDGE])
        send_ref[send_ref.shape[0] - rows :, :] = tile.reshape(rows, lanes)
    again_ref[...] = near_ref[...]
    held_ref[...] = tile_of(tile_refs, place, device_at).reshape(groups * cols, lanes)


def bounds(counts_ref, block, token):
    tok_here = counts_ref.shape[1]
    counts = counts_ref[pl.ds(block, 1), :].astype(F32).astype(BF16)
    counts = jnp.broadcast_to(counts, (8, tok_here))
    before = iota((tok_here, token.shape[1]), 0)
    first = dot(counts, (before < token).astype(BF16))[:1]
    last = dot(counts, (before <= token).astype(BF16))[:1]
    return first.astype(jnp.int32), last.astype(jnp.int32)


def one_hot(reach, offset, count):
    first, last = reach
    position = iota((count, first.shape[1]), 0) + offset
    return ((first <= position) & (position < last)).astype(F32).astype(BF16)


def expand(hot, tile, groups):
    tile = tile.reshape(groups, -1, tile.shape[-1])
    tile = jnp.concatenate([tile[part] for part in range(groups)], 1)
    return dot(hot, tile).astype(BF16)


def attend(heads, reach, windows, query_ref, gate_ref, gated_ref):
    samples, _, width = query_ref.shape
    head_dim = width // heads
    lanes = reach[0].shape[1]
    rows = heads * Q_WIN
    lane_head = iota((rows, lanes), 1) // GROUP % heads
    row_head = iota((rows, lanes), 0) // Q_WIN
    same_head = (lane_head == row_head).astype(F32).astype(BF16)
    own_head = iota((rows, width), 1) // head_dim == iota((rows, width), 0) // Q_WIN
    own_head = own_head.astype(F32).astype(BF16)
    channel_head = iota((Q_WIN, 2 * width), 1) % width // head_dim
    ones = jnp.ones((K_WIN, width), BF16)
    scaling = LOG2E / math.sqrt(head_dim)

    biases = []
    for start, _, near, mask in windows:
        pick = jnp.concatenate([one_hot(reach, start, Q_WIN)] * heads, 0) * same_head
        bias = lax.dot_general(pick, near, LAST, preferred_element_type=F32) * LOG2E
        biases.append(bias if mask is None else jnp.where(mask, bias, MASKED))
    units = [(sample, i) for i in range(len(windows)) for sample in range(samples)]
    scores = []
    for sample, i in units:
        query = query_ref[sample, pl.ds(windows[i][0], Q_WIN), :]
        query = jnp.concatenate([query] * heads, 0) * own_head
        keys = windows[i][1](sample)[0]
        product = lax.dot_general(query, keys, LAST, preferred_element_type=F32)
        scores.append(product * scaling + biases[i])
    tops = [jnp.max(score, axis=-1, keepdims=True) for score in scores]
    raised = [jnp.exp2(score - top).astype(BF16) for score, top in zip(scores, tops)]
    for (sample, i), weight in zip(units, raised):
        values = windows[i][1](sample)[1]
        mixed = dot(weight, jnp.concatenate([values, ones], 1))
        picked = mixed[:Q_WIN]
        for head in range(1, heads):
            picked = jnp.where(
                channel_head == head, mixed[head * Q_WIN : (head + 1) * Q_WIN], picked
            )
        attended = picked[:, :width] * pl.reciprocal(picked[:, width:], approx=True)
        at = pl.ds(windows[i][0], Q_WIN)
        gate = gate_ref[sample, at, :].astype(F32)
        gated_ref[sample, at, :] = (gate * attended).astype(BF16)


def close(sample, cut, gated_ref, open_ref, trans_ref, w_out_ref):
    mixed = dot(gated_ref[sample, cut, :], w_out_ref[...])
    opened, trans = open_ref[cut, :].astype(F32), trans_ref[sample, cut, :].astype(F32)
    return (opened * mixed + trans).astype(BF16)


def row_tokens(heads, tok_here):
    lane = iota((tok_here, heads * tok_here), 1)
    return lane // (heads * GROUP) * GROUP + lane % GROUP


def inner_kernel(
    heads,
    at_ref,
    counts_ref,
    query_ref,
    key_ref,
    value_ref,
    gate_ref,
    open_ref,
    trans_ref,
    w_out_ref,
    held_ref,
    out_ref,
    near_ref,
    gated_ref,
):
    samples, atoms_here, width = query_ref.shape
    tok_here = counts_ref.shape[1]
    device_at = at_ref[0]
    hot = one_hot(
        bounds(counts_ref, device_at, iota((tok_here, tok_here), 1)), 0, atoms_here
    )
    near_ref[...] = expand(hot, held_ref[...], tok_here // GROUP)
    reach = bounds(counts_ref, device_at, row_tokens(heads, tok_here))
    skip = -(-EDGE // Q_WIN)
    inner = atoms_here // Q_WIN - 2 * skip
    batch = math.gcd(inner, 12)

    @pl.loop(0, inner // batch)
    def _(turn):
        windows = []
        for i in range(batch):
            start = pl.multiple_of((turn * batch + i + skip) * Q_WIN, Q_WIN)
            cut = pl.ds(pl.multiple_of(start - EDGE, 16), K_WIN)
            parts = lambda sample, cut=cut: (key_ref[sample, cut, :], value_ref[sample, cut, :])
            windows.append((start, parts, near_ref[cut, :], None))
        attend(heads, reach, windows, query_ref, gate_ref, gated_ref)

    cut = slice(skip * Q_WIN, atoms_here - skip * Q_WIN)
    for sample in range(samples):
        out_ref[sample] = close(sample, cut, gated_ref, open_ref, trans_ref, w_out_ref)


def outer_kernel(
    heads,
    blocks,
    at_ref,
    counts_ref,
    query_ref,
    own_key_ref,
    own_value_ref,
    gate_ref,
    open_ref,
    trans_ref,
    w_out_ref,
    held_ref,
    inner_ref,
    w_kv,
    early_ref,
    second_ref,
    late_ref,
    out_hbm,
    key_ref,
    value_ref,
    near_ref,
    gated_ref,
    out_ref,
    sem,
):
    samples, atoms_here, width = query_ref.shape
    tok_here = counts_ref.shape[1]
    device_at = at_ref[0]
    ends = atoms_here * blocks
    skip = -(-EDGE // Q_WIN)
    margin = skip * Q_WIN
    reach_keys = key_ref.shape[2]
    inside = reach_keys - EDGE

    whole = pltpu.make_async_copy(
        inner_ref, out_hbm.at[:, pl.ds(margin, atoms_here - 2 * margin)], sem.at[0]
    )
    whole.start()

    even = device_at % 2 == 0
    first = jnp.where(device_at % 4 < 2, early_ref[...], late_ref[...])
    second = second_ref[...]
    arrived = (jnp.where(even, second, first), jnp.where(even, first, second))
    count = samples * EDGE
    edges = jnp.concatenate([rows[:count] for rows in arrived], 0)
    edges = dot(edges, w_kv[...]).astype(BF16).reshape(2, samples, EDGE, 2 * width)
    groups = tok_here // GROUP
    token = iota((tok_here, tok_here), 1)
    own_reach = bounds(counts_ref, device_at, token)
    sides = (
        (jnp.maximum(device_at - 1, 0), atoms_here - EDGE, 0, EDGE, 0),
        (jnp.minimum(device_at + 1, blocks - 1), 0, inside, 0, atoms_here - inside),
    )
    for side, (block, offset, place, own_place, own_start) in enumerate(sides):
        for i, (ref, own_ref) in enumerate(((key_ref, own_key_ref), (value_ref, own_value_ref))):
            ref[side, :, place : place + EDGE, :] = edges[side, :, :, i * width : (i + 1) * width]
            ref[side, :, own_place : own_place + inside, :] = own_ref[
                :, own_start : own_start + inside, :
            ]
        nearest = iota((tok_here, EDGE), 1) + (tok_here - EDGE if side == 0 else 0)
        hot = one_hot(bounds(counts_ref, block, nearest), offset, EDGE)
        near_ref[side, place : place + EDGE, :] = expand(hot, arrived[side][count:], groups)
        hot = one_hot(own_reach, own_start, inside)
        near_ref[side, own_place : own_place + inside, :] = expand(hot, held_ref[...], groups)

    reach = bounds(counts_ref, device_at, row_tokens(heads, tok_here))
    windows = []
    for side in range(2):
        for i in range(skip):
            start = i * Q_WIN + side * (atoms_here - margin)
            cut = slice(i * Q_WIN, i * Q_WIN + K_WIN)
            parts = lambda sample, side=side, cut=cut: (
                key_ref[side, sample, cut, :],
                value_ref[side, sample, cut, :],
            )
            key_at = iota((heads * Q_WIN, K_WIN), 1) + (device_at * atoms_here + start - EDGE)
            mask = (key_at >= 0) & (key_at < ends)
            windows.append((start, parts, near_ref[side, cut, :], mask))
    attend(heads, reach, windows, query_ref, gate_ref, gated_ref)
    copies = []
    for side in range(2):
        cut = slice(side * (atoms_here - margin), side * (atoms_here - margin) + margin)
        for sample in range(samples):
            out_ref[side, sample] = close(sample, cut, gated_ref, open_ref, trans_ref, w_out_ref)
        target = out_hbm.at[:, pl.ds(side * (atoms_here - margin), margin)]
        copies.append(pltpu.make_async_copy(out_ref.at[side], target, sem.at[1 + side]))
        copies[-1].start()
    for copy in copies:
        copy.wait()
    whole.wait()


def shards(
    atom_single,
    atom_cond,
    pair_cond,
    atom_counts,
    ada_attn_scale,
    ada_attn_shift,
    w_query,
    w_key,
    w_value,
    w_gate,
    w_out,
    attn_gate,
    w_pair,
    ada_trans_scale,
    ada_trans_shift,
    w_swish,
    w_linear,
    w_down,
    trans_gate,
):
    device_at = lax.axis_index("atoms")
    blocks = lax.axis_size("atoms")
    samples, atoms_here, width = atom_single.shape
    tok_here = atom_counts.shape[1]
    heads = w_pair.shape[1]
    groups = tok_here // GROUP
    pairs = lax.axis_size("pair")
    assert pair_cond.shape[0] == lax.axis_size("samp") * tok_here
    at = device_at.astype(jnp.int32).reshape(1)
    pair_at = lax.axis_index("pair").astype(jnp.int32).reshape(1)
    core_at = lax.axis_index("samp").astype(jnp.int32).reshape(1)
    in_hbm = lambda array: pltpu.with_memory_space_constraint(array, pltpu.HBM)
    in_vmem = lambda array: pltpu.with_memory_space_constraint(array, pltpu.VMEM)

    packing = (
        (ada_attn_scale, ada_attn_shift),
        (ada_trans_scale, ada_trans_shift),
        (attn_gate, trans_gate),
        (w_key, w_value),
        (w_query, w_gate),
        (w_swish, w_linear),
        (w_down,),
        (w_out,),
    )
    flat = [array for arrays in packing for array in arrays]
    cols = pair_cond.shape[1]
    lanes = heads * GROUP
    wide = (samples, atoms_here, width)
    params = pltpu.CompilerParams(vmem_limit_bytes=VMEM_LIMIT)

    def cost(products):
        return pl.CostEstimate(flops=2 * products, bytes_accessed=4 << 20, transcendentals=0)

    sent = pltpu.VMEM((samples * EDGE + groups * EDGE, lanes), BF16)
    shapes = [
        pltpu.VMEM((groups, cols, lanes), BF16),
        pltpu.VMEM(wide, BF16),
        pltpu.VMEM(atom_cond.shape, BF16),
    ] + [
        pltpu.VMEM((arrays[0].shape[0], sum(a.shape[1] for a in arrays)), BF16)
        for arrays in packing
    ]
    made = pl.pallas_call(
        functools.partial(pair_kernel, [len(arrays) for arrays in packing]),
        in_specs=[IN_SMEM] + [IN_HBM] * (4 + len(flat)),
        out_specs=[IN_VMEM] * len(shapes),
        out_shape=shapes,
        scratch_shapes=[
            pltpu.VMEM((heads, width), BF16),
            pltpu.VMEM((tok_here, cols, width), BF16),
            pltpu.SemaphoreType.DMA((2 * groups,)),
            pltpu.SemaphoreType.DMA((3 + len(flat),)),
        ],
        compiler_params=params,
        cost_estimate=cost(tok_here * cols * width * width * 2),
    )(core_at, *map(in_hbm, (w_pair.T, pair_cond, atom_single, atom_cond, *flat)))
    own, single, cond, *packed = made
    ada_attn, ada_trans, gates, w_kv, w_qg, w_up, w_down, w_out = packed
    if pairs == 2:
        swapped = [(0, 1), (1, 0)]
        across = lax.ppermute(own, "pair", swapped)
        diagonal = lax.ppermute(own, ("pair", "samp"), [(0, 3), (1, 2), (2, 1), (3, 0)])
        tiles = (own, lax.ppermute(own, "samp", swapped), across, diagonal)
    else:
        tiles = (lax.all_gather(own, ("pair", "samp")),)

    operands = (single, cond, ada_attn, ada_trans, gates, w_kv, w_qg, w_up, w_down)
    query, keys, values, gate, opened, trans, near, far = pl.pallas_call(
        project_kernel,
        in_specs=[IN_SMEM] + [IN_VMEM] * len(operands),
        out_specs=[IN_VMEM] * 8,
        out_shape=[pltpu.VMEM(wide, BF16)] * 4
        + [pltpu.VMEM((atoms_here, width), BF16), pltpu.VMEM(wide, BF16), sent, sent],
        compiler_params=params,
        cost_estimate=cost(samples * atoms_here * width * width * 20),
    )(at, *map(in_vmem, operands))

    operands = (*tiles, near, far, opened)
    first = 3 + len(tiles)
    near, far, opened, held, again = pl.pallas_call(
        functools.partial(select_kernel, blocks),
        in_specs=[IN_SMEM] * 3 + [IN_VMEM] * len(operands),
        out_specs=[IN_VMEM] * 5,
        out_shape=[
            sent,
            sent,
            pltpu.VMEM((atoms_here, width), BF16),
            pltpu.VMEM((groups * cols, lanes), BF16),
            sent,
        ],
        input_output_aliases={first: 0, first + 1: 1, first + 2: 2},
        compiler_params=params,
    )(at, pair_at, core_at, *map(in_vmem, operands))

    def swap(value, start, step):
        cores = lax.axis_size("samp")
        other_of = {}
        for i in range(start, blocks - 1, step):
            other_of[i], other_of[i + 1] = i + 1, i
        sides = []
        for i in range(blocks):
            for core in range(cores):
                target = (other_of[i], core) if i in other_of else (i, (core + 1) % cores)
                sides.append((i * cores + core, target[0] * cores + target[1]))
        return lax.ppermute(value, ("atoms", "samp"), sides)

    early, second, later = swap(near, 0, 4), swap(far, 1, 2), swap(again, 2, 4)

    margin = -(-EDGE // Q_WIN) * Q_WIN
    operands = (query, keys, values, gate, opened, trans, w_out, held)
    inner = pl.pallas_call(
        functools.partial(inner_kernel, heads),
        in_specs=[IN_SMEM] + [IN_VMEM] * (1 + len(operands)),
        out_specs=IN_VMEM,
        out_shape=pltpu.VMEM((samples, atoms_here - 2 * margin, width), BF16),
        scratch_shapes=[
            pltpu.VMEM((atoms_here, heads * tok_here), BF16),
            pltpu.VMEM(wide, BF16),
        ],
        compiler_params=params,
        cost_estimate=cost(samples * atoms_here * width * width * 12),
    )(at, atom_counts, *map(in_vmem, operands))

    reach = margin - Q_WIN + K_WIN
    operands += (inner, w_kv, early, second, later)
    return pl.pallas_call(
        functools.partial(outer_kernel, heads, blocks),
        in_specs=[IN_SMEM] + [IN_VMEM] * (1 + len(operands)),
        out_specs=IN_HBM,
        out_shape=pltpu.HBM(wide, BF16),
        scratch_shapes=[
            pltpu.VMEM((2, samples, reach, width), BF16),
            pltpu.VMEM((2, samples, reach, width), BF16),
            pltpu.VMEM((2, reach, heads * tok_here), BF16),
            pltpu.VMEM(wide, BF16),
            pltpu.VMEM((2, samples, margin, width), BF16),
            pltpu.SemaphoreType.DMA((3,)),
        ],
        compiler_params=params,
        cost_estimate=cost(samples * atoms_here * width * width * 4),
    )(at, atom_counts, *map(in_vmem, operands))


def solution(mesh):
    return jax.shard_map(
        shards,
        mesh=mesh,
        in_specs=(
            P(("groups", "pair", "samp"), "atoms", None),
            P(("groups", "atoms"), None),
            P(("groups", "pair"), "atoms", None),
            P("groups", None),
        )
        + (P(),) * 15,
        out_specs=P(("groups", "pair", "samp"), "atoms", None),
        check_vma=False,
    )
```

```python
import functools
import math

import jax
import jax.numpy as jnp
from jax import lax
from jax.experimental import pallas as pl
from jax.experimental.pallas import tpu as pltpu
from jax.sharding import PartitionSpec as P

Q_WIN = 32
K_WIN = 128
EDGE = 48
GROUP = 32

EPSILON = 1e-05
MASKED = -1e30
LOG2E = math.log2(math.e)
BF16 = jnp.bfloat16
F32 = jnp.float32
LAST = (((1,), (1,)), ((), ()))
VMEM_LIMIT = 32 << 20
IN_VMEM = pl.BlockSpec(memory_space=pltpu.VMEM)
IN_HBM = pl.BlockSpec(memory_space=pltpu.HBM)
IN_SMEM = pl.BlockSpec(memory_space=pltpu.SMEM)


def dot(a, b):
    return jnp.dot(a, b, preferred_element_type=F32)


def iota(shape, dim):
    return lax.broadcasted_iota(jnp.int32, shape, dim)


def twice(matrix):
    blank = jnp.zeros_like(matrix)
    return jnp.concatenate(
        [jnp.concatenate([matrix, blank], 1), jnp.concatenate([blank, matrix], 1)], 0
    )


def side_by_side(rows):
    half = rows.shape[0] // 2
    return jnp.concatenate([rows[:half], rows[half:]], 1)


def centre(rows):
    values = rows.astype(F32)
    centred = values - jnp.mean(values, axis=-1, keepdims=True)
    return centred, jnp.mean(centred * centred, axis=-1, keepdims=True)


def layer_norm(rows):
    centred, variance = centre(rows)
    return centred * lax.rsqrt(variance + EPSILON)


def sigmoid(values):
    return 0.5 * jnp.tanh(0.5 * values) + 0.5


def attn_norm(cond, single, ada):
    width = single.shape[-1]
    mixed = dot(cond, ada)
    return (sigmoid(mixed[:, :width])[None] * single + mixed[None, :, width:]).astype(BF16)


def pair_kernel(core_ref, w_pair_hbm, pair_hbm, tile_ref, w_pair_ref, pair_ref, pair_sem, sem):
    rows, cols, width = pair_ref.shape
    heads = w_pair_ref.shape[0]
    group = GROUP
    lanes = heads * group
    half = group // 2
    pieces = rows // half
    row_start = core_ref[0] * rows

    def pair_copy(i):
        source = pair_hbm.at[pl.ds(row_start + i * half, half)]
        return pltpu.make_async_copy(source, pair_ref.at[pl.ds(i * half, half)], pair_sem.at[i])

    w_pair_copy = pltpu.make_async_copy(w_pair_hbm, w_pair_ref, sem)
    w_pair_copy.start()
    for i in range(pieces):
        pair_copy(i).start()
    w_pair_copy.wait()
    w_pair = w_pair_ref[...].astype(F32)
    spread = jnp.concatenate(
        [jnp.broadcast_to(w_pair[h : h + 1], (group, width)) for h in range(heads)], 0
    )
    mix = twice(spread.T.astype(BF16))
    slot = iota((cols, lanes), 1) % group

    @pl.loop(0, rows // group)
    def _(chunk):
        for part in range(2):
            pair_copy(chunk * 2 + part).wait()

        pair = pair_ref[pl.ds(chunk * group, group)].reshape(group * cols, width)
        centred, variance = centre(pair)
        variance = variance.reshape(group, cols, 1)
        mixed = dot(side_by_side(centred.astype(BF16)), mix).reshape(half, cols, 2 * lanes)
        total = jnp.zeros((cols, lanes), F32)
        spread_out = jnp.zeros((cols, lanes), F32)
        for i in range(group):
            side = slice(i // half * lanes, (i // half + 1) * lanes)
            total = jnp.where(slot == i, mixed[i % half, :, side], total)
            spread_out = jnp.where(slot == i, variance[i], spread_out)
        bias = (total * lax.rsqrt(spread_out + EPSILON)).astype(BF16)
        tile_ref[chunk] = bias


def beside(first, second):
    return jnp.concatenate([first[...], second[...]], 1)


def project_kernel(
    at_ref,
    single_ref,
    cond_ref,
    ada_attn,
    ada_attn_shift,
    ada_trans,
    ada_trans_shift,
    attn_gate,
    trans_gate,
    w_key,
    w_value,
    w_query,
    w_gate,
    w_swish,
    w_linear,
    w_down,
    query_ref,
    key_ref,
    value_ref,
    gate_ref,
    open_ref,
    trans_ref,
    near_ref,
    far_ref,
):
    samples, atoms_here, width = single_ref.shape
    step = math.gcd(atoms_here, 256)
    for start in range(0, atoms_here, step):
        at = slice(start, start + step)
        cond = layer_norm(cond_ref[at, :]).astype(BF16)
        single = layer_norm(single_ref[:, at, :].reshape(-1, width))
        single = single.reshape(samples, step, width)
        normed = attn_norm(cond, single, beside(ada_attn, ada_attn_shift))
        if start == 0:
            heads_of = [normed[sample, :EDGE] for sample in range(samples)]
        if start + step == atoms_here:
            tails_of = [normed[sample, step - EDGE :] for sample in range(samples)]
        normed = normed.reshape(-1, width)
        both = dot(normed, beside(w_key, w_value)).astype(BF16).reshape(samples, step, 2 * width)
        key_ref[:, at, :] = both[:, :, :width]
        value_ref[:, at, :] = both[:, :, width:]
        both = dot(normed, beside(w_query, w_gate)).reshape(samples, step, 2 * width)
        query_ref[:, at, :] = both[:, :, :width].astype(BF16)
        gate_ref[:, at, :] = sigmoid(both[:, :, width:]).astype(BF16)
        gates = dot(cond, beside(attn_gate, trans_gate))
        open_ref[at, :] = sigmoid(gates[:, :width]).astype(BF16)
        normed = attn_norm(cond, single, beside(ada_trans, ada_trans_shift)).reshape(-1, width)
        swish = dot(normed, w_swish[...])
        hidden = (swish * sigmoid(swish) * dot(normed, w_linear[...])).astype(BF16)
        down = dot(hidden, w_down[...]).reshape(samples, step, width)
        trans_ref[:, at, :] = (sigmoid(gates[:, width:])[None] * down).astype(BF16)
    even = at_ref[0] % 2 == 0
    for sample, (head, tail) in enumerate(zip(heads_of, tails_of)):
        cut = slice(sample * EDGE, (sample + 1) * EDGE)
        near_ref[cut, :] = jnp.where(even, tail, head)
        far_ref[cut, :] = jnp.where(even, head, tail)


def tile_of(refs, place, row_block):
    if len(refs) == 1:
        return refs[0][row_block]
    pair_at, core_at = place
    owners = 2
    mine, theirs, across, diagonal = [ref[...] for ref in refs]
    near = jnp.where(row_block % owners == core_at, mine, theirs)
    far = jnp.where(row_block % owners == core_at, across, diagonal)
    return jnp.where(row_block // owners == pair_at, near, far)


def select_kernel(blocks, at_ref, pair_ref, core_ref, *refs):
    *tile_refs, _, __, ___, near_ref, far_ref, ____, held_ref, again_ref = refs
    groups, cols, lanes = tile_refs[0].shape[-3:]
    rows = groups * EDGE
    device_at, place = at_ref[0], (pair_ref[0], core_ref[0])
    for send_ref, parity in ((near_ref, 0), (far_ref, 1)):
        above = device_at % 2 == parity
        beside = jnp.where(above, device_at + 1, device_at - 1)
        tile = tile_of(tile_refs, place, jnp.clip(beside, 0, blocks - 1))
        tile = jnp.where(above, tile[:, cols - EDGE :], tile[:, :EDGE])
        send_ref[send_ref.shape[0] - rows :, :] = tile.reshape(rows, lanes)
    again_ref[...] = near_ref[...]
    held_ref[...] = tile_of(tile_refs, place, device_at).reshape(groups * cols, lanes)


def bounds(counts_ref, block, token):
    tok_here = counts_ref.shape[1]
    counts = counts_ref[pl.ds(block, 1), :].astype(F32).astype(BF16)
    counts = jnp.broadcast_to(counts, (8, tok_here))
    before = iota((tok_here, token.shape[1]), 0)
    first = dot(counts, (before < token).astype(BF16))[:1]
    last = dot(counts, (before <= token).astype(BF16))[:1]
    return first.astype(jnp.int32), last.astype(jnp.int32)


def one_hot(reach, offset, count):
    first, last = reach
    position = iota((count, first.shape[1]), 0) + offset
    return ((first <= position) & (position < last)).astype(F32).astype(BF16)


def expand(hot, tile, groups):
    tile = tile.reshape(groups, -1, tile.shape[-1])
    tile = jnp.concatenate([tile[part] for part in range(groups)], 1)
    return dot(hot, tile).astype(BF16)


def attend(heads, reach, windows, query_ref, gate_ref, gated_ref):
    samples, _, width = query_ref.shape
    head_dim = width // heads
    lanes = reach[0].shape[1]
    rows = heads * Q_WIN
    lane_head = iota((rows, lanes), 1) // GROUP % heads
    row_head = iota((rows, lanes), 0) // Q_WIN
    same_head = (lane_head == row_head).astype(F32).astype(BF16)
    own_head = iota((rows, width), 1) // head_dim == iota((rows, width), 0) // Q_WIN
    own_head = own_head.astype(F32).astype(BF16)
    channel_head = iota((Q_WIN, 2 * width), 1) % width // head_dim
    ones = jnp.ones((K_WIN, width), BF16)
    scaling = LOG2E / math.sqrt(head_dim)

    biases = []
    for start, _, near, mask in windows:
        pick = jnp.concatenate([one_hot(reach, start, Q_WIN)] * heads, 0) * same_head
        bias = lax.dot_general(pick, near, LAST, preferred_element_type=F32) * LOG2E
        biases.append(bias if mask is None else jnp.where(mask, bias, MASKED))
    units = [(sample, i) for i in range(len(windows)) for sample in range(samples)]
    scores = []
    for sample, i in units:
        query = query_ref[sample, pl.ds(windows[i][0], Q_WIN), :]
        query = jnp.concatenate([query] * heads, 0) * own_head
        keys = windows[i][1](sample)[0]
        product = lax.dot_general(query, keys, LAST, preferred_element_type=F32)
        scores.append(product * scaling + biases[i])
    tops = [jnp.max(score, axis=-1, keepdims=True) for score in scores]
    raised = [jnp.exp2(score - top).astype(BF16) for score, top in zip(scores, tops)]
    for (sample, i), weight in zip(units, raised):
        values = windows[i][1](sample)[1]
        mixed = dot(weight, jnp.concatenate([values, ones], 1))
        picked = mixed[:Q_WIN]
        for head in range(1, heads):
            picked = jnp.where(
                channel_head == head, mixed[head * Q_WIN : (head + 1) * Q_WIN], picked
            )
        attended = picked[:, :width] * pl.reciprocal(picked[:, width:], approx=True)
        at = pl.ds(windows[i][0], Q_WIN)
        gate = gate_ref[sample, at, :].astype(F32)
        gated_ref[sample, at, :] = (gate * attended).astype(BF16)


def close(sample, cut, gated_ref, open_ref, trans_ref, w_out_ref):
    mixed = dot(gated_ref[sample, cut, :], w_out_ref[...])
    opened, trans = open_ref[cut, :].astype(F32), trans_ref[sample, cut, :].astype(F32)
    return (opened * mixed + trans).astype(BF16)


def row_tokens(heads, tok_here):
    lane = iota((tok_here, heads * tok_here), 1)
    return lane // (heads * GROUP) * GROUP + lane % GROUP


def inner_kernel(
    heads,
    at_ref,
    counts_ref,
    query_ref,
    key_ref,
    value_ref,
    gate_ref,
    open_ref,
    trans_ref,
    w_out_ref,
    held_ref,
    out_ref,
    near_ref,
    gated_ref,
):
    samples, atoms_here, width = query_ref.shape
    tok_here = counts_ref.shape[1]
    device_at = at_ref[0]
    hot = one_hot(
        bounds(counts_ref, device_at, iota((tok_here, tok_here), 1)), 0, atoms_here
    )
    near_ref[...] = expand(hot, held_ref[...], tok_here // GROUP)
    reach = bounds(counts_ref, device_at, row_tokens(heads, tok_here))
    skip = -(-EDGE // Q_WIN)
    inner = atoms_here // Q_WIN - 2 * skip
    batch = math.gcd(inner, 12)

    @pl.loop(0, inner // batch)
    def _(turn):
        windows = []
        for i in range(batch):
            start = pl.multiple_of((turn * batch + i + skip) * Q_WIN, Q_WIN)
            cut = pl.ds(pl.multiple_of(start - EDGE, 16), K_WIN)
            parts = lambda sample, cut=cut: (key_ref[sample, cut, :], value_ref[sample, cut, :])
            windows.append((start, parts, near_ref[cut, :], None))
        attend(heads, reach, windows, query_ref, gate_ref, gated_ref)

    cut = slice(skip * Q_WIN, atoms_here - skip * Q_WIN)
    for sample in range(samples):
        out_ref[sample] = close(sample, cut, gated_ref, open_ref, trans_ref, w_out_ref)


def outer_kernel(
    heads,
    blocks,
    at_ref,
    counts_ref,
    query_ref,
    own_key_ref,
    own_value_ref,
    gate_ref,
    open_ref,
    trans_ref,
    w_out_ref,
    held_ref,
    inner_ref,
    w_key,
    w_value,
    early_ref,
    second_ref,
    late_ref,
    out_hbm,
    key_ref,
    value_ref,
    near_ref,
    gated_ref,
    out_ref,
    sem,
):
    samples, atoms_here, width = query_ref.shape
    tok_here = counts_ref.shape[1]
    device_at = at_ref[0]
    ends = atoms_here * blocks
    skip = -(-EDGE // Q_WIN)
    margin = skip * Q_WIN
    reach_keys = key_ref.shape[2]
    inside = reach_keys - EDGE

    whole = pltpu.make_async_copy(
        inner_ref, out_hbm.at[:, pl.ds(margin, atoms_here - 2 * margin)], sem.at[0]
    )
    whole.start()

    even = device_at % 2 == 0
    first = jnp.where(device_at % 4 < 2, early_ref[...], late_ref[...])
    second = second_ref[...]
    arrived = (jnp.where(even, second, first), jnp.where(even, first, second))
    count = samples * EDGE
    edges = jnp.concatenate([rows[:count] for rows in arrived], 0)
    edges = dot(edges, beside(w_key, w_value)).astype(BF16).reshape(2, samples, EDGE, 2 * width)
    groups = tok_here // GROUP
    token = iota((tok_here, tok_here), 1)
    own_reach = bounds(counts_ref, device_at, token)
    sides = (
        (jnp.maximum(device_at - 1, 0), atoms_here - EDGE, 0, EDGE, 0),
        (jnp.minimum(device_at + 1, blocks - 1), 0, inside, 0, atoms_here - inside),
    )
    for side, (block, offset, place, own_place, own_start) in enumerate(sides):
        for i, (ref, own_ref) in enumerate(((key_ref, own_key_ref), (value_ref, own_value_ref))):
            ref[side, :, place : place + EDGE, :] = edges[side, :, :, i * width : (i + 1) * width]
            ref[side, :, own_place : own_place + inside, :] = own_ref[
                :, own_start : own_start + inside, :
            ]
        nearest = iota((tok_here, EDGE), 1) + (tok_here - EDGE if side == 0 else 0)
        hot = one_hot(bounds(counts_ref, block, nearest), offset, EDGE)
        near_ref[side, place : place + EDGE, :] = expand(hot, arrived[side][count:], groups)
        hot = one_hot(own_reach, own_start, inside)
        near_ref[side, own_place : own_place + inside, :] = expand(hot, held_ref[...], groups)

    reach = bounds(counts_ref, device_at, row_tokens(heads, tok_here))
    windows = []
    for side in range(2):
        for i in range(skip):
            start = i * Q_WIN + side * (atoms_here - margin)
            cut = slice(i * Q_WIN, i * Q_WIN + K_WIN)
            parts = lambda sample, side=side, cut=cut: (
                key_ref[side, sample, cut, :],
                value_ref[side, sample, cut, :],
            )
            key_at = iota((heads * Q_WIN, K_WIN), 1) + (device_at * atoms_here + start - EDGE)
            mask = (key_at >= 0) & (key_at < ends)
            windows.append((start, parts, near_ref[side, cut, :], mask))
    attend(heads, reach, windows, query_ref, gate_ref, gated_ref)
    copies = []
    for side in range(2):
        cut = slice(side * (atoms_here - margin), side * (atoms_here - margin) + margin)
        for sample in range(samples):
            out_ref[side, sample] = close(sample, cut, gated_ref, open_ref, trans_ref, w_out_ref)
        target = out_hbm.at[:, pl.ds(side * (atoms_here - margin), margin)]
        copies.append(pltpu.make_async_copy(out_ref.at[side], target, sem.at[1 + side]))
        copies[-1].start()
    for copy in copies:
        copy.wait()
    whole.wait()


def shards(
    atom_single,
    atom_cond,
    pair_cond,
    atom_counts,
    ada_attn_scale,
    ada_attn_shift,
    w_query,
    w_key,
    w_value,
    w_gate,
    w_out,
    attn_gate,
    w_pair,
    ada_trans_scale,
    ada_trans_shift,
    w_swish,
    w_linear,
    w_down,
    trans_gate,
):
    device_at = lax.axis_index("atoms")
    blocks = lax.axis_size("atoms")
    samples, atoms_here, width = atom_single.shape
    tok_here = atom_counts.shape[1]
    heads = w_pair.shape[1]
    groups = tok_here // GROUP
    pairs = lax.axis_size("pair")
    assert pair_cond.shape[0] == lax.axis_size("samp") * tok_here
    at = device_at.astype(jnp.int32).reshape(1)
    pair_at = lax.axis_index("pair").astype(jnp.int32).reshape(1)
    core_at = lax.axis_index("samp").astype(jnp.int32).reshape(1)
    in_hbm = lambda array: pltpu.with_memory_space_constraint(array, pltpu.HBM)
    in_vmem = lambda array: pltpu.with_memory_space_constraint(array, pltpu.VMEM)

    cols = pair_cond.shape[1]
    lanes = heads * GROUP
    wide = (samples, atoms_here, width)
    params = pltpu.CompilerParams(vmem_limit_bytes=VMEM_LIMIT)

    def cost(products):
        return pl.CostEstimate(flops=2 * products, bytes_accessed=4 << 20, transcendentals=0)

    sent = pltpu.VMEM((samples * EDGE + groups * EDGE, lanes), BF16)
    own = pl.pallas_call(
        pair_kernel,
        in_specs=[IN_SMEM] + [IN_HBM] * 2,
        out_specs=IN_VMEM,
        out_shape=pltpu.VMEM((groups, cols, lanes), BF16),
        scratch_shapes=[
            pltpu.VMEM((heads, width), BF16),
            pltpu.VMEM((tok_here, cols, width), BF16),
            pltpu.SemaphoreType.DMA((2 * groups,)),
            pltpu.SemaphoreType.DMA,
        ],
        compiler_params=params,
        cost_estimate=cost(tok_here * cols * width * width * 2),
    )(core_at, *map(in_hbm, (w_pair.T, pair_cond)))
    if pairs == 2:
        swapped = [(0, 1), (1, 0)]
        across = lax.ppermute(own, "pair", swapped)
        diagonal = lax.ppermute(own, ("pair", "samp"), [(0, 3), (1, 2), (2, 1), (3, 0)])
        tiles = (own, lax.ppermute(own, "samp", swapped), across, diagonal)
    else:
        tiles = (lax.all_gather(own, ("pair", "samp")),)

    operands = (
        atom_single,
        atom_cond,
        ada_attn_scale,
        ada_attn_shift,
        ada_trans_scale,
        ada_trans_shift,
        attn_gate,
        trans_gate,
        w_key,
        w_value,
        w_query,
        w_gate,
        w_swish,
        w_linear,
        w_down,
    )
    query, keys, values, gate, opened, trans, near, far = pl.pallas_call(
        project_kernel,
        in_specs=[IN_SMEM] + [IN_VMEM] * len(operands),
        out_specs=[IN_VMEM] * 8,
        out_shape=[pltpu.VMEM(wide, BF16)] * 4
        + [pltpu.VMEM((atoms_here, width), BF16), pltpu.VMEM(wide, BF16), sent, sent],
        compiler_params=params,
        cost_estimate=cost(samples * atoms_here * width * width * 20),
    )(at, *map(in_vmem, operands))

    operands = (*tiles, near, far, opened)
    first = 3 + len(tiles)
    near, far, opened, held, again = pl.pallas_call(
        functools.partial(select_kernel, blocks),
        in_specs=[IN_SMEM] * 3 + [IN_VMEM] * len(operands),
        out_specs=[IN_VMEM] * 5,
        out_shape=[
            sent,
            sent,
            pltpu.VMEM((atoms_here, width), BF16),
            pltpu.VMEM((groups * cols, lanes), BF16),
            sent,
        ],
        input_output_aliases={first: 0, first + 1: 1, first + 2: 2},
        compiler_params=params,
    )(at, pair_at, core_at, *map(in_vmem, operands))

    def swap(value, start, step):
        cores = lax.axis_size("samp")
        other_of = {}
        for i in range(start, blocks - 1, step):
            other_of[i], other_of[i + 1] = i + 1, i
        sides = []
        for i in range(blocks):
            for core in range(cores):
                target = (other_of[i], core) if i in other_of else (i, (core + 1) % cores)
                sides.append((i * cores + core, target[0] * cores + target[1]))
        return lax.ppermute(value, ("atoms", "samp"), sides)

    early, second, later = swap(near, 0, 4), swap(far, 1, 2), swap(again, 2, 4)

    margin = -(-EDGE // Q_WIN) * Q_WIN
    operands = (query, keys, values, gate, opened, trans, w_out, held)
    inner = pl.pallas_call(
        functools.partial(inner_kernel, heads),
        in_specs=[IN_SMEM] + [IN_VMEM] * (1 + len(operands)),
        out_specs=IN_VMEM,
        out_shape=pltpu.VMEM((samples, atoms_here - 2 * margin, width), BF16),
        scratch_shapes=[
            pltpu.VMEM((atoms_here, heads * tok_here), BF16),
            pltpu.VMEM(wide, BF16),
        ],
        compiler_params=params,
        cost_estimate=cost(samples * atoms_here * width * width * 12),
    )(at, atom_counts, *map(in_vmem, operands))

    reach = margin - Q_WIN + K_WIN
    operands += (inner, w_key, w_value, early, second, later)
    return pl.pallas_call(
        functools.partial(outer_kernel, heads, blocks),
        in_specs=[IN_SMEM] + [IN_VMEM] * (1 + len(operands)),
        out_specs=IN_HBM,
        out_shape=pltpu.HBM(wide, BF16),
        scratch_shapes=[
            pltpu.VMEM((2, samples, reach, width), BF16),
            pltpu.VMEM((2, samples, reach, width), BF16),
            pltpu.VMEM((2, reach, heads * tok_here), BF16),
            pltpu.VMEM(wide, BF16),
            pltpu.VMEM((2, samples, margin, width), BF16),
            pltpu.SemaphoreType.DMA((3,)),
        ],
        compiler_params=params,
        cost_estimate=cost(samples * atoms_here * width * width * 4),
    )(at, atom_counts, *map(in_vmem, operands))


def solution(mesh):
    return jax.shard_map(
        shards,
        mesh=mesh,
        in_specs=(
            P(("groups", "pair", "samp"), "atoms", None),
            P(("groups", "atoms"), None),
            P(("groups", "pair"), "atoms", None),
            P("groups", None),
        )
        + (P(),) * 15,
        out_specs=P(("groups", "pair", "samp"), "atoms", None),
        check_vma=False,
    )
```

```python
import functools
import math

import jax
import jax.numpy as jnp
from jax import lax
from jax.experimental import pallas as pl
from jax.experimental.pallas import tpu as pltpu
from jax.sharding import PartitionSpec as P

Q_WIN = 32
K_WIN = 128
EDGE = 48
GROUP = 32

EPSILON = 1e-05
MASKED = -1e30
LOG2E = math.log2(math.e)
BF16 = jnp.bfloat16
F32 = jnp.float32
LAST = (((1,), (1,)), ((), ()))
VMEM_LIMIT = 32 << 20
IN_VMEM = pl.BlockSpec(memory_space=pltpu.VMEM)
IN_HBM = pl.BlockSpec(memory_space=pltpu.HBM)
IN_SMEM = pl.BlockSpec(memory_space=pltpu.SMEM)


def dot(a, b):
    return jnp.dot(a, b, preferred_element_type=F32)


def iota(shape, dim):
    return lax.broadcasted_iota(jnp.int32, shape, dim)


def twice(matrix):
    blank = jnp.zeros_like(matrix)
    return jnp.concatenate(
        [jnp.concatenate([matrix, blank], 1), jnp.concatenate([blank, matrix], 1)], 0
    )


def side_by_side(rows):
    half = rows.shape[0] // 2
    return jnp.concatenate([rows[:half], rows[half:]], 1)


def centring(width):
    same = iota((width, width), 0) == iota((width, width), 1)
    return jnp.where(same, 1.0 - 1.0 / width, -1.0 / width).astype(BF16)


def mean_square(centred):
    return jnp.mean(centred * centred, axis=-1, keepdims=True)


def layer_norm(rows):
    width = rows.shape[1]
    both = dot(side_by_side(rows), twice(centring(width)))
    centred = jnp.concatenate([both[:, :width], both[:, width:]], 0)
    return centred * lax.rsqrt(mean_square(centred) + EPSILON)


def sigmoid(values):
    return 0.5 * jnp.tanh(0.5 * values) + 0.5


def attn_norm(cond, single, ada):
    width = single.shape[-1]
    mixed = dot(cond, ada)
    return (sigmoid(mixed[:, :width])[None] * single + mixed[None, :, width:]).astype(BF16)


def pair_kernel(core_ref, w_pair_hbm, pair_hbm, tile_ref, w_pair_ref, pair_ref, pair_sem, sem):
    rows, cols, width = pair_ref.shape
    heads = w_pair_ref.shape[0]
    group = GROUP
    lanes = heads * group
    half = group // 2
    pieces = rows // half
    row_start = core_ref[0] * rows

    def pair_copy(i):
        source = pair_hbm.at[pl.ds(row_start + i * half, half)]
        return pltpu.make_async_copy(source, pair_ref.at[pl.ds(i * half, half)], pair_sem.at[i])

    w_pair_copy = pltpu.make_async_copy(w_pair_hbm, w_pair_ref, sem)
    w_pair_copy.start()
    for i in range(pieces):
        pair_copy(i).start()
    w_pair_copy.wait()
    w_pair = w_pair_ref[...].astype(F32)
    spread = jnp.concatenate(
        [jnp.broadcast_to(w_pair[h : h + 1], (group, width)) for h in range(heads)], 0
    )
    mix = twice(spread.T.astype(BF16))
    centre = twice(centring(width))
    slot = iota((cols, lanes), 1) % group

    @pl.loop(0, rows // group)
    def _(chunk):
        for part in range(2):
            pair_copy(chunk * 2 + part).wait()

        pair = pair_ref[pl.ds(chunk * group, group)].reshape(group * cols, width)
        centred = dot(side_by_side(pair), centre)
        mixed = dot(centred.astype(BF16), mix).reshape(half, cols, 2 * lanes)
        variances = [
            mean_square(centred[:, part * width : (part + 1) * width]).reshape(half, cols, 1)
            for part in range(2)
        ]
        total = jnp.zeros((cols, lanes), F32)
        spread_out = jnp.zeros((cols, lanes), F32)
        for i in range(group):
            side = slice(i // half * lanes, (i // half + 1) * lanes)
            total = jnp.where(slot == i, mixed[i % half, :, side], total)
            spread_out = jnp.where(slot == i, variances[i // half][i % half], spread_out)
        bias = (total * lax.rsqrt(spread_out + EPSILON)).astype(BF16)
        tile_ref[chunk] = bias


def beside(first, second):
    return jnp.concatenate([first[...], second[...]], 1)


def project_kernel(
    at_ref,
    single_ref,
    cond_ref,
    ada_attn,
    ada_attn_shift,
    ada_trans,
    ada_trans_shift,
    attn_gate,
    trans_gate,
    w_key,
    w_value,
    w_query,
    w_gate,
    w_swish,
    w_linear,
    w_down,
    query_ref,
    key_ref,
    value_ref,
    gate_ref,
    open_ref,
    trans_ref,
    near_ref,
    far_ref,
):
    samples, atoms_here, width = single_ref.shape
    step = math.gcd(atoms_here, 256)
    for start in range(0, atoms_here, step):
        at = slice(start, start + step)
        cond = layer_norm(cond_ref[at, :]).astype(BF16)
        single = layer_norm(single_ref[:, at, :].reshape(-1, width))
        single = single.reshape(samples, step, width)
        normed = attn_norm(cond, single, beside(ada_attn, ada_attn_shift))
        if start == 0:
            heads_of = [normed[sample, :EDGE] for sample in range(samples)]
        if start + step == atoms_here:
            tails_of = [normed[sample, step - EDGE :] for sample in range(samples)]
        normed = normed.reshape(-1, width)
        both = dot(normed, beside(w_key, w_value)).astype(BF16).reshape(samples, step, 2 * width)
        key_ref[:, at, :] = both[:, :, :width]
        value_ref[:, at, :] = both[:, :, width:]
        both = dot(normed, beside(w_query, w_gate)).reshape(samples, step, 2 * width)
        query_ref[:, at, :] = both[:, :, :width].astype(BF16)
        gate_ref[:, at, :] = sigmoid(both[:, :, width:]).astype(BF16)
        gates = dot(cond, beside(attn_gate, trans_gate))
        open_ref[at, :] = sigmoid(gates[:, :width]).astype(BF16)
        normed = attn_norm(cond, single, beside(ada_trans, ada_trans_shift)).reshape(-1, width)
        swish = dot(normed, w_swish[...])
        hidden = (swish * sigmoid(swish) * dot(normed, w_linear[...])).astype(BF16)
        down = dot(hidden, w_down[...]).reshape(samples, step, width)
        trans_ref[:, at, :] = (sigmoid(gates[:, width:])[None] * down).astype(BF16)
    even = at_ref[0] % 2 == 0
    for sample, (head, tail) in enumerate(zip(heads_of, tails_of)):
        cut = slice(sample * EDGE, (sample + 1) * EDGE)
        near_ref[cut, :] = jnp.where(even, tail, head)
        far_ref[cut, :] = jnp.where(even, head, tail)


def tile_of(refs, place, row_block):
    if len(refs) == 1:
        return refs[0][row_block]
    pair_at, core_at = place
    owners = 2
    mine, theirs, across, diagonal = [ref[...] for ref in refs]
    near = jnp.where(row_block % owners == core_at, mine, theirs)
    far = jnp.where(row_block % owners == core_at, across, diagonal)
    return jnp.where(row_block // owners == pair_at, near, far)


def select_kernel(blocks, at_ref, pair_ref, core_ref, *refs):
    *tile_refs, _, __, ___, near_ref, far_ref, ____, held_ref, again_ref = refs
    groups, cols, lanes = tile_refs[0].shape[-3:]
    rows = groups * EDGE
    device_at, place = at_ref[0], (pair_ref[0], core_ref[0])
    for send_ref, parity in ((near_ref, 0), (far_ref, 1)):
        above = device_at % 2 == parity
        beside = jnp.where(above, device_at + 1, device_at - 1)
        tile = tile_of(tile_refs, place, jnp.clip(beside, 0, blocks - 1))
        tile = jnp.where(above, tile[:, cols - EDGE :], tile[:, :EDGE])
        send_ref[send_ref.shape[0] - rows :, :] = tile.reshape(rows, lanes)
    again_ref[...] = near_ref[...]
    held_ref[...] = tile_of(tile_refs, place, device_at).reshape(groups * cols, lanes)


def bounds(counts_ref, block, token):
    tok_here = counts_ref.shape[1]
    counts = counts_ref[pl.ds(block, 1), :].astype(F32).astype(BF16)
    counts = jnp.broadcast_to(counts, (8, tok_here))
    before = iota((tok_here, token.shape[1]), 0)
    first = dot(counts, (before < token).astype(BF16))[:1]
    last = dot(counts, (before <= token).astype(BF16))[:1]
    return first.astype(jnp.int32), last.astype(jnp.int32)


def one_hot(reach, offset, count):
    first, last = reach
    position = iota((count, first.shape[1]), 0) + offset
    return ((first <= position) & (position < last)).astype(F32).astype(BF16)


def expand(hot, tile, groups):
    tile = tile.reshape(groups, -1, tile.shape[-1])
    tile = jnp.concatenate([tile[part] for part in range(groups)], 1)
    return dot(hot, tile).astype(BF16)


def attend(heads, reach, windows, query_ref, gate_ref, gated_ref):
    samples, _, width = query_ref.shape
    head_dim = width // heads
    lanes = reach[0].shape[1]
    rows = heads * Q_WIN
    lane_head = iota((rows, lanes), 1) // GROUP % heads
    row_head = iota((rows, lanes), 0) // Q_WIN
    same_head = (lane_head == row_head).astype(F32).astype(BF16)
    own_head = iota((rows, width), 1) // head_dim == iota((rows, width), 0) // Q_WIN
    own_head = own_head.astype(F32).astype(BF16)
    channel_head = iota((Q_WIN, 2 * width), 1) % width // head_dim
    ones = jnp.ones((K_WIN, width), BF16)
    scaling = LOG2E / math.sqrt(head_dim)

    biases = []
    for start, _, near, mask in windows:
        pick = jnp.concatenate([one_hot(reach, start, Q_WIN)] * heads, 0) * same_head
        bias = lax.dot_general(pick, near, LAST, preferred_element_type=F32) * LOG2E
        biases.append(bias if mask is None else jnp.where(mask, bias, MASKED))
    units = [(sample, i) for i in range(len(windows)) for sample in range(samples)]
    scores = []
    for first in range(0, len(units), 2):
        couple = units[first : first + 2]
        queries, keys = [], []
        for sample, i in couple:
            query = query_ref[sample, pl.ds(windows[i][0], Q_WIN), :]
            queries.append(jnp.concatenate([query] * heads, 0) * own_head)
            keys.append(windows[i][1](sample)[0])
        if len(couple) == 2:
            blank = jnp.zeros_like(keys[0])
            keys = [jnp.concatenate([keys[0], blank], 1), jnp.concatenate([blank, keys[1]], 1)]
        product = lax.dot_general(
            jnp.concatenate(queries, 1),
            jnp.concatenate(keys, 0),
            LAST,
            preferred_element_type=F32,
        )
        for j, (_, i) in enumerate(couple):
            scores.append(product[:, j * K_WIN : (j + 1) * K_WIN] * scaling + biases[i])
    tops = [jnp.max(score, axis=-1, keepdims=True) for score in scores]
    raised = [jnp.exp2(score - top).astype(BF16) for score, top in zip(scores, tops)]
    for (sample, i), weight in zip(units, raised):
        values = windows[i][1](sample)[1]
        mixed = dot(weight, jnp.concatenate([values, ones], 1))
        picked = mixed[:Q_WIN]
        for head in range(1, heads):
            picked = jnp.where(
                channel_head == head, mixed[head * Q_WIN : (head + 1) * Q_WIN], picked
            )
        attended = picked[:, :width] * pl.reciprocal(picked[:, width:], approx=True)
        at = pl.ds(windows[i][0], Q_WIN)
        gate = gate_ref[sample, at, :].astype(F32)
        gated_ref[sample, at, :] = (gate * attended).astype(BF16)


def close(sample, cut, gated_ref, open_ref, trans_ref, w_out_ref):
    mixed = dot(gated_ref[sample, cut, :], w_out_ref[...])
    opened, trans = open_ref[cut, :].astype(F32), trans_ref[sample, cut, :].astype(F32)
    return (opened * mixed + trans).astype(BF16)


def row_tokens(heads, tok_here):
    lane = iota((tok_here, heads * tok_here), 1)
    return lane // (heads * GROUP) * GROUP + lane % GROUP


def inner_kernel(
    heads,
    at_ref,
    counts_ref,
    query_ref,
    key_ref,
    value_ref,
    gate_ref,
    open_ref,
    trans_ref,
    w_out_ref,
    held_ref,
    out_ref,
    near_ref,
    gated_ref,
):
    samples, atoms_here, width = query_ref.shape
    tok_here = counts_ref.shape[1]
    device_at = at_ref[0]
    hot = one_hot(
        bounds(counts_ref, device_at, iota((tok_here, tok_here), 1)), 0, atoms_here
    )
    near_ref[...] = expand(hot, held_ref[...], tok_here // GROUP)
    reach = bounds(counts_ref, device_at, row_tokens(heads, tok_here))
    skip = -(-EDGE // Q_WIN)
    inner = atoms_here // Q_WIN - 2 * skip
    batch = math.gcd(inner, 12)

    @pl.loop(0, inner // batch)
    def _(turn):
        windows = []
        for i in range(batch):
            start = pl.multiple_of((turn * batch + i + skip) * Q_WIN, Q_WIN)
            cut = pl.ds(pl.multiple_of(start - EDGE, 16), K_WIN)
            parts = lambda sample, cut=cut: (key_ref[sample, cut, :], value_ref[sample, cut, :])
            windows.append((start, parts, near_ref[cut, :], None))
        attend(heads, reach, windows, query_ref, gate_ref, gated_ref)

    cut = slice(skip * Q_WIN, atoms_here - skip * Q_WIN)
    for sample in range(samples):
        out_ref[sample] = close(sample, cut, gated_ref, open_ref, trans_ref, w_out_ref)


def outer_kernel(
    heads,
    blocks,
    at_ref,
    counts_ref,
    query_ref,
    own_key_ref,
    own_value_ref,
    gate_ref,
    open_ref,
    trans_ref,
    w_out_ref,
    held_ref,
    inner_ref,
    w_key,
    w_value,
    early_ref,
    second_ref,
    late_ref,
    out_hbm,
    key_ref,
    value_ref,
    near_ref,
    gated_ref,
    out_ref,
    sem,
):
    samples, atoms_here, width = query_ref.shape
    tok_here = counts_ref.shape[1]
    device_at = at_ref[0]
    ends = atoms_here * blocks
    skip = -(-EDGE // Q_WIN)
    margin = skip * Q_WIN
    reach_keys = key_ref.shape[2]
    inside = reach_keys - EDGE

    whole = pltpu.make_async_copy(
        inner_ref, out_hbm.at[:, pl.ds(margin, atoms_here - 2 * margin)], sem.at[0]
    )
    whole.start()

    even = device_at % 2 == 0
    first = jnp.where(device_at % 4 < 2, early_ref[...], late_ref[...])
    second = second_ref[...]
    arrived = (jnp.where(even, second, first), jnp.where(even, first, second))
    count = samples * EDGE
    edges = jnp.concatenate([rows[:count] for rows in arrived], 0)
    edges = dot(edges, beside(w_key, w_value)).astype(BF16).reshape(2, samples, EDGE, 2 * width)
    groups = tok_here // GROUP
    token = iota((tok_here, tok_here), 1)
    own_reach = bounds(counts_ref, device_at, token)
    sides = (
        (jnp.maximum(device_at - 1, 0), atoms_here - EDGE, 0, EDGE, 0),
        (jnp.minimum(device_at + 1, blocks - 1), 0, inside, 0, atoms_here - inside),
    )
    for side, (block, offset, place, own_place, own_start) in enumerate(sides):
        for i, (ref, own_ref) in enumerate(((key_ref, own_key_ref), (value_ref, own_value_ref))):
            ref[side, :, place : place + EDGE, :] = edges[side, :, :, i * width : (i + 1) * width]
            ref[side, :, own_place : own_place + inside, :] = own_ref[
                :, own_start : own_start + inside, :
            ]
        nearest = iota((tok_here, EDGE), 1) + (tok_here - EDGE if side == 0 else 0)
        hot = one_hot(bounds(counts_ref, block, nearest), offset, EDGE)
        near_ref[side, place : place + EDGE, :] = expand(hot, arrived[side][count:], groups)
        hot = one_hot(own_reach, own_start, inside)
        near_ref[side, own_place : own_place + inside, :] = expand(hot, held_ref[...], groups)

    reach = bounds(counts_ref, device_at, row_tokens(heads, tok_here))
    windows = []
    for side in range(2):
        for i in range(skip):
            start = i * Q_WIN + side * (atoms_here - margin)
            cut = slice(i * Q_WIN, i * Q_WIN + K_WIN)
            parts = lambda sample, side=side, cut=cut: (
                key_ref[side, sample, cut, :],
                value_ref[side, sample, cut, :],
            )
            key_at = iota((heads * Q_WIN, K_WIN), 1) + (device_at * atoms_here + start - EDGE)
            mask = (key_at >= 0) & (key_at < ends)
            windows.append((start, parts, near_ref[side, cut, :], mask))
    attend(heads, reach, windows, query_ref, gate_ref, gated_ref)
    copies = []
    for side in range(2):
        cut = slice(side * (atoms_here - margin), side * (atoms_here - margin) + margin)
        for sample in range(samples):
            out_ref[side, sample] = close(sample, cut, gated_ref, open_ref, trans_ref, w_out_ref)
        target = out_hbm.at[:, pl.ds(side * (atoms_here - margin), margin)]
        copies.append(pltpu.make_async_copy(out_ref.at[side], target, sem.at[1 + side]))
        copies[-1].start()
    for copy in copies:
        copy.wait()
    whole.wait()


def shards(
    atom_single,
    atom_cond,
    pair_cond,
    atom_counts,
    ada_attn_scale,
    ada_attn_shift,
    w_query,
    w_key,
    w_value,
    w_gate,
    w_out,
    attn_gate,
    w_pair,
    ada_trans_scale,
    ada_trans_shift,
    w_swish,
    w_linear,
    w_down,
    trans_gate,
):
    device_at = lax.axis_index("atoms")
    blocks = lax.axis_size("atoms")
    samples, atoms_here, width = atom_single.shape
    tok_here = atom_counts.shape[1]
    heads = w_pair.shape[1]
    groups = tok_here // GROUP
    pairs = lax.axis_size("pair")
    assert pair_cond.shape[0] == lax.axis_size("samp") * tok_here
    at = device_at.astype(jnp.int32).reshape(1)
    pair_at = lax.axis_index("pair").astype(jnp.int32).reshape(1)
    core_at = lax.axis_index("samp").astype(jnp.int32).reshape(1)
    in_hbm = lambda array: pltpu.with_memory_space_constraint(array, pltpu.HBM)
    in_vmem = lambda array: pltpu.with_memory_space_constraint(array, pltpu.VMEM)

    cols = pair_cond.shape[1]
    lanes = heads * GROUP
    wide = (samples, atoms_here, width)
    params = pltpu.CompilerParams(vmem_limit_bytes=VMEM_LIMIT)

    def cost(products):
        return pl.CostEstimate(flops=2 * products, bytes_accessed=4 << 20, transcendentals=0)

    sent = pltpu.VMEM((samples * EDGE + groups * EDGE, lanes), BF16)
    own = pl.pallas_call(
        pair_kernel,
        in_specs=[IN_SMEM] + [IN_HBM] * 2,
        out_specs=IN_VMEM,
        out_shape=pltpu.VMEM((groups, cols, lanes), BF16),
        scratch_shapes=[
            pltpu.VMEM((heads, width), BF16),
            pltpu.VMEM((tok_here, cols, width), BF16),
            pltpu.SemaphoreType.DMA((2 * groups,)),
            pltpu.SemaphoreType.DMA,
        ],
        compiler_params=params,
        cost_estimate=cost(tok_here * cols * width * width * 2),
    )(core_at, *map(in_hbm, (w_pair.T, pair_cond)))
    if pairs == 2:
        swapped = [(0, 1), (1, 0)]
        across = lax.ppermute(own, "pair", swapped)
        diagonal = lax.ppermute(own, ("pair", "samp"), [(0, 3), (1, 2), (2, 1), (3, 0)])
        tiles = (own, lax.ppermute(own, "samp", swapped), across, diagonal)
    else:
        tiles = (lax.all_gather(own, ("pair", "samp")),)

    operands = (
        atom_single,
        atom_cond,
        ada_attn_scale,
        ada_attn_shift,
        ada_trans_scale,
        ada_trans_shift,
        attn_gate,
        trans_gate,
        w_key,
        w_value,
        w_query,
        w_gate,
        w_swish,
        w_linear,
        w_down,
    )
    query, keys, values, gate, opened, trans, near, far = pl.pallas_call(
        project_kernel,
        in_specs=[IN_SMEM] + [IN_VMEM] * len(operands),
        out_specs=[IN_VMEM] * 8,
        out_shape=[pltpu.VMEM(wide, BF16)] * 4
        + [pltpu.VMEM((atoms_here, width), BF16), pltpu.VMEM(wide, BF16), sent, sent],
        compiler_params=params,
        cost_estimate=cost(samples * atoms_here * width * width * 20),
    )(at, *map(in_vmem, operands))

    operands = (*tiles, near, far, opened)
    first = 3 + len(tiles)
    near, far, opened, held, again = pl.pallas_call(
        functools.partial(select_kernel, blocks),
        in_specs=[IN_SMEM] * 3 + [IN_VMEM] * len(operands),
        out_specs=[IN_VMEM] * 5,
        out_shape=[
            sent,
            sent,
            pltpu.VMEM((atoms_here, width), BF16),
            pltpu.VMEM((groups * cols, lanes), BF16),
            sent,
        ],
        input_output_aliases={first: 0, first + 1: 1, first + 2: 2},
        compiler_params=params,
    )(at, pair_at, core_at, *map(in_vmem, operands))

    def swap(value, start, step):
        cores = lax.axis_size("samp")
        other_of = {}
        for i in range(start, blocks - 1, step):
            other_of[i], other_of[i + 1] = i + 1, i
        sides = []
        for i in range(blocks):
            for core in range(cores):
                target = (other_of[i], core) if i in other_of else (i, (core + 1) % cores)
                sides.append((i * cores + core, target[0] * cores + target[1]))
        return lax.ppermute(value, ("atoms", "samp"), sides)

    early, second, later = swap(near, 0, 4), swap(far, 1, 2), swap(again, 2, 4)

    margin = -(-EDGE // Q_WIN) * Q_WIN
    operands = (query, keys, values, gate, opened, trans, w_out, held)
    inner = pl.pallas_call(
        functools.partial(inner_kernel, heads),
        in_specs=[IN_SMEM] + [IN_VMEM] * (1 + len(operands)),
        out_specs=IN_VMEM,
        out_shape=pltpu.VMEM((samples, atoms_here - 2 * margin, width), BF16),
        scratch_shapes=[
            pltpu.VMEM((atoms_here, heads * tok_here), BF16),
            pltpu.VMEM(wide, BF16),
        ],
        compiler_params=params,
        cost_estimate=cost(samples * atoms_here * width * width * 12),
    )(at, atom_counts, *map(in_vmem, operands))

    reach = margin - Q_WIN + K_WIN
    operands += (inner, w_key, w_value, early, second, later)
    return pl.pallas_call(
        functools.partial(outer_kernel, heads, blocks),
        in_specs=[IN_SMEM] + [IN_VMEM] * (1 + len(operands)),
        out_specs=IN_HBM,
        out_shape=pltpu.HBM(wide, BF16),
        scratch_shapes=[
            pltpu.VMEM((2, samples, reach, width), BF16),
            pltpu.VMEM((2, samples, reach, width), BF16),
            pltpu.VMEM((2, reach, heads * tok_here), BF16),
            pltpu.VMEM(wide, BF16),
            pltpu.VMEM((2, samples, margin, width), BF16),
            pltpu.SemaphoreType.DMA((3,)),
        ],
        compiler_params=params,
        cost_estimate=cost(samples * atoms_here * width * width * 4),
    )(at, atom_counts, *map(in_vmem, operands))


def solution(mesh):
    return jax.shard_map(
        shards,
        mesh=mesh,
        in_specs=(
            P(("groups", "pair", "samp"), "atoms", None),
            P(("groups", "atoms"), None),
            P(("groups", "pair"), "atoms", None),
            P("groups", None),
        )
        + (P(),) * 15,
        out_specs=P(("groups", "pair", "samp"), "atoms", None),
        check_vma=False,
    )
```

```python
import functools
import math

import jax
import jax.numpy as jnp
from jax import lax
from jax.experimental import pallas as pl
from jax.experimental.pallas import tpu as pltpu
from jax.sharding import PartitionSpec as P

Q_WIN = 32
K_WIN = 128
EDGE = 48
GROUP = 32

EPSILON = 1e-05
MASKED = -1e30
LOG2E = math.log2(math.e)
BF16 = jnp.bfloat16
F32 = jnp.float32
LAST = (((1,), (1,)), ((), ()))
VMEM_LIMIT = 32 << 20
IN_VMEM = pl.BlockSpec(memory_space=pltpu.VMEM)
IN_HBM = pl.BlockSpec(memory_space=pltpu.HBM)
IN_SMEM = pl.BlockSpec(memory_space=pltpu.SMEM)


def dot(a, b):
    return jnp.dot(a, b, preferred_element_type=F32)


def iota(shape, dim):
    return lax.broadcasted_iota(jnp.int32, shape, dim)


def twice(matrix):
    blank = jnp.zeros_like(matrix)
    return jnp.concatenate(
        [jnp.concatenate([matrix, blank], 1), jnp.concatenate([blank, matrix], 1)], 0
    )


def side_by_side(rows):
    half = rows.shape[0] // 2
    return jnp.concatenate([rows[:half], rows[half:]], 1)


def centring(width):
    same = iota((width, width), 0) == iota((width, width), 1)
    return jnp.where(same, 1.0 - 1.0 / width, -1.0 / width).astype(BF16)


def mean_square(centred):
    return jnp.mean(centred * centred, axis=-1, keepdims=True)


def layer_norm(rows):
    width = rows.shape[1]
    both = dot(side_by_side(rows), twice(centring(width)))
    centred = jnp.concatenate([both[:, :width], both[:, width:]], 0)
    return centred * lax.rsqrt(mean_square(centred) + EPSILON)


def sigmoid(values):
    return 0.5 * jnp.tanh(0.5 * values) + 0.5


def attn_norm(cond, single, ada):
    width = single.shape[-1]
    mixed = dot(cond, ada)
    return (sigmoid(mixed[:, :width])[None] * single + mixed[None, :, width:]).astype(BF16)


def pair_kernel(core_ref, w_pair_hbm, pair_hbm, tile_ref, w_pair_ref, pair_ref, pair_sem, sem):
    rows, cols, width = pair_ref.shape
    heads = w_pair_ref.shape[0]
    group = GROUP
    lanes = heads * group
    half = group // 2
    pieces = rows // half
    row_start = core_ref[0] * rows

    def pair_copy(i):
        source = pair_hbm.at[pl.ds(row_start + i * half, half)]
        return pltpu.make_async_copy(source, pair_ref.at[pl.ds(i * half, half)], pair_sem.at[i])

    w_pair_copy = pltpu.make_async_copy(w_pair_hbm, w_pair_ref, sem)
    w_pair_copy.start()
    for i in range(pieces):
        pair_copy(i).start(priority=i % 2)
    w_pair_copy.wait()
    w_pair = w_pair_ref[...].astype(F32)
    spread = jnp.concatenate(
        [jnp.broadcast_to(w_pair[h : h + 1], (group, width)) for h in range(heads)], 0
    )
    mix = twice(spread.T.astype(BF16))
    centre = twice(centring(width))
    slot = iota((cols, lanes), 1) % group

    @pl.loop(0, rows // group)
    def _(chunk):
        for part in range(2):
            pair_copy(chunk * 2 + part).wait()

        pair = pair_ref[pl.ds(chunk * group, group)].reshape(group * cols, width)
        centred = dot(side_by_side(pair), centre)
        mixed = dot(centred.astype(BF16), mix).reshape(half, cols, 2 * lanes)
        variances = [
            mean_square(centred[:, part * width : (part + 1) * width]).reshape(half, cols, 1)
            for part in range(2)
        ]
        total = jnp.zeros((cols, lanes), F32)
        spread_out = jnp.zeros((cols, lanes), F32)
        for i in range(group):
            side = slice(i // half * lanes, (i // half + 1) * lanes)
            total = jnp.where(slot == i, mixed[i % half, :, side], total)
            spread_out = jnp.where(slot == i, variances[i // half][i % half], spread_out)
        bias = (total * lax.rsqrt(spread_out + EPSILON)).astype(BF16)
        tile_ref[chunk] = bias


def beside(first, second):
    return jnp.concatenate([first[...], second[...]], 1)


def project_kernel(
    at_ref,
    single_ref,
    cond_ref,
    ada_attn_scale,
    ada_attn_shift,
    ada_trans_scale,
    ada_trans_shift,
    w_key,
    w_value,
    w_query,
    w_gate,
    query_ref,
    key_ref,
    value_ref,
    gate_ref,
    cond_norm_ref,
    trans_norm_ref,
    near_ref,
    far_ref,
):
    samples, atoms_here, width = single_ref.shape
    step = math.gcd(atoms_here, 256)
    for start in range(0, atoms_here, step):
        at = slice(start, start + step)
        cond = layer_norm(cond_ref[at, :]).astype(BF16)
        cond_norm_ref[at, :] = cond
        single = layer_norm(single_ref[:, at, :].reshape(-1, width))
        single = single.reshape(samples, step, width)
        normed = attn_norm(cond, single, beside(ada_attn_scale, ada_attn_shift))
        if start == 0:
            heads_of = [normed[sample, :EDGE] for sample in range(samples)]
        if start + step == atoms_here:
            tails_of = [normed[sample, step - EDGE :] for sample in range(samples)]
        normed = normed.reshape(-1, width)
        both = dot(normed, beside(w_key, w_value)).astype(BF16)
        both = both.reshape(samples, step, 2 * width)
        key_ref[:, at, :] = both[:, :, :width]
        value_ref[:, at, :] = both[:, :, width:]
        both = dot(normed, beside(w_query, w_gate)).reshape(samples, step, 2 * width)
        query_ref[:, at, :] = both[:, :, :width].astype(BF16)
        gate_ref[:, at, :] = sigmoid(both[:, :, width:]).astype(BF16)
        ada = beside(ada_trans_scale, ada_trans_shift)
        trans_norm_ref[:, at, :] = attn_norm(cond, single, ada)

    even = at_ref[0] % 2 == 0
    for sample, (head, tail) in enumerate(zip(heads_of, tails_of)):
        cut = slice(sample * EDGE, (sample + 1) * EDGE)
        near_ref[cut, :] = jnp.where(even, tail, head)
        far_ref[cut, :] = jnp.where(even, head, tail)


def transition_kernel(
    cond_norm_ref,
    trans_norm_ref,
    attn_gate,
    trans_gate,
    w_swish,
    w_linear,
    w_down,
    open_ref,
    trans_ref,
):
    samples, atoms_here, width = trans_norm_ref.shape
    step = math.gcd(atoms_here, 256)
    for start in range(0, atoms_here, step):
        at = slice(start, start + step)
        gates = sigmoid(dot(cond_norm_ref[at, :], beside(attn_gate, trans_gate)))
        open_ref[at, :] = gates[:, :width].astype(BF16)
        normed = trans_norm_ref[:, at, :].reshape(-1, width)
        swish = dot(normed, w_swish[...])
        hidden = (swish * sigmoid(swish) * dot(normed, w_linear[...])).astype(BF16)
        down = dot(hidden, w_down[...]).reshape(samples, step, width)
        trans_ref[:, at, :] = (gates[None, :, width:] * down).astype(BF16)


def gather_kernel(own_ref, across_ref, _, both_ref, __):
    both_ref[0] = own_ref[...]
    both_ref[1] = across_ref[...]


def tile_of(refs, place, row_block):
    if len(refs) == 1:
        return refs[0][row_block]
    pair_at, core_at = place
    owners = 2
    mine, theirs = [jnp.where(row_block // owners == pair_at, ref[0], ref[1]) for ref in refs]
    return jnp.where(row_block % owners == core_at, mine, theirs)


def select_kernel(blocks, at_ref, pair_ref, core_ref, *refs):
    *tile_refs, _, __, ___, near_ref, far_ref, ____, held_ref, again_ref = refs
    groups, cols, lanes = tile_refs[0].shape[-3:]
    rows = groups * EDGE
    device_at, place = at_ref[0], (pair_ref[0], core_ref[0])
    for send_ref, parity in ((near_ref, 0), (far_ref, 1)):
        above = device_at % 2 == parity
        beside = jnp.where(above, device_at + 1, device_at - 1)
        tile = tile_of(tile_refs, place, jnp.clip(beside, 0, blocks - 1))
        tile = jnp.where(above, tile[:, cols - EDGE :], tile[:, :EDGE])
        send_ref[send_ref.shape[0] - rows :, :] = tile.reshape(rows, lanes)
    again_ref[...] = near_ref[...]
    held_ref[...] = tile_of(tile_refs, place, device_at).reshape(groups * cols, lanes)


def bounds(counts_ref, block, token):
    tok_here = counts_ref.shape[1]
    counts = counts_ref[pl.ds(block, 1), :].astype(F32).astype(BF16)
    counts = jnp.broadcast_to(counts, (8, tok_here))
    before = iota((tok_here, token.shape[1]), 0)
    first = dot(counts, (before < token).astype(BF16))[:1]
    last = dot(counts, (before <= token).astype(BF16))[:1]
    return first.astype(jnp.int32), last.astype(jnp.int32)


def one_hot(reach, offset, count):
    first, last = reach
    position = iota((count, first.shape[1]), 0) + offset
    return ((first <= position) & (position < last)).astype(F32).astype(BF16)


def expand(hot, tile, groups):
    tile = tile.reshape(groups, -1, tile.shape[-1])
    tile = jnp.concatenate([tile[part] for part in range(groups)], 1)
    return dot(hot, tile).astype(BF16)


def attend(heads, reach, windows, query_ref, gate_ref, gated_ref):
    samples, _, width = query_ref.shape
    head_dim = width // heads
    lanes = reach[0].shape[1]
    rows = heads * Q_WIN
    lane_head = iota((rows, lanes), 1) // GROUP % heads
    row_head = iota((rows, lanes), 0) // Q_WIN
    same_head = (lane_head == row_head).astype(F32).astype(BF16)
    own_head = iota((rows, width), 1) // head_dim == iota((rows, width), 0) // Q_WIN
    own_head = own_head.astype(F32).astype(BF16)
    channel_head = iota((Q_WIN, 2 * width), 1) % width // head_dim
    ones = jnp.ones((K_WIN, width), BF16)
    scaling = LOG2E / math.sqrt(head_dim)

    biases = []
    for start, _, near, mask in windows:
        pick = jnp.concatenate([one_hot(reach, start, Q_WIN)] * heads, 0) * same_head
        bias = lax.dot_general(pick, near, LAST, preferred_element_type=F32) * LOG2E
        biases.append(bias if mask is None else jnp.where(mask, bias, MASKED))
    units = [(sample, i) for i in range(len(windows)) for sample in range(samples)]
    scores = []
    for first in range(0, len(units), 2):
        couple = units[first : first + 2]
        queries, keys = [], []
        for sample, i in couple:
            query = query_ref[sample, pl.ds(windows[i][0], Q_WIN), :]
            queries.append(jnp.concatenate([query] * heads, 0) * own_head)
            keys.append(windows[i][1](sample)[0])
        if len(couple) == 2:
            blank = jnp.zeros_like(keys[0])
            keys = [jnp.concatenate([keys[0], blank], 1), jnp.concatenate([blank, keys[1]], 1)]
        product = lax.dot_general(
            jnp.concatenate(queries, 1),
            jnp.concatenate(keys, 0),
            LAST,
            preferred_element_type=F32,
        )
        for j, (_, i) in enumerate(couple):
            scores.append(product[:, j * K_WIN : (j + 1) * K_WIN] * scaling + biases[i])
    tops = [jnp.max(score, axis=-1, keepdims=True) for score in scores]
    raised = [jnp.exp2(score - top).astype(BF16) for score, top in zip(scores, tops)]
    for (sample, i), weight in zip(units, raised):
        values = windows[i][1](sample)[1]
        mixed = dot(weight, jnp.concatenate([values, ones], 1))
        picked = mixed[:Q_WIN]
        for head in range(1, heads):
            picked = jnp.where(
                channel_head == head, mixed[head * Q_WIN : (head + 1) * Q_WIN], picked
            )
        attended = picked[:, :width] * pl.reciprocal(picked[:, width:], approx=True)
        at = pl.ds(windows[i][0], Q_WIN)
        gate = gate_ref[sample, at, :].astype(F32)
        gated_ref[sample, at, :] = (gate * attended).astype(BF16)


def close(sample, cut, gated_ref, open_ref, trans_ref, w_out_ref):
    mixed = dot(gated_ref[sample, cut, :], w_out_ref[...])
    opened, trans = open_ref[cut, :].astype(F32), trans_ref[sample, cut, :].astype(F32)
    return (opened * mixed + trans).astype(BF16)


def row_tokens(heads, tok_here):
    lane = iota((tok_here, heads * tok_here), 1)
    return lane // (heads * GROUP) * GROUP + lane % GROUP


def inner_kernel(
    heads,
    at_ref,
    counts_ref,
    query_ref,
    key_ref,
    value_ref,
    gate_ref,
    open_ref,
    trans_ref,
    w_out_ref,
    held_ref,
    out_ref,
    near_ref,
    gated_ref,
):
    samples, atoms_here, width = query_ref.shape
    tok_here = counts_ref.shape[1]
    device_at = at_ref[0]
    hot = one_hot(
        bounds(counts_ref, device_at, iota((tok_here, tok_here), 1)), 0, atoms_here
    )
    near_ref[...] = expand(hot, held_ref[...], tok_here // GROUP)
    reach = bounds(counts_ref, device_at, row_tokens(heads, tok_here))
    skip = -(-EDGE // Q_WIN)
    inner = atoms_here // Q_WIN - 2 * skip
    batch = math.gcd(inner, 12)

    @pl.loop(0, inner // batch)
    def _(turn):
        windows = []
        for i in range(batch):
            start = pl.multiple_of((turn * batch + i + skip) * Q_WIN, Q_WIN)
            cut = pl.ds(pl.multiple_of(start - EDGE, 16), K_WIN)
            parts = lambda sample, cut=cut: (key_ref[sample, cut, :], value_ref[sample, cut, :])
            windows.append((start, parts, near_ref[cut, :], None))
        attend(heads, reach, windows, query_ref, gate_ref, gated_ref)

    cut = slice(skip * Q_WIN, atoms_here - skip * Q_WIN)
    for sample in range(samples):
        out_ref[sample] = close(sample, cut, gated_ref, open_ref, trans_ref, w_out_ref)


def outer_kernel(
    heads,
    blocks,
    at_ref,
    counts_ref,
    query_ref,
    own_key_ref,
    own_value_ref,
    gate_ref,
    open_ref,
    trans_ref,
    w_out_ref,
    held_ref,
    inner_ref,
    w_key,
    w_value,
    early_ref,
    second_ref,
    late_ref,
    out_hbm,
    key_ref,
    value_ref,
    near_ref,
    gated_ref,
    out_ref,
    sem,
):
    samples, atoms_here, width = query_ref.shape
    tok_here = counts_ref.shape[1]
    device_at = at_ref[0]
    ends = atoms_here * blocks
    skip = -(-EDGE // Q_WIN)
    margin = skip * Q_WIN
    reach_keys = key_ref.shape[2]
    inside = reach_keys - EDGE

    whole = pltpu.make_async_copy(
        inner_ref, out_hbm.at[:, pl.ds(margin, atoms_here - 2 * margin)], sem.at[0]
    )
    whole.start()

    even = device_at % 2 == 0
    first = jnp.where(device_at % 4 < 2, early_ref[...], late_ref[...])
    second = second_ref[...]
    arrived = (jnp.where(even, second, first), jnp.where(even, first, second))
    count = samples * EDGE
    edges = jnp.concatenate([rows[:count] for rows in arrived], 0)
    edges = dot(edges, beside(w_key, w_value)).astype(BF16).reshape(2, samples, EDGE, 2 * width)
    groups = tok_here // GROUP
    token = iota((tok_here, tok_here), 1)
    own_reach = bounds(counts_ref, device_at, token)
    sides = (
        (jnp.maximum(device_at - 1, 0), atoms_here - EDGE, 0, EDGE, 0),
        (jnp.minimum(device_at + 1, blocks - 1), 0, inside, 0, atoms_here - inside),
    )
    for side, (block, offset, place, own_place, own_start) in enumerate(sides):
        for i, (ref, own_ref) in enumerate(((key_ref, own_key_ref), (value_ref, own_value_ref))):
            ref[side, :, place : place + EDGE, :] = edges[side, :, :, i * width : (i + 1) * width]
            ref[side, :, own_place : own_place + inside, :] = own_ref[
                :, own_start : own_start + inside, :
            ]
        nearest = iota((tok_here, EDGE), 1) + (tok_here - EDGE if side == 0 else 0)
        hot = one_hot(bounds(counts_ref, block, nearest), offset, EDGE)
        near_ref[side, place : place + EDGE, :] = expand(hot, arrived[side][count:], groups)
        hot = one_hot(own_reach, own_start, inside)
        near_ref[side, own_place : own_place + inside, :] = expand(hot, held_ref[...], groups)

    reach = bounds(counts_ref, device_at, row_tokens(heads, tok_here))
    windows = []
    for side in range(2):
        for i in range(skip):
            start = i * Q_WIN + side * (atoms_here - margin)
            cut = slice(i * Q_WIN, i * Q_WIN + K_WIN)
            parts = lambda sample, side=side, cut=cut: (
                key_ref[side, sample, cut, :],
                value_ref[side, sample, cut, :],
            )
            key_at = iota((heads * Q_WIN, K_WIN), 1) + (device_at * atoms_here + start - EDGE)
            mask = (key_at >= 0) & (key_at < ends)
            windows.append((start, parts, near_ref[side, cut, :], mask))
    attend(heads, reach, windows, query_ref, gate_ref, gated_ref)
    copies = []
    for side in range(2):
        cut = slice(side * (atoms_here - margin), side * (atoms_here - margin) + margin)
        for sample in range(samples):
            out_ref[side, sample] = close(sample, cut, gated_ref, open_ref, trans_ref, w_out_ref)
        target = out_hbm.at[:, pl.ds(side * (atoms_here - margin), margin)]
        copies.append(pltpu.make_async_copy(out_ref.at[side], target, sem.at[1 + side]))
        copies[-1].start()
    for copy in copies:
        copy.wait()
    whole.wait()


def shards(
    atom_single,
    atom_cond,
    pair_cond,
    atom_counts,
    ada_attn_scale,
    ada_attn_shift,
    w_query,
    w_key,
    w_value,
    w_gate,
    w_out,
    attn_gate,
    w_pair,
    ada_trans_scale,
    ada_trans_shift,
    w_swish,
    w_linear,
    w_down,
    trans_gate,
):
    device_at = lax.axis_index("atoms")
    blocks = lax.axis_size("atoms")
    samples, atoms_here, width = atom_single.shape
    tok_here = atom_counts.shape[1]
    heads = w_pair.shape[1]
    groups = tok_here // GROUP
    pairs = lax.axis_size("pair")
    assert pair_cond.shape[0] == lax.axis_size("samp") * tok_here
    at = device_at.astype(jnp.int32).reshape(1)
    pair_at = lax.axis_index("pair").astype(jnp.int32).reshape(1)
    core_at = lax.axis_index("samp").astype(jnp.int32).reshape(1)
    in_hbm = lambda array: pltpu.with_memory_space_constraint(array, pltpu.HBM)
    in_vmem = lambda array: pltpu.with_memory_space_constraint(array, pltpu.VMEM)

    cols = pair_cond.shape[1]
    lanes = heads * GROUP
    wide = (samples, atoms_here, width)
    params = pltpu.CompilerParams(vmem_limit_bytes=VMEM_LIMIT)

    def cost(products):
        return pl.CostEstimate(flops=2 * products, bytes_accessed=4 << 20, transcendentals=0)

    sent = pltpu.VMEM((samples * EDGE + groups * EDGE, lanes), BF16)
    own = pl.pallas_call(
        pair_kernel,
        in_specs=[IN_SMEM] + [IN_HBM] * 2,
        out_specs=IN_VMEM,
        out_shape=pltpu.VMEM((groups, cols, lanes), BF16),
        scratch_shapes=[
            pltpu.VMEM((heads, width), BF16),
            pltpu.VMEM((tok_here, cols, width), BF16),
            pltpu.SemaphoreType.DMA((2 * groups,)),
            pltpu.SemaphoreType.DMA,
        ],
        compiler_params=params,
        cost_estimate=cost(tok_here * cols * width * width * 2),
    )(core_at, *map(in_hbm, (w_pair.T, pair_cond)))
    swapped = [(0, 1), (1, 0)]
    if pairs == 2:
        across = lax.ppermute(own, "pair", swapped)
    else:
        tiles = (lax.all_gather(own, ("pair", "samp")),)

    operands = (
        atom_single,
        atom_cond,
        ada_attn_scale,
        ada_attn_shift,
        ada_trans_scale,
        ada_trans_shift,
        w_key,
        w_value,
        w_query,
        w_gate,
    )
    query, keys, values, gate, cond_norm, trans_norm, near, far = pl.pallas_call(
        project_kernel,
        in_specs=[IN_SMEM] + [IN_VMEM] * len(operands),
        out_specs=[IN_VMEM] * 8,
        out_shape=[pltpu.VMEM(wide, BF16)] * 4
        + [pltpu.VMEM((atoms_here, width), BF16), pltpu.VMEM(wide, BF16), sent, sent],
        compiler_params=params,
        cost_estimate=cost(samples * atoms_here * width * width * 10),
    )(at, *map(in_vmem, operands))

    if pairs == 2:
        operands = (own, across, trans_norm)
        both, trans_norm = pl.pallas_call(
            gather_kernel,
            in_specs=[IN_VMEM] * 3,
            out_specs=[IN_VMEM] * 2,
            out_shape=[pltpu.VMEM((2, groups, cols, lanes), BF16), pltpu.VMEM(wide, BF16)],
            input_output_aliases={2: 1},
            compiler_params=params,
        )(*map(in_vmem, operands))
        tiles = (both, lax.ppermute(both, "samp", swapped))

    operands = (cond_norm, trans_norm, attn_gate, trans_gate, w_swish, w_linear, w_down)
    opened, trans = pl.pallas_call(
        transition_kernel,
        in_specs=[IN_VMEM] * len(operands),
        out_specs=[IN_VMEM] * 2,
        out_shape=[pltpu.VMEM((atoms_here, width), BF16), pltpu.VMEM(wide, BF16)],
        compiler_params=params,
        cost_estimate=cost(samples * atoms_here * width * width * 10),
    )(*map(in_vmem, operands))

    operands = (*tiles, near, far, opened)
    first = 3 + len(tiles)
    near, far, opened, held, again = pl.pallas_call(
        functools.partial(select_kernel, blocks),
        in_specs=[IN_SMEM] * 3 + [IN_VMEM] * len(operands),
        out_specs=[IN_VMEM] * 5,
        out_shape=[
            sent,
            sent,
            pltpu.VMEM((atoms_here, width), BF16),
            pltpu.VMEM((groups * cols, lanes), BF16),
            sent,
        ],
        input_output_aliases={first: 0, first + 1: 1, first + 2: 2},
        compiler_params=params,
    )(at, pair_at, core_at, *map(in_vmem, operands))

    def swap(value, start, step):
        cores = lax.axis_size("samp")
        other_of = {}
        for i in range(start, blocks - 1, step):
            other_of[i], other_of[i + 1] = i + 1, i
        sides = []
        for i in range(blocks):
            for core in range(cores):
                target = (other_of[i], core) if i in other_of else (i, (core + 1) % cores)
                sides.append((i * cores + core, target[0] * cores + target[1]))
        return lax.ppermute(value, ("atoms", "samp"), sides)

    early, second, later = swap(near, 0, 4), swap(far, 1, 2), swap(again, 2, 4)

    margin = -(-EDGE // Q_WIN) * Q_WIN
    operands = (query, keys, values, gate, opened, trans, w_out, held)
    inner = pl.pallas_call(
        functools.partial(inner_kernel, heads),
        in_specs=[IN_SMEM] + [IN_VMEM] * (1 + len(operands)),
        out_specs=IN_VMEM,
        out_shape=pltpu.VMEM((samples, atoms_here - 2 * margin, width), BF16),
        scratch_shapes=[
            pltpu.VMEM((atoms_here, heads * tok_here), BF16),
            pltpu.VMEM(wide, BF16),
        ],
        compiler_params=params,
        cost_estimate=cost(samples * atoms_here * width * width * 12),
    )(at, atom_counts, *map(in_vmem, operands))

    reach = margin - Q_WIN + K_WIN
    operands += (inner, w_key, w_value, early, second, later)
    return pl.pallas_call(
        functools.partial(outer_kernel, heads, blocks),
        in_specs=[IN_SMEM] + [IN_VMEM] * (1 + len(operands)),
        out_specs=IN_HBM,
        out_shape=pltpu.HBM(wide, BF16),
        scratch_shapes=[
            pltpu.VMEM((2, samples, reach, width), BF16),
            pltpu.VMEM((2, samples, reach, width), BF16),
            pltpu.VMEM((2, reach, heads * tok_here), BF16),
            pltpu.VMEM(wide, BF16),
            pltpu.VMEM((2, samples, margin, width), BF16),
            pltpu.SemaphoreType.DMA((3,)),
        ],
        compiler_params=params,
        cost_estimate=cost(samples * atoms_here * width * width * 4),
    )(at, atom_counts, *map(in_vmem, operands))


def solution(mesh):
    return jax.shard_map(
        shards,
        mesh=mesh,
        in_specs=(
            P(("groups", "pair", "samp"), "atoms", None),
            P(("groups", "atoms"), None),
            P(("groups", "pair"), "atoms", None),
            P("groups", None),
        )
        + (P(),) * 15,
        out_specs=P(("groups", "pair", "samp"), "atoms", None),
        check_vma=False,
    )
```

```python
import functools
import math

import jax
import jax.numpy as jnp
from jax import lax
from jax.experimental import pallas as pl
from jax.experimental.pallas import tpu as pltpu
from jax.sharding import PartitionSpec as P

Q_WIN = 32
K_WIN = 128
EDGE = 48
GROUP = 32

EPSILON = 1e-05
MASKED = -1e30
LOG2E = math.log2(math.e)
BF16 = jnp.bfloat16
F32 = jnp.float32
LAST = (((1,), (1,)), ((), ()))
VMEM_LIMIT = 32 << 20
IN_VMEM = pl.BlockSpec(memory_space=pltpu.VMEM)
IN_HBM = pl.BlockSpec(memory_space=pltpu.HBM)
IN_SMEM = pl.BlockSpec(memory_space=pltpu.SMEM)


def dot(a, b):
    return jnp.dot(a, b, preferred_element_type=F32)


def iota(shape, dim):
    return lax.broadcasted_iota(jnp.int32, shape, dim)


def twice(matrix):
    blank = jnp.zeros_like(matrix)
    return jnp.concatenate(
        [jnp.concatenate([matrix, blank], 1), jnp.concatenate([blank, matrix], 1)], 0
    )


def side_by_side(rows):
    half = rows.shape[0] // 2
    return jnp.concatenate([rows[:half], rows[half:]], 1)


def centring(width):
    same = iota((width, width), 0) == iota((width, width), 1)
    return jnp.where(same, 1.0 - 1.0 / width, -1.0 / width).astype(BF16)


def mean_square(centred):
    return jnp.mean(centred * centred, axis=-1, keepdims=True)


def layer_norm(rows):
    width = rows.shape[1]
    both = dot(side_by_side(rows), twice(centring(width)))
    centred = jnp.concatenate([both[:, :width], both[:, width:]], 0)
    return centred * lax.rsqrt(mean_square(centred) + EPSILON)


def sigmoid(values):
    return 0.5 * jnp.tanh(0.5 * values) + 0.5


def attn_norm(cond, single, ada):
    width = single.shape[-1]
    mixed = dot(cond, ada)
    return (sigmoid(mixed[:, :width])[None] * single + mixed[None, :, width:]).astype(BF16)


def pair_kernel(core_ref, w_pair_hbm, pair_hbm, tile_ref, w_pair_ref, pair_ref, pair_sem, sem):
    rows, cols, width = pair_ref.shape
    heads = w_pair_ref.shape[0]
    group = GROUP
    lanes = heads * group
    half = group // 2
    pieces = rows // half
    row_start = core_ref[0] * rows

    def pair_copy(i):
        source = pair_hbm.at[pl.ds(row_start + i * half, half)]
        return pltpu.make_async_copy(source, pair_ref.at[pl.ds(i * half, half)], pair_sem.at[i])

    w_pair_copy = pltpu.make_async_copy(w_pair_hbm, w_pair_ref, sem)
    w_pair_copy.start()
    for i in range(pieces):
        pair_copy(i).start()
    w_pair_copy.wait()
    w_pair = w_pair_ref[...].astype(F32)
    spread = jnp.concatenate(
        [jnp.broadcast_to(w_pair[h : h + 1], (group, width)) for h in range(heads)], 0
    )
    mix = twice(spread.T.astype(BF16))
    centre = twice(centring(width))
    slot = iota((cols, lanes), 1) % group

    @pl.loop(0, rows // group)
    def _(chunk):
        for part in range(2):
            pair_copy(chunk * 2 + part).wait()

        pair = pair_ref[pl.ds(chunk * group, group)].reshape(group * cols, width)
        centred = dot(side_by_side(pair), centre)
        mixed = dot(centred.astype(BF16), mix).reshape(half, cols, 2 * lanes)
        variances = [
            mean_square(centred[:, part * width : (part + 1) * width]).reshape(half, cols, 1)
            for part in range(2)
        ]
        total = jnp.zeros((cols, lanes), F32)
        spread_out = jnp.zeros((cols, lanes), F32)
        for i in range(group):
            side = slice(i // half * lanes, (i // half + 1) * lanes)
            total = jnp.where(slot == i, mixed[i % half, :, side], total)
            spread_out = jnp.where(slot == i, variances[i // half][i % half], spread_out)
        bias = (total * lax.rsqrt(spread_out + EPSILON)).astype(BF16)
        tile_ref[chunk] = bias


def beside(first, second):
    return jnp.concatenate([first[...], second[...]], 1)


def project_kernel(
    heads,
    at_ref,
    single_ref,
    cond_ref,
    ada_attn,
    ada_attn_shift,
    ada_trans,
    ada_trans_shift,
    attn_gate,
    trans_gate,
    w_key,
    w_value,
    w_query,
    w_gate,
    w_swish,
    w_linear,
    w_down,
    query_ref,
    key_ref,
    value_ref,
    gate_ref,
    open_ref,
    trans_ref,
    near_ref,
    far_ref,
    score_ref,
):
    samples, atoms_here, width = single_ref.shape
    step = math.gcd(atoms_here, 256)
    for start in range(0, atoms_here, step):
        at = slice(start, start + step)
        cond = layer_norm(cond_ref[at, :]).astype(BF16)
        single = layer_norm(single_ref[:, at, :].reshape(-1, width))
        single = single.reshape(samples, step, width)
        normed = attn_norm(cond, single, beside(ada_attn, ada_attn_shift))
        if start == 0:
            heads_of = [normed[sample, :EDGE] for sample in range(samples)]
        if start + step == atoms_here:
            tails_of = [normed[sample, step - EDGE :] for sample in range(samples)]
        normed = normed.reshape(-1, width)
        both = dot(normed, beside(w_key, w_value)).astype(BF16).reshape(samples, step, 2 * width)
        key_ref[:, at, :] = both[:, :, :width]
        value_ref[:, at, :] = both[:, :, width:]
        both = dot(normed, beside(w_query, w_gate)).reshape(samples, step, 2 * width)
        query_ref[:, at, :] = both[:, :, :width].astype(BF16)
        gate_ref[:, at, :] = sigmoid(both[:, :, width:]).astype(BF16)
        gates = dot(cond, beside(attn_gate, trans_gate))
        open_ref[at, :] = sigmoid(gates[:, :width]).astype(BF16)
        normed = attn_norm(cond, single, beside(ada_trans, ada_trans_shift)).reshape(-1, width)
        swish = dot(normed, w_swish[...])
        hidden = (swish * sigmoid(swish) * dot(normed, w_linear[...])).astype(BF16)
        down = dot(hidden, w_down[...]).reshape(samples, step, width)
        trans_ref[:, at, :] = (sigmoid(gates[:, width:])[None] * down).astype(BF16)
    even = at_ref[0] % 2 == 0
    for sample, (head, tail) in enumerate(zip(heads_of, tails_of)):
        cut = slice(sample * EDGE, (sample + 1) * EDGE)
        near_ref[cut, :] = jnp.where(even, tail, head)
        far_ref[cut, :] = jnp.where(even, head, tail)

    units = []
    for start in inner_windows(atoms_here):
        for sample in range(samples):
            keys = key_ref[sample, start - EDGE : start - EDGE + K_WIN, :]
            units.append((query_ref[sample, start : start + Q_WIN, :], keys))
    for i, score in enumerate(raw_scores(heads, in_couples(units))):
        score_ref[i] = score


def tile_of(refs, place, row_block):
    if len(refs) == 1:
        return refs[0][row_block]
    pair_at, core_at = place
    owners = 2
    mine, theirs, across, diagonal = [ref[...] for ref in refs]
    near = jnp.where(row_block % owners == core_at, mine, theirs)
    far = jnp.where(row_block % owners == core_at, across, diagonal)
    return jnp.where(row_block // owners == pair_at, near, far)


def select_kernel(blocks, at_ref, pair_ref, core_ref, *refs):
    *tile_refs, _, __, ___, near_ref, far_ref, ____, held_ref = refs
    groups, cols, lanes = tile_refs[0].shape[-3:]
    rows = groups * EDGE
    device_at, place = at_ref[0], (pair_ref[0], core_ref[0])
    for send_ref, parity in ((near_ref, 0), (far_ref, 1)):
        above = device_at % 2 == parity
        beside = jnp.where(above, device_at + 1, device_at - 1)
        tile = tile_of(tile_refs, place, jnp.clip(beside, 0, blocks - 1))
        tile = jnp.where(above, tile[:, cols - EDGE :], tile[:, :EDGE])
        send_ref[send_ref.shape[0] - rows :, :] = tile.reshape(rows, lanes)
    held_ref[...] = tile_of(tile_refs, place, device_at).reshape(groups * cols, lanes)


def bounds(counts_ref, block, token):
    tok_here = counts_ref.shape[1]
    counts = counts_ref[pl.ds(block, 1), :].astype(F32).astype(BF16)
    counts = jnp.broadcast_to(counts, (8, tok_here))
    before = iota((tok_here, token.shape[1]), 0)
    first = dot(counts, (before < token).astype(BF16))[:1]
    last = dot(counts, (before <= token).astype(BF16))[:1]
    return first.astype(jnp.int32), last.astype(jnp.int32)


def one_hot(reach, offset, count):
    first, last = reach
    position = iota((count, first.shape[1]), 0) + offset
    return ((first <= position) & (position < last)).astype(F32).astype(BF16)


def expand(hot, tile, groups):
    tile = tile.reshape(groups, -1, tile.shape[-1])
    tile = jnp.concatenate([tile[part] for part in range(groups)], 1)
    return dot(hot, tile).astype(BF16)


def raw_scores(heads, couples):
    width = couples[0][0][0].shape[1]
    rows = heads * Q_WIN
    own_head = iota((rows, width), 1) // (width // heads) == iota((rows, width), 0) // Q_WIN
    own_head = own_head.astype(F32).astype(BF16)
    scaling = LOG2E / math.sqrt(width // heads)
    scores = []
    for couple in couples:
        queries = [jnp.concatenate([query] * heads, 0) * own_head for query, _ in couple]
        keys = [key for _, key in couple]
        if len(couple) == 2:
            blank = jnp.zeros_like(keys[0])
            keys = [jnp.concatenate([keys[0], blank], 1), jnp.concatenate([blank, keys[1]], 1)]
        product = lax.dot_general(
            jnp.concatenate(queries, 1),
            jnp.concatenate(keys, 0),
            LAST,
            preferred_element_type=F32,
        )
        for j in range(len(couple)):
            scores.append(product[:, j * K_WIN : (j + 1) * K_WIN] * scaling)
    return scores


def in_couples(items):
    return [items[i : i + 2] for i in range(0, len(items), 2)]


def inner_windows(atoms_here):
    skip = -(-EDGE // Q_WIN)
    return [window * Q_WIN for window in range(skip, atoms_here // Q_WIN - skip)]


def attend(heads, reach, windows, scores, gate_ref, gated_ref):
    samples, _, width = gate_ref.shape
    head_dim = width // heads
    lanes = reach[0].shape[1]
    rows = heads * Q_WIN
    lane_head = iota((rows, lanes), 1) // GROUP % heads
    row_head = iota((rows, lanes), 0) // Q_WIN
    same_head = (lane_head == row_head).astype(F32).astype(BF16)
    channel_head = iota((Q_WIN, 2 * width), 1) % width // head_dim
    ones = jnp.ones((K_WIN, width), BF16)

    biases = []
    for start, _, near, mask in windows:
        pick = jnp.concatenate([one_hot(reach, start, Q_WIN)] * heads, 0) * same_head
        bias = lax.dot_general(pick, near, LAST, preferred_element_type=F32) * LOG2E
        biases.append(bias if mask is None else jnp.where(mask, bias, MASKED))
    units = [(sample, i) for i in range(len(windows)) for sample in range(samples)]
    scores = [score + biases[i] for score, (_, i) in zip(scores, units)]
    tops = [jnp.max(score, axis=-1, keepdims=True) for score in scores]
    raised = [jnp.exp2(score - top).astype(BF16) for score, top in zip(scores, tops)]
    for (sample, i), weight in zip(units, raised):
        mixed = dot(weight, jnp.concatenate([windows[i][1](sample), ones], 1))
        picked = mixed[:Q_WIN]
        for head in range(1, heads):
            picked = jnp.where(
                channel_head == head, mixed[head * Q_WIN : (head + 1) * Q_WIN], picked
            )
        attended = picked[:, :width] * pl.reciprocal(picked[:, width:], approx=True)
        at = pl.ds(windows[i][0], Q_WIN)
        gate = gate_ref[sample, at, :].astype(F32)
        gated_ref[sample, at, :] = (gate * attended).astype(BF16)


def close(sample, cut, gated_ref, open_ref, trans_ref, w_out_ref):
    mixed = dot(gated_ref[sample, cut, :], w_out_ref[...])
    opened, trans = open_ref[cut, :].astype(F32), trans_ref[sample, cut, :].astype(F32)
    return (opened * mixed + trans).astype(BF16)


def row_tokens(heads, tok_here):
    lane = iota((tok_here, heads * tok_here), 1)
    return lane // (heads * GROUP) * GROUP + lane % GROUP


def inner_kernel(
    heads,
    at_ref,
    counts_ref,
    value_ref,
    gate_ref,
    open_ref,
    trans_ref,
    w_out_ref,
    held_ref,
    score_ref,
    out_ref,
    near_ref,
    gated_ref,
):
    samples, atoms_here, width = value_ref.shape
    tok_here = counts_ref.shape[1]
    device_at = at_ref[0]
    hot = one_hot(
        bounds(counts_ref, device_at, iota((tok_here, tok_here), 1)), 0, atoms_here
    )
    near_ref[...] = expand(hot, held_ref[...], tok_here // GROUP)
    reach = bounds(counts_ref, device_at, row_tokens(heads, tok_here))
    starts = inner_windows(atoms_here)
    windows = []
    for start in starts:
        cut = slice(start - EDGE, start - EDGE + K_WIN)
        parts = lambda sample, cut=cut: value_ref[sample, cut, :]
        windows.append((start, parts, near_ref[cut, :], None))
    scores = [score_ref[i] for i in range(score_ref.shape[0])]
    attend(heads, reach, windows, scores, gate_ref, gated_ref)

    cut = slice(starts[0], starts[-1] + Q_WIN)
    for sample in range(samples):
        out_ref[sample] = close(sample, cut, gated_ref, open_ref, trans_ref, w_out_ref)


def outer_kernel(
    heads,
    blocks,
    at_ref,
    counts_ref,
    query_ref,
    own_key_ref,
    own_value_ref,
    gate_ref,
    open_ref,
    trans_ref,
    w_out_ref,
    held_ref,
    inner_ref,
    w_key,
    w_value,
    first_ref,
    second_ref,
    out_hbm,
    key_ref,
    value_ref,
    near_ref,
    gated_ref,
    out_ref,
    sem,
):
    samples, atoms_here, width = query_ref.shape
    tok_here = counts_ref.shape[1]
    device_at = at_ref[0]
    ends = atoms_here * blocks
    skip = -(-EDGE // Q_WIN)
    margin = skip * Q_WIN
    reach_keys = key_ref.shape[2]
    inside = reach_keys - EDGE

    whole = pltpu.make_async_copy(
        inner_ref, out_hbm.at[:, pl.ds(margin, atoms_here - 2 * margin)], sem.at[0]
    )
    whole.start()

    even = device_at % 2 == 0
    first, second = first_ref[...], second_ref[...]
    arrived = (jnp.where(even, second, first), jnp.where(even, first, second))
    count = samples * EDGE
    edges = jnp.concatenate([rows[:count] for rows in arrived], 0)
    edges = dot(edges, beside(w_key, w_value)).astype(BF16).reshape(2, samples, EDGE, 2 * width)
    groups = tok_here // GROUP
    token = iota((tok_here, tok_here), 1)
    own_reach = bounds(counts_ref, device_at, token)
    sides = (
        (jnp.maximum(device_at - 1, 0), atoms_here - EDGE, 0, EDGE, 0),
        (jnp.minimum(device_at + 1, blocks - 1), 0, inside, 0, atoms_here - inside),
    )
    for side, (block, offset, place, own_place, own_start) in enumerate(sides):
        for i, (ref, own_ref) in enumerate(((key_ref, own_key_ref), (value_ref, own_value_ref))):
            ref[side, :, place : place + EDGE, :] = edges[side, :, :, i * width : (i + 1) * width]
            ref[side, :, own_place : own_place + inside, :] = own_ref[
                :, own_start : own_start + inside, :
            ]
        nearest = iota((tok_here, EDGE), 1) + (tok_here - EDGE if side == 0 else 0)
        hot = one_hot(bounds(counts_ref, block, nearest), offset, EDGE)
        near_ref[side, place : place + EDGE, :] = expand(hot, arrived[side][count:], groups)
        hot = one_hot(own_reach, own_start, inside)
        near_ref[side, own_place : own_place + inside, :] = expand(hot, held_ref[...], groups)

    reach = bounds(counts_ref, device_at, row_tokens(heads, tok_here))
    windows, units = [], []
    for side in range(2):
        for i in range(skip):
            start = i * Q_WIN + side * (atoms_here - margin)
            cut = slice(i * Q_WIN, i * Q_WIN + K_WIN)
            parts = lambda sample, side=side, cut=cut: value_ref[side, sample, cut, :]
            for sample in range(samples):
                query = query_ref[sample, start : start + Q_WIN, :]
                units.append((query, key_ref[side, sample, cut, :]))
            key_at = iota((heads * Q_WIN, K_WIN), 1) + (device_at * atoms_here + start - EDGE)
            mask = (key_at >= 0) & (key_at < ends)
            windows.append((start, parts, near_ref[side, cut, :], mask))
    scores = raw_scores(heads, in_couples(units))
    attend(heads, reach, windows, scores, gate_ref, gated_ref)
    copies = []
    for side in range(2):
        cut = slice(side * (atoms_here - margin), side * (atoms_here - margin) + margin)
        for sample in range(samples):
            out_ref[side, sample] = close(sample, cut, gated_ref, open_ref, trans_ref, w_out_ref)
        target = out_hbm.at[:, pl.ds(side * (atoms_here - margin), margin)]
        copies.append(pltpu.make_async_copy(out_ref.at[side], target, sem.at[1 + side]))
        copies[-1].start()
    for copy in copies:
        copy.wait()
    whole.wait()


def shards(
    atom_single,
    atom_cond,
    pair_cond,
    atom_counts,
    ada_attn_scale,
    ada_attn_shift,
    w_query,
    w_key,
    w_value,
    w_gate,
    w_out,
    attn_gate,
    w_pair,
    ada_trans_scale,
    ada_trans_shift,
    w_swish,
    w_linear,
    w_down,
    trans_gate,
):
    device_at = lax.axis_index("atoms")
    blocks = lax.axis_size("atoms")
    samples, atoms_here, width = atom_single.shape
    tok_here = atom_counts.shape[1]
    heads = w_pair.shape[1]
    groups = tok_here // GROUP
    pairs = lax.axis_size("pair")
    assert pair_cond.shape[0] == lax.axis_size("samp") * tok_here
    at = device_at.astype(jnp.int32).reshape(1)
    pair_at = lax.axis_index("pair").astype(jnp.int32).reshape(1)
    core_at = lax.axis_index("samp").astype(jnp.int32).reshape(1)
    in_hbm = lambda array: pltpu.with_memory_space_constraint(array, pltpu.HBM)
    in_vmem = lambda array: pltpu.with_memory_space_constraint(array, pltpu.VMEM)

    cols = pair_cond.shape[1]
    lanes = heads * GROUP
    wide = (samples, atoms_here, width)
    params = pltpu.CompilerParams(vmem_limit_bytes=VMEM_LIMIT)

    def cost(products):
        return pl.CostEstimate(flops=2 * products, bytes_accessed=4 << 20, transcendentals=0)

    sent = pltpu.VMEM((samples * EDGE + groups * EDGE, lanes), BF16)
    own = pl.pallas_call(
        pair_kernel,
        in_specs=[IN_SMEM] + [IN_HBM] * 2,
        out_specs=IN_VMEM,
        out_shape=pltpu.VMEM((groups, cols, lanes), BF16),
        scratch_shapes=[
            pltpu.VMEM((heads, width), BF16),
            pltpu.VMEM((tok_here, cols, width), BF16),
            pltpu.SemaphoreType.DMA((2 * groups,)),
            pltpu.SemaphoreType.DMA,
        ],
        compiler_params=params,
        cost_estimate=cost(tok_here * cols * width * width * 2),
    )(core_at, *map(in_hbm, (w_pair.T, pair_cond)))
    if pairs == 2:
        swapped = [(0, 1), (1, 0)]
        across = lax.ppermute(own, "pair", swapped)
        diagonal = lax.ppermute(own, ("pair", "samp"), [(0, 3), (1, 2), (2, 1), (3, 0)])
        tiles = (own, lax.ppermute(own, "samp", swapped), across, diagonal)
    else:
        tiles = (lax.all_gather(own, ("pair", "samp")),)

    operands = (
        atom_single,
        atom_cond,
        ada_attn_scale,
        ada_attn_shift,
        ada_trans_scale,
        ada_trans_shift,
        attn_gate,
        trans_gate,
        w_key,
        w_value,
        w_query,
        w_gate,
        w_swish,
        w_linear,
        w_down,
    )
    units = samples * len(inner_windows(atoms_here))
    query, keys, values, gate, opened, trans, near, far, scores = pl.pallas_call(
        functools.partial(project_kernel, heads),
        in_specs=[IN_SMEM] + [IN_VMEM] * len(operands),
        out_specs=[IN_VMEM] * 9,
        out_shape=[pltpu.VMEM(wide, BF16)] * 4
        + [pltpu.VMEM((atoms_here, width), BF16), pltpu.VMEM(wide, BF16), sent, sent]
        + [pltpu.VMEM((units, heads * Q_WIN, K_WIN), F32)],
        compiler_params=params,
        cost_estimate=cost(samples * atoms_here * width * width * 20),
    )(at, *map(in_vmem, operands))

    operands = (*tiles, near, far, opened)
    first = 3 + len(tiles)
    near, far, opened, held = pl.pallas_call(
        functools.partial(select_kernel, blocks),
        in_specs=[IN_SMEM] * 3 + [IN_VMEM] * len(operands),
        out_specs=[IN_VMEM] * 4,
        out_shape=[
            sent,
            sent,
            pltpu.VMEM((atoms_here, width), BF16),
            pltpu.VMEM((groups * cols, lanes), BF16),
        ],
        input_output_aliases={first: 0, first + 1: 1, first + 2: 2},
        compiler_params=params,
    )(at, pair_at, core_at, *map(in_vmem, operands))

    def swap(value, start):
        cores = lax.axis_size("samp")
        other_of = {}
        for i in range(start, blocks - 1, 2):
            other_of[i], other_of[i + 1] = i + 1, i
        sides = []
        for i in range(blocks):
            for core in range(cores):
                target = (other_of[i], core) if i in other_of else (i, (core + 1) % cores)
                sides.append((i * cores + core, target[0] * cores + target[1]))
        return lax.ppermute(value, ("atoms", "samp"), sides)

    first, second = swap(near, 0), swap(far, 1)

    margin = -(-EDGE // Q_WIN) * Q_WIN
    operands = (values, gate, opened, trans, w_out, held, scores)
    inner = pl.pallas_call(
        functools.partial(inner_kernel, heads),
        in_specs=[IN_SMEM] + [IN_VMEM] * (1 + len(operands)),
        out_specs=IN_VMEM,
        out_shape=pltpu.VMEM((samples, atoms_here - 2 * margin, width), BF16),
        scratch_shapes=[
            pltpu.VMEM((atoms_here, heads * tok_here), BF16),
            pltpu.VMEM(wide, BF16),
        ],
        compiler_params=params,
        cost_estimate=cost(samples * atoms_here * width * width * 12),
    )(at, atom_counts, *map(in_vmem, operands))

    reach = margin - Q_WIN + K_WIN
    operands = (query, keys, values, gate, opened, trans, w_out, held)
    operands += (inner, w_key, w_value, first, second)
    return pl.pallas_call(
        functools.partial(outer_kernel, heads, blocks),
        in_specs=[IN_SMEM] + [IN_VMEM] * (1 + len(operands)),
        out_specs=IN_HBM,
        out_shape=pltpu.HBM(wide, BF16),
        scratch_shapes=[
            pltpu.VMEM((2, samples, reach, width), BF16),
            pltpu.VMEM((2, samples, reach, width), BF16),
            pltpu.VMEM((2, reach, heads * tok_here), BF16),
            pltpu.VMEM(wide, BF16),
            pltpu.VMEM((2, samples, margin, width), BF16),
            pltpu.SemaphoreType.DMA((3,)),
        ],
        compiler_params=params,
        cost_estimate=cost(samples * atoms_here * width * width * 4),
    )(at, atom_counts, *map(in_vmem, operands))


def solution(mesh):
    return jax.shard_map(
        shards,
        mesh=mesh,
        in_specs=(
            P(("groups", "pair", "samp"), "atoms", None),
            P(("groups", "atoms"), None),
            P(("groups", "pair"), "atoms", None),
            P("groups", None),
        )
        + (P(),) * 15,
        out_specs=P(("groups", "pair", "samp"), "atoms", None),
        check_vma=False,
    )
```

```python
import functools
import math

import jax
import jax.numpy as jnp
from jax import lax
from jax.experimental import pallas as pl
from jax.experimental.pallas import tpu as pltpu
from jax.sharding import PartitionSpec as P

Q_WIN = 32
K_WIN = 128
EDGE = 48
GROUP = 32

EPSILON = 1e-05
MASKED = -1e30
LOG2E = math.log2(math.e)
BF16 = jnp.bfloat16
F32 = jnp.float32
LAST = (((1,), (1,)), ((), ()))
VMEM_LIMIT = 32 << 20
IN_VMEM = pl.BlockSpec(memory_space=pltpu.VMEM)
IN_HBM = pl.BlockSpec(memory_space=pltpu.HBM)
IN_SMEM = pl.BlockSpec(memory_space=pltpu.SMEM)


def dot(a, b):
    return jnp.dot(a, b, preferred_element_type=F32)


def iota(shape, dim):
    return lax.broadcasted_iota(jnp.int32, shape, dim)


def twice(matrix):
    blank = jnp.zeros_like(matrix)
    return jnp.concatenate(
        [jnp.concatenate([matrix, blank], 1), jnp.concatenate([blank, matrix], 1)], 0
    )


def side_by_side(rows):
    half = rows.shape[0] // 2
    return jnp.concatenate([rows[:half], rows[half:]], 1)


def centring(width):
    same = iota((width, width), 0) == iota((width, width), 1)
    return jnp.where(same, 1.0 - 1.0 / width, -1.0 / width).astype(BF16)


def mean_square(centred):
    return jnp.mean(centred * centred, axis=-1, keepdims=True)


def layer_norm(rows):
    width = rows.shape[1]
    both = dot(side_by_side(rows), twice(centring(width)))
    centred = jnp.concatenate([both[:, :width], both[:, width:]], 0)
    return centred * lax.rsqrt(mean_square(centred) + EPSILON)


def sigmoid(values):
    return 0.5 * jnp.tanh(0.5 * values) + 0.5


def attn_norm(cond, single, ada):
    width = single.shape[-1]
    mixed = dot(cond, ada)
    return (sigmoid(mixed[:, :width])[None] * single + mixed[None, :, width:]).astype(BF16)


def pair_kernel(core_ref, w_pair_hbm, pair_hbm, tile_ref, w_pair_ref, pair_ref, pair_sem, sem):
    rows, cols, width = pair_ref.shape
    heads = w_pair_ref.shape[0]
    group = GROUP
    lanes = heads * group
    half = group // 2
    pieces = rows // half
    row_start = core_ref[0] * rows

    def pair_copy(i):
        source = pair_hbm.at[pl.ds(row_start + i * half, half)]
        return pltpu.make_async_copy(source, pair_ref.at[pl.ds(i * half, half)], pair_sem.at[i])

    w_pair_copy = pltpu.make_async_copy(w_pair_hbm, w_pair_ref, sem)
    w_pair_copy.start()
    for i in range(pieces):
        pair_copy(i).start()
    w_pair_copy.wait()
    w_pair = w_pair_ref[...].astype(F32)
    spread = jnp.concatenate(
        [jnp.broadcast_to(w_pair[h : h + 1], (group, width)) for h in range(heads)], 0
    )
    mix = twice(spread.T.astype(BF16))
    centre = twice(centring(width))
    slot = iota((cols, lanes), 1) % group

    chunks = []
    for chunk in range(rows // group):
        for part in range(2):
            pair_copy(chunk * 2 + part).wait()
        pair = pair_ref[chunk * group : (chunk + 1) * group].reshape(group * cols, width)
        chunks.append(dot(side_by_side(pair), centre))
    mixes = [dot(centred.astype(BF16), mix).reshape(half, cols, 2 * lanes) for centred in chunks]
    for chunk, (centred, mixed) in enumerate(zip(chunks, mixes)):
        variances = [
            mean_square(centred[:, part * width : (part + 1) * width]).reshape(half, cols, 1)
            for part in range(2)
        ]
        total = jnp.zeros((cols, lanes), F32)
        spread_out = jnp.zeros((cols, lanes), F32)
        for i in range(group):
            side = slice(i // half * lanes, (i // half + 1) * lanes)
            total = jnp.where(slot == i, mixed[i % half, :, side], total)
            spread_out = jnp.where(slot == i, variances[i // half][i % half], spread_out)
        tile_ref[chunk] = (total * lax.rsqrt(spread_out + EPSILON)).astype(BF16)


def beside(first, second):
    return jnp.concatenate([first[...], second[...]], 1)


def project_kernel(
    at_ref,
    single_ref,
    cond_ref,
    ada_attn,
    ada_attn_shift,
    ada_trans,
    ada_trans_shift,
    attn_gate,
    trans_gate,
    w_key,
    w_value,
    w_query,
    w_gate,
    w_swish,
    w_linear,
    w_down,
    query_ref,
    key_ref,
    value_ref,
    gate_ref,
    open_ref,
    trans_ref,
    near_ref,
    far_ref,
):
    samples, atoms_here, width = single_ref.shape
    step = math.gcd(atoms_here, 512)
    for start in range(0, atoms_here, step):
        at = slice(start, start + step)
        cond = layer_norm(cond_ref[at, :]).astype(BF16)
        single = layer_norm(single_ref[:, at, :].reshape(-1, width))
        single = single.reshape(samples, step, width)
        normed = attn_norm(cond, single, beside(ada_attn, ada_attn_shift))
        if start == 0:
            heads_of = [normed[sample, :EDGE] for sample in range(samples)]
        if start + step == atoms_here:
            tails_of = [normed[sample, step - EDGE :] for sample in range(samples)]
        normed = normed.reshape(-1, width)
        both = dot(normed, beside(w_key, w_value)).astype(BF16).reshape(samples, step, 2 * width)
        key_ref[:, at, :] = both[:, :, :width]
        value_ref[:, at, :] = both[:, :, width:]
        both = dot(normed, beside(w_query, w_gate)).reshape(samples, step, 2 * width)
        query_ref[:, at, :] = both[:, :, :width].astype(BF16)
        gate_ref[:, at, :] = sigmoid(both[:, :, width:]).astype(BF16)
        gates = dot(cond, beside(attn_gate, trans_gate))
        open_ref[at, :] = sigmoid(gates[:, :width]).astype(BF16)
        normed = attn_norm(cond, single, beside(ada_trans, ada_trans_shift)).reshape(-1, width)
        swish = dot(normed, w_swish[...])
        hidden = (swish * sigmoid(swish) * dot(normed, w_linear[...])).astype(BF16)
        down = dot(hidden, w_down[...]).reshape(samples, step, width)
        trans_ref[:, at, :] = (sigmoid(gates[:, width:])[None] * down).astype(BF16)
    even = at_ref[0] % 2 == 0
    for sample, (head, tail) in enumerate(zip(heads_of, tails_of)):
        cut = slice(sample * EDGE, (sample + 1) * EDGE)
        near_ref[cut, :] = jnp.where(even, tail, head)
        far_ref[cut, :] = jnp.where(even, head, tail)


def tile_of(refs, place, row_block):
    if len(refs) == 1:
        return refs[0][row_block]
    pair_at, core_at = place
    owners = 2
    mine, theirs, across, diagonal = [ref[...] for ref in refs]
    near = jnp.where(row_block % owners == core_at, mine, theirs)
    far = jnp.where(row_block % owners == core_at, across, diagonal)
    return jnp.where(row_block // owners == pair_at, near, far)


def select_kernel(blocks, at_ref, pair_ref, core_ref, *refs):
    *tile_refs, _, __, ___, near_ref, far_ref, ____, held_ref = refs
    groups, cols, lanes = tile_refs[0].shape[-3:]
    rows = groups * EDGE
    device_at, place = at_ref[0], (pair_ref[0], core_ref[0])
    for send_ref, parity in ((near_ref, 0), (far_ref, 1)):
        above = device_at % 2 == parity
        beside = jnp.where(above, device_at + 1, device_at - 1)
        tile = tile_of(tile_refs, place, jnp.clip(beside, 0, blocks - 1))
        tile = jnp.where(above, tile[:, cols - EDGE :], tile[:, :EDGE])
        send_ref[send_ref.shape[0] - rows :, :] = tile.reshape(rows, lanes)
    held_ref[...] = tile_of(tile_refs, place, device_at).reshape(groups * cols, lanes)


def bounds(counts_ref, block, token):
    tok_here = counts_ref.shape[1]
    counts = counts_ref[pl.ds(block, 1), :].astype(F32).astype(BF16)
    counts = jnp.broadcast_to(counts, (8, tok_here))
    before = iota((tok_here, token.shape[1]), 0)
    first = dot(counts, (before < token).astype(BF16))[:1]
    last = dot(counts, (before <= token).astype(BF16))[:1]
    return first.astype(jnp.int32), last.astype(jnp.int32)


def one_hot(reach, offset, count):
    first, last = reach
    position = iota((count, first.shape[1]), 0) + offset
    return ((first <= position) & (position < last)).astype(F32).astype(BF16)


def expand(hot, tile, groups):
    tile = tile.reshape(groups, -1, tile.shape[-1])
    tile = jnp.concatenate([tile[part] for part in range(groups)], 1)
    return dot(hot, tile).astype(BF16)


def attend(heads, reach, windows, query_ref, gate_ref, gated_ref):
    samples, _, width = query_ref.shape
    head_dim = width // heads
    lanes = reach[0].shape[1]
    rows = heads * Q_WIN
    lane_head = iota((rows, lanes), 1) // GROUP % heads
    row_head = iota((rows, lanes), 0) // Q_WIN
    same_head = (lane_head == row_head).astype(F32).astype(BF16)
    own_head = iota((rows, width), 1) // head_dim == iota((rows, width), 0) // Q_WIN
    own_head = own_head.astype(F32).astype(BF16)
    channel_head = iota((Q_WIN, 2 * width), 1) % width // head_dim
    ones = jnp.ones((K_WIN, width), BF16)
    scaling = LOG2E / math.sqrt(head_dim)

    biases = []
    for start, _, near, mask in windows:
        pick = jnp.concatenate([one_hot(reach, start, Q_WIN)] * heads, 0) * same_head
        bias = lax.dot_general(pick, near, LAST, preferred_element_type=F32) * LOG2E
        biases.append(bias if mask is None else jnp.where(mask, bias, MASKED))
    units = [(sample, i) for i in range(len(windows)) for sample in range(samples)]
    scores = []
    for first in range(0, len(units), 2):
        couple = units[first : first + 2]
        queries, keys = [], []
        for sample, i in couple:
            query = query_ref[sample, pl.ds(windows[i][0], Q_WIN), :]
            queries.append(jnp.concatenate([query] * heads, 0) * own_head)
            keys.append(windows[i][1](sample)[0])
        if len(couple) == 2:
            blank = jnp.zeros_like(keys[0])
            keys = [jnp.concatenate([keys[0], blank], 1), jnp.concatenate([blank, keys[1]], 1)]
        product = lax.dot_general(
            jnp.concatenate(queries, 1),
            jnp.concatenate(keys, 0),
            LAST,
            preferred_element_type=F32,
        )
        for j, (_, i) in enumerate(couple):
            scores.append(product[:, j * K_WIN : (j + 1) * K_WIN] * scaling + biases[i])
    tops = [jnp.max(score, axis=-1, keepdims=True) for score in scores]
    raised = [jnp.exp2(score - top).astype(BF16) for score, top in zip(scores, tops)]
    for (sample, i), weight in zip(units, raised):
        values = windows[i][1](sample)[1]
        mixed = dot(weight, jnp.concatenate([values, ones], 1))
        picked = mixed[:Q_WIN]
        for head in range(1, heads):
            picked = jnp.where(
                channel_head == head, mixed[head * Q_WIN : (head + 1) * Q_WIN], picked
            )
        attended = picked[:, :width] * pl.reciprocal(picked[:, width:], approx=True)
        at = pl.ds(windows[i][0], Q_WIN)
        gate = gate_ref[sample, at, :].astype(F32)
        gated_ref[sample, at, :] = (gate * attended).astype(BF16)


def close(sample, cut, gated_ref, open_ref, trans_ref, w_out_ref):
    mixed = dot(gated_ref[sample, cut, :], w_out_ref[...])
    opened, trans = open_ref[cut, :].astype(F32), trans_ref[sample, cut, :].astype(F32)
    return (opened * mixed + trans).astype(BF16)


def row_tokens(heads, tok_here):
    lane = iota((tok_here, heads * tok_here), 1)
    return lane // (heads * GROUP) * GROUP + lane % GROUP


def inner_kernel(
    heads,
    at_ref,
    counts_ref,
    query_ref,
    key_ref,
    value_ref,
    gate_ref,
    open_ref,
    trans_ref,
    w_out_ref,
    held_ref,
    out_ref,
    near_ref,
    gated_ref,
):
    samples, atoms_here, width = query_ref.shape
    tok_here = counts_ref.shape[1]
    device_at = at_ref[0]
    hot = one_hot(
        bounds(counts_ref, device_at, iota((tok_here, tok_here), 1)), 0, atoms_here
    )
    near_ref[...] = expand(hot, held_ref[...], tok_here // GROUP)
    reach = bounds(counts_ref, device_at, row_tokens(heads, tok_here))
    skip = -(-EDGE // Q_WIN)
    inner = atoms_here // Q_WIN - 2 * skip
    batch = math.gcd(inner, 12)

    @pl.loop(0, inner // batch)
    def _(turn):
        windows = []
        for i in range(batch):
            start = pl.multiple_of((turn * batch + i + skip) * Q_WIN, Q_WIN)
            cut = pl.ds(pl.multiple_of(start - EDGE, 16), K_WIN)
            parts = lambda sample, cut=cut: (key_ref[sample, cut, :], value_ref[sample, cut, :])
            windows.append((start, parts, near_ref[cut, :], None))
        attend(heads, reach, windows, query_ref, gate_ref, gated_ref)

    cut = slice(skip * Q_WIN, atoms_here - skip * Q_WIN)
    for sample in range(samples):
        out_ref[sample] = close(sample, cut, gated_ref, open_ref, trans_ref, w_out_ref)


def outer_kernel(
    heads,
    blocks,
    at_ref,
    counts_ref,
    query_ref,
    own_key_ref,
    own_value_ref,
    gate_ref,
    open_ref,
    trans_ref,
    w_out_ref,
    held_ref,
    inner_ref,
    w_key,
    w_value,
    first_ref,
    second_ref,
    out_hbm,
    key_ref,
    value_ref,
    near_ref,
    gated_ref,
    out_ref,
    sem,
):
    samples, atoms_here, width = query_ref.shape
    tok_here = counts_ref.shape[1]
    device_at = at_ref[0]
    ends = atoms_here * blocks
    skip = -(-EDGE // Q_WIN)
    margin = skip * Q_WIN
    reach_keys = key_ref.shape[2]
    inside = reach_keys - EDGE

    whole = pltpu.make_async_copy(
        inner_ref, out_hbm.at[:, pl.ds(margin, atoms_here - 2 * margin)], sem.at[0]
    )
    whole.start()

    even = device_at % 2 == 0
    first, second = first_ref[...], second_ref[...]
    arrived = (jnp.where(even, second, first), jnp.where(even, first, second))
    count = samples * EDGE
    edges = jnp.concatenate([rows[:count] for rows in arrived], 0)
    edges = dot(edges, beside(w_key, w_value)).astype(BF16).reshape(2, samples, EDGE, 2 * width)
    groups = tok_here // GROUP
    token = iota((tok_here, tok_here), 1)
    own_reach = bounds(counts_ref, device_at, token)
    sides = (
        (jnp.maximum(device_at - 1, 0), atoms_here - EDGE, 0, EDGE, 0),
        (jnp.minimum(device_at + 1, blocks - 1), 0, inside, 0, atoms_here - inside),
    )
    for side, (block, offset, place, own_place, own_start) in enumerate(sides):
        for i, (ref, own_ref) in enumerate(((key_ref, own_key_ref), (value_ref, own_value_ref))):
            ref[side, :, place : place + EDGE, :] = edges[side, :, :, i * width : (i + 1) * width]
            ref[side, :, own_place : own_place + inside, :] = own_ref[
                :, own_start : own_start + inside, :
            ]
        nearest = iota((tok_here, EDGE), 1) + (tok_here - EDGE if side == 0 else 0)
        hot = one_hot(bounds(counts_ref, block, nearest), offset, EDGE)
        near_ref[side, place : place + EDGE, :] = expand(hot, arrived[side][count:], groups)
        hot = one_hot(own_reach, own_start, inside)
        near_ref[side, own_place : own_place + inside, :] = expand(hot, held_ref[...], groups)

    reach = bounds(counts_ref, device_at, row_tokens(heads, tok_here))
    windows = []
    for side in range(2):
        for i in range(skip):
            start = i * Q_WIN + side * (atoms_here - margin)
            cut = slice(i * Q_WIN, i * Q_WIN + K_WIN)
            parts = lambda sample, side=side, cut=cut: (
                key_ref[side, sample, cut, :],
                value_ref[side, sample, cut, :],
            )
            key_at = iota((heads * Q_WIN, K_WIN), 1) + (device_at * atoms_here + start - EDGE)
            mask = (key_at >= 0) & (key_at < ends)
            windows.append((start, parts, near_ref[side, cut, :], mask))
    attend(heads, reach, windows, query_ref, gate_ref, gated_ref)
    copies = []
    for side in range(2):
        cut = slice(side * (atoms_here - margin), side * (atoms_here - margin) + margin)
        for sample in range(samples):
            out_ref[side, sample] = close(sample, cut, gated_ref, open_ref, trans_ref, w_out_ref)
        target = out_hbm.at[:, pl.ds(side * (atoms_here - margin), margin)]
        copies.append(pltpu.make_async_copy(out_ref.at[side], target, sem.at[1 + side]))
        copies[-1].start()
    for copy in copies:
        copy.wait()
    whole.wait()


def shards(
    atom_single,
    atom_cond,
    pair_cond,
    atom_counts,
    ada_attn_scale,
    ada_attn_shift,
    w_query,
    w_key,
    w_value,
    w_gate,
    w_out,
    attn_gate,
    w_pair,
    ada_trans_scale,
    ada_trans_shift,
    w_swish,
    w_linear,
    w_down,
    trans_gate,
):
    device_at = lax.axis_index("atoms")
    blocks = lax.axis_size("atoms")
    samples, atoms_here, width = atom_single.shape
    tok_here = atom_counts.shape[1]
    heads = w_pair.shape[1]
    groups = tok_here // GROUP
    pairs = lax.axis_size("pair")
    assert pair_cond.shape[0] == lax.axis_size("samp") * tok_here
    at = device_at.astype(jnp.int32).reshape(1)
    pair_at = lax.axis_index("pair").astype(jnp.int32).reshape(1)
    core_at = lax.axis_index("samp").astype(jnp.int32).reshape(1)
    in_hbm = lambda array: pltpu.with_memory_space_constraint(array, pltpu.HBM)
    in_vmem = lambda array: pltpu.with_memory_space_constraint(array, pltpu.VMEM)

    cols = pair_cond.shape[1]
    lanes = heads * GROUP
    wide = (samples, atoms_here, width)
    params = pltpu.CompilerParams(vmem_limit_bytes=VMEM_LIMIT)

    def cost(products):
        return pl.CostEstimate(flops=2 * products, bytes_accessed=4 << 20, transcendentals=0)

    sent = pltpu.VMEM((samples * EDGE + groups * EDGE, lanes), BF16)
    own = pl.pallas_call(
        pair_kernel,
        in_specs=[IN_SMEM] + [IN_HBM] * 2,
        out_specs=IN_VMEM,
        out_shape=pltpu.VMEM((groups, cols, lanes), BF16),
        scratch_shapes=[
            pltpu.VMEM((heads, width), BF16),
            pltpu.VMEM((tok_here, cols, width), BF16),
            pltpu.SemaphoreType.DMA((2 * groups,)),
            pltpu.SemaphoreType.DMA,
        ],
        compiler_params=params,
        cost_estimate=cost(tok_here * cols * width * width * 2),
    )(core_at, *map(in_hbm, (w_pair.T, pair_cond)))
    if pairs == 2:
        swapped = [(0, 1), (1, 0)]
        across = lax.ppermute(own, "pair", swapped)
        diagonal = lax.ppermute(own, ("pair", "samp"), [(0, 3), (1, 2), (2, 1), (3, 0)])
        tiles = (own, lax.ppermute(own, "samp", swapped), across, diagonal)
    else:
        tiles = (lax.all_gather(own, ("pair", "samp")),)

    operands = (
        atom_single,
        atom_cond,
        ada_attn_scale,
        ada_attn_shift,
        ada_trans_scale,
        ada_trans_shift,
        attn_gate,
        trans_gate,
        w_key,
        w_value,
        w_query,
        w_gate,
        w_swish,
        w_linear,
        w_down,
    )
    query, keys, values, gate, opened, trans, near, far = pl.pallas_call(
        project_kernel,
        in_specs=[IN_SMEM] + [IN_VMEM] * len(operands),
        out_specs=[IN_VMEM] * 8,
        out_shape=[pltpu.VMEM(wide, BF16)] * 4
        + [pltpu.VMEM((atoms_here, width), BF16), pltpu.VMEM(wide, BF16), sent, sent],
        compiler_params=params,
        cost_estimate=cost(samples * atoms_here * width * width * 20),
    )(at, *map(in_vmem, operands))

    operands = (*tiles, near, far, opened)
    first = 3 + len(tiles)
    near, far, opened, held = pl.pallas_call(
        functools.partial(select_kernel, blocks),
        in_specs=[IN_SMEM] * 3 + [IN_VMEM] * len(operands),
        out_specs=[IN_VMEM] * 4,
        out_shape=[
            sent,
            sent,
            pltpu.VMEM((atoms_here, width), BF16),
            pltpu.VMEM((groups * cols, lanes), BF16),
        ],
        input_output_aliases={first: 0, first + 1: 1, first + 2: 2},
        compiler_params=params,
    )(at, pair_at, core_at, *map(in_vmem, operands))

    def swap(value, start):
        cores = lax.axis_size("samp")
        other_of = {}
        for i in range(start, blocks - 1, 2):
            other_of[i], other_of[i + 1] = i + 1, i
        sides = []
        for i in range(blocks):
            for core in range(cores):
                target = (other_of[i], core) if i in other_of else (i, (core + 1) % cores)
                sides.append((i * cores + core, target[0] * cores + target[1]))
        return lax.ppermute(value, ("atoms", "samp"), sides)

    first, second = swap(near, 0), swap(far, 1)

    margin = -(-EDGE // Q_WIN) * Q_WIN
    operands = (query, keys, values, gate, opened, trans, w_out, held)
    inner = pl.pallas_call(
        functools.partial(inner_kernel, heads),
        in_specs=[IN_SMEM] + [IN_VMEM] * (1 + len(operands)),
        out_specs=IN_VMEM,
        out_shape=pltpu.VMEM((samples, atoms_here - 2 * margin, width), BF16),
        scratch_shapes=[
            pltpu.VMEM((atoms_here, heads * tok_here), BF16),
            pltpu.VMEM(wide, BF16),
        ],
        compiler_params=params,
        cost_estimate=cost(samples * atoms_here * width * width * 12),
    )(at, atom_counts, *map(in_vmem, operands))

    reach = margin - Q_WIN + K_WIN
    operands += (inner, w_key, w_value, first, second)
    return pl.pallas_call(
        functools.partial(outer_kernel, heads, blocks),
        in_specs=[IN_SMEM] + [IN_VMEM] * (1 + len(operands)),
        out_specs=IN_HBM,
        out_shape=pltpu.HBM(wide, BF16),
        scratch_shapes=[
            pltpu.VMEM((2, samples, reach, width), BF16),
            pltpu.VMEM((2, samples, reach, width), BF16),
            pltpu.VMEM((2, reach, heads * tok_here), BF16),
            pltpu.VMEM(wide, BF16),
            pltpu.VMEM((2, samples, margin, width), BF16),
            pltpu.SemaphoreType.DMA((3,)),
        ],
        compiler_params=params,
        cost_estimate=cost(samples * atoms_here * width * width * 4),
    )(at, atom_counts, *map(in_vmem, operands))


def solution(mesh):
    return jax.shard_map(
        shards,
        mesh=mesh,
        in_specs=(
            P(("groups", "pair", "samp"), "atoms", None),
            P(("groups", "atoms"), None),
            P(("groups", "pair"), "atoms", None),
            P("groups", None),
        )
        + (P(),) * 15,
        out_specs=P(("groups", "pair", "samp"), "atoms", None),
        check_vma=False,
    )
```

```python
import functools
import math

import jax
import jax.numpy as jnp
from jax import lax
from jax.experimental import pallas as pl
from jax.experimental.pallas import tpu as pltpu
from jax.sharding import PartitionSpec as P

Q_WIN = 32
K_WIN = 128
EDGE = 48
GROUP = 32

EPSILON = 1e-05
MASKED = -1e30
LOG2E = math.log2(math.e)
BF16 = jnp.bfloat16
F32 = jnp.float32
LAST = (((1,), (1,)), ((), ()))
VMEM_LIMIT = 32 << 20
IN_VMEM = pl.BlockSpec(memory_space=pltpu.VMEM)
IN_HBM = pl.BlockSpec(memory_space=pltpu.HBM)
IN_SMEM = pl.BlockSpec(memory_space=pltpu.SMEM)


def dot(a, b):
    return jnp.dot(a, b, preferred_element_type=F32)


def iota(shape, dim):
    return lax.broadcasted_iota(jnp.int32, shape, dim)


def twice(matrix):
    blank = jnp.zeros_like(matrix)
    return jnp.concatenate(
        [jnp.concatenate([matrix, blank], 1), jnp.concatenate([blank, matrix], 1)], 0
    )


def side_by_side(rows):
    half = rows.shape[0] // 2
    return jnp.concatenate([rows[:half], rows[half:]], 1)


def centring(width):
    same = iota((width, width), 0) == iota((width, width), 1)
    return jnp.where(same, 1.0 - 1.0 / width, -1.0 / width).astype(BF16)


def mean_square(centred):
    return jnp.mean(centred * centred, axis=-1, keepdims=True)


def layer_norm(rows):
    width = rows.shape[1]
    both = dot(side_by_side(rows), twice(centring(width)))
    centred = jnp.concatenate([both[:, :width], both[:, width:]], 0)
    return centred * lax.rsqrt(mean_square(centred) + EPSILON)


def sigmoid(values):
    return 0.5 * jnp.tanh(0.5 * values) + 0.5


def attn_norm(cond, single, ada):
    width = single.shape[-1]
    mixed = dot(cond, ada)
    return (sigmoid(mixed[:, :width])[None] * single + mixed[None, :, width:]).astype(BF16)


def pair_kernel(core_ref, w_pair_hbm, pair_hbm, tile_ref, w_pair_ref, pair_ref, pair_sem, sem):
    rows, cols, width = pair_ref.shape
    heads = w_pair_ref.shape[0]
    group = GROUP
    lanes = heads * group
    half = group // 2
    pieces = rows // half
    row_start = core_ref[0] * rows

    def pair_copy(i):
        source = pair_hbm.at[pl.ds(row_start + i * half, half)]
        return pltpu.make_async_copy(source, pair_ref.at[pl.ds(i * half, half)], pair_sem.at[i])

    w_pair_copy = pltpu.make_async_copy(w_pair_hbm, w_pair_ref, sem)
    w_pair_copy.start()
    for i in range(pieces):
        pair_copy(i).start()
    w_pair_copy.wait()
    w_pair = w_pair_ref[...].astype(F32)
    spread = jnp.concatenate(
        [jnp.broadcast_to(w_pair[h : h + 1], (group, width)) for h in range(heads)], 0
    )
    mix = twice(spread.T.astype(BF16))
    centre = twice(centring(width))
    slot = iota((cols, lanes), 1) % group

    chunks = []
    for chunk in range(rows // group):
        for part in range(2):
            pair_copy(chunk * 2 + part).wait()
        pair = pair_ref[chunk * group : (chunk + 1) * group].reshape(group * cols, width)
        chunks.append(dot(side_by_side(pair), centre))
    mixes = [dot(centred.astype(BF16), mix).reshape(half, cols, 2 * lanes) for centred in chunks]
    for chunk, (centred, mixed) in enumerate(zip(chunks, mixes)):
        variances = [
            mean_square(centred[:, part * width : (part + 1) * width]).reshape(half, cols, 1)
            for part in range(2)
        ]
        total = jnp.zeros((cols, lanes), F32)
        spread_out = jnp.zeros((cols, lanes), F32)
        for i in range(group):
            side = slice(i // half * lanes, (i // half + 1) * lanes)
            total = jnp.where(slot == i, mixed[i % half, :, side], total)
            spread_out = jnp.where(slot == i, variances[i // half][i % half], spread_out)
        tile_ref[chunk] = (total * lax.rsqrt(spread_out + EPSILON)).astype(BF16)


def beside(first, second):
    return jnp.concatenate([first[...], second[...]], 1)


def project_kernel(
    at_ref,
    single_ref,
    cond_ref,
    ada_attn_scale,
    ada_attn_shift,
    w_key,
    w_value,
    w_query,
    w_gate,
    *refs,
):
    late_hbm, refs = refs[:7], refs[7:]
    query_ref, key_ref, value_ref, gate_ref, open_ref, trans_ref, near_ref, far_ref = refs[:8]
    late_refs, sem = refs[8:15], refs[15]
    ada_trans_scale, ada_trans_shift, attn_gate, trans_gate, w_swish, w_linear, w_down = late_refs
    samples, atoms_here, width = single_ref.shape
    copies = [
        pltpu.make_async_copy(source, target, sem.at[i])
        for i, (source, target) in enumerate(zip(late_hbm, late_refs))
    ]
    for copy in copies:
        copy.start()

    cond = layer_norm(cond_ref[...]).astype(BF16)
    single = layer_norm(single_ref[...].reshape(-1, width)).reshape(samples, atoms_here, width)
    normed = attn_norm(cond, single, beside(ada_attn_scale, ada_attn_shift))
    even = at_ref[0] % 2 == 0
    for sample in range(samples):
        cut = slice(sample * EDGE, (sample + 1) * EDGE)
        head, tail = normed[sample, :EDGE], normed[sample, atoms_here - EDGE :]
        near_ref[cut, :] = jnp.where(even, tail, head)
        far_ref[cut, :] = jnp.where(even, head, tail)
    normed = normed.reshape(-1, width)
    both = dot(normed, beside(w_key, w_value)).astype(BF16).reshape(samples, -1, 2 * width)
    key_ref[...] = both[:, :, :width]
    value_ref[...] = both[:, :, width:]
    both = dot(normed, beside(w_query, w_gate)).reshape(samples, -1, 2 * width)
    query_ref[...] = both[:, :, :width].astype(BF16)
    gate_ref[...] = sigmoid(both[:, :, width:]).astype(BF16)

    for copy in copies:
        copy.wait()
    gates = dot(cond, beside(attn_gate, trans_gate))
    open_ref[...] = sigmoid(gates[:, :width]).astype(BF16)
    normed = attn_norm(cond, single, beside(ada_trans_scale, ada_trans_shift)).reshape(-1, width)
    swish = dot(normed, w_swish[...])
    hidden = (swish * sigmoid(swish) * dot(normed, w_linear[...])).astype(BF16)
    down = dot(hidden, w_down[...]).reshape(samples, -1, width)
    trans_ref[...] = (sigmoid(gates[:, width:])[None] * down).astype(BF16)


def tile_of(refs, place, row_block):
    if len(refs) == 1:
        return refs[0][row_block]
    pair_at, core_at = place
    owners = 2
    mine, theirs, across, diagonal = [ref[...] for ref in refs]
    near = jnp.where(row_block % owners == core_at, mine, theirs)
    far = jnp.where(row_block % owners == core_at, across, diagonal)
    return jnp.where(row_block // owners == pair_at, near, far)


def select_kernel(blocks, at_ref, pair_ref, core_ref, *refs):
    *tile_refs, _, __, ___, near_ref, far_ref, ____, held_ref = refs
    groups, cols, lanes = tile_refs[0].shape[-3:]
    rows = groups * EDGE
    device_at, place = at_ref[0], (pair_ref[0], core_ref[0])
    for send_ref, parity in ((near_ref, 0), (far_ref, 1)):
        above = device_at % 2 == parity
        beside = jnp.where(above, device_at + 1, device_at - 1)
        tile = tile_of(tile_refs, place, jnp.clip(beside, 0, blocks - 1))
        tile = jnp.where(above, tile[:, cols - EDGE :], tile[:, :EDGE])
        send_ref[send_ref.shape[0] - rows :, :] = tile.reshape(rows, lanes)
    held_ref[...] = tile_of(tile_refs, place, device_at).reshape(groups * cols, lanes)


def bounds(counts_ref, block, token):
    tok_here = counts_ref.shape[1]
    counts = counts_ref[pl.ds(block, 1), :].astype(F32).astype(BF16)
    counts = jnp.broadcast_to(counts, (8, tok_here))
    before = iota((tok_here, token.shape[1]), 0)
    first = dot(counts, (before < token).astype(BF16))[:1]
    last = dot(counts, (before <= token).astype(BF16))[:1]
    return first.astype(jnp.int32), last.astype(jnp.int32)


def one_hot(reach, offset, count):
    first, last = reach
    position = iota((count, first.shape[1]), 0) + offset
    return ((first <= position) & (position < last)).astype(F32).astype(BF16)


def expand(hot, tile, groups):
    tile = tile.reshape(groups, -1, tile.shape[-1])
    tile = jnp.concatenate([tile[part] for part in range(groups)], 1)
    return dot(hot, tile).astype(BF16)


def head_mask(heads, lanes):
    rows = heads * Q_WIN
    lane_head = iota((rows, lanes), 1) // GROUP % heads
    row_head = iota((rows, lanes), 0) // Q_WIN
    return (lane_head == row_head).astype(F32).astype(BF16)


def picks_of(heads, reach, starts):
    same_head = head_mask(heads, reach[0].shape[1])
    return [
        jnp.concatenate([one_hot(reach, start, Q_WIN)] * heads, 0) * same_head for start in starts
    ]


def attend(heads, windows, query_ref, gate_ref, gated_ref):
    samples, _, width = query_ref.shape
    head_dim = width // heads
    rows = heads * Q_WIN
    own_head = iota((rows, width), 1) // head_dim == iota((rows, width), 0) // Q_WIN
    own_head = own_head.astype(F32).astype(BF16)
    channel_head = iota((Q_WIN, 2 * width), 1) % width // head_dim
    ones = jnp.ones((K_WIN, width), BF16)
    scaling = LOG2E / math.sqrt(head_dim)

    biases = []
    for _, _, near, pick, mask in windows:
        bias = lax.dot_general(pick, near, LAST, preferred_element_type=F32) * LOG2E
        biases.append(bias if mask is None else jnp.where(mask, bias, MASKED))
    units = [(sample, i) for i in range(len(windows)) for sample in range(samples)]
    scores = []
    for first in range(0, len(units), 2):
        couple = units[first : first + 2]
        queries, keys = [], []
        for sample, i in couple:
            query = query_ref[sample, pl.ds(windows[i][0], Q_WIN), :]
            queries.append(jnp.concatenate([query] * heads, 0) * own_head)
            keys.append(windows[i][1][sample][0])
        if len(couple) == 2:
            blank = jnp.zeros_like(keys[0])
            keys = [jnp.concatenate([keys[0], blank], 1), jnp.concatenate([blank, keys[1]], 1)]
        product = lax.dot_general(
            jnp.concatenate(queries, 1),
            jnp.concatenate(keys, 0),
            LAST,
            preferred_element_type=F32,
        )
        for j, (_, i) in enumerate(couple):
            scores.append(product[:, j * K_WIN : (j + 1) * K_WIN] * scaling + biases[i])
    tops = [jnp.max(score, axis=-1, keepdims=True) for score in scores]
    raised = [jnp.exp2(score - top).astype(BF16) for score, top in zip(scores, tops)]
    for (sample, i), weight in zip(units, raised):
        values = windows[i][1][sample][1]
        mixed = dot(weight, jnp.concatenate([values, ones], 1))
        picked = mixed[:Q_WIN]
        for head in range(1, heads):
            picked = jnp.where(
                channel_head == head, mixed[head * Q_WIN : (head + 1) * Q_WIN], picked
            )
        attended = picked[:, :width] * pl.reciprocal(picked[:, width:], approx=True)
        at = pl.ds(windows[i][0], Q_WIN)
        gate = gate_ref[sample, at, :].astype(F32)
        gated_ref[sample, at, :] = (gate * attended).astype(BF16)


def close(sample, cut, gated_ref, open_ref, trans_ref, w_out_ref):
    mixed = dot(gated_ref[sample, cut, :], w_out_ref[...])
    opened, trans = open_ref[cut, :].astype(F32), trans_ref[sample, cut, :].astype(F32)
    return (opened * mixed + trans).astype(BF16)


def row_tokens(heads, tok_here):
    lane = iota((tok_here, heads * tok_here), 1)
    return lane // (heads * GROUP) * GROUP + lane % GROUP


def outer_starts(atoms_here):
    skip = -(-EDGE // Q_WIN)
    return [
        [side * (atoms_here - skip * Q_WIN) + i * Q_WIN for i in range(skip)] for side in range(2)
    ]


def inner_kernel(
    heads,
    blocks,
    at_ref,
    counts_ref,
    query_ref,
    key_ref,
    value_ref,
    gate_ref,
    open_ref,
    trans_ref,
    w_out_ref,
    held_ref,
    out_ref,
    pick_ref,
    hot_ref,
    side_ref,
    near_ref,
    gated_ref,
):
    samples, atoms_here, width = query_ref.shape
    tok_here = counts_ref.shape[1]
    device_at = at_ref[0]
    hot = one_hot(
        bounds(counts_ref, device_at, iota((tok_here, tok_here), 1)), 0, atoms_here
    )
    near_ref[...] = expand(hot, held_ref[...], tok_here // GROUP)
    reach = bounds(counts_ref, device_at, row_tokens(heads, tok_here))
    skip = -(-EDGE // Q_WIN)
    starts = [window * Q_WIN for window in range(skip, atoms_here // Q_WIN - skip)]
    windows = []
    for start, pick in zip(starts, picks_of(heads, reach, starts)):
        cut = slice(start - EDGE, start - EDGE + K_WIN)
        parts = [(key_ref[i, cut, :], value_ref[i, cut, :]) for i in range(samples)]
        windows.append((start, parts, near_ref[cut, :], pick, None))
    attend(heads, windows, query_ref, gate_ref, gated_ref)

    cut = slice(starts[0], starts[-1] + Q_WIN)
    for sample in range(samples):
        out_ref[sample] = close(sample, cut, gated_ref, open_ref, trans_ref, w_out_ref)

    inside = side_ref.shape[1]
    sides = (
        (jnp.maximum(device_at - 1, 0), atoms_here - EDGE, tok_here - EDGE, 0),
        (jnp.minimum(device_at + 1, blocks - 1), 0, 0, atoms_here - inside),
    )
    for side, (block, offset, token, own_start) in enumerate(sides):
        nearest = bounds(counts_ref, block, iota((tok_here, EDGE), 1) + token)
        hot_ref[side] = one_hot(nearest, offset, EDGE)
        side_ref[side] = near_ref[own_start : own_start + inside, :]
        for i, pick in enumerate(picks_of(heads, reach, outer_starts(atoms_here)[side])):
            pick_ref[side, i] = pick


def outer_kernel(
    heads,
    blocks,
    groups,
    at_ref,
    query_ref,
    own_key_ref,
    own_value_ref,
    gate_ref,
    open_ref,
    trans_ref,
    w_out_ref,
    inner_ref,
    pick_ref,
    hot_ref,
    side_ref,
    w_key,
    w_value,
    first_ref,
    second_ref,
    out_hbm,
    gated_ref,
    out_ref,
    sem,
):
    samples, atoms_here, width = query_ref.shape
    device_at = at_ref[0]
    ends = atoms_here * blocks
    starts = outer_starts(atoms_here)
    margin = len(starts[0]) * Q_WIN
    inside = side_ref.shape[1]

    whole = pltpu.make_async_copy(
        inner_ref, out_hbm.at[:, pl.ds(margin, atoms_here - 2 * margin)], sem.at[0]
    )
    whole.start()

    even = device_at % 2 == 0
    first, second = first_ref[...], second_ref[...]
    arrived = (jnp.where(even, second, first), jnp.where(even, first, second))
    count = samples * EDGE
    edges = jnp.concatenate([rows[:count] for rows in arrived], 0)
    edges = dot(edges, beside(w_key, w_value)).astype(BF16).reshape(2, samples, EDGE, 2 * width)

    def joined(side, edge, own):
        return jnp.concatenate([own, edge] if side else [edge, own], 0)

    windows = []
    for side in range(2):
        own = slice(side * (atoms_here - inside), side * (atoms_here - inside) + inside)
        parts = [
            (
                joined(side, edges[side, i, :, :width], own_key_ref[i, own, :]),
                joined(side, edges[side, i, :, width:], own_value_ref[i, own, :]),
            )
            for i in range(samples)
        ]
        near = expand(hot_ref[side], arrived[side][count:], groups)
        near = joined(side, near, side_ref[side])
        for i, start in enumerate(starts[side]):
            cut = slice(i * Q_WIN, i * Q_WIN + K_WIN)
            key_at = iota((heads * Q_WIN, K_WIN), 1) + (device_at * atoms_here + start - EDGE)
            mask = (key_at >= 0) & (key_at < ends)
            pieces = [(keys[cut], values[cut]) for keys, values in parts]
            windows.append((start, pieces, near[cut], pick_ref[side, i], mask))
    attend(heads, windows, query_ref, gate_ref, gated_ref)
    copies = []
    for side in range(2):
        cut = slice(starts[side][0], starts[side][0] + margin)
        for sample in range(samples):
            out_ref[side, sample] = close(sample, cut, gated_ref, open_ref, trans_ref, w_out_ref)
        target = out_hbm.at[:, pl.ds(starts[side][0], margin)]
        copies.append(pltpu.make_async_copy(out_ref.at[side], target, sem.at[1 + side]))
        copies[-1].start()
    for copy in copies:
        copy.wait()
    whole.wait()


def shards(
    atom_single,
    atom_cond,
    pair_cond,
    atom_counts,
    ada_attn_scale,
    ada_attn_shift,
    w_query,
    w_key,
    w_value,
    w_gate,
    w_out,
    attn_gate,
    w_pair,
    ada_trans_scale,
    ada_trans_shift,
    w_swish,
    w_linear,
    w_down,
    trans_gate,
):
    device_at = lax.axis_index("atoms")
    blocks = lax.axis_size("atoms")
    samples, atoms_here, width = atom_single.shape
    tok_here = atom_counts.shape[1]
    heads = w_pair.shape[1]
    groups = tok_here // GROUP
    pairs = lax.axis_size("pair")
    assert pair_cond.shape[0] == lax.axis_size("samp") * tok_here
    at = device_at.astype(jnp.int32).reshape(1)
    pair_at = lax.axis_index("pair").astype(jnp.int32).reshape(1)
    core_at = lax.axis_index("samp").astype(jnp.int32).reshape(1)
    in_hbm = lambda array: pltpu.with_memory_space_constraint(array, pltpu.HBM)
    in_vmem = lambda array: pltpu.with_memory_space_constraint(array, pltpu.VMEM)

    cols = pair_cond.shape[1]
    lanes = heads * GROUP
    wide = (samples, atoms_here, width)
    params = pltpu.CompilerParams(vmem_limit_bytes=VMEM_LIMIT)

    def cost(products):
        return pl.CostEstimate(flops=2 * products, bytes_accessed=4 << 20, transcendentals=0)

    sent = pltpu.VMEM((samples * EDGE + groups * EDGE, lanes), BF16)
    own = pl.pallas_call(
        pair_kernel,
        in_specs=[IN_SMEM] + [IN_HBM] * 2,
        out_specs=IN_VMEM,
        out_shape=pltpu.VMEM((groups, cols, lanes), BF16),
        scratch_shapes=[
            pltpu.VMEM((heads, width), BF16),
            pltpu.VMEM((tok_here, cols, width), BF16),
            pltpu.SemaphoreType.DMA((2 * groups,)),
            pltpu.SemaphoreType.DMA,
        ],
        compiler_params=params,
        cost_estimate=cost(tok_here * cols * width * width * 2),
    )(core_at, *map(in_hbm, (w_pair.T, pair_cond)))
    if pairs == 2:
        swapped = [(0, 1), (1, 0)]
        across = lax.ppermute(own, "pair", swapped)
        diagonal = lax.ppermute(own, ("pair", "samp"), [(0, 3), (1, 2), (2, 1), (3, 0)])
        tiles = (own, lax.ppermute(own, "samp", swapped), across, diagonal)
    else:
        tiles = (lax.all_gather(own, ("pair", "samp")),)

    operands = (
        atom_single,
        atom_cond,
        ada_attn_scale,
        ada_attn_shift,
        w_key,
        w_value,
        w_query,
        w_gate,
    )
    late = (ada_trans_scale, ada_trans_shift, attn_gate, trans_gate, w_swish, w_linear, w_down)
    query, keys, values, gate, opened, trans, near, far = pl.pallas_call(
        project_kernel,
        in_specs=[IN_SMEM] + [IN_VMEM] * len(operands) + [IN_HBM] * len(late),
        out_specs=[IN_VMEM] * 8,
        out_shape=[pltpu.VMEM(wide, BF16)] * 4
        + [pltpu.VMEM((atoms_here, width), BF16), pltpu.VMEM(wide, BF16), sent, sent],
        scratch_shapes=[pltpu.VMEM(weight.shape, BF16) for weight in late]
        + [pltpu.SemaphoreType.DMA((len(late),))],
        compiler_params=params,
        cost_estimate=cost(samples * atoms_here * width * width * 20),
    )(at, *map(in_vmem, operands), *map(in_hbm, late))

    operands = (*tiles, near, far, opened)
    first = 3 + len(tiles)
    near, far, opened, held = pl.pallas_call(
        functools.partial(select_kernel, blocks),
        in_specs=[IN_SMEM] * 3 + [IN_VMEM] * len(operands),
        out_specs=[IN_VMEM] * 4,
        out_shape=[
            sent,
            sent,
            pltpu.VMEM((atoms_here, width), BF16),
            pltpu.VMEM((groups * cols, lanes), BF16),
        ],
        input_output_aliases={first: 0, first + 1: 1, first + 2: 2},
        compiler_params=params,
    )(at, pair_at, core_at, *map(in_vmem, operands))

    def swap(value, start):
        cores = lax.axis_size("samp")
        other_of = {}
        for i in range(start, blocks - 1, 2):
            other_of[i], other_of[i + 1] = i + 1, i
        sides = []
        for i in range(blocks):
            for core in range(cores):
                target = (other_of[i], core) if i in other_of else (i, (core + 1) % cores)
                sides.append((i * cores + core, target[0] * cores + target[1]))
        return lax.ppermute(value, ("atoms", "samp"), sides)

    first, second = swap(near, 0), swap(far, 1)

    margin = -(-EDGE // Q_WIN) * Q_WIN
    inside = margin - Q_WIN + K_WIN - EDGE
    expanded = heads * tok_here
    operands = (query, keys, values, gate, opened, trans, w_out)
    inner, picks, hots, beside_edges = pl.pallas_call(
        functools.partial(inner_kernel, heads, blocks),
        in_specs=[IN_SMEM] + [IN_VMEM] * (2 + len(operands)),
        out_specs=[IN_VMEM] * 4,
        out_shape=[
            pltpu.VMEM((samples, atoms_here - 2 * margin, width), BF16),
            pltpu.VMEM((2, margin // Q_WIN, heads * Q_WIN, expanded), BF16),
            pltpu.VMEM((2, EDGE, EDGE), BF16),
            pltpu.VMEM((2, inside, expanded), BF16),
        ],
        scratch_shapes=[
            pltpu.VMEM((atoms_here, expanded), BF16),
            pltpu.VMEM(wide, BF16),
        ],
        compiler_params=params,
        cost_estimate=cost(samples * atoms_here * width * width * 12),
    )(at, atom_counts, *map(in_vmem, (*operands, held)))

    operands += (inner, picks, hots, beside_edges, w_key, w_value, first, second)
    return pl.pallas_call(
        functools.partial(outer_kernel, heads, blocks, groups),
        in_specs=[IN_SMEM] + [IN_VMEM] * len(operands),
        out_specs=IN_HBM,
        out_shape=pltpu.HBM(wide, BF16),
        scratch_shapes=[
            pltpu.VMEM(wide, BF16),
            pltpu.VMEM((2, samples, margin, width), BF16),
            pltpu.SemaphoreType.DMA((3,)),
        ],
        compiler_params=params,
        cost_estimate=cost(samples * atoms_here * width * width * 4),
    )(at, *map(in_vmem, operands))


def solution(mesh):
    return jax.shard_map(
        shards,
        mesh=mesh,
        in_specs=(
            P(("groups", "pair", "samp"), "atoms", None),
            P(("groups", "atoms"), None),
            P(("groups", "pair"), "atoms", None),
            P("groups", None),
        )
        + (P(),) * 15,
        out_specs=P(("groups", "pair", "samp"), "atoms", None),
        check_vma=False,
    )
```

```python
import functools
import math

import jax
import jax.numpy as jnp
from jax import lax
from jax.experimental import pallas as pl
from jax.experimental.pallas import tpu as pltpu
from jax.sharding import PartitionSpec as P

Q_WIN = 32
K_WIN = 128
EDGE = 48
GROUP = 32

EPSILON = 1e-05
MASKED = -1e30
LOG2E = math.log2(math.e)
BF16 = jnp.bfloat16
F32 = jnp.float32
LAST = (((1,), (1,)), ((), ()))
VMEM_LIMIT = 32 << 20
IN_VMEM = pl.BlockSpec(memory_space=pltpu.VMEM)
IN_HBM = pl.BlockSpec(memory_space=pltpu.HBM)
IN_SMEM = pl.BlockSpec(memory_space=pltpu.SMEM)


def dot(a, b):
    return jnp.dot(a, b, preferred_element_type=F32)


def iota(shape, dim):
    return lax.broadcasted_iota(jnp.int32, shape, dim)


def twice(matrix):
    blank = jnp.zeros_like(matrix)
    return jnp.concatenate(
        [jnp.concatenate([matrix, blank], 1), jnp.concatenate([blank, matrix], 1)], 0
    )


def side_by_side(rows):
    half = rows.shape[0] // 2
    return jnp.concatenate([rows[:half], rows[half:]], 1)


def centring(width):
    same = iota((width, width), 0) == iota((width, width), 1)
    return jnp.where(same, 1.0 - 1.0 / width, -1.0 / width).astype(BF16)


def averaging(width):
    return jnp.full((width, width), 1.0 / width, BF16)


def mean_square(centred):
    return jnp.mean(centred * centred, axis=-1, keepdims=True)


def layer_norm(rows):
    width = rows.shape[1]
    both = dot(side_by_side(rows), twice(centring(width)))
    centred = jnp.concatenate([both[:, :width], both[:, width:]], 0)
    return centred * lax.rsqrt(mean_square(centred) + EPSILON)


def sigmoid(values):
    return 0.5 * jnp.tanh(0.5 * values) + 0.5


def attn_norm(cond, single, ada):
    width = single.shape[-1]
    mixed = dot(cond, ada)
    return (sigmoid(mixed[:, :width])[None] * single + mixed[None, :, width:]).astype(BF16)


def pair_kernel(core_ref, w_pair_hbm, pair_hbm, tile_ref, w_pair_ref, pair_ref, pair_sem, sem):
    rows, cols, width = pair_ref.shape
    heads = w_pair_ref.shape[0]
    group = GROUP
    lanes = heads * group
    half = group // 2
    pieces = rows // half
    row_start = core_ref[0] * rows

    def pair_copy(i):
        source = pair_hbm.at[pl.ds(row_start + i * half, half)]
        return pltpu.make_async_copy(source, pair_ref.at[pl.ds(i * half, half)], pair_sem.at[i])

    w_pair_copy = pltpu.make_async_copy(w_pair_hbm, w_pair_ref, sem)
    w_pair_copy.start()
    for i in range(pieces):
        pair_copy(i).start()
    w_pair_copy.wait()
    w_pair = w_pair_ref[...].astype(F32)
    spread = jnp.concatenate(
        [jnp.broadcast_to(w_pair[h : h + 1], (group, width)) for h in range(heads)], 0
    )
    mix = twice(spread.T.astype(BF16))
    centre = twice(centring(width))
    slot = iota((cols, lanes), 1) % group

    chunks = []
    for chunk in range(rows // group):
        for part in range(2):
            pair_copy(chunk * 2 + part).wait()
        pair = pair_ref[chunk * group : (chunk + 1) * group].reshape(group * cols, width)
        chunks.append(dot(side_by_side(pair), centre))
    mixes = [dot(centred.astype(BF16), mix).reshape(half, cols, 2 * lanes) for centred in chunks]
    squares = [(centred[:, :width] * centred[:, :width]).astype(BF16) for centred in chunks]
    averages = [
        dot(jnp.concatenate(squares[i : i + 2], 1), twice(averaging(width)))
        for i in range(0, len(squares), 2)
    ]
    for chunk, (centred, mixed) in enumerate(zip(chunks, mixes)):
        pick = slice(chunk % 2 * width, (chunk % 2 + 1) * width)
        variances = [
            averages[chunk // 2][:, pick].reshape(half, cols, width),
            mean_square(centred[:, width:]).reshape(half, cols, 1),
        ]
        total = jnp.zeros((cols, lanes), F32)
        spread_out = jnp.zeros((cols, lanes), F32)
        for i in range(group):
            side = slice(i // half * lanes, (i // half + 1) * lanes)
            total = jnp.where(slot == i, mixed[i % half, :, side], total)
            spread_out = jnp.where(slot == i, variances[i // half][i % half], spread_out)
        tile_ref[chunk] = (total * lax.rsqrt(spread_out + EPSILON)).astype(BF16)


def beside(first, second):
    return jnp.concatenate([first[...], second[...]], 1)


def project_kernel(
    core_ref,
    single_ref,
    cond_ref,
    ada_attn_scale,
    ada_attn_shift,
    w_key,
    w_value,
    w_query,
    w_gate,
    *refs,
):
    late_hbm, refs = refs[:7], refs[7:]
    query_ref, key_ref, value_ref, gate_ref, open_ref, trans_ref, near_ref, far_ref = refs[:8]
    late_refs, sem = refs[8:15], refs[15]
    ada_trans_scale, ada_trans_shift, attn_gate, trans_gate, w_swish, w_linear, w_down = late_refs
    samples, atoms_here, width = single_ref.shape
    copies = [
        pltpu.make_async_copy(source, target, sem.at[i])
        for i, (source, target) in enumerate(zip(late_hbm, late_refs))
    ]
    for copy in copies:
        copy.start()

    cond = layer_norm(cond_ref[...]).astype(BF16)
    single = layer_norm(single_ref[...].reshape(-1, width)).reshape(samples, atoms_here, width)
    normed = attn_norm(cond, single, beside(ada_attn_scale, ada_attn_shift))
    down = core_ref[0] == 0
    for sample in range(samples):
        cut = slice(sample * EDGE, (sample + 1) * EDGE)
        head, tail = normed[sample, :EDGE], normed[sample, atoms_here - EDGE :]
        near_ref[cut, :] = jnp.where(down, head, tail)
        far_ref[cut, :] = jnp.where(down, tail, head)
    normed = normed.reshape(-1, width)
    both = dot(normed, beside(w_key, w_value)).astype(BF16).reshape(samples, -1, 2 * width)
    key_ref[...] = both[:, :, :width]
    value_ref[...] = both[:, :, width:]
    both = dot(normed, beside(w_query, w_gate)).reshape(samples, -1, 2 * width)
    query_ref[...] = both[:, :, :width].astype(BF16)
    gate_ref[...] = sigmoid(both[:, :, width:]).astype(BF16)

    for copy in copies:
        copy.wait()
    gates = dot(cond, beside(attn_gate, trans_gate))
    open_ref[...] = sigmoid(gates[:, :width]).astype(BF16)
    normed = attn_norm(cond, single, beside(ada_trans_scale, ada_trans_shift)).reshape(-1, width)
    swish = dot(normed, w_swish[...])
    hidden = (swish * sigmoid(swish) * dot(normed, w_linear[...])).astype(BF16)
    down = dot(hidden, w_down[...]).reshape(samples, -1, width)
    trans_ref[...] = (sigmoid(gates[:, width:])[None] * down).astype(BF16)


def tile_of(refs, place, row_block):
    if len(refs) == 1:
        return refs[0][row_block]
    pair_at, core_at = place
    owners = 2
    mine, theirs, across, diagonal = [ref[...] for ref in refs]
    near = jnp.where(row_block % owners == core_at, mine, theirs)
    far = jnp.where(row_block % owners == core_at, across, diagonal)
    return jnp.where(row_block // owners == pair_at, near, far)


def select_kernel(blocks, at_ref, pair_ref, core_ref, *refs):
    *tile_refs, _, __, ___, near_ref, far_ref, ____, held_ref = refs
    groups, cols, lanes = tile_refs[0].shape[-3:]
    rows = groups * EDGE
    device_at, place = at_ref[0], (pair_ref[0], core_ref[0])
    for send_ref, core in ((near_ref, 1), (far_ref, 0)):
        above = core_ref[0] == core
        beside = jnp.where(above, device_at + 1, device_at - 1)
        tile = tile_of(tile_refs, place, jnp.clip(beside, 0, blocks - 1))
        tile = jnp.where(above, tile[:, cols - EDGE :], tile[:, :EDGE])
        send_ref[send_ref.shape[0] - rows :, :] = tile.reshape(rows, lanes)
    held_ref[...] = tile_of(tile_refs, place, device_at).reshape(groups * cols, lanes)


def bounds(counts_ref, block, token):
    tok_here = counts_ref.shape[1]
    counts = counts_ref[pl.ds(block, 1), :].astype(F32).astype(BF16)
    counts = jnp.broadcast_to(counts, (8, tok_here))
    before = iota((tok_here, token.shape[1]), 0)
    first = dot(counts, (before < token).astype(BF16))[:1]
    last = dot(counts, (before <= token).astype(BF16))[:1]
    return first.astype(jnp.int32), last.astype(jnp.int32)


def one_hot(reach, offset, count):
    first, last = reach
    position = iota((count, first.shape[1]), 0) + offset
    return ((first <= position) & (position < last)).astype(F32).astype(BF16)


def expand(hot, tile, groups):
    tile = tile.reshape(groups, -1, tile.shape[-1])
    tile = jnp.concatenate([tile[part] for part in range(groups)], 1)
    return dot(hot, tile).astype(BF16)


def head_mask(heads, lanes):
    rows = heads * Q_WIN
    lane_head = iota((rows, lanes), 1) // GROUP % heads
    row_head = iota((rows, lanes), 0) // Q_WIN
    return (lane_head == row_head).astype(F32).astype(BF16)


def picks_of(heads, reach, starts):
    same_head = head_mask(heads, reach[0].shape[1])
    return [
        jnp.concatenate([one_hot(reach, start, Q_WIN)] * heads, 0) * same_head for start in starts
    ]


def attend(heads, windows, query_ref, gate_ref, gated_ref):
    samples, _, width = query_ref.shape
    head_dim = width // heads
    rows = heads * Q_WIN
    own_head = iota((rows, width), 1) // head_dim == iota((rows, width), 0) // Q_WIN
    own_head = own_head.astype(F32).astype(BF16)
    channel_head = iota((Q_WIN, 2 * width), 1) % width // head_dim
    ones = jnp.ones((K_WIN, width), BF16)
    scaling = LOG2E / math.sqrt(head_dim)

    biases = []
    for _, _, near, pick, mask in windows:
        bias = lax.dot_general(pick, near, LAST, preferred_element_type=F32) * LOG2E
        biases.append(bias if mask is None else jnp.where(mask, bias, MASKED))
    units = [(sample, i) for i in range(len(windows)) for sample in range(samples)]
    scores = []
    for first in range(0, len(units), 2):
        couple = units[first : first + 2]
        queries, keys = [], []
        for sample, i in couple:
            query = query_ref[sample, pl.ds(windows[i][0], Q_WIN), :]
            queries.append(jnp.concatenate([query] * heads, 0) * own_head)
            keys.append(windows[i][1][sample][0])
        if len(couple) == 2:
            blank = jnp.zeros_like(keys[0])
            keys = [jnp.concatenate([keys[0], blank], 1), jnp.concatenate([blank, keys[1]], 1)]
        product = lax.dot_general(
            jnp.concatenate(queries, 1),
            jnp.concatenate(keys, 0),
            LAST,
            preferred_element_type=F32,
        )
        for j, (_, i) in enumerate(couple):
            scores.append(product[:, j * K_WIN : (j + 1) * K_WIN] * scaling + biases[i])
    tops = [jnp.max(score, axis=-1, keepdims=True) for score in scores]
    raised = [jnp.exp2(score - top).astype(BF16) for score, top in zip(scores, tops)]
    for (sample, i), weight in zip(units, raised):
        values = windows[i][1][sample][1]
        mixed = dot(weight, jnp.concatenate([values, ones], 1))
        picked = mixed[:Q_WIN]
        for head in range(1, heads):
            picked = jnp.where(
                channel_head == head, mixed[head * Q_WIN : (head + 1) * Q_WIN], picked
            )
        attended = picked[:, :width] * pl.reciprocal(picked[:, width:], approx=True)
        at = pl.ds(windows[i][0], Q_WIN)
        gate = gate_ref[sample, at, :].astype(F32)
        gated_ref[sample, at, :] = (gate * attended).astype(BF16)


def close(sample, cut, gated_ref, open_ref, trans_ref, w_out_ref):
    mixed = dot(gated_ref[sample, cut, :], w_out_ref[...])
    opened, trans = open_ref[cut, :].astype(F32), trans_ref[sample, cut, :].astype(F32)
    return (opened * mixed + trans).astype(BF16)


def row_tokens(heads, tok_here):
    lane = iota((tok_here, heads * tok_here), 1)
    return lane // (heads * GROUP) * GROUP + lane % GROUP


def outer_starts(atoms_here):
    skip = -(-EDGE // Q_WIN)
    return [
        [side * (atoms_here - skip * Q_WIN) + i * Q_WIN for i in range(skip)] for side in range(2)
    ]


def inner_kernel(
    heads,
    blocks,
    at_ref,
    counts_ref,
    query_ref,
    key_ref,
    value_ref,
    gate_ref,
    open_ref,
    trans_ref,
    w_out_ref,
    held_ref,
    out_ref,
    pick_ref,
    hot_ref,
    side_ref,
    near_ref,
    gated_ref,
):
    samples, atoms_here, width = query_ref.shape
    tok_here = counts_ref.shape[1]
    device_at = at_ref[0]
    hot = one_hot(
        bounds(counts_ref, device_at, iota((tok_here, tok_here), 1)), 0, atoms_here
    )
    near_ref[...] = expand(hot, held_ref[...], tok_here // GROUP)
    reach = bounds(counts_ref, device_at, row_tokens(heads, tok_here))
    skip = -(-EDGE // Q_WIN)
    starts = [window * Q_WIN for window in range(skip, atoms_here // Q_WIN - skip)]
    windows = []
    for start, pick in zip(starts, picks_of(heads, reach, starts)):
        cut = slice(start - EDGE, start - EDGE + K_WIN)
        parts = [(key_ref[i, cut, :], value_ref[i, cut, :]) for i in range(samples)]
        windows.append((start, parts, near_ref[cut, :], pick, None))
    attend(heads, windows, query_ref, gate_ref, gated_ref)

    cut = slice(starts[0], starts[-1] + Q_WIN)
    for sample in range(samples):
        out_ref[sample] = close(sample, cut, gated_ref, open_ref, trans_ref, w_out_ref)

    inside = side_ref.shape[1]
    sides = (
        (jnp.maximum(device_at - 1, 0), atoms_here - EDGE, tok_here - EDGE, 0),
        (jnp.minimum(device_at + 1, blocks - 1), 0, 0, atoms_here - inside),
    )
    for side, (block, offset, token, own_start) in enumerate(sides):
        nearest = bounds(counts_ref, block, iota((tok_here, EDGE), 1) + token)
        hot_ref[side] = one_hot(nearest, offset, EDGE)
        side_ref[side] = near_ref[own_start : own_start + inside, :]
        for i, pick in enumerate(picks_of(heads, reach, outer_starts(atoms_here)[side])):
            pick_ref[side, i] = pick


def outer_kernel(
    heads,
    blocks,
    groups,
    at_ref,
    core_ref,
    query_ref,
    own_key_ref,
    own_value_ref,
    gate_ref,
    open_ref,
    trans_ref,
    w_out_ref,
    inner_ref,
    pick_ref,
    hot_ref,
    side_ref,
    w_key,
    w_value,
    first_ref,
    second_ref,
    out_hbm,
    gated_ref,
    out_ref,
    sem,
):
    samples, atoms_here, width = query_ref.shape
    device_at = at_ref[0]
    ends = atoms_here * blocks
    starts = outer_starts(atoms_here)
    margin = len(starts[0]) * Q_WIN
    inside = side_ref.shape[1]

    whole = pltpu.make_async_copy(
        inner_ref, out_hbm.at[:, pl.ds(margin, atoms_here - 2 * margin)], sem.at[0]
    )
    whole.start()

    down = core_ref[0] == 0
    first, second = first_ref[...], second_ref[...]
    arrived = (jnp.where(down, second, first), jnp.where(down, first, second))
    count = samples * EDGE
    edges = jnp.concatenate([rows[:count] for rows in arrived], 0)
    edges = dot(edges, beside(w_key, w_value)).astype(BF16).reshape(2, samples, EDGE, 2 * width)

    def joined(side, edge, own):
        return jnp.concatenate([own, edge] if side else [edge, own], 0)

    windows = []
    for side in range(2):
        own = slice(side * (atoms_here - inside), side * (atoms_here - inside) + inside)
        parts = [
            (
                joined(side, edges[side, i, :, :width], own_key_ref[i, own, :]),
                joined(side, edges[side, i, :, width:], own_value_ref[i, own, :]),
            )
            for i in range(samples)
        ]
        near = expand(hot_ref[side], arrived[side][count:], groups)
        near = joined(side, near, side_ref[side])
        for i, start in enumerate(starts[side]):
            cut = slice(i * Q_WIN, i * Q_WIN + K_WIN)
            key_at = iota((heads * Q_WIN, K_WIN), 1) + (device_at * atoms_here + start - EDGE)
            mask = (key_at >= 0) & (key_at < ends)
            pieces = [(keys[cut], values[cut]) for keys, values in parts]
            windows.append((start, pieces, near[cut], pick_ref[side, i], mask))
    attend(heads, windows, query_ref, gate_ref, gated_ref)
    copies = []
    for side in range(2):
        cut = slice(starts[side][0], starts[side][0] + margin)
        for sample in range(samples):
            out_ref[side, sample] = close(sample, cut, gated_ref, open_ref, trans_ref, w_out_ref)
        target = out_hbm.at[:, pl.ds(starts[side][0], margin)]
        copies.append(pltpu.make_async_copy(out_ref.at[side], target, sem.at[1 + side]))
        copies[-1].start()
    for copy in copies:
        copy.wait()
    whole.wait()


def shards(
    atom_single,
    atom_cond,
    pair_cond,
    atom_counts,
    ada_attn_scale,
    ada_attn_shift,
    w_query,
    w_key,
    w_value,
    w_gate,
    w_out,
    attn_gate,
    w_pair,
    ada_trans_scale,
    ada_trans_shift,
    w_swish,
    w_linear,
    w_down,
    trans_gate,
):
    device_at = lax.axis_index("atoms")
    blocks = lax.axis_size("atoms")
    samples, atoms_here, width = atom_single.shape
    tok_here = atom_counts.shape[1]
    heads = w_pair.shape[1]
    groups = tok_here // GROUP
    pairs = lax.axis_size("pair")
    assert pair_cond.shape[0] == lax.axis_size("samp") * tok_here
    at = device_at.astype(jnp.int32).reshape(1)
    pair_at = lax.axis_index("pair").astype(jnp.int32).reshape(1)
    core_at = lax.axis_index("samp").astype(jnp.int32).reshape(1)
    in_hbm = lambda array: pltpu.with_memory_space_constraint(array, pltpu.HBM)
    in_vmem = lambda array: pltpu.with_memory_space_constraint(array, pltpu.VMEM)

    cols = pair_cond.shape[1]
    lanes = heads * GROUP
    wide = (samples, atoms_here, width)
    params = pltpu.CompilerParams(vmem_limit_bytes=VMEM_LIMIT)

    def cost(products):
        return pl.CostEstimate(flops=2 * products, bytes_accessed=4 << 20, transcendentals=0)

    sent = pltpu.VMEM((samples * EDGE + groups * EDGE, lanes), BF16)
    own = pl.pallas_call(
        pair_kernel,
        in_specs=[IN_SMEM] + [IN_HBM] * 2,
        out_specs=IN_VMEM,
        out_shape=pltpu.VMEM((groups, cols, lanes), BF16),
        scratch_shapes=[
            pltpu.VMEM((heads, width), BF16),
            pltpu.VMEM((tok_here, cols, width), BF16),
            pltpu.SemaphoreType.DMA((2 * groups,)),
            pltpu.SemaphoreType.DMA,
        ],
        compiler_params=params,
        cost_estimate=cost(tok_here * cols * width * width * 2),
    )(core_at, *map(in_hbm, (w_pair.T, pair_cond)))
    if pairs == 2:
        swapped = [(0, 1), (1, 0)]
        across = lax.ppermute(own, "pair", swapped)
        diagonal = lax.ppermute(own, ("pair", "samp"), [(0, 3), (1, 2), (2, 1), (3, 0)])
        tiles = (own, lax.ppermute(own, "samp", swapped), across, diagonal)
    else:
        tiles = (lax.all_gather(own, ("pair", "samp")),)

    operands = (
        atom_single,
        atom_cond,
        ada_attn_scale,
        ada_attn_shift,
        w_key,
        w_value,
        w_query,
        w_gate,
    )
    late = (ada_trans_scale, ada_trans_shift, attn_gate, trans_gate, w_swish, w_linear, w_down)
    query, keys, values, gate, opened, trans, near, far = pl.pallas_call(
        project_kernel,
        in_specs=[IN_SMEM] + [IN_VMEM] * len(operands) + [IN_HBM] * len(late),
        out_specs=[IN_VMEM] * 8,
        out_shape=[pltpu.VMEM(wide, BF16)] * 4
        + [pltpu.VMEM((atoms_here, width), BF16), pltpu.VMEM(wide, BF16), sent, sent],
        scratch_shapes=[pltpu.VMEM(weight.shape, BF16) for weight in late]
        + [pltpu.SemaphoreType.DMA((len(late),))],
        compiler_params=params,
        cost_estimate=cost(samples * atoms_here * width * width * 20),
    )(core_at, *map(in_vmem, operands), *map(in_hbm, late))

    operands = (*tiles, near, far, opened)
    first = 3 + len(tiles)
    near, far, opened, held = pl.pallas_call(
        functools.partial(select_kernel, blocks),
        in_specs=[IN_SMEM] * 3 + [IN_VMEM] * len(operands),
        out_specs=[IN_VMEM] * 4,
        out_shape=[
            sent,
            sent,
            pltpu.VMEM((atoms_here, width), BF16),
            pltpu.VMEM((groups * cols, lanes), BF16),
        ],
        input_output_aliases={first: 0, first + 1: 1, first + 2: 2},
        compiler_params=params,
    )(at, pair_at, core_at, *map(in_vmem, operands))

    down = [(2 * i, 2 * (i - 1)) for i in range(1, blocks)] + [(0, 1)]
    up = [(2 * i + 1, 2 * (i + 1) + 1) for i in range(blocks - 1)] + [(2 * blocks - 1, 2 * blocks - 2)]
    cycle = down + up
    first = lax.ppermute(near, ("atoms", "samp"), cycle)
    second = lax.ppermute(far, ("atoms", "samp"), [(target, source) for source, target in cycle])

    margin = -(-EDGE // Q_WIN) * Q_WIN
    inside = margin - Q_WIN + K_WIN - EDGE
    expanded = heads * tok_here
    operands = (query, keys, values, gate, opened, trans, w_out)
    inner, picks, hots, beside_edges = pl.pallas_call(
        functools.partial(inner_kernel, heads, blocks),
        in_specs=[IN_SMEM] + [IN_VMEM] * (2 + len(operands)),
        out_specs=[IN_VMEM] * 4,
        out_shape=[
            pltpu.VMEM((samples, atoms_here - 2 * margin, width), BF16),
            pltpu.VMEM((2, margin // Q_WIN, heads * Q_WIN, expanded), BF16),
            pltpu.VMEM((2, EDGE, EDGE), BF16),
            pltpu.VMEM((2, inside, expanded), BF16),
        ],
        scratch_shapes=[
            pltpu.VMEM((atoms_here, expanded), BF16),
            pltpu.VMEM(wide, BF16),
        ],
        compiler_params=params,
        cost_estimate=cost(samples * atoms_here * width * width * 12),
    )(at, atom_counts, *map(in_vmem, (*operands, held)))

    operands += (inner, picks, hots, beside_edges, w_key, w_value, first, second)
    return pl.pallas_call(
        functools.partial(outer_kernel, heads, blocks, groups),
        in_specs=[IN_SMEM] * 2 + [IN_VMEM] * len(operands),
        out_specs=IN_HBM,
        out_shape=pltpu.HBM(wide, BF16),
        scratch_shapes=[
            pltpu.VMEM(wide, BF16),
            pltpu.VMEM((2, samples, margin, width), BF16),
            pltpu.SemaphoreType.DMA((3,)),
        ],
        compiler_params=params,
        cost_estimate=cost(samples * atoms_here * width * width * 4),
    )(at, core_at, *map(in_vmem, operands))


def solution(mesh):
    return jax.shard_map(
        shards,
        mesh=mesh,
        in_specs=(
            P(("groups", "pair", "samp"), "atoms", None),
            P(("groups", "atoms"), None),
            P(("groups", "pair"), "atoms", None),
            P("groups", None),
        )
        + (P(),) * 15,
        out_specs=P(("groups", "pair", "samp"), "atoms", None),
        check_vma=False,
    )
```

```python
import functools
import math

import jax
import jax.numpy as jnp
from jax import lax
from jax.experimental import pallas as pl
from jax.experimental.pallas import tpu as pltpu
from jax.sharding import PartitionSpec as P

Q_WIN = 32
K_WIN = 128
EDGE = 48
GROUP = 32

EPSILON = 1e-05
MASKED = -1e30
LOG2E = math.log2(math.e)
BF16 = jnp.bfloat16
F32 = jnp.float32
LAST = (((1,), (1,)), ((), ()))
VMEM_LIMIT = 32 << 20
IN_VMEM = pl.BlockSpec(memory_space=pltpu.VMEM)
IN_HBM = pl.BlockSpec(memory_space=pltpu.HBM)
IN_SMEM = pl.BlockSpec(memory_space=pltpu.SMEM)


def dot(a, b):
    return jnp.dot(a, b, preferred_element_type=F32)


def iota(shape, dim):
    return lax.broadcasted_iota(jnp.int32, shape, dim)


def twice(matrix):
    blank = jnp.zeros_like(matrix)
    return jnp.concatenate(
        [jnp.concatenate([matrix, blank], 1), jnp.concatenate([blank, matrix], 1)], 0
    )


def side_by_side(rows):
    half = rows.shape[0] // 2
    return jnp.concatenate([rows[:half], rows[half:]], 1)


def centring(width):
    same = iota((width, width), 0) == iota((width, width), 1)
    return jnp.where(same, 1.0 - 1.0 / width, -1.0 / width).astype(BF16)


def averaging(width):
    return jnp.full((width, width), 1.0 / width, BF16)


def mean_square(centred):
    return jnp.mean(centred * centred, axis=-1, keepdims=True)


def layer_norm(rows):
    width = rows.shape[1]
    both = dot(side_by_side(rows), twice(centring(width)))
    centred = jnp.concatenate([both[:, :width], both[:, width:]], 0)
    return centred * lax.rsqrt(mean_square(centred) + EPSILON)


def sigmoid(values):
    return 0.5 * jnp.tanh(0.5 * values) + 0.5


def attn_norm(cond, single, ada):
    width = single.shape[-1]
    mixed = dot(cond, ada)
    return (sigmoid(mixed[:, :width])[None] * single + mixed[None, :, width:]).astype(BF16)


def pair_kernel(core_ref, w_pair_hbm, pair_hbm, tile_ref, w_pair_ref, pair_ref, pair_sem, sem):
    rows, cols, width = pair_ref.shape
    heads = w_pair_ref.shape[0]
    group = GROUP
    lanes = heads * group
    half = group // 2
    piece = rows // pair_sem.shape[0]
    row_start = core_ref[0] * rows

    def pair_copy(i):
        source = pair_hbm.at[pl.ds(row_start + i * piece, piece)]
        return pltpu.make_async_copy(source, pair_ref.at[pl.ds(i * piece, piece)], pair_sem.at[i])

    w_pair_copy = pltpu.make_async_copy(w_pair_hbm, w_pair_ref, sem)
    for i in range(pair_sem.shape[0]):
        pair_copy(i).start()
    w_pair_copy.start()

    centre = twice(centring(width))
    chunks = []
    for chunk in range(rows // group):
        for i in range(group // piece):
            pair_copy(chunk * (group // piece) + i).wait()
        pair = pair_ref[chunk * group : (chunk + 1) * group].reshape(group * cols, width)
        chunks.append(dot(side_by_side(pair), centre))
    w_pair_copy.wait()
    w_pair = w_pair_ref[...].astype(F32)
    spread = jnp.concatenate(
        [jnp.broadcast_to(w_pair[h : h + 1], (group, width)) for h in range(heads)], 0
    )
    mix = twice(spread.T.astype(BF16))
    slot = iota((cols, lanes), 1) % group
    mixes = [dot(centred.astype(BF16), mix).reshape(half, cols, 2 * lanes) for centred in chunks]
    squares = [(centred[:, :width] * centred[:, :width]).astype(BF16) for centred in chunks]
    averages = [
        dot(jnp.concatenate(squares[i : i + 2], 1), twice(averaging(width)))
        for i in range(0, len(squares), 2)
    ]
    for chunk, (centred, mixed) in enumerate(zip(chunks, mixes)):
        pick = slice(chunk % 2 * width, (chunk % 2 + 1) * width)
        variances = [
            averages[chunk // 2][:, pick].reshape(half, cols, width),
            mean_square(centred[:, width:]).reshape(half, cols, 1),
        ]
        total = jnp.zeros((cols, lanes), F32)
        spread_out = jnp.zeros((cols, lanes), F32)
        for i in range(group):
            side = slice(i // half * lanes, (i // half + 1) * lanes)
            total = jnp.where(slot == i, mixed[i % half, :, side], total)
            spread_out = jnp.where(slot == i, variances[i // half][i % half], spread_out)
        tile_ref[chunk] = (total * lax.rsqrt(spread_out + EPSILON)).astype(BF16)


def beside(first, second):
    return jnp.concatenate([first[...], second[...]], 1)


def project_kernel(
    core_ref,
    single_ref,
    cond_ref,
    ada_attn_scale,
    ada_attn_shift,
    w_key,
    w_value,
    w_query,
    w_gate,
    *refs,
):
    late_hbm, refs = refs[:7], refs[7:]
    query_ref, key_ref, value_ref, gate_ref, open_ref, trans_ref, near_ref, far_ref = refs[:8]
    late_refs, sem = refs[8:15], refs[15]
    ada_trans_scale, ada_trans_shift, attn_gate, trans_gate, w_swish, w_linear, w_down = late_refs
    samples, atoms_here, width = single_ref.shape
    copies = [
        pltpu.make_async_copy(source, target, sem.at[i])
        for i, (source, target) in enumerate(zip(late_hbm, late_refs))
    ]
    for copy in copies:
        copy.start()

    cond = layer_norm(cond_ref[...]).astype(BF16)
    single = layer_norm(single_ref[...].reshape(-1, width)).reshape(samples, atoms_here, width)
    normed = attn_norm(cond, single, beside(ada_attn_scale, ada_attn_shift))
    down = core_ref[0] == 0
    for sample in range(samples):
        cut = slice(sample * EDGE, (sample + 1) * EDGE)
        head, tail = normed[sample, :EDGE], normed[sample, atoms_here - EDGE :]
        near_ref[cut, :] = jnp.where(down, head, tail)
        far_ref[cut, :] = jnp.where(down, tail, head)
    normed = normed.reshape(-1, width)
    both = dot(normed, beside(w_key, w_value)).astype(BF16).reshape(samples, -1, 2 * width)
    key_ref[...] = both[:, :, :width]
    value_ref[...] = both[:, :, width:]
    both = dot(normed, beside(w_query, w_gate)).reshape(samples, -1, 2 * width)
    query_ref[...] = both[:, :, :width].astype(BF16)
    gate_ref[...] = sigmoid(both[:, :, width:]).astype(BF16)

    for copy in copies:
        copy.wait()
    gates = dot(cond, beside(attn_gate, trans_gate))
    open_ref[...] = sigmoid(gates[:, :width]).astype(BF16)
    normed = attn_norm(cond, single, beside(ada_trans_scale, ada_trans_shift)).reshape(-1, width)
    swish = dot(normed, w_swish[...])
    hidden = (swish * sigmoid(swish) * dot(normed, w_linear[...])).astype(BF16)
    down = dot(hidden, w_down[...]).reshape(samples, -1, width)
    trans_ref[...] = (sigmoid(gates[:, width:])[None] * down).astype(BF16)


def tile_of(refs, place, row_block):
    if len(refs) == 1:
        return refs[0][row_block]
    pair_at, core_at = place
    owners = 2
    mine, theirs, across, diagonal = [ref[...] for ref in refs]
    near = jnp.where(row_block % owners == core_at, mine, theirs)
    far = jnp.where(row_block % owners == core_at, across, diagonal)
    return jnp.where(row_block // owners == pair_at, near, far)


def select_kernel(blocks, at_ref, pair_ref, core_ref, *refs):
    *tile_refs, _, __, ___, near_ref, far_ref, ____, held_ref = refs
    groups, cols, lanes = tile_refs[0].shape[-3:]
    rows = groups * EDGE
    device_at, place = at_ref[0], (pair_ref[0], core_ref[0])
    for send_ref, core in ((near_ref, 1), (far_ref, 0)):
        above = core_ref[0] == core
        beside = jnp.where(above, device_at + 1, device_at - 1)
        tile = tile_of(tile_refs, place, jnp.clip(beside, 0, blocks - 1))
        tile = jnp.where(above, tile[:, cols - EDGE :], tile[:, :EDGE])
        send_ref[send_ref.shape[0] - rows :, :] = tile.reshape(rows, lanes)
    held_ref[...] = tile_of(tile_refs, place, device_at).reshape(groups * cols, lanes)


def bounds(counts_ref, block, token):
    tok_here = counts_ref.shape[1]
    counts = counts_ref[pl.ds(block, 1), :].astype(F32).astype(BF16)
    counts = jnp.broadcast_to(counts, (8, tok_here))
    before = iota((tok_here, token.shape[1]), 0)
    first = dot(counts, (before < token).astype(BF16))[:1]
    last = dot(counts, (before <= token).astype(BF16))[:1]
    return first.astype(jnp.int32), last.astype(jnp.int32)


def one_hot(reach, offset, count):
    first, last = reach
    position = iota((count, first.shape[1]), 0) + offset
    return ((first <= position) & (position < last)).astype(F32).astype(BF16)


def expand(hot, tile, groups):
    tile = tile.reshape(groups, -1, tile.shape[-1])
    tile = jnp.concatenate([tile[part] for part in range(groups)], 1)
    return dot(hot, tile).astype(BF16)


def head_mask(heads, lanes):
    rows = heads * Q_WIN
    lane_head = iota((rows, lanes), 1) // GROUP % heads
    row_head = iota((rows, lanes), 0) // Q_WIN
    return (lane_head == row_head).astype(F32).astype(BF16)


def picks_of(heads, reach, starts):
    same_head = head_mask(heads, reach[0].shape[1])
    return [
        jnp.concatenate([one_hot(reach, start, Q_WIN)] * heads, 0) * same_head for start in starts
    ]


def attend(heads, windows, query_ref, gate_ref, gated_ref):
    samples, _, width = query_ref.shape
    head_dim = width // heads
    rows = heads * Q_WIN
    own_head = iota((rows, width), 1) // head_dim == iota((rows, width), 0) // Q_WIN
    own_head = own_head.astype(F32).astype(BF16)
    channel_head = iota((Q_WIN, 2 * width), 1) % width // head_dim
    ones = jnp.ones((K_WIN, width), BF16)
    scaling = LOG2E / math.sqrt(head_dim)

    biases = []
    for _, _, near, pick, mask in windows:
        bias = lax.dot_general(pick, near, LAST, preferred_element_type=F32) * LOG2E
        biases.append(bias if mask is None else jnp.where(mask, bias, MASKED))
    units = [(sample, i) for i in range(len(windows)) for sample in range(samples)]
    scores = []
    for first in range(0, len(units), 2):
        couple = units[first : first + 2]
        queries, keys = [], []
        for sample, i in couple:
            query = query_ref[sample, pl.ds(windows[i][0], Q_WIN), :]
            queries.append(jnp.concatenate([query] * heads, 0) * own_head)
            keys.append(windows[i][1][sample][0])
        if len(couple) == 2:
            blank = jnp.zeros_like(keys[0])
            keys = [jnp.concatenate([keys[0], blank], 1), jnp.concatenate([blank, keys[1]], 1)]
        product = lax.dot_general(
            jnp.concatenate(queries, 1),
            jnp.concatenate(keys, 0),
            LAST,
            preferred_element_type=F32,
        )
        for j, (_, i) in enumerate(couple):
            scores.append(product[:, j * K_WIN : (j + 1) * K_WIN] * scaling + biases[i])
    tops = [jnp.max(score, axis=-1, keepdims=True) for score in scores]
    raised = [jnp.exp2(score - top).astype(BF16) for score, top in zip(scores, tops)]
    for (sample, i), weight in zip(units, raised):
        values = windows[i][1][sample][1]
        mixed = dot(weight, jnp.concatenate([values, ones], 1))
        picked = mixed[:Q_WIN]
        for head in range(1, heads):
            picked = jnp.where(
                channel_head == head, mixed[head * Q_WIN : (head + 1) * Q_WIN], picked
            )
        attended = picked[:, :width] * pl.reciprocal(picked[:, width:], approx=True)
        at = pl.ds(windows[i][0], Q_WIN)
        gate = gate_ref[sample, at, :].astype(F32)
        gated_ref[sample, at, :] = (gate * attended).astype(BF16)


def close(sample, cut, gated_ref, open_ref, trans_ref, w_out_ref):
    mixed = dot(gated_ref[sample, cut, :], w_out_ref[...])
    opened, trans = open_ref[cut, :].astype(F32), trans_ref[sample, cut, :].astype(F32)
    return (opened * mixed + trans).astype(BF16)


def row_tokens(heads, tok_here):
    lane = iota((tok_here, heads * tok_here), 1)
    return lane // (heads * GROUP) * GROUP + lane % GROUP


def outer_starts(atoms_here):
    skip = -(-EDGE // Q_WIN)
    return [
        [side * (atoms_here - skip * Q_WIN) + i * Q_WIN for i in range(skip)] for side in range(2)
    ]


def inner_kernel(
    heads,
    blocks,
    at_ref,
    counts_ref,
    query_ref,
    key_ref,
    value_ref,
    gate_ref,
    open_ref,
    trans_ref,
    w_out_ref,
    held_ref,
    out_ref,
    pick_ref,
    hot_ref,
    side_ref,
    near_ref,
    gated_ref,
):
    samples, atoms_here, width = query_ref.shape
    tok_here = counts_ref.shape[1]
    device_at = at_ref[0]
    hot = one_hot(
        bounds(counts_ref, device_at, iota((tok_here, tok_here), 1)), 0, atoms_here
    )
    near_ref[...] = expand(hot, held_ref[...], tok_here // GROUP)
    reach = bounds(counts_ref, device_at, row_tokens(heads, tok_here))
    skip = -(-EDGE // Q_WIN)
    starts = [window * Q_WIN for window in range(skip, atoms_here // Q_WIN - skip)]
    windows = []
    for start, pick in zip(starts, picks_of(heads, reach, starts)):
        cut = slice(start - EDGE, start - EDGE + K_WIN)
        parts = [(key_ref[i, cut, :], value_ref[i, cut, :]) for i in range(samples)]
        windows.append((start, parts, near_ref[cut, :], pick, None))
    attend(heads, windows, query_ref, gate_ref, gated_ref)

    cut = slice(starts[0], starts[-1] + Q_WIN)
    for sample in range(samples):
        out_ref[sample] = close(sample, cut, gated_ref, open_ref, trans_ref, w_out_ref)

    inside = side_ref.shape[1]
    sides = (
        (jnp.maximum(device_at - 1, 0), atoms_here - EDGE, tok_here - EDGE, 0),
        (jnp.minimum(device_at + 1, blocks - 1), 0, 0, atoms_here - inside),
    )
    for side, (block, offset, token, own_start) in enumerate(sides):
        nearest = bounds(counts_ref, block, iota((tok_here, EDGE), 1) + token)
        hot_ref[side] = one_hot(nearest, offset, EDGE)
        side_ref[side] = near_ref[own_start : own_start + inside, :]
        for i, pick in enumerate(picks_of(heads, reach, outer_starts(atoms_here)[side])):
            pick_ref[side, i] = pick


def outer_kernel(
    heads,
    blocks,
    groups,
    at_ref,
    core_ref,
    query_ref,
    own_key_ref,
    own_value_ref,
    gate_ref,
    open_ref,
    trans_ref,
    w_out_ref,
    inner_ref,
    pick_ref,
    hot_ref,
    side_ref,
    w_key,
    w_value,
    first_ref,
    second_ref,
    out_hbm,
    gated_ref,
    out_ref,
    sem,
):
    samples, atoms_here, width = query_ref.shape
    device_at = at_ref[0]
    ends = atoms_here * blocks
    starts = outer_starts(atoms_here)
    margin = len(starts[0]) * Q_WIN
    inside = side_ref.shape[1]

    whole = pltpu.make_async_copy(
        inner_ref, out_hbm.at[:, pl.ds(margin, atoms_here - 2 * margin)], sem.at[0]
    )
    whole.start()

    down = core_ref[0] == 0
    first, second = first_ref[...], second_ref[...]
    arrived = (jnp.where(down, second, first), jnp.where(down, first, second))
    count = samples * EDGE
    edges = jnp.concatenate([rows[:count] for rows in arrived], 0)
    edges = dot(edges, beside(w_key, w_value)).astype(BF16).reshape(2, samples, EDGE, 2 * width)

    def joined(side, edge, own):
        return jnp.concatenate([own, edge] if side else [edge, own], 0)

    windows = []
    for side in range(2):
        own = slice(side * (atoms_here - inside), side * (atoms_here - inside) + inside)
        parts = [
            (
                joined(side, edges[side, i, :, :width], own_key_ref[i, own, :]),
                joined(side, edges[side, i, :, width:], own_value_ref[i, own, :]),
            )
            for i in range(samples)
        ]
        near = expand(hot_ref[side], arrived[side][count:], groups)
        near = joined(side, near, side_ref[side])
        for i, start in enumerate(starts[side]):
            cut = slice(i * Q_WIN, i * Q_WIN + K_WIN)
            key_at = iota((heads * Q_WIN, K_WIN), 1) + (device_at * atoms_here + start - EDGE)
            mask = (key_at >= 0) & (key_at < ends)
            pieces = [(keys[cut], values[cut]) for keys, values in parts]
            windows.append((start, pieces, near[cut], pick_ref[side, i], mask))
    attend(heads, windows, query_ref, gate_ref, gated_ref)
    copies = []
    for side in range(2):
        cut = slice(starts[side][0], starts[side][0] + margin)
        for sample in range(samples):
            out_ref[side, sample] = close(sample, cut, gated_ref, open_ref, trans_ref, w_out_ref)
        target = out_hbm.at[:, pl.ds(starts[side][0], margin)]
        copies.append(pltpu.make_async_copy(out_ref.at[side], target, sem.at[1 + side]))
        copies[-1].start()
    for copy in copies:
        copy.wait()
    whole.wait()


def shards(
    atom_single,
    atom_cond,
    pair_cond,
    atom_counts,
    ada_attn_scale,
    ada_attn_shift,
    w_query,
    w_key,
    w_value,
    w_gate,
    w_out,
    attn_gate,
    w_pair,
    ada_trans_scale,
    ada_trans_shift,
    w_swish,
    w_linear,
    w_down,
    trans_gate,
):
    device_at = lax.axis_index("atoms")
    blocks = lax.axis_size("atoms")
    samples, atoms_here, width = atom_single.shape
    tok_here = atom_counts.shape[1]
    heads = w_pair.shape[1]
    groups = tok_here // GROUP
    pairs = lax.axis_size("pair")
    assert pair_cond.shape[0] == lax.axis_size("samp") * tok_here
    at = device_at.astype(jnp.int32).reshape(1)
    pair_at = lax.axis_index("pair").astype(jnp.int32).reshape(1)
    core_at = lax.axis_index("samp").astype(jnp.int32).reshape(1)
    in_hbm = lambda array: pltpu.with_memory_space_constraint(array, pltpu.HBM)
    in_vmem = lambda array: pltpu.with_memory_space_constraint(array, pltpu.VMEM)

    cols = pair_cond.shape[1]
    lanes = heads * GROUP
    wide = (samples, atoms_here, width)
    params = pltpu.CompilerParams(vmem_limit_bytes=VMEM_LIMIT)

    def cost(products):
        return pl.CostEstimate(flops=2 * products, bytes_accessed=4 << 20, transcendentals=0)

    sent = pltpu.VMEM((samples * EDGE + groups * EDGE, lanes), BF16)
    own = pl.pallas_call(
        pair_kernel,
        in_specs=[IN_SMEM] + [IN_HBM] * 2,
        out_specs=IN_VMEM,
        out_shape=pltpu.VMEM((groups, cols, lanes), BF16),
        scratch_shapes=[
            pltpu.VMEM((heads, width), BF16),
            pltpu.VMEM((tok_here, cols, width), BF16),
            pltpu.SemaphoreType.DMA((8 * groups,)),
            pltpu.SemaphoreType.DMA,
        ],
        compiler_params=params,
        cost_estimate=cost(tok_here * cols * width * width * 2),
    )(core_at, *map(in_hbm, (w_pair.T, pair_cond)))
    if pairs == 2:
        swapped = [(0, 1), (1, 0)]
        across = lax.ppermute(own, "pair", swapped)
        diagonal = lax.ppermute(own, ("pair", "samp"), [(0, 3), (1, 2), (2, 1), (3, 0)])
        tiles = (own, lax.ppermute(own, "samp", swapped), across, diagonal)
    else:
        tiles = (lax.all_gather(own, ("pair", "samp")),)

    operands = (
        atom_single,
        atom_cond,
        ada_attn_scale,
        ada_attn_shift,
        w_key,
        w_value,
        w_query,
        w_gate,
    )
    late = (ada_trans_scale, ada_trans_shift, attn_gate, trans_gate, w_swish, w_linear, w_down)
    query, keys, values, gate, opened, trans, near, far = pl.pallas_call(
        project_kernel,
        in_specs=[IN_SMEM] + [IN_VMEM] * len(operands) + [IN_HBM] * len(late),
        out_specs=[IN_VMEM] * 8,
        out_shape=[pltpu.VMEM(wide, BF16)] * 4
        + [pltpu.VMEM((atoms_here, width), BF16), pltpu.VMEM(wide, BF16), sent, sent],
        scratch_shapes=[pltpu.VMEM(weight.shape, BF16) for weight in late]
        + [pltpu.SemaphoreType.DMA((len(late),))],
        compiler_params=params,
        cost_estimate=cost(samples * atoms_here * width * width * 20),
    )(core_at, *map(in_vmem, operands), *map(in_hbm, late))

    operands = (*tiles, near, far, opened)
    first = 3 + len(tiles)
    near, far, opened, held = pl.pallas_call(
        functools.partial(select_kernel, blocks),
        in_specs=[IN_SMEM] * 3 + [IN_VMEM] * len(operands),
        out_specs=[IN_VMEM] * 4,
        out_shape=[
            sent,
            sent,
            pltpu.VMEM((atoms_here, width), BF16),
            pltpu.VMEM((groups * cols, lanes), BF16),
        ],
        input_output_aliases={first: 0, first + 1: 1, first + 2: 2},
        compiler_params=params,
    )(at, pair_at, core_at, *map(in_vmem, operands))

    down = [(2 * i, 2 * (i - 1)) for i in range(1, blocks)] + [(0, 1)]
    up = [(2 * i + 1, 2 * (i + 1) + 1) for i in range(blocks - 1)] + [(2 * blocks - 1, 2 * blocks - 2)]
    cycle = down + up
    first = lax.ppermute(near, ("atoms", "samp"), cycle)
    second = lax.ppermute(far, ("atoms", "samp"), [(target, source) for source, target in cycle])

    margin = -(-EDGE // Q_WIN) * Q_WIN
    inside = margin - Q_WIN + K_WIN - EDGE
    expanded = heads * tok_here
    operands = (query, keys, values, gate, opened, trans, w_out)
    inner, picks, hots, beside_edges = pl.pallas_call(
        functools.partial(inner_kernel, heads, blocks),
        in_specs=[IN_SMEM] + [IN_VMEM] * (2 + len(operands)),
        out_specs=[IN_VMEM] * 4,
        out_shape=[
            pltpu.VMEM((samples, atoms_here - 2 * margin, width), BF16),
            pltpu.VMEM((2, margin // Q_WIN, heads * Q_WIN, expanded), BF16),
            pltpu.VMEM((2, EDGE, EDGE), BF16),
            pltpu.VMEM((2, inside, expanded), BF16),
        ],
        scratch_shapes=[
            pltpu.VMEM((atoms_here, expanded), BF16),
            pltpu.VMEM(wide, BF16),
        ],
        compiler_params=params,
        cost_estimate=cost(samples * atoms_here * width * width * 12),
    )(at, atom_counts, *map(in_vmem, (*operands, held)))

    operands += (inner, picks, hots, beside_edges, w_key, w_value, first, second)
    return pl.pallas_call(
        functools.partial(outer_kernel, heads, blocks, groups),
        in_specs=[IN_SMEM] * 2 + [IN_VMEM] * len(operands),
        out_specs=IN_HBM,
        out_shape=pltpu.HBM(wide, BF16),
        scratch_shapes=[
            pltpu.VMEM(wide, BF16),
            pltpu.VMEM((2, samples, margin, width), BF16),
            pltpu.SemaphoreType.DMA((3,)),
        ],
        compiler_params=params,
        cost_estimate=cost(samples * atoms_here * width * width * 4),
    )(at, core_at, *map(in_vmem, operands))


def solution(mesh):
    return jax.shard_map(
        shards,
        mesh=mesh,
        in_specs=(
            P(("groups", "pair", "samp"), "atoms", None),
            P(("groups", "atoms"), None),
            P(("groups", "pair"), "atoms", None),
            P("groups", None),
        )
        + (P(),) * 15,
        out_specs=P(("groups", "pair", "samp"), "atoms", None),
        check_vma=False,
    )
```

```python
import functools
import math

import jax
import jax.numpy as jnp
from jax import lax
from jax.experimental import pallas as pl
from jax.experimental.pallas import tpu as pltpu
from jax.sharding import PartitionSpec as P

Q_WIN = 32
K_WIN = 128
EDGE = 48
GROUP = 32

EPSILON = 1e-05
MASKED = -1e30
LOG2E = math.log2(math.e)
BF16 = jnp.bfloat16
F32 = jnp.float32
LAST = (((1,), (1,)), ((), ()))
VMEM_LIMIT = 32 << 20
IN_VMEM = pl.BlockSpec(memory_space=pltpu.VMEM)
IN_HBM = pl.BlockSpec(memory_space=pltpu.HBM)
IN_SMEM = pl.BlockSpec(memory_space=pltpu.SMEM)


def dot(a, b):
    return jnp.dot(a, b, preferred_element_type=F32)


def iota(shape, dim):
    return lax.broadcasted_iota(jnp.int32, shape, dim)


def twice(matrix):
    blank = jnp.zeros_like(matrix)
    return jnp.concatenate(
        [jnp.concatenate([matrix, blank], 1), jnp.concatenate([blank, matrix], 1)], 0
    )


def side_by_side(rows):
    half = rows.shape[0] // 2
    return jnp.concatenate([rows[:half], rows[half:]], 1)


def centring(width):
    same = iota((width, width), 0) == iota((width, width), 1)
    return jnp.where(same, 1.0 - 1.0 / width, -1.0 / width).astype(BF16)


def averaging(width):
    return jnp.full((width, width), 1.0 / width, BF16)


def mean_square(centred):
    return jnp.mean(centred * centred, axis=-1, keepdims=True)


def layer_norm(rows):
    width = rows.shape[1]
    both = dot(side_by_side(rows), twice(centring(width)))
    centred = jnp.concatenate([both[:, :width], both[:, width:]], 0)
    return centred * lax.rsqrt(mean_square(centred) + EPSILON)


def sigmoid(values):
    return 0.5 * jnp.tanh(0.5 * values) + 0.5


def attn_norm(cond, single, ada):
    width = single.shape[-1]
    mixed = dot(cond, ada)
    return (sigmoid(mixed[:, :width])[None] * single + mixed[None, :, width:]).astype(BF16)


def pair_kernel(core_ref, w_pair_hbm, pair_hbm, tile_ref, w_pair_ref, pair_ref, pair_sem, sem):
    rows, cols, width = pair_ref.shape
    heads = w_pair_ref.shape[0]
    group = GROUP
    lanes = heads * group
    half = group // 2
    row_start = core_ref[0] * rows

    def pair_copy(i):
        source = pair_hbm.at[pl.ds(row_start + i * group, group)]
        return pltpu.make_async_copy(source, pair_ref.at[pl.ds(i * group, group)], pair_sem.at[i])

    w_pair_copy = pltpu.make_async_copy(w_pair_hbm, w_pair_ref, sem)
    w_pair_copy.start()
    for i in range(rows // group):
        pair_copy(i).start()
    w_pair_copy.wait()
    w_pair = w_pair_ref[...].astype(F32)
    spread = jnp.concatenate(
        [jnp.broadcast_to(w_pair[h : h + 1], (group, width)) for h in range(heads)], 0
    )
    mix = twice(spread.T.astype(BF16))
    centre = twice(centring(width))
    slot = iota((cols, lanes), 1) % group

    chunks = []
    for chunk in range(rows // group):
        pair_copy(chunk).wait()
        pair = pair_ref[chunk * group : (chunk + 1) * group].reshape(group * cols, width)
        chunks.append(dot(side_by_side(pair), centre).astype(BF16))
    mixes = [dot(centred, mix).reshape(half, cols, 2 * lanes) for centred in chunks]
    squares = [centred[:, :width] * centred[:, :width] for centred in chunks]
    averages = [
        dot(jnp.concatenate(squares[i : i + 2], 1), twice(averaging(width)))
        for i in range(0, len(squares), 2)
    ]
    for chunk, (centred, mixed) in enumerate(zip(chunks, mixes)):
        pick = slice(chunk % 2 * width, (chunk % 2 + 1) * width)
        variances = [
            averages[chunk // 2][:, pick].reshape(half, cols, width),
            mean_square(centred[:, width:].astype(F32)).reshape(half, cols, 1),
        ]
        total = jnp.zeros((cols, lanes), F32)
        spread_out = jnp.zeros((cols, lanes), F32)
        for i in range(group):
            side = slice(i // half * lanes, (i // half + 1) * lanes)
            total = jnp.where(slot == i, mixed[i % half, :, side], total)
            spread_out = jnp.where(slot == i, variances[i // half][i % half], spread_out)
        tile_ref[chunk] = (total * lax.rsqrt(spread_out + EPSILON)).astype(BF16)


def beside(first, second):
    return jnp.concatenate([first[...], second[...]], 1)


def project_kernel(
    core_ref,
    single_ref,
    cond_ref,
    ada_attn_scale,
    ada_attn_shift,
    w_key,
    w_value,
    w_query,
    w_gate,
    *refs,
):
    late_hbm, refs = refs[:7], refs[7:]
    query_ref, key_ref, value_ref, gate_ref, open_ref, trans_ref, near_ref, far_ref = refs[:8]
    late_refs, sem = refs[8:15], refs[15]
    ada_trans_scale, ada_trans_shift, attn_gate, trans_gate, w_swish, w_linear, w_down = late_refs
    samples, atoms_here, width = single_ref.shape
    copies = [
        pltpu.make_async_copy(source, target, sem.at[i])
        for i, (source, target) in enumerate(zip(late_hbm, late_refs))
    ]
    for copy in copies:
        copy.start()

    cond = layer_norm(cond_ref[...]).astype(BF16)
    single = layer_norm(single_ref[...].reshape(-1, width)).reshape(samples, atoms_here, width)
    normed = attn_norm(cond, single, beside(ada_attn_scale, ada_attn_shift))
    down = core_ref[0] == 0
    for sample in range(samples):
        cut = slice(sample * EDGE, (sample + 1) * EDGE)
        head, tail = normed[sample, :EDGE], normed[sample, atoms_here - EDGE :]
        near_ref[cut, :] = jnp.where(down, head, tail)
        far_ref[cut, :] = jnp.where(down, tail, head)
    normed = normed.reshape(-1, width)
    both = dot(normed, beside(w_key, w_value)).astype(BF16).reshape(samples, -1, 2 * width)
    key_ref[...] = both[:, :, :width]
    value_ref[...] = both[:, :, width:]
    both = dot(normed, beside(w_query, w_gate)).reshape(samples, -1, 2 * width)
    query_ref[...] = both[:, :, :width].astype(BF16)
    gate_ref[...] = sigmoid(both[:, :, width:]).astype(BF16)

    for copy in copies:
        copy.wait()
    gates = dot(cond, beside(attn_gate, trans_gate))
    open_ref[...] = sigmoid(gates[:, :width]).astype(BF16)
    normed = attn_norm(cond, single, beside(ada_trans_scale, ada_trans_shift)).reshape(-1, width)
    swish = dot(normed, w_swish[...])
    hidden = (swish * sigmoid(swish) * dot(normed, w_linear[...])).astype(BF16)
    down = dot(hidden, w_down[...]).reshape(samples, -1, width)
    trans_ref[...] = (sigmoid(gates[:, width:])[None] * down).astype(BF16)


def tile_of(refs, place, row_block):
    if len(refs) == 1:
        return refs[0][row_block]
    pair_at, core_at = place
    owners = 2
    mine, theirs, across, diagonal = [ref[...] for ref in refs]
    near = jnp.where(row_block % owners == core_at, mine, theirs)
    far = jnp.where(row_block % owners == core_at, across, diagonal)
    return jnp.where(row_block // owners == pair_at, near, far)


def select_kernel(blocks, at_ref, pair_ref, core_ref, *refs):
    *tile_refs, _, __, ___, near_ref, far_ref, ____, held_ref = refs
    groups, cols, lanes = tile_refs[0].shape[-3:]
    rows = groups * EDGE
    device_at, place = at_ref[0], (pair_ref[0], core_ref[0])
    for send_ref, core in ((near_ref, 1), (far_ref, 0)):
        above = core_ref[0] == core
        beside = jnp.where(above, device_at + 1, device_at - 1)
        tile = tile_of(tile_refs, place, jnp.clip(beside, 0, blocks - 1))
        tile = jnp.where(above, tile[:, cols - EDGE :], tile[:, :EDGE])
        send_ref[send_ref.shape[0] - rows :, :] = tile.reshape(rows, lanes)
    held_ref[...] = tile_of(tile_refs, place, device_at).reshape(groups * cols, lanes)


def bounds(counts_ref, block, token):
    tok_here = counts_ref.shape[1]
    counts = counts_ref[pl.ds(block, 1), :].astype(F32).astype(BF16)
    counts = jnp.broadcast_to(counts, (8, tok_here))
    before = iota((tok_here, token.shape[1]), 0)
    first = dot(counts, (before < token).astype(BF16))[:1]
    last = dot(counts, (before <= token).astype(BF16))[:1]
    return first.astype(jnp.int32), last.astype(jnp.int32)


def one_hot(reach, offset, count):
    first, last = reach
    position = iota((count, first.shape[1]), 0) + offset
    return ((first <= position) & (position < last)).astype(F32).astype(BF16)


def expand(hot, tile, groups):
    tile = tile.reshape(groups, -1, tile.shape[-1])
    tile = jnp.concatenate([tile[part] for part in range(groups)], 1)
    return dot(hot, tile).astype(BF16)


def head_mask(heads, lanes):
    rows = heads * Q_WIN
    lane_head = iota((rows, lanes), 1) // GROUP % heads
    row_head = iota((rows, lanes), 0) // Q_WIN
    return (lane_head == row_head).astype(F32).astype(BF16)


def picks_of(heads, reach, starts):
    same_head = head_mask(heads, reach[0].shape[1])
    return [
        jnp.concatenate([one_hot(reach, start, Q_WIN)] * heads, 0) * same_head for start in starts
    ]


def attend(heads, windows, query_ref, gate_ref, gated_ref):
    samples, _, width = query_ref.shape
    head_dim = width // heads
    rows = heads * Q_WIN
    own_head = iota((rows, width), 1) // head_dim == iota((rows, width), 0) // Q_WIN
    own_head = own_head.astype(F32).astype(BF16)
    channel_head = iota((Q_WIN, 2 * width), 1) % width // head_dim
    ones = jnp.ones((K_WIN, width), BF16)
    scaling = LOG2E / math.sqrt(head_dim)

    biases = []
    for _, _, near, pick, mask in windows:
        bias = lax.dot_general(pick, near, LAST, preferred_element_type=F32) * LOG2E
        biases.append(bias if mask is None else jnp.where(mask, bias, MASKED))
    units = [(sample, i) for i in range(len(windows)) for sample in range(samples)]
    scores = []
    for first in range(0, len(units), 2):
        couple = units[first : first + 2]
        queries, keys = [], []
        for sample, i in couple:
            query = query_ref[sample, pl.ds(windows[i][0], Q_WIN), :]
            queries.append(jnp.concatenate([query] * heads, 0) * own_head)
            keys.append(windows[i][1][sample][0])
        if len(couple) == 2:
            blank = jnp.zeros_like(keys[0])
            keys = [jnp.concatenate([keys[0], blank], 1), jnp.concatenate([blank, keys[1]], 1)]
        product = lax.dot_general(
            jnp.concatenate(queries, 1),
            jnp.concatenate(keys, 0),
            LAST,
            preferred_element_type=F32,
        )
        for j, (_, i) in enumerate(couple):
            scores.append(product[:, j * K_WIN : (j + 1) * K_WIN] * scaling + biases[i])
    tops = [jnp.max(score, axis=-1, keepdims=True) for score in scores]
    raised = [jnp.exp2(score - top).astype(BF16) for score, top in zip(scores, tops)]
    for (sample, i), weight in zip(units, raised):
        values = windows[i][1][sample][1]
        mixed = dot(weight, jnp.concatenate([values, ones], 1))
        picked = mixed[:Q_WIN]
        for head in range(1, heads):
            picked = jnp.where(
                channel_head == head, mixed[head * Q_WIN : (head + 1) * Q_WIN], picked
            )
        attended = picked[:, :width] * pl.reciprocal(picked[:, width:], approx=True)
        at = pl.ds(windows[i][0], Q_WIN)
        gate = gate_ref[sample, at, :].astype(F32)
        gated_ref[sample, at, :] = (gate * attended).astype(BF16)


def close(sample, cut, gated_ref, open_ref, trans_ref, w_out_ref):
    mixed = dot(gated_ref[sample, cut, :], w_out_ref[...])
    opened, trans = open_ref[cut, :].astype(F32), trans_ref[sample, cut, :].astype(F32)
    return (opened * mixed + trans).astype(BF16)


def row_tokens(heads, tok_here):
    lane = iota((tok_here, heads * tok_here), 1)
    return lane // (heads * GROUP) * GROUP + lane % GROUP


def outer_starts(atoms_here):
    skip = -(-EDGE // Q_WIN)
    return [
        [side * (atoms_here - skip * Q_WIN) + i * Q_WIN for i in range(skip)] for side in range(2)
    ]


def inner_kernel(
    heads,
    blocks,
    at_ref,
    counts_ref,
    query_ref,
    key_ref,
    value_ref,
    gate_ref,
    open_ref,
    trans_ref,
    w_out_ref,
    held_ref,
    out_ref,
    pick_ref,
    hot_ref,
    side_ref,
    near_ref,
    gated_ref,
):
    samples, atoms_here, width = query_ref.shape
    tok_here = counts_ref.shape[1]
    device_at = at_ref[0]
    hot = one_hot(
        bounds(counts_ref, device_at, iota((tok_here, tok_here), 1)), 0, atoms_here
    )
    near_ref[...] = expand(hot, held_ref[...], tok_here // GROUP)
    reach = bounds(counts_ref, device_at, row_tokens(heads, tok_here))
    skip = -(-EDGE // Q_WIN)
    starts = [window * Q_WIN for window in range(skip, atoms_here // Q_WIN - skip)]
    windows = []
    for start, pick in zip(starts, picks_of(heads, reach, starts)):
        cut = slice(start - EDGE, start - EDGE + K_WIN)
        parts = [(key_ref[i, cut, :], value_ref[i, cut, :]) for i in range(samples)]
        windows.append((start, parts, near_ref[cut, :], pick, None))
    attend(heads, windows, query_ref, gate_ref, gated_ref)

    cut = slice(starts[0], starts[-1] + Q_WIN)
    for sample in range(samples):
        out_ref[sample] = close(sample, cut, gated_ref, open_ref, trans_ref, w_out_ref)

    inside = side_ref.shape[1]
    sides = (
        (jnp.maximum(device_at - 1, 0), atoms_here - EDGE, tok_here - EDGE, 0),
        (jnp.minimum(device_at + 1, blocks - 1), 0, 0, atoms_here - inside),
    )
    for side, (block, offset, token, own_start) in enumerate(sides):
        nearest = bounds(counts_ref, block, iota((tok_here, EDGE), 1) + token)
        hot_ref[side] = one_hot(nearest, offset, EDGE)
        side_ref[side] = near_ref[own_start : own_start + inside, :]
        for i, pick in enumerate(picks_of(heads, reach, outer_starts(atoms_here)[side])):
            pick_ref[side, i] = pick


def outer_kernel(
    heads,
    blocks,
    groups,
    at_ref,
    core_ref,
    query_ref,
    own_key_ref,
    own_value_ref,
    gate_ref,
    open_ref,
    trans_ref,
    w_out_ref,
    inner_ref,
    pick_ref,
    hot_ref,
    side_ref,
    w_key,
    w_value,
    first_ref,
    second_ref,
    out_hbm,
    gated_ref,
    out_ref,
    sem,
):
    samples, atoms_here, width = query_ref.shape
    device_at = at_ref[0]
    ends = atoms_here * blocks
    starts = outer_starts(atoms_here)
    margin = len(starts[0]) * Q_WIN
    inside = side_ref.shape[1]

    whole = pltpu.make_async_copy(
        inner_ref, out_hbm.at[:, pl.ds(margin, atoms_here - 2 * margin)], sem.at[0]
    )
    whole.start()

    down = core_ref[0] == 0
    first, second = first_ref[...], second_ref[...]
    arrived = (jnp.where(down, second, first), jnp.where(down, first, second))
    count = samples * EDGE
    edges = jnp.concatenate([rows[:count] for rows in arrived], 0)
    edges = dot(edges, beside(w_key, w_value)).astype(BF16).reshape(2, samples, EDGE, 2 * width)

    def joined(side, edge, own):
        return jnp.concatenate([own, edge] if side else [edge, own], 0)

    windows = []
    for side in range(2):
        own = slice(side * (atoms_here - inside), side * (atoms_here - inside) + inside)
        parts = [
            (
                joined(side, edges[side, i, :, :width], own_key_ref[i, own, :]),
                joined(side, edges[side, i, :, width:], own_value_ref[i, own, :]),
            )
            for i in range(samples)
        ]
        near = expand(hot_ref[side], arrived[side][count:], groups)
        near = joined(side, near, side_ref[side])
        for i, start in enumerate(starts[side]):
            cut = slice(i * Q_WIN, i * Q_WIN + K_WIN)
            key_at = iota((heads * Q_WIN, K_WIN), 1) + (device_at * atoms_here + start - EDGE)
            mask = (key_at >= 0) & (key_at < ends)
            pieces = [(keys[cut], values[cut]) for keys, values in parts]
            windows.append((start, pieces, near[cut], pick_ref[side, i], mask))
    attend(heads, windows, query_ref, gate_ref, gated_ref)
    copies = []
    for side in range(2):
        cut = slice(starts[side][0], starts[side][0] + margin)
        for sample in range(samples):
            out_ref[side, sample] = close(sample, cut, gated_ref, open_ref, trans_ref, w_out_ref)
        target = out_hbm.at[:, pl.ds(starts[side][0], margin)]
        copies.append(pltpu.make_async_copy(out_ref.at[side], target, sem.at[1 + side]))
        copies[-1].start()
    for copy in copies:
        copy.wait()
    whole.wait()


def shards(
    atom_single,
    atom_cond,
    pair_cond,
    atom_counts,
    ada_attn_scale,
    ada_attn_shift,
    w_query,
    w_key,
    w_value,
    w_gate,
    w_out,
    attn_gate,
    w_pair,
    ada_trans_scale,
    ada_trans_shift,
    w_swish,
    w_linear,
    w_down,
    trans_gate,
):
    device_at = lax.axis_index("atoms")
    blocks = lax.axis_size("atoms")
    samples, atoms_here, width = atom_single.shape
    tok_here = atom_counts.shape[1]
    heads = w_pair.shape[1]
    groups = tok_here // GROUP
    pairs = lax.axis_size("pair")
    assert pair_cond.shape[0] == lax.axis_size("samp") * tok_here
    at = device_at.astype(jnp.int32).reshape(1)
    pair_at = lax.axis_index("pair").astype(jnp.int32).reshape(1)
    core_at = lax.axis_index("samp").astype(jnp.int32).reshape(1)
    in_hbm = lambda array: pltpu.with_memory_space_constraint(array, pltpu.HBM)
    in_vmem = lambda array: pltpu.with_memory_space_constraint(array, pltpu.VMEM)

    cols = pair_cond.shape[1]
    lanes = heads * GROUP
    wide = (samples, atoms_here, width)
    params = pltpu.CompilerParams(vmem_limit_bytes=VMEM_LIMIT)

    def cost(products):
        return pl.CostEstimate(flops=2 * products, bytes_accessed=4 << 20, transcendentals=0)

    sent = pltpu.VMEM((samples * EDGE + groups * EDGE, lanes), BF16)
    own = pl.pallas_call(
        pair_kernel,
        in_specs=[IN_SMEM] + [IN_HBM] * 2,
        out_specs=IN_VMEM,
        out_shape=pltpu.VMEM((groups, cols, lanes), BF16),
        scratch_shapes=[
            pltpu.VMEM((heads, width), BF16),
            pltpu.VMEM((tok_here, cols, width), BF16),
            pltpu.SemaphoreType.DMA((groups,)),
            pltpu.SemaphoreType.DMA,
        ],
        compiler_params=params,
        cost_estimate=cost(tok_here * cols * width * width * 2),
    )(core_at, *map(in_hbm, (w_pair.T, pair_cond)))
    if pairs == 2:
        swapped = [(0, 1), (1, 0)]
        across = lax.ppermute(own, "pair", swapped)
        diagonal = lax.ppermute(own, ("pair", "samp"), [(0, 3), (1, 2), (2, 1), (3, 0)])
        tiles = (own, lax.ppermute(own, "samp", swapped), across, diagonal)
    else:
        tiles = (lax.all_gather(own, ("pair", "samp")),)

    operands = (
        atom_single,
        atom_cond,
        ada_attn_scale,
        ada_attn_shift,
        w_key,
        w_value,
        w_query,
        w_gate,
    )
    late = (ada_trans_scale, ada_trans_shift, attn_gate, trans_gate, w_swish, w_linear, w_down)
    query, keys, values, gate, opened, trans, near, far = pl.pallas_call(
        project_kernel,
        in_specs=[IN_SMEM] + [IN_VMEM] * len(operands) + [IN_HBM] * len(late),
        out_specs=[IN_VMEM] * 8,
        out_shape=[pltpu.VMEM(wide, BF16)] * 4
        + [pltpu.VMEM((atoms_here, width), BF16), pltpu.VMEM(wide, BF16), sent, sent],
        scratch_shapes=[pltpu.VMEM(weight.shape, BF16) for weight in late]
        + [pltpu.SemaphoreType.DMA((len(late),))],
        compiler_params=params,
        cost_estimate=cost(samples * atoms_here * width * width * 20),
    )(core_at, *map(in_vmem, operands), *map(in_hbm, late))

    operands = (*tiles, near, far, opened)
    first = 3 + len(tiles)
    near, far, opened, held = pl.pallas_call(
        functools.partial(select_kernel, blocks),
        in_specs=[IN_SMEM] * 3 + [IN_VMEM] * len(operands),
        out_specs=[IN_VMEM] * 4,
        out_shape=[
            sent,
            sent,
            pltpu.VMEM((atoms_here, width), BF16),
            pltpu.VMEM((groups * cols, lanes), BF16),
        ],
        input_output_aliases={first: 0, first + 1: 1, first + 2: 2},
        compiler_params=params,
    )(at, pair_at, core_at, *map(in_vmem, operands))

    down = [(2 * i, 2 * (i - 1)) for i in range(1, blocks)] + [(0, 1)]
    up = [(2 * i + 1, 2 * (i + 1) + 1) for i in range(blocks - 1)] + [(2 * blocks - 1, 2 * blocks - 2)]
    cycle = down + up
    first = lax.ppermute(near, ("atoms", "samp"), cycle)
    second = lax.ppermute(far, ("atoms", "samp"), [(target, source) for source, target in cycle])

    margin = -(-EDGE // Q_WIN) * Q_WIN
    inside = margin - Q_WIN + K_WIN - EDGE
    expanded = heads * tok_here
    operands = (query, keys, values, gate, opened, trans, w_out)
    inner, picks, hots, beside_edges = pl.pallas_call(
        functools.partial(inner_kernel, heads, blocks),
        in_specs=[IN_SMEM] + [IN_VMEM] * (2 + len(operands)),
        out_specs=[IN_VMEM] * 4,
        out_shape=[
            pltpu.VMEM((samples, atoms_here - 2 * margin, width), BF16),
            pltpu.VMEM((2, margin // Q_WIN, heads * Q_WIN, expanded), BF16),
            pltpu.VMEM((2, EDGE, EDGE), BF16),
            pltpu.VMEM((2, inside, expanded), BF16),
        ],
        scratch_shapes=[
            pltpu.VMEM((atoms_here, expanded), BF16),
            pltpu.VMEM(wide, BF16),
        ],
        compiler_params=params,
        cost_estimate=cost(samples * atoms_here * width * width * 12),
    )(at, atom_counts, *map(in_vmem, (*operands, held)))

    operands += (inner, picks, hots, beside_edges, w_key, w_value, first, second)
    return pl.pallas_call(
        functools.partial(outer_kernel, heads, blocks, groups),
        in_specs=[IN_SMEM] * 2 + [IN_VMEM] * len(operands),
        out_specs=IN_HBM,
        out_shape=pltpu.HBM(wide, BF16),
        scratch_shapes=[
            pltpu.VMEM(wide, BF16),
            pltpu.VMEM((2, samples, margin, width), BF16),
            pltpu.SemaphoreType.DMA((3,)),
        ],
        compiler_params=params,
        cost_estimate=cost(samples * atoms_here * width * width * 4),
    )(at, core_at, *map(in_vmem, operands))


def solution(mesh):
    return jax.shard_map(
        shards,
        mesh=mesh,
        in_specs=(
            P(("groups", "pair", "samp"), "atoms", None),
            P(("groups", "atoms"), None),
            P(("groups", "pair"), "atoms", None),
            P("groups", None),
        )
        + (P(),) * 15,
        out_specs=P(("groups", "pair", "samp"), "atoms", None),
        check_vma=False,
    )
```

```python
import functools
import math

import jax
import jax.numpy as jnp
from jax import lax
from jax.experimental import pallas as pl
from jax.experimental.pallas import tpu as pltpu
from jax.sharding import PartitionSpec as P

Q_WIN = 32
K_WIN = 128
EDGE = 48
GROUP = 32

EPSILON = 1e-05
MASKED = -1e30
LOG2E = math.log2(math.e)
BF16 = jnp.bfloat16
F32 = jnp.float32
LAST = (((1,), (1,)), ((), ()))
VMEM_LIMIT = 32 << 20
IN_VMEM = pl.BlockSpec(memory_space=pltpu.VMEM)
IN_HBM = pl.BlockSpec(memory_space=pltpu.HBM)
IN_SMEM = pl.BlockSpec(memory_space=pltpu.SMEM)


def dot(a, b):
    return jnp.dot(a, b, preferred_element_type=F32)


def iota(shape, dim):
    return lax.broadcasted_iota(jnp.int32, shape, dim)


def twice(matrix):
    blank = jnp.zeros_like(matrix)
    return jnp.concatenate(
        [jnp.concatenate([matrix, blank], 1), jnp.concatenate([blank, matrix], 1)], 0
    )


def side_by_side(rows):
    half = rows.shape[0] // 2
    return jnp.concatenate([rows[:half], rows[half:]], 1)


def centring(width):
    same = iota((width, width), 0) == iota((width, width), 1)
    return jnp.where(same, 1.0 - 1.0 / width, -1.0 / width).astype(BF16)


def mean_square(centred):
    return jnp.mean(centred * centred, axis=-1, keepdims=True)


def layer_norm(rows):
    width = rows.shape[1]
    both = dot(side_by_side(rows), twice(centring(width)))
    centred = jnp.concatenate([both[:, :width], both[:, width:]], 0)
    return centred * lax.rsqrt(mean_square(centred) + EPSILON)


def sigmoid(values):
    return 0.5 * jnp.tanh(0.5 * values) + 0.5


def attn_norm(cond, single, ada):
    width = single.shape[-1]
    mixed = dot(cond, ada)
    return (sigmoid(mixed[:, :width])[None] * single + mixed[None, :, width:]).astype(BF16)


def pair_kernel(core_ref, w_pair_hbm, pair_hbm, tile_ref, w_pair_ref, pair_ref, pair_sem, sem):
    rows, cols, width = pair_ref.shape
    heads = w_pair_ref.shape[0]
    group = GROUP
    lanes = heads * group
    half = group // 2
    row_start = core_ref[0] * rows

    def pair_copy(i):
        source = pair_hbm.at[pl.ds(row_start + i * group, group)]
        return pltpu.make_async_copy(source, pair_ref.at[pl.ds(i * group, group)], pair_sem.at[i])

    w_pair_copy = pltpu.make_async_copy(w_pair_hbm, w_pair_ref, sem)
    w_pair_copy.start()
    for i in range(rows // group):
        pair_copy(i).start()
    w_pair_copy.wait()
    w_pair = w_pair_ref[...].astype(F32)
    spread = jnp.concatenate(
        [jnp.broadcast_to(w_pair[h : h + 1], (group, width)) for h in range(heads)], 0
    )
    mix = twice(spread.T.astype(BF16))
    centre = twice(centring(width))
    slot = iota((cols, lanes), 1) % group

    chunks = []
    for chunk in range(rows // group):
        pair_copy(chunk).wait()
        pair = pair_ref[chunk * group : (chunk + 1) * group].reshape(group * cols, width)
        chunks.append(dot(side_by_side(pair), centre).astype(BF16))
    mixes = [dot(centred, mix).reshape(half, cols, 2 * lanes) for centred in chunks]
    for chunk, (centred, mixed) in enumerate(zip(chunks, mixes)):
        variances = [
            mean_square(centred[:, part * width : (part + 1) * width].astype(F32))
            for part in range(2)
        ]
        variances = [variance.reshape(half, cols, 1) for variance in variances]
        total = jnp.zeros((cols, lanes), F32)
        spread_out = jnp.zeros((cols, lanes), F32)
        for i in range(group):
            side = slice(i // half * lanes, (i // half + 1) * lanes)
            total = jnp.where(slot == i, mixed[i % half, :, side], total)
            spread_out = jnp.where(slot == i, variances[i // half][i % half], spread_out)
        tile_ref[chunk] = (total * lax.rsqrt(spread_out + EPSILON)).astype(BF16)


def beside(first, second):
    return jnp.concatenate([first[...], second[...]], 1)


def project_kernel(
    core_ref,
    single_ref,
    cond_ref,
    ada_attn_scale,
    ada_attn_shift,
    w_key,
    w_value,
    w_query,
    w_gate,
    *refs,
):
    late_hbm, refs = refs[:7], refs[7:]
    query_ref, key_ref, value_ref, gate_ref, open_ref, trans_ref, near_ref, far_ref = refs[:8]
    late_refs, sem = refs[8:15], refs[15]
    ada_trans_scale, ada_trans_shift, attn_gate, trans_gate, w_swish, w_linear, w_down = late_refs
    samples, atoms_here, width = single_ref.shape
    copies = [
        pltpu.make_async_copy(source, target, sem.at[i])
        for i, (source, target) in enumerate(zip(late_hbm, late_refs))
    ]
    for copy in copies:
        copy.start()

    cond = layer_norm(cond_ref[...]).astype(BF16)
    single = layer_norm(single_ref[...].reshape(-1, width)).reshape(samples, atoms_here, width)
    normed = attn_norm(cond, single, beside(ada_attn_scale, ada_attn_shift))
    down = core_ref[0] == 0
    for sample in range(samples):
        cut = slice(sample * EDGE, (sample + 1) * EDGE)
        head, tail = normed[sample, :EDGE], normed[sample, atoms_here - EDGE :]
        near_ref[cut, :] = jnp.where(down, head, tail)
        far_ref[cut, :] = jnp.where(down, tail, head)
    normed = normed.reshape(-1, width)
    both = dot(normed, beside(w_key, w_value)).astype(BF16).reshape(samples, -1, 2 * width)
    key_ref[...] = both[:, :, :width]
    value_ref[...] = both[:, :, width:]
    both = dot(normed, beside(w_query, w_gate)).reshape(samples, -1, 2 * width)
    query_ref[...] = both[:, :, :width].astype(BF16)
    gate_ref[...] = sigmoid(both[:, :, width:]).astype(BF16)

    for copy in copies:
        copy.wait()
    gates = dot(cond, beside(attn_gate, trans_gate))
    open_ref[...] = sigmoid(gates[:, :width]).astype(BF16)
    normed = attn_norm(cond, single, beside(ada_trans_scale, ada_trans_shift)).reshape(-1, width)
    swish = dot(normed, w_swish[...])
    hidden = (swish * sigmoid(swish) * dot(normed, w_linear[...])).astype(BF16)
    down = dot(hidden, w_down[...]).reshape(samples, -1, width)
    trans_ref[...] = (sigmoid(gates[:, width:])[None] * down).astype(BF16)


def tile_of(refs, place, row_block):
    if len(refs) == 1:
        return refs[0][row_block]
    pair_at, core_at = place
    owners = 2
    mine, theirs, diagonal, across = [ref[...] for ref in refs]
    near = jnp.where(row_block % owners == core_at, mine, theirs)
    far = jnp.where(row_block % owners == core_at, across, diagonal)
    return jnp.where(row_block // owners == pair_at, near, far)


def select_kernel(blocks, at_ref, pair_ref, core_ref, *refs):
    *tile_refs, _, __, ___, near_ref, far_ref, ____, held_ref = refs
    groups, cols, lanes = tile_refs[0].shape[-3:]
    rows = groups * EDGE
    device_at, place = at_ref[0], (pair_ref[0], core_ref[0])
    for send_ref, core in ((near_ref, 1), (far_ref, 0)):
        above = core_ref[0] == core
        beside = jnp.where(above, device_at + 1, device_at - 1)
        tile = tile_of(tile_refs, place, jnp.clip(beside, 0, blocks - 1))
        tile = jnp.where(above, tile[:, cols - EDGE :], tile[:, :EDGE])
        send_ref[send_ref.shape[0] - rows :, :] = tile.reshape(rows, lanes)
    held_ref[...] = tile_of(tile_refs, place, device_at).reshape(groups * cols, lanes)


def bounds(counts_ref, block, token):
    tok_here = counts_ref.shape[1]
    counts = counts_ref[pl.ds(block, 1), :].astype(F32).astype(BF16)
    counts = jnp.broadcast_to(counts, (8, tok_here))
    before = iota((tok_here, token.shape[1]), 0)
    first = dot(counts, (before < token).astype(BF16))[:1]
    last = dot(counts, (before <= token).astype(BF16))[:1]
    return first.astype(jnp.int32), last.astype(jnp.int32)


def one_hot(reach, offset, count):
    first, last = reach
    position = iota((count, first.shape[1]), 0) + offset
    return ((first <= position) & (position < last)).astype(F32).astype(BF16)


def expand(hot, tile, groups):
    tile = tile.reshape(groups, -1, tile.shape[-1])
    tile = jnp.concatenate([tile[part] for part in range(groups)], 1)
    return dot(hot, tile).astype(BF16)


def head_mask(heads, lanes):
    rows = heads * Q_WIN
    lane_head = iota((rows, lanes), 1) // GROUP % heads
    row_head = iota((rows, lanes), 0) // Q_WIN
    return (lane_head == row_head).astype(F32).astype(BF16)


def picks_of(heads, reach, starts):
    same_head = head_mask(heads, reach[0].shape[1])
    return [
        jnp.concatenate([one_hot(reach, start, Q_WIN)] * heads, 0) * same_head for start in starts
    ]


def attend(heads, windows, query_ref, gate_ref, gated_ref):
    samples, _, width = query_ref.shape
    head_dim = width // heads
    rows = heads * Q_WIN
    own_head = iota((rows, width), 1) // head_dim == iota((rows, width), 0) // Q_WIN
    own_head = own_head.astype(F32).astype(BF16)
    channel_head = iota((Q_WIN, 2 * width), 1) % width // head_dim
    ones = jnp.ones((K_WIN, width), BF16)
    scaling = LOG2E / math.sqrt(head_dim)

    biases = []
    for _, _, near, pick, mask in windows:
        bias = lax.dot_general(pick, near, LAST, preferred_element_type=F32) * LOG2E
        biases.append(bias if mask is None else jnp.where(mask, bias, MASKED))
    units = [(sample, i) for i in range(len(windows)) for sample in range(samples)]
    scores = []
    for first in range(0, len(units), 2):
        couple = units[first : first + 2]
        queries, keys = [], []
        for sample, i in couple:
            query = query_ref[sample, pl.ds(windows[i][0], Q_WIN), :]
            queries.append(jnp.concatenate([query] * heads, 0) * own_head)
            keys.append(windows[i][1][sample][0])
        if len(couple) == 2:
            blank = jnp.zeros_like(keys[0])
            keys = [jnp.concatenate([keys[0], blank], 1), jnp.concatenate([blank, keys[1]], 1)]
        product = lax.dot_general(
            jnp.concatenate(queries, 1),
            jnp.concatenate(keys, 0),
            LAST,
            preferred_element_type=F32,
        )
        for j, (_, i) in enumerate(couple):
            scores.append(product[:, j * K_WIN : (j + 1) * K_WIN] * scaling + biases[i])
    tops = [jnp.max(score, axis=-1, keepdims=True) for score in scores]
    raised = [jnp.exp2(score - top).astype(BF16) for score, top in zip(scores, tops)]
    for (sample, i), weight in zip(units, raised):
        values = windows[i][1][sample][1]
        mixed = dot(weight, jnp.concatenate([values, ones], 1))
        picked = mixed[:Q_WIN]
        for head in range(1, heads):
            picked = jnp.where(
                channel_head == head, mixed[head * Q_WIN : (head + 1) * Q_WIN], picked
            )
        attended = picked[:, :width] * pl.reciprocal(picked[:, width:], approx=True)
        at = pl.ds(windows[i][0], Q_WIN)
        gate = gate_ref[sample, at, :].astype(F32)
        gated_ref[sample, at, :] = (gate * attended).astype(BF16)


def close(sample, cut, gated_ref, open_ref, trans_ref, w_out_ref):
    mixed = dot(gated_ref[sample, cut, :], w_out_ref[...])
    opened, trans = open_ref[cut, :].astype(F32), trans_ref[sample, cut, :].astype(F32)
    return (opened * mixed + trans).astype(BF16)


def row_tokens(heads, tok_here):
    lane = iota((tok_here, heads * tok_here), 1)
    return lane // (heads * GROUP) * GROUP + lane % GROUP


def outer_starts(atoms_here):
    skip = -(-EDGE // Q_WIN)
    return [
        [side * (atoms_here - skip * Q_WIN) + i * Q_WIN for i in range(skip)] for side in range(2)
    ]


def inner_kernel(
    heads,
    blocks,
    at_ref,
    counts_ref,
    query_ref,
    key_ref,
    value_ref,
    gate_ref,
    open_ref,
    trans_ref,
    w_out_ref,
    held_ref,
    out_ref,
    pick_ref,
    hot_ref,
    side_ref,
    near_ref,
    gated_ref,
):
    samples, atoms_here, width = query_ref.shape
    tok_here = counts_ref.shape[1]
    device_at = at_ref[0]
    hot = one_hot(
        bounds(counts_ref, device_at, iota((tok_here, tok_here), 1)), 0, atoms_here
    )
    near_ref[...] = expand(hot, held_ref[...], tok_here // GROUP)
    reach = bounds(counts_ref, device_at, row_tokens(heads, tok_here))
    skip = -(-EDGE // Q_WIN)
    starts = [window * Q_WIN for window in range(skip, atoms_here // Q_WIN - skip)]
    windows = []
    for start, pick in zip(starts, picks_of(heads, reach, starts)):
        cut = slice(start - EDGE, start - EDGE + K_WIN)
        parts = [(key_ref[i, cut, :], value_ref[i, cut, :]) for i in range(samples)]
        windows.append((start, parts, near_ref[cut, :], pick, None))
    attend(heads, windows, query_ref, gate_ref, gated_ref)

    cut = slice(starts[0], starts[-1] + Q_WIN)
    for sample in range(samples):
        out_ref[sample] = close(sample, cut, gated_ref, open_ref, trans_ref, w_out_ref)

    inside = side_ref.shape[1]
    sides = (
        (jnp.maximum(device_at - 1, 0), atoms_here - EDGE, tok_here - EDGE, 0),
        (jnp.minimum(device_at + 1, blocks - 1), 0, 0, atoms_here - inside),
    )
    for side, (block, offset, token, own_start) in enumerate(sides):
        nearest = bounds(counts_ref, block, iota((tok_here, EDGE), 1) + token)
        hot_ref[side] = one_hot(nearest, offset, EDGE)
        side_ref[side] = near_ref[own_start : own_start + inside, :]
        for i, pick in enumerate(picks_of(heads, reach, outer_starts(atoms_here)[side])):
            pick_ref[side, i] = pick


def outer_kernel(
    heads,
    blocks,
    groups,
    at_ref,
    core_ref,
    query_ref,
    own_key_ref,
    own_value_ref,
    gate_ref,
    open_ref,
    trans_ref,
    w_out_ref,
    inner_ref,
    pick_ref,
    hot_ref,
    side_ref,
    w_key,
    w_value,
    first_ref,
    second_ref,
    out_hbm,
    gated_ref,
    out_ref,
    sem,
):
    samples, atoms_here, width = query_ref.shape
    device_at = at_ref[0]
    ends = atoms_here * blocks
    starts = outer_starts(atoms_here)
    margin = len(starts[0]) * Q_WIN
    inside = side_ref.shape[1]

    whole = pltpu.make_async_copy(
        inner_ref, out_hbm.at[:, pl.ds(margin, atoms_here - 2 * margin)], sem.at[0]
    )
    whole.start()

    down = core_ref[0] == 0
    first, second = first_ref[...], second_ref[...]
    arrived = (jnp.where(down, second, first), jnp.where(down, first, second))
    count = samples * EDGE
    edges = jnp.concatenate([rows[:count] for rows in arrived], 0)
    edges = dot(edges, beside(w_key, w_value)).astype(BF16).reshape(2, samples, EDGE, 2 * width)

    def joined(side, edge, own):
        return jnp.concatenate([own, edge] if side else [edge, own], 0)

    windows = []
    for side in range(2):
        own = slice(side * (atoms_here - inside), side * (atoms_here - inside) + inside)
        parts = [
            (
                joined(side, edges[side, i, :, :width], own_key_ref[i, own, :]),
                joined(side, edges[side, i, :, width:], own_value_ref[i, own, :]),
            )
            for i in range(samples)
        ]
        near = expand(hot_ref[side], arrived[side][count:], groups)
        near = joined(side, near, side_ref[side])
        for i, start in enumerate(starts[side]):
            cut = slice(i * Q_WIN, i * Q_WIN + K_WIN)
            key_at = iota((heads * Q_WIN, K_WIN), 1) + (device_at * atoms_here + start - EDGE)
            mask = (key_at >= 0) & (key_at < ends)
            pieces = [(keys[cut], values[cut]) for keys, values in parts]
            windows.append((start, pieces, near[cut], pick_ref[side, i], mask))
    attend(heads, windows, query_ref, gate_ref, gated_ref)
    copies = []
    for side in range(2):
        cut = slice(starts[side][0], starts[side][0] + margin)
        for sample in range(samples):
            out_ref[side, sample] = close(sample, cut, gated_ref, open_ref, trans_ref, w_out_ref)
        target = out_hbm.at[:, pl.ds(starts[side][0], margin)]
        copies.append(pltpu.make_async_copy(out_ref.at[side], target, sem.at[1 + side]))
        copies[-1].start()
    for copy in copies:
        copy.wait()
    whole.wait()


def shards(
    atom_single,
    atom_cond,
    pair_cond,
    atom_counts,
    ada_attn_scale,
    ada_attn_shift,
    w_query,
    w_key,
    w_value,
    w_gate,
    w_out,
    attn_gate,
    w_pair,
    ada_trans_scale,
    ada_trans_shift,
    w_swish,
    w_linear,
    w_down,
    trans_gate,
):
    device_at = lax.axis_index("atoms")
    blocks = lax.axis_size("atoms")
    samples, atoms_here, width = atom_single.shape
    tok_here = atom_counts.shape[1]
    heads = w_pair.shape[1]
    groups = tok_here // GROUP
    pairs = lax.axis_size("pair")
    assert pair_cond.shape[0] == lax.axis_size("samp") * tok_here
    at = device_at.astype(jnp.int32).reshape(1)
    pair_at = lax.axis_index("pair").astype(jnp.int32).reshape(1)
    core_at = lax.axis_index("samp").astype(jnp.int32).reshape(1)
    in_hbm = lambda array: pltpu.with_memory_space_constraint(array, pltpu.HBM)
    in_vmem = lambda array: pltpu.with_memory_space_constraint(array, pltpu.VMEM)

    cols = pair_cond.shape[1]
    lanes = heads * GROUP
    wide = (samples, atoms_here, width)
    params = pltpu.CompilerParams(vmem_limit_bytes=VMEM_LIMIT)

    def cost(products):
        return pl.CostEstimate(flops=2 * products, bytes_accessed=4 << 20, transcendentals=0)

    sent = pltpu.VMEM((samples * EDGE + groups * EDGE, lanes), BF16)
    own = pl.pallas_call(
        pair_kernel,
        in_specs=[IN_SMEM] + [IN_HBM] * 2,
        out_specs=IN_VMEM,
        out_shape=pltpu.VMEM((groups, cols, lanes), BF16),
        scratch_shapes=[
            pltpu.VMEM((heads, width), BF16),
            pltpu.VMEM((tok_here, cols, width), BF16),
            pltpu.SemaphoreType.DMA((groups,)),
            pltpu.SemaphoreType.DMA,
        ],
        compiler_params=params,
        cost_estimate=cost(tok_here * cols * width * width * 2),
    )(core_at, *map(in_hbm, (w_pair.T, pair_cond)))
    if pairs == 2:
        swapped = [(0, 1), (1, 0)]
        across = lax.ppermute(own, "pair", swapped)
        diagonal = lax.ppermute(own, ("pair", "samp"), [(0, 3), (1, 2), (2, 1), (3, 0)])
        tiles = (own, lax.ppermute(own, "samp", swapped), diagonal, across)
    else:
        tiles = (lax.all_gather(own, ("pair", "samp")),)

    operands = (
        atom_single,
        atom_cond,
        ada_attn_scale,
        ada_attn_shift,
        w_key,
        w_value,
        w_query,
        w_gate,
    )
    late = (ada_trans_scale, ada_trans_shift, attn_gate, trans_gate, w_swish, w_linear, w_down)
    query, keys, values, gate, opened, trans, near, far = pl.pallas_call(
        project_kernel,
        in_specs=[IN_SMEM] + [IN_VMEM] * len(operands) + [IN_HBM] * len(late),
        out_specs=[IN_VMEM] * 8,
        out_shape=[pltpu.VMEM(wide, BF16)] * 4
        + [pltpu.VMEM((atoms_here, width), BF16), pltpu.VMEM(wide, BF16), sent, sent],
        scratch_shapes=[pltpu.VMEM(weight.shape, BF16) for weight in late]
        + [pltpu.SemaphoreType.DMA((len(late),))],
        compiler_params=params,
        cost_estimate=cost(samples * atoms_here * width * width * 20),
    )(core_at, *map(in_vmem, operands), *map(in_hbm, late))

    operands = (*tiles, near, far, opened)
    first = 3 + len(tiles)
    near, far, opened, held = pl.pallas_call(
        functools.partial(select_kernel, blocks),
        in_specs=[IN_SMEM] * 3 + [IN_VMEM] * len(operands),
        out_specs=[IN_VMEM] * 4,
        out_shape=[
            sent,
            sent,
            pltpu.VMEM((atoms_here, width), BF16),
            pltpu.VMEM((groups * cols, lanes), BF16),
        ],
        input_output_aliases={first: 0, first + 1: 1, first + 2: 2},
        compiler_params=params,
    )(at, pair_at, core_at, *map(in_vmem, operands))

    down = [(2 * i, 2 * (i - 1)) for i in range(1, blocks)] + [(0, 1)]
    up = [(2 * i + 1, 2 * (i + 1) + 1) for i in range(blocks - 1)] + [(2 * blocks - 1, 2 * blocks - 2)]
    cycle = down + up
    first = lax.ppermute(near, ("atoms", "samp"), cycle)
    second = lax.ppermute(far, ("atoms", "samp"), [(target, source) for source, target in cycle])

    margin = -(-EDGE // Q_WIN) * Q_WIN
    inside = margin - Q_WIN + K_WIN - EDGE
    expanded = heads * tok_here
    operands = (query, keys, values, gate, opened, trans, w_out)
    inner, picks, hots, beside_edges = pl.pallas_call(
        functools.partial(inner_kernel, heads, blocks),
        in_specs=[IN_SMEM] + [IN_VMEM] * (2 + len(operands)),
        out_specs=[IN_VMEM] * 4,
        out_shape=[
            pltpu.VMEM((samples, atoms_here - 2 * margin, width), BF16),
            pltpu.VMEM((2, margin // Q_WIN, heads * Q_WIN, expanded), BF16),
            pltpu.VMEM((2, EDGE, EDGE), BF16),
            pltpu.VMEM((2, inside, expanded), BF16),
        ],
        scratch_shapes=[
            pltpu.VMEM((atoms_here, expanded), BF16),
            pltpu.VMEM(wide, BF16),
        ],
        compiler_params=params,
        cost_estimate=cost(samples * atoms_here * width * width * 12),
    )(at, atom_counts, *map(in_vmem, (*operands, held)))

    operands += (inner, picks, hots, beside_edges, w_key, w_value, first, second)
    return pl.pallas_call(
        functools.partial(outer_kernel, heads, blocks, groups),
        in_specs=[IN_SMEM] * 2 + [IN_VMEM] * len(operands),
        out_specs=IN_HBM,
        out_shape=pltpu.HBM(wide, BF16),
        scratch_shapes=[
            pltpu.VMEM(wide, BF16),
            pltpu.VMEM((2, samples, margin, width), BF16),
            pltpu.SemaphoreType.DMA((3,)),
        ],
        compiler_params=params,
        cost_estimate=cost(samples * atoms_here * width * width * 4),
    )(at, core_at, *map(in_vmem, operands))


def solution(mesh):
    return jax.shard_map(
        shards,
        mesh=mesh,
        in_specs=(
            P(("groups", "pair", "samp"), "atoms", None),
            P(("groups", "atoms"), None),
            P(("groups", "pair"), "atoms", None),
            P("groups", None),
        )
        + (P(),) * 15,
        out_specs=P(("groups", "pair", "samp"), "atoms", None),
        check_vma=False,
    )
```

```python
import functools
import math

import jax
import jax.numpy as jnp
from jax import lax
from jax.experimental import pallas as pl
from jax.experimental.pallas import tpu as pltpu
from jax.sharding import PartitionSpec as P

Q_WIN = 32
K_WIN = 128
EDGE = 48
GROUP = 32

EPSILON = 1e-05
MASKED = -1e30
LOG2E = math.log2(math.e)
BF16 = jnp.bfloat16
F32 = jnp.float32
LAST = (((1,), (1,)), ((), ()))
VMEM_LIMIT = 32 << 20
IN_VMEM = pl.BlockSpec(memory_space=pltpu.VMEM)
IN_HBM = pl.BlockSpec(memory_space=pltpu.HBM)
IN_SMEM = pl.BlockSpec(memory_space=pltpu.SMEM)


def dot(a, b):
    return jnp.dot(a, b, preferred_element_type=F32)


def iota(shape, dim):
    return lax.broadcasted_iota(jnp.int32, shape, dim)


def twice(matrix):
    blank = jnp.zeros_like(matrix)
    return jnp.concatenate(
        [jnp.concatenate([matrix, blank], 1), jnp.concatenate([blank, matrix], 1)], 0
    )


def side_by_side(rows):
    half = rows.shape[0] // 2
    return jnp.concatenate([rows[:half], rows[half:]], 1)


def centring(width):
    same = iota((width, width), 0) == iota((width, width), 1)
    return jnp.where(same, 1.0 - 1.0 / width, -1.0 / width).astype(BF16)


def averaging(width):
    return jnp.full((width, width), 1.0 / width, BF16)


def mean_square(centred):
    return jnp.mean(centred * centred, axis=-1, keepdims=True)


def layer_norm(rows):
    width = rows.shape[1]
    both = dot(side_by_side(rows), twice(centring(width)))
    centred = jnp.concatenate([both[:, :width], both[:, width:]], 0)
    return centred * lax.rsqrt(mean_square(centred) + EPSILON)


def sigmoid(values):
    return 0.5 * jnp.tanh(0.5 * values) + 0.5


def attn_norm(cond, single, ada):
    width = single.shape[-1]
    mixed = dot(cond, ada)
    return (sigmoid(mixed[:, :width])[None] * single + mixed[None, :, width:]).astype(BF16)


def pair_kernel(core_ref, w_pair_hbm, pair_hbm, tile_ref, w_pair_ref, pair_ref, pair_sem, sem):
    rows, cols, width = pair_ref.shape
    heads = w_pair_ref.shape[0]
    group = GROUP
    lanes = heads * group
    half = group // 2
    row_start = core_ref[0] * rows

    def pair_copy(i):
        source = pair_hbm.at[pl.ds(row_start + i * group, group)]
        return pltpu.make_async_copy(source, pair_ref.at[pl.ds(i * group, group)], pair_sem.at[i])

    w_pair_copy = pltpu.make_async_copy(w_pair_hbm, w_pair_ref, sem)
    w_pair_copy.start()
    for i in range(rows // group):
        pair_copy(i).start()
    w_pair_copy.wait()
    w_pair = w_pair_ref[...].astype(F32)
    spread = jnp.concatenate(
        [jnp.broadcast_to(w_pair[h : h + 1], (group, width)) for h in range(heads)], 0
    )
    mix = twice(spread.T.astype(BF16))
    centre = twice(centring(width))
    slot = iota((cols, lanes), 1) % group

    chunks = []
    for chunk in range(rows // group):
        pair_copy(chunk).wait()
        pair = pair_ref[chunk * group : (chunk + 1) * group].reshape(group * cols, width)
        chunks.append(dot(side_by_side(pair), centre).astype(BF16))
    mixes = [dot(centred, mix).reshape(half, cols, 2 * lanes) for centred in chunks]
    squares = [centred[:, :width] * centred[:, :width] for centred in chunks]
    averages = [
        dot(jnp.concatenate(squares[i : i + 2], 1), twice(averaging(width)))
        for i in range(0, len(squares), 2)
    ]
    for chunk, (centred, mixed) in enumerate(zip(chunks, mixes)):
        pick = slice(chunk % 2 * width, (chunk % 2 + 1) * width)
        variances = [
            averages[chunk // 2][:, pick].reshape(half, cols, width),
            mean_square(centred[:, width:].astype(F32)).reshape(half, cols, 1),
        ]
        total = jnp.zeros((cols, lanes), F32)
        spread_out = jnp.zeros((cols, lanes), F32)
        for i in range(group):
            side = slice(i // half * lanes, (i // half + 1) * lanes)
            total = jnp.where(slot == i, mixed[i % half, :, side], total)
            spread_out = jnp.where(slot == i, variances[i // half][i % half], spread_out)
        tile_ref[chunk] = (total * lax.rsqrt(spread_out + EPSILON)).astype(BF16)


def beside(first, second):
    return jnp.concatenate([first[...], second[...]], 1)


def project_kernel(
    core_ref,
    single_ref,
    cond_ref,
    ada_attn_scale,
    ada_attn_shift,
    w_key,
    w_value,
    w_query,
    w_gate,
    *refs,
):
    late_hbm, refs = refs[:7], refs[7:]
    query_ref, key_ref, value_ref, gate_ref, open_ref, trans_ref, near_ref, far_ref = refs[:8]
    late_refs, sem = refs[8:15], refs[15]
    ada_trans_scale, ada_trans_shift, attn_gate, trans_gate, w_swish, w_linear, w_down = late_refs
    samples, atoms_here, width = single_ref.shape
    copies = [
        pltpu.make_async_copy(source, target, sem.at[i])
        for i, (source, target) in enumerate(zip(late_hbm, late_refs))
    ]
    for copy in copies:
        copy.start()

    cond = layer_norm(cond_ref[...]).astype(BF16)
    single = layer_norm(single_ref[...].reshape(-1, width)).reshape(samples, atoms_here, width)
    normed = attn_norm(cond, single, beside(ada_attn_scale, ada_attn_shift))
    down = core_ref[0] == 0
    for sample in range(samples):
        cut = slice(sample * EDGE, (sample + 1) * EDGE)
        head, tail = normed[sample, :EDGE], normed[sample, atoms_here - EDGE :]
        near_ref[cut, :] = jnp.where(down, head, tail)
        far_ref[cut, :] = jnp.where(down, tail, head)
    normed = normed.reshape(-1, width)
    both = dot(normed, beside(w_key, w_value)).astype(BF16).reshape(samples, -1, 2 * width)
    key_ref[...] = both[:, :, :width]
    value_ref[...] = both[:, :, width:]
    both = dot(normed, beside(w_query, w_gate)).reshape(samples, -1, 2 * width)
    query_ref[...] = both[:, :, :width].astype(BF16)
    gate_ref[...] = sigmoid(both[:, :, width:]).astype(BF16)

    for copy in copies:
        copy.wait()
    gates = dot(cond, beside(attn_gate, trans_gate))
    open_ref[...] = sigmoid(gates[:, :width]).astype(BF16)
    normed = attn_norm(cond, single, beside(ada_trans_scale, ada_trans_shift)).reshape(-1, width)
    swish = dot(normed, w_swish[...])
    hidden = (swish * sigmoid(swish) * dot(normed, w_linear[...])).astype(BF16)
    down = dot(hidden, w_down[...]).reshape(samples, -1, width)
    trans_ref[...] = (sigmoid(gates[:, width:])[None] * down).astype(BF16)


def tile_of(refs, place, row_block):
    if len(refs) == 1:
        return refs[0][row_block]
    pair_at, core_at = place
    owners = 2
    mine, theirs, across, diagonal = [ref[...] for ref in refs]
    near = jnp.where(row_block % owners == core_at, mine, theirs)
    far = jnp.where(row_block % owners == core_at, across, diagonal)
    return jnp.where(row_block // owners == pair_at, near, far)


def shifted(values, lanes):
    return pltpu.roll(values, lanes % values.shape[1], 1)


def unpacked(rows, side):
    half = EDGE // 2
    whole, packed = rows[:EDGE], rows[EDGE:].astype(F32)
    if side == 0:
        part = jnp.concatenate([packed, shifted(packed, -GROUP // 2)], 0).astype(BF16)
        return jnp.concatenate([whole, part], 1)
    part = jnp.concatenate([shifted(packed, GROUP // 2), packed], 0).astype(BF16)
    return jnp.concatenate([part, whole], 1)


def select_kernel(blocks, at_ref, pair_ref, core_ref, *refs):
    *tile_refs, _, __, ___, near_ref, far_ref, ____, held_ref = refs
    groups, cols, lanes = tile_refs[0].shape[-3:]
    device_at, place = at_ref[0], (pair_ref[0], core_ref[0])
    half = EDGE // 2
    for send_ref, core in ((near_ref, 1), (far_ref, 0)):
        above = core_ref[0] == core
        beside = jnp.where(above, device_at + 1, device_at - 1)
        tile = tile_of(tile_refs, place, jnp.clip(beside, 0, blocks - 1))
        tile = jnp.where(above, tile[:, cols - EDGE :], tile[:, :EDGE])
        whole = jnp.where(above, tile[0], tile[1])
        part = jnp.where(above, tile[1], tile[0]).astype(F32)
        first, last = part[:half], part[half:]
        first = jnp.where(above, first, shifted(first, -GROUP // 2))
        last = jnp.where(above, shifted(last, GROUP // 2), last)
        low = iota((half, lanes), 1) % GROUP < GROUP // 2
        packed = jnp.where(low, first, last).astype(BF16)
        send_ref[send_ref.shape[0] - EDGE - half :, :] = jnp.concatenate([whole, packed], 0)
    held_ref[...] = tile_of(tile_refs, place, device_at).reshape(groups * cols, lanes)


def bounds(counts_ref, block, token):
    tok_here = counts_ref.shape[1]
    counts = counts_ref[pl.ds(block, 1), :].astype(F32).astype(BF16)
    counts = jnp.broadcast_to(counts, (8, tok_here))
    before = iota((tok_here, token.shape[1]), 0)
    first = dot(counts, (before < token).astype(BF16))[:1]
    last = dot(counts, (before <= token).astype(BF16))[:1]
    return first.astype(jnp.int32), last.astype(jnp.int32)


def one_hot(reach, offset, count):
    first, last = reach
    position = iota((count, first.shape[1]), 0) + offset
    return ((first <= position) & (position < last)).astype(F32).astype(BF16)


def expand(hot, tile, groups):
    tile = tile.reshape(groups, -1, tile.shape[-1])
    tile = jnp.concatenate([tile[part] for part in range(groups)], 1)
    return dot(hot, tile).astype(BF16)


def head_mask(heads, lanes):
    rows = heads * Q_WIN
    lane_head = iota((rows, lanes), 1) // GROUP % heads
    row_head = iota((rows, lanes), 0) // Q_WIN
    return (lane_head == row_head).astype(F32).astype(BF16)


def picks_of(heads, reach, starts):
    same_head = head_mask(heads, reach[0].shape[1])
    return [
        jnp.concatenate([one_hot(reach, start, Q_WIN)] * heads, 0) * same_head for start in starts
    ]


def attend(heads, windows, query_ref, gate_ref, gated_ref, paired=0):
    samples, _, width = query_ref.shape
    head_dim = width // heads
    rows = heads * Q_WIN
    own_head = iota((rows, width), 1) // head_dim == iota((rows, width), 0) // Q_WIN
    own_head = own_head.astype(F32).astype(BF16)
    channel_head = iota((Q_WIN, 2 * width), 1) % width // head_dim
    ones = jnp.ones((K_WIN, width), BF16)
    scaling = LOG2E / math.sqrt(head_dim)

    biases = []
    for _, _, near, pick, mask in windows:
        bias = lax.dot_general(pick, near, LAST, preferred_element_type=F32) * LOG2E
        biases.append(bias if mask is None else jnp.where(mask, bias, MASKED))
    units = [(sample, i) for i in range(len(windows)) for sample in range(samples)]
    scores = []
    for first in range(0, len(units), 2):
        couple = units[first : first + 2]
        queries, keys = [], []
        for sample, i in couple:
            query = query_ref[sample, pl.ds(windows[i][0], Q_WIN), :]
            queries.append(jnp.concatenate([query] * heads, 0) * own_head)
            keys.append(windows[i][1][sample][0])
        if len(couple) == 2:
            blank = jnp.zeros_like(keys[0])
            keys = [jnp.concatenate([keys[0], blank], 1), jnp.concatenate([blank, keys[1]], 1)]
        product = lax.dot_general(
            jnp.concatenate(queries, 1),
            jnp.concatenate(keys, 0),
            LAST,
            preferred_element_type=F32,
        )
        for j, (_, i) in enumerate(couple):
            scores.append(product[:, j * K_WIN : (j + 1) * K_WIN] * scaling + biases[i])
    tops = [jnp.max(score, axis=-1, keepdims=True) for score in scores]
    raised = [jnp.exp2(score - top) for score, top in zip(scores, tops)]

    def by_head(parts, like):
        picked = jnp.broadcast_to(parts[:Q_WIN], (Q_WIN, like.shape[1]))
        for head in range(1, heads):
            part = parts[head * Q_WIN : (head + 1) * Q_WIN]
            picked = jnp.where(like == head, part, picked)
        return picked

    mixes = []
    for first in range(0, len(units), 2):
        couple = units[first : first + 2]
        values = [windows[i][1][sample][1] for sample, i in couple]
        weights = [weight.astype(BF16) for weight in raised[first : first + 2]]
        if paired and first // 2 % paired == 0 and len(couple) == 2:
            blank = jnp.zeros_like(values[0])
            values = [
                jnp.concatenate([values[0], blank], 1),
                jnp.concatenate([blank, values[1]], 1),
            ]
            both = dot(jnp.concatenate(weights, 1), jnp.concatenate(values, 0))
            for j in range(2):
                total = jnp.sum(raised[first + j], axis=-1, keepdims=True)
                narrow = channel_head[:, :width]
                attended = by_head(both[:, j * width : (j + 1) * width], narrow)
                mixes.append((attended, by_head(total, narrow)))
        else:
            for value, weight in zip(values, weights):
                picked = by_head(dot(weight, jnp.concatenate([value, ones], 1)), channel_head)
                mixes.append((picked[:, :width], picked[:, width:]))
    for (sample, i), (attended, total) in zip(units, mixes):
        attended = attended * pl.reciprocal(total, approx=True)
        at = pl.ds(windows[i][0], Q_WIN)
        gate = gate_ref[sample, at, :].astype(F32)
        gated_ref[sample, at, :] = (gate * attended).astype(BF16)


def close(sample, cut, gated_ref, open_ref, trans_ref, w_out_ref):
    mixed = dot(gated_ref[sample, cut, :], w_out_ref[...])
    opened, trans = open_ref[cut, :].astype(F32), trans_ref[sample, cut, :].astype(F32)
    return (opened * mixed + trans).astype(BF16)


def row_tokens(heads, tok_here):
    lane = iota((tok_here, heads * tok_here), 1)
    return lane // (heads * GROUP) * GROUP + lane % GROUP


def outer_starts(atoms_here):
    skip = -(-EDGE // Q_WIN)
    return [
        [side * (atoms_here - skip * Q_WIN) + i * Q_WIN for i in range(skip)] for side in range(2)
    ]


def inner_kernel(
    heads,
    blocks,
    at_ref,
    counts_ref,
    query_ref,
    key_ref,
    value_ref,
    gate_ref,
    open_ref,
    trans_ref,
    w_out_ref,
    held_ref,
    out_ref,
    pick_ref,
    hot_ref,
    side_ref,
    near_ref,
    gated_ref,
):
    samples, atoms_here, width = query_ref.shape
    tok_here = counts_ref.shape[1]
    device_at = at_ref[0]
    hot = one_hot(
        bounds(counts_ref, device_at, iota((tok_here, tok_here), 1)), 0, atoms_here
    )
    near_ref[...] = expand(hot, held_ref[...], tok_here // GROUP)
    reach = bounds(counts_ref, device_at, row_tokens(heads, tok_here))
    skip = -(-EDGE // Q_WIN)
    starts = [window * Q_WIN for window in range(skip, atoms_here // Q_WIN - skip)]
    windows = []
    for start, pick in zip(starts, picks_of(heads, reach, starts)):
        cut = slice(start - EDGE, start - EDGE + K_WIN)
        parts = [(key_ref[i, cut, :], value_ref[i, cut, :]) for i in range(samples)]
        windows.append((start, parts, near_ref[cut, :], pick, None))
    attend(heads, windows, query_ref, gate_ref, gated_ref, paired=2)

    cut = slice(starts[0], starts[-1] + Q_WIN)
    for sample in range(samples):
        out_ref[sample] = close(sample, cut, gated_ref, open_ref, trans_ref, w_out_ref)

    inside = side_ref.shape[1]
    sides = (
        (jnp.maximum(device_at - 1, 0), atoms_here - EDGE, tok_here - EDGE, 0),
        (jnp.minimum(device_at + 1, blocks - 1), 0, 0, atoms_here - inside),
    )
    for side, (block, offset, token, own_start) in enumerate(sides):
        nearest = bounds(counts_ref, block, iota((tok_here, EDGE), 1) + token)
        hot_ref[side] = one_hot(nearest, offset, EDGE)
        side_ref[side] = near_ref[own_start : own_start + inside, :]
        for i, pick in enumerate(picks_of(heads, reach, outer_starts(atoms_here)[side])):
            pick_ref[side, i] = pick


def outer_kernel(
    heads,
    blocks,
    at_ref,
    core_ref,
    query_ref,
    own_key_ref,
    own_value_ref,
    gate_ref,
    open_ref,
    trans_ref,
    w_out_ref,
    inner_ref,
    pick_ref,
    hot_ref,
    side_ref,
    w_key,
    w_value,
    first_ref,
    second_ref,
    out_hbm,
    gated_ref,
    out_ref,
    sem,
):
    samples, atoms_here, width = query_ref.shape
    device_at = at_ref[0]
    ends = atoms_here * blocks
    starts = outer_starts(atoms_here)
    margin = len(starts[0]) * Q_WIN
    inside = side_ref.shape[1]

    whole = pltpu.make_async_copy(
        inner_ref, out_hbm.at[:, pl.ds(margin, atoms_here - 2 * margin)], sem.at[0]
    )
    whole.start()

    down = core_ref[0] == 0
    first, second = first_ref[...], second_ref[...]
    arrived = (jnp.where(down, second, first), jnp.where(down, first, second))
    count = samples * EDGE
    edges = jnp.concatenate([rows[:count] for rows in arrived], 0)
    edges = dot(edges, beside(w_key, w_value)).astype(BF16).reshape(2, samples, EDGE, 2 * width)

    def joined(side, edge, own):
        return jnp.concatenate([own, edge] if side else [edge, own], 0)

    windows = []
    for side in range(2):
        own = slice(side * (atoms_here - inside), side * (atoms_here - inside) + inside)
        parts = [
            (
                joined(side, edges[side, i, :, :width], own_key_ref[i, own, :]),
                joined(side, edges[side, i, :, width:], own_value_ref[i, own, :]),
            )
            for i in range(samples)
        ]
        near = dot(hot_ref[side], unpacked(arrived[side][count:], side)).astype(BF16)
        near = joined(side, near, side_ref[side])
        for i, start in enumerate(starts[side]):
            cut = slice(i * Q_WIN, i * Q_WIN + K_WIN)
            key_at = iota((heads * Q_WIN, K_WIN), 1) + (device_at * atoms_here + start - EDGE)
            mask = (key_at >= 0) & (key_at < ends)
            pieces = [(keys[cut], values[cut]) for keys, values in parts]
            windows.append((start, pieces, near[cut], pick_ref[side, i], mask))
    attend(heads, windows, query_ref, gate_ref, gated_ref)
    copies = []
    for side in range(2):
        cut = slice(starts[side][0], starts[side][0] + margin)
        for sample in range(samples):
            out_ref[side, sample] = close(sample, cut, gated_ref, open_ref, trans_ref, w_out_ref)
        target = out_hbm.at[:, pl.ds(starts[side][0], margin)]
        copies.append(pltpu.make_async_copy(out_ref.at[side], target, sem.at[1 + side]))
        copies[-1].start()
    for copy in copies:
        copy.wait()
    whole.wait()


def shards(
    atom_single,
    atom_cond,
    pair_cond,
    atom_counts,
    ada_attn_scale,
    ada_attn_shift,
    w_query,
    w_key,
    w_value,
    w_gate,
    w_out,
    attn_gate,
    w_pair,
    ada_trans_scale,
    ada_trans_shift,
    w_swish,
    w_linear,
    w_down,
    trans_gate,
):
    device_at = lax.axis_index("atoms")
    blocks = lax.axis_size("atoms")
    samples, atoms_here, width = atom_single.shape
    tok_here = atom_counts.shape[1]
    heads = w_pair.shape[1]
    groups = tok_here // GROUP
    pairs = lax.axis_size("pair")
    assert pair_cond.shape[0] == lax.axis_size("samp") * tok_here
    assert groups == 2 and tok_here - EDGE == GROUP // 2
    at = device_at.astype(jnp.int32).reshape(1)
    pair_at = lax.axis_index("pair").astype(jnp.int32).reshape(1)
    core_at = lax.axis_index("samp").astype(jnp.int32).reshape(1)
    in_hbm = lambda array: pltpu.with_memory_space_constraint(array, pltpu.HBM)
    in_vmem = lambda array: pltpu.with_memory_space_constraint(array, pltpu.VMEM)

    cols = pair_cond.shape[1]
    lanes = heads * GROUP
    wide = (samples, atoms_here, width)
    params = pltpu.CompilerParams(vmem_limit_bytes=VMEM_LIMIT)

    def cost(products):
        return pl.CostEstimate(flops=2 * products, bytes_accessed=4 << 20, transcendentals=0)

    sent = pltpu.VMEM((samples * EDGE + EDGE + EDGE // 2, lanes), BF16)
    own = pl.pallas_call(
        pair_kernel,
        in_specs=[IN_SMEM] + [IN_HBM] * 2,
        out_specs=IN_VMEM,
        out_shape=pltpu.VMEM((groups, cols, lanes), BF16),
        scratch_shapes=[
            pltpu.VMEM((heads, width), BF16),
            pltpu.VMEM((tok_here, cols, width), BF16),
            pltpu.SemaphoreType.DMA((groups,)),
            pltpu.SemaphoreType.DMA,
        ],
        compiler_params=params,
        cost_estimate=cost(tok_here * cols * width * width * 2),
    )(core_at, *map(in_hbm, (w_pair.T, pair_cond)))
    if pairs == 2:
        swapped = [(0, 1), (1, 0)]
        across = lax.ppermute(own, "pair", swapped)
        diagonal = lax.ppermute(own, ("pair", "samp"), [(0, 3), (1, 2), (2, 1), (3, 0)])
        tiles = (own, lax.ppermute(own, "samp", swapped), across, diagonal)
    else:
        tiles = (lax.all_gather(own, ("pair", "samp")),)

    operands = (
        atom_single,
        atom_cond,
        ada_attn_scale,
        ada_attn_shift,
        w_key,
        w_value,
        w_query,
        w_gate,
    )
    late = (ada_trans_scale, ada_trans_shift, attn_gate, trans_gate, w_swish, w_linear, w_down)
    query, keys, values, gate, opened, trans, near, far = pl.pallas_call(
        project_kernel,
        in_specs=[IN_SMEM] + [IN_VMEM] * len(operands) + [IN_HBM] * len(late),
        out_specs=[IN_VMEM] * 8,
        out_shape=[pltpu.VMEM(wide, BF16)] * 4
        + [pltpu.VMEM((atoms_here, width), BF16), pltpu.VMEM(wide, BF16), sent, sent],
        scratch_shapes=[pltpu.VMEM(weight.shape, BF16) for weight in late]
        + [pltpu.SemaphoreType.DMA((len(late),))],
        compiler_params=params,
        cost_estimate=cost(samples * atoms_here * width * width * 20),
    )(core_at, *map(in_vmem, operands), *map(in_hbm, late))

    operands = (*tiles, near, far, opened)
    first = 3 + len(tiles)
    near, far, opened, held = pl.pallas_call(
        functools.partial(select_kernel, blocks),
        in_specs=[IN_SMEM] * 3 + [IN_VMEM] * len(operands),
        out_specs=[IN_VMEM] * 4,
        out_shape=[
            sent,
            sent,
            pltpu.VMEM((atoms_here, width), BF16),
            pltpu.VMEM((groups * cols, lanes), BF16),
        ],
        input_output_aliases={first: 0, first + 1: 1, first + 2: 2},
        compiler_params=params,
    )(at, pair_at, core_at, *map(in_vmem, operands))

    down = [(2 * i, 2 * (i - 1)) for i in range(1, blocks)] + [(0, 1)]
    up = [(2 * i + 1, 2 * (i + 1) + 1) for i in range(blocks - 1)] + [(2 * blocks - 1, 2 * blocks - 2)]
    cycle = down + up
    first = lax.ppermute(near, ("atoms", "samp"), cycle)
    second = lax.ppermute(far, ("atoms", "samp"), [(target, source) for source, target in cycle])

    margin = -(-EDGE // Q_WIN) * Q_WIN
    inside = margin - Q_WIN + K_WIN - EDGE
    expanded = heads * tok_here
    operands = (query, keys, values, gate, opened, trans, w_out)
    inner, picks, hots, beside_edges = pl.pallas_call(
        functools.partial(inner_kernel, heads, blocks),
        in_specs=[IN_SMEM] + [IN_VMEM] * (2 + len(operands)),
        out_specs=[IN_VMEM] * 4,
        out_shape=[
            pltpu.VMEM((samples, atoms_here - 2 * margin, width), BF16),
            pltpu.VMEM((2, margin // Q_WIN, heads * Q_WIN, expanded), BF16),
            pltpu.VMEM((2, EDGE, EDGE), BF16),
            pltpu.VMEM((2, inside, expanded), BF16),
        ],
        scratch_shapes=[
            pltpu.VMEM((atoms_here, expanded), BF16),
            pltpu.VMEM(wide, BF16),
        ],
        compiler_params=params,
        cost_estimate=cost(samples * atoms_here * width * width * 12),
    )(at, atom_counts, *map(in_vmem, (*operands, held)))

    operands += (inner, picks, hots, beside_edges, w_key, w_value, first, second)
    return pl.pallas_call(
        functools.partial(outer_kernel, heads, blocks),
        in_specs=[IN_SMEM] * 2 + [IN_VMEM] * len(operands),
        out_specs=IN_HBM,
        out_shape=pltpu.HBM(wide, BF16),
        scratch_shapes=[
            pltpu.VMEM(wide, BF16),
            pltpu.VMEM((2, samples, margin, width), BF16),
            pltpu.SemaphoreType.DMA((3,)),
        ],
        compiler_params=params,
        cost_estimate=cost(samples * atoms_here * width * width * 4),
    )(at, core_at, *map(in_vmem, operands))


def solution(mesh):
    return jax.shard_map(
        shards,
        mesh=mesh,
        in_specs=(
            P(("groups", "pair", "samp"), "atoms", None),
            P(("groups", "atoms"), None),
            P(("groups", "pair"), "atoms", None),
            P("groups", None),
        )
        + (P(),) * 15,
        out_specs=P(("groups", "pair", "samp"), "atoms", None),
        check_vma=False,
    )
```

```python
import functools
import math

import jax
import jax.numpy as jnp
from jax import lax
from jax.experimental import pallas as pl
from jax.experimental.pallas import tpu as pltpu
from jax.sharding import PartitionSpec as P

Q_WIN = 32
K_WIN = 128
EDGE = 48
GROUP = 32

EPSILON = 1e-05
MASKED = -1e30
LOG2E = math.log2(math.e)
BF16 = jnp.bfloat16
F32 = jnp.float32
LAST = (((1,), (1,)), ((), ()))
VMEM_LIMIT = 32 << 20
IN_VMEM = pl.BlockSpec(memory_space=pltpu.VMEM)
IN_HBM = pl.BlockSpec(memory_space=pltpu.HBM)
IN_SMEM = pl.BlockSpec(memory_space=pltpu.SMEM)


def dot(a, b):
    return jnp.dot(a, b, preferred_element_type=F32)


def iota(shape, dim):
    return lax.broadcasted_iota(jnp.int32, shape, dim)


def twice(matrix):
    blank = jnp.zeros_like(matrix)
    return jnp.concatenate(
        [jnp.concatenate([matrix, blank], 1), jnp.concatenate([blank, matrix], 1)], 0
    )


def side_by_side(rows):
    half = rows.shape[0] // 2
    return jnp.concatenate([rows[:half], rows[half:]], 1)


def centring(width):
    same = iota((width, width), 0) == iota((width, width), 1)
    return jnp.where(same, 1.0 - 1.0 / width, -1.0 / width).astype(BF16)


def averaging(width):
    return jnp.full((width, width), 1.0 / width, BF16)


def mean_square(centred):
    return jnp.mean(centred * centred, axis=-1, keepdims=True)


def layer_norm(rows):
    width = rows.shape[1]
    both = dot(side_by_side(rows), twice(centring(width)))
    centred = jnp.concatenate([both[:, :width], both[:, width:]], 0)
    return centred * lax.rsqrt(mean_square(centred) + EPSILON)


def sigmoid(values):
    return 0.5 * jnp.tanh(0.5 * values) + 0.5


def attn_norm(cond, single, ada):
    width = single.shape[-1]
    mixed = dot(cond, ada)
    return (sigmoid(mixed[:, :width])[None] * single + mixed[None, :, width:]).astype(BF16)


def pair_kernel(
    core_ref,
    w_pair_hbm,
    pair_hbm,
    single_hbm,
    cond_hbm,
    tile_ref,
    single_ref,
    cond_ref,
    w_pair_ref,
    pair_ref,
    pair_sem,
    sem,
):
    rows, cols, width = pair_ref.shape
    heads = w_pair_ref.shape[0]
    group = GROUP
    lanes = heads * group
    half = group // 2
    row_start = core_ref[0] * rows

    def pair_copy(i):
        source = pair_hbm.at[pl.ds(row_start + i * group, group)]
        return pltpu.make_async_copy(source, pair_ref.at[pl.ds(i * group, group)], pair_sem.at[i])

    w_pair_copy = pltpu.make_async_copy(w_pair_hbm, w_pair_ref, sem.at[0])
    atom_copies = [
        pltpu.make_async_copy(single_hbm, single_ref, sem.at[1]),
        pltpu.make_async_copy(cond_hbm, cond_ref, sem.at[2]),
    ]
    w_pair_copy.start()
    for i in range(rows // group):
        pair_copy(i).start()
    for copy in atom_copies:
        copy.start()
    w_pair_copy.wait()
    w_pair = w_pair_ref[...].astype(F32)
    spread = jnp.concatenate(
        [jnp.broadcast_to(w_pair[h : h + 1], (group, width)) for h in range(heads)], 0
    )
    mix = twice(spread.T.astype(BF16))
    centre = twice(centring(width))
    slot = iota((cols, lanes), 1) % group

    chunks = []
    for chunk in range(rows // group):
        pair_copy(chunk).wait()
        pair = pair_ref[chunk * group : (chunk + 1) * group].reshape(group * cols, width)
        chunks.append(dot(side_by_side(pair), centre).astype(BF16))
    mixes = [dot(centred, mix).reshape(half, cols, 2 * lanes) for centred in chunks]
    squares = [centred[:, :width] * centred[:, :width] for centred in chunks]
    averages = [
        dot(jnp.concatenate(squares[i : i + 2], 1), twice(averaging(width)))
        for i in range(0, len(squares), 2)
    ]
    for chunk, (centred, mixed) in enumerate(zip(chunks, mixes)):
        pick = slice(chunk % 2 * width, (chunk % 2 + 1) * width)
        variances = [
            averages[chunk // 2][:, pick].reshape(half, cols, width),
            mean_square(centred[:, width:].astype(F32)).reshape(half, cols, 1),
        ]
        total = jnp.zeros((cols, lanes), F32)
        spread_out = jnp.zeros((cols, lanes), F32)
        for i in range(group):
            side = slice(i // half * lanes, (i // half + 1) * lanes)
            total = jnp.where(slot == i, mixed[i % half, :, side], total)
            spread_out = jnp.where(slot == i, variances[i // half][i % half], spread_out)
        tile_ref[chunk] = (total * lax.rsqrt(spread_out + EPSILON)).astype(BF16)
    for copy in atom_copies:
        copy.wait()


def beside(first, second):
    return jnp.concatenate([first[...], second[...]], 1)


def project_kernel(
    core_ref,
    single_ref,
    cond_ref,
    ada_attn_scale,
    ada_attn_shift,
    w_key,
    w_value,
    w_query,
    w_gate,
    *refs,
):
    late_hbm, refs = refs[:7], refs[7:]
    query_ref, key_ref, value_ref, gate_ref, open_ref, trans_ref, near_ref, far_ref = refs[:8]
    late_refs, sem = refs[8:15], refs[15]
    ada_trans_scale, ada_trans_shift, attn_gate, trans_gate, w_swish, w_linear, w_down = late_refs
    samples, atoms_here, width = single_ref.shape
    copies = [
        pltpu.make_async_copy(source, target, sem.at[i])
        for i, (source, target) in enumerate(zip(late_hbm, late_refs))
    ]
    for copy in copies:
        copy.start()

    cond = layer_norm(cond_ref[...]).astype(BF16)
    single = layer_norm(single_ref[...].reshape(-1, width)).reshape(samples, atoms_here, width)
    normed = attn_norm(cond, single, beside(ada_attn_scale, ada_attn_shift))
    down = core_ref[0] == 0
    for sample in range(samples):
        cut = slice(sample * EDGE, (sample + 1) * EDGE)
        head, tail = normed[sample, :EDGE], normed[sample, atoms_here - EDGE :]
        near_ref[cut, :] = jnp.where(down, head, tail)
        far_ref[cut, :] = jnp.where(down, tail, head)
    normed = normed.reshape(-1, width)
    both = dot(normed, beside(w_key, w_value)).astype(BF16).reshape(samples, -1, 2 * width)
    key_ref[...] = both[:, :, :width]
    value_ref[...] = both[:, :, width:]
    both = dot(normed, beside(w_query, w_gate)).reshape(samples, -1, 2 * width)
    query_ref[...] = both[:, :, :width].astype(BF16)
    gate_ref[...] = sigmoid(both[:, :, width:]).astype(BF16)

    for copy in copies:
        copy.wait()
    gates = dot(cond, beside(attn_gate, trans_gate))
    open_ref[...] = sigmoid(gates[:, :width]).astype(BF16)
    normed = attn_norm(cond, single, beside(ada_trans_scale, ada_trans_shift)).reshape(-1, width)
    swish = dot(normed, w_swish[...])
    hidden = (swish * sigmoid(swish) * dot(normed, w_linear[...])).astype(BF16)
    down = dot(hidden, w_down[...]).reshape(samples, -1, width)
    trans_ref[...] = (sigmoid(gates[:, width:])[None] * down).astype(BF16)


def tile_of(refs, place, row_block):
    if len(refs) == 1:
        return refs[0][row_block]
    pair_at, core_at = place
    owners = 2
    mine, theirs, across, diagonal = [ref[...] for ref in refs]
    near = jnp.where(row_block % owners == core_at, mine, theirs)
    far = jnp.where(row_block % owners == core_at, across, diagonal)
    return jnp.where(row_block // owners == pair_at, near, far)


def shifted(values, lanes):
    return pltpu.roll(values, lanes % values.shape[1], 1)


def unpacked(rows, side):
    half = EDGE // 2
    whole, packed = rows[:EDGE], rows[EDGE:].astype(F32)
    if side == 0:
        part = jnp.concatenate([packed, shifted(packed, -GROUP // 2)], 0).astype(BF16)
        return jnp.concatenate([whole, part], 1)
    part = jnp.concatenate([shifted(packed, GROUP // 2), packed], 0).astype(BF16)
    return jnp.concatenate([part, whole], 1)


def select_kernel(blocks, at_ref, pair_ref, core_ref, *refs):
    *tile_refs, _, __, ___, near_ref, far_ref, ____, held_ref = refs
    groups, cols, lanes = tile_refs[0].shape[-3:]
    device_at, place = at_ref[0], (pair_ref[0], core_ref[0])
    half = EDGE // 2
    for send_ref, core in ((near_ref, 1), (far_ref, 0)):
        above = core_ref[0] == core
        beside = jnp.where(above, device_at + 1, device_at - 1)
        tile = tile_of(tile_refs, place, jnp.clip(beside, 0, blocks - 1))
        tile = jnp.where(above, tile[:, cols - EDGE :], tile[:, :EDGE])
        whole = jnp.where(above, tile[0], tile[1])
        part = jnp.where(above, tile[1], tile[0]).astype(F32)
        first, last = part[:half], part[half:]
        first = jnp.where(above, first, shifted(first, -GROUP // 2))
        last = jnp.where(above, shifted(last, GROUP // 2), last)
        low = iota((half, lanes), 1) % GROUP < GROUP // 2
        packed = jnp.where(low, first, last).astype(BF16)
        send_ref[send_ref.shape[0] - EDGE - half :, :] = jnp.concatenate([whole, packed], 0)
    held_ref[...] = tile_of(tile_refs, place, device_at).reshape(groups * cols, lanes)


def bounds(counts_ref, block, token):
    tok_here = counts_ref.shape[1]
    counts = counts_ref[pl.ds(block, 1), :].astype(F32).astype(BF16)
    counts = jnp.broadcast_to(counts, (8, tok_here))
    before = iota((tok_here, token.shape[1]), 0)
    first = dot(counts, (before < token).astype(BF16))[:1]
    last = dot(counts, (before <= token).astype(BF16))[:1]
    return first.astype(jnp.int32), last.astype(jnp.int32)


def one_hot(reach, offset, count):
    first, last = reach
    position = iota((count, first.shape[1]), 0) + offset
    return ((first <= position) & (position < last)).astype(F32).astype(BF16)


def expand(hot, tile, groups):
    tile = tile.reshape(groups, -1, tile.shape[-1])
    tile = jnp.concatenate([tile[part] for part in range(groups)], 1)
    return dot(hot, tile).astype(BF16)


def head_mask(heads, lanes):
    rows = heads * Q_WIN
    lane_head = iota((rows, lanes), 1) // GROUP % heads
    row_head = iota((rows, lanes), 0) // Q_WIN
    return (lane_head == row_head).astype(F32).astype(BF16)


def picks_of(heads, reach, starts):
    same_head = head_mask(heads, reach[0].shape[1])
    return [
        jnp.concatenate([one_hot(reach, start, Q_WIN)] * heads, 0) * same_head for start in starts
    ]


def attend(heads, windows, query_ref, gate_ref, gated_ref, paired=0):
    samples, _, width = query_ref.shape
    head_dim = width // heads
    rows = heads * Q_WIN
    own_head = iota((rows, width), 1) // head_dim == iota((rows, width), 0) // Q_WIN
    own_head = own_head.astype(F32).astype(BF16)
    channel_head = iota((Q_WIN, 2 * width), 1) % width // head_dim
    ones = jnp.ones((K_WIN, width), BF16)
    scaling = LOG2E / math.sqrt(head_dim)

    biases = []
    for _, _, near, pick, mask in windows:
        bias = lax.dot_general(pick, near, LAST, preferred_element_type=F32) * LOG2E
        biases.append(bias if mask is None else jnp.where(mask, bias, MASKED))
    units = [(sample, i) for i in range(len(windows)) for sample in range(samples)]
    scores = []
    for first in range(0, len(units), 2):
        couple = units[first : first + 2]
        queries, keys = [], []
        for sample, i in couple:
            query = query_ref[sample, pl.ds(windows[i][0], Q_WIN), :]
            queries.append(jnp.concatenate([query] * heads, 0) * own_head)
            keys.append(windows[i][1][sample][0])
        if len(couple) == 2:
            blank = jnp.zeros_like(keys[0])
            keys = [jnp.concatenate([keys[0], blank], 1), jnp.concatenate([blank, keys[1]], 1)]
        product = lax.dot_general(
            jnp.concatenate(queries, 1),
            jnp.concatenate(keys, 0),
            LAST,
            preferred_element_type=F32,
        )
        for j, (_, i) in enumerate(couple):
            scores.append(product[:, j * K_WIN : (j + 1) * K_WIN] * scaling + biases[i])
    tops = [jnp.max(score, axis=-1, keepdims=True) for score in scores]
    raised = [jnp.exp2(score - top) for score, top in zip(scores, tops)]

    def by_head(parts, like):
        picked = jnp.broadcast_to(parts[:Q_WIN], (Q_WIN, like.shape[1]))
        for head in range(1, heads):
            part = parts[head * Q_WIN : (head + 1) * Q_WIN]
            picked = jnp.where(like == head, part, picked)
        return picked

    mixes = []
    for first in range(0, len(units), 2):
        couple = units[first : first + 2]
        values = [windows[i][1][sample][1] for sample, i in couple]
        weights = [weight.astype(BF16) for weight in raised[first : first + 2]]
        if paired and first // 2 % paired == 0 and len(couple) == 2:
            blank = jnp.zeros_like(values[0])
            values = [
                jnp.concatenate([values[0], blank], 1),
                jnp.concatenate([blank, values[1]], 1),
            ]
            both = dot(jnp.concatenate(weights, 1), jnp.concatenate(values, 0))
            for j in range(2):
                total = jnp.sum(raised[first + j], axis=-1, keepdims=True)
                narrow = channel_head[:, :width]
                attended = by_head(both[:, j * width : (j + 1) * width], narrow)
                mixes.append((attended, by_head(total, narrow)))
        else:
            for value, weight in zip(values, weights):
                picked = by_head(dot(weight, jnp.concatenate([value, ones], 1)), channel_head)
                mixes.append((picked[:, :width], picked[:, width:]))
    for (sample, i), (attended, total) in zip(units, mixes):
        attended = attended * pl.reciprocal(total, approx=True)
        at = pl.ds(windows[i][0], Q_WIN)
        gate = gate_ref[sample, at, :].astype(F32)
        gated_ref[sample, at, :] = (gate * attended).astype(BF16)


def close(sample, cut, gated_ref, open_ref, trans_ref, w_out_ref):
    mixed = dot(gated_ref[sample, cut, :], w_out_ref[...])
    opened, trans = open_ref[cut, :].astype(F32), trans_ref[sample, cut, :].astype(F32)
    return (opened * mixed + trans).astype(BF16)


def row_tokens(heads, tok_here):
    lane = iota((tok_here, heads * tok_here), 1)
    return lane // (heads * GROUP) * GROUP + lane % GROUP


def outer_starts(atoms_here):
    skip = -(-EDGE // Q_WIN)
    return [
        [side * (atoms_here - skip * Q_WIN) + i * Q_WIN for i in range(skip)] for side in range(2)
    ]


def inner_kernel(
    heads,
    blocks,
    at_ref,
    counts_ref,
    query_ref,
    key_ref,
    value_ref,
    gate_ref,
    open_ref,
    trans_ref,
    w_out_ref,
    held_ref,
    out_ref,
    pick_ref,
    hot_ref,
    side_ref,
    near_ref,
    gated_ref,
):
    samples, atoms_here, width = query_ref.shape
    tok_here = counts_ref.shape[1]
    device_at = at_ref[0]
    hot = one_hot(
        bounds(counts_ref, device_at, iota((tok_here, tok_here), 1)), 0, atoms_here
    )
    near_ref[...] = expand(hot, held_ref[...], tok_here // GROUP)
    reach = bounds(counts_ref, device_at, row_tokens(heads, tok_here))
    skip = -(-EDGE // Q_WIN)
    starts = [window * Q_WIN for window in range(skip, atoms_here // Q_WIN - skip)]
    windows = []
    for start, pick in zip(starts, picks_of(heads, reach, starts)):
        cut = slice(start - EDGE, start - EDGE + K_WIN)
        parts = [(key_ref[i, cut, :], value_ref[i, cut, :]) for i in range(samples)]
        windows.append((start, parts, near_ref[cut, :], pick, None))
    attend(heads, windows, query_ref, gate_ref, gated_ref, paired=2)

    cut = slice(starts[0], starts[-1] + Q_WIN)
    for sample in range(samples):
        out_ref[sample] = close(sample, cut, gated_ref, open_ref, trans_ref, w_out_ref)

    inside = side_ref.shape[1]
    sides = (
        (jnp.maximum(device_at - 1, 0), atoms_here - EDGE, tok_here - EDGE, 0),
        (jnp.minimum(device_at + 1, blocks - 1), 0, 0, atoms_here - inside),
    )
    for side, (block, offset, token, own_start) in enumerate(sides):
        nearest = bounds(counts_ref, block, iota((tok_here, EDGE), 1) + token)
        hot_ref[side] = one_hot(nearest, offset, EDGE)
        side_ref[side] = near_ref[own_start : own_start + inside, :]
        for i, pick in enumerate(picks_of(heads, reach, outer_starts(atoms_here)[side])):
            pick_ref[side, i] = pick


def outer_kernel(
    heads,
    blocks,
    at_ref,
    core_ref,
    query_ref,
    own_key_ref,
    own_value_ref,
    gate_ref,
    open_ref,
    trans_ref,
    w_out_ref,
    inner_ref,
    pick_ref,
    hot_ref,
    side_ref,
    w_key,
    w_value,
    first_ref,
    second_ref,
    out_hbm,
    gated_ref,
    out_ref,
    sem,
):
    samples, atoms_here, width = query_ref.shape
    device_at = at_ref[0]
    ends = atoms_here * blocks
    starts = outer_starts(atoms_here)
    margin = len(starts[0]) * Q_WIN
    inside = side_ref.shape[1]

    whole = pltpu.make_async_copy(
        inner_ref, out_hbm.at[:, pl.ds(margin, atoms_here - 2 * margin)], sem.at[0]
    )
    whole.start()

    down = core_ref[0] == 0
    first, second = first_ref[...], second_ref[...]
    arrived = (jnp.where(down, second, first), jnp.where(down, first, second))
    count = samples * EDGE
    edges = jnp.concatenate([rows[:count] for rows in arrived], 0)
    edges = dot(edges, beside(w_key, w_value)).astype(BF16).reshape(2, samples, EDGE, 2 * width)

    def joined(side, edge, own):
        return jnp.concatenate([own, edge] if side else [edge, own], 0)

    windows = []
    for side in range(2):
        own = slice(side * (atoms_here - inside), side * (atoms_here - inside) + inside)
        parts = [
            (
                joined(side, edges[side, i, :, :width], own_key_ref[i, own, :]),
                joined(side, edges[side, i, :, width:], own_value_ref[i, own, :]),
            )
            for i in range(samples)
        ]
        near = dot(hot_ref[side], unpacked(arrived[side][count:], side)).astype(BF16)
        near = joined(side, near, side_ref[side])
        for i, start in enumerate(starts[side]):
            cut = slice(i * Q_WIN, i * Q_WIN + K_WIN)
            key_at = iota((heads * Q_WIN, K_WIN), 1) + (device_at * atoms_here + start - EDGE)
            mask = (key_at >= 0) & (key_at < ends)
            pieces = [(keys[cut], values[cut]) for keys, values in parts]
            windows.append((start, pieces, near[cut], pick_ref[side, i], mask))
    attend(heads, windows, query_ref, gate_ref, gated_ref)
    copies = []
    for side in range(2):
        cut = slice(starts[side][0], starts[side][0] + margin)
        for sample in range(samples):
            out_ref[side, sample] = close(sample, cut, gated_ref, open_ref, trans_ref, w_out_ref)
        target = out_hbm.at[:, pl.ds(starts[side][0], margin)]
        copies.append(pltpu.make_async_copy(out_ref.at[side], target, sem.at[1 + side]))
        copies[-1].start()
    for copy in copies:
        copy.wait()
    whole.wait()


def shards(
    atom_single,
    atom_cond,
    pair_cond,
    atom_counts,
    ada_attn_scale,
    ada_attn_shift,
    w_query,
    w_key,
    w_value,
    w_gate,
    w_out,
    attn_gate,
    w_pair,
    ada_trans_scale,
    ada_trans_shift,
    w_swish,
    w_linear,
    w_down,
    trans_gate,
):
    device_at = lax.axis_index("atoms")
    blocks = lax.axis_size("atoms")
    samples, atoms_here, width = atom_single.shape
    tok_here = atom_counts.shape[1]
    heads = w_pair.shape[1]
    groups = tok_here // GROUP
    pairs = lax.axis_size("pair")
    assert pair_cond.shape[0] == lax.axis_size("samp") * tok_here
    assert groups == 2 and tok_here - EDGE == GROUP // 2
    at = device_at.astype(jnp.int32).reshape(1)
    pair_at = lax.axis_index("pair").astype(jnp.int32).reshape(1)
    core_at = lax.axis_index("samp").astype(jnp.int32).reshape(1)
    in_hbm = lambda array: pltpu.with_memory_space_constraint(array, pltpu.HBM)
    in_vmem = lambda array: pltpu.with_memory_space_constraint(array, pltpu.VMEM)

    cols = pair_cond.shape[1]
    lanes = heads * GROUP
    wide = (samples, atoms_here, width)
    params = pltpu.CompilerParams(vmem_limit_bytes=VMEM_LIMIT)

    def cost(products):
        return pl.CostEstimate(flops=2 * products, bytes_accessed=4 << 20, transcendentals=0)

    sent = pltpu.VMEM((samples * EDGE + EDGE + EDGE // 2, lanes), BF16)
    own, single, cond = pl.pallas_call(
        pair_kernel,
        in_specs=[IN_SMEM] + [IN_HBM] * 4,
        out_specs=[IN_VMEM] * 3,
        out_shape=[
            pltpu.VMEM((groups, cols, lanes), BF16),
            pltpu.VMEM(wide, BF16),
            pltpu.VMEM(atom_cond.shape, BF16),
        ],
        scratch_shapes=[
            pltpu.VMEM((heads, width), BF16),
            pltpu.VMEM((tok_here, cols, width), BF16),
            pltpu.SemaphoreType.DMA((groups,)),
            pltpu.SemaphoreType.DMA((3,)),
        ],
        compiler_params=params,
        cost_estimate=cost(tok_here * cols * width * width * 2),
    )(core_at, *map(in_hbm, (w_pair.T, pair_cond, atom_single, atom_cond)))
    if pairs == 2:
        swapped = [(0, 1), (1, 0)]
        across = lax.ppermute(own, "pair", swapped)
        diagonal = lax.ppermute(own, ("pair", "samp"), [(0, 3), (1, 2), (2, 1), (3, 0)])
        tiles = (own, lax.ppermute(own, "samp", swapped), across, diagonal)
    else:
        tiles = (lax.all_gather(own, ("pair", "samp")),)

    operands = (
        single,
        cond,
        ada_attn_scale,
        ada_attn_shift,
        w_key,
        w_value,
        w_query,
        w_gate,
    )
    late = (ada_trans_scale, ada_trans_shift, attn_gate, trans_gate, w_swish, w_linear, w_down)
    query, keys, values, gate, opened, trans, near, far = pl.pallas_call(
        project_kernel,
        in_specs=[IN_SMEM] + [IN_VMEM] * len(operands) + [IN_HBM] * len(late),
        out_specs=[IN_VMEM] * 8,
        out_shape=[pltpu.VMEM(wide, BF16)] * 4
        + [pltpu.VMEM((atoms_here, width), BF16), pltpu.VMEM(wide, BF16), sent, sent],
        scratch_shapes=[pltpu.VMEM(weight.shape, BF16) for weight in late]
        + [pltpu.SemaphoreType.DMA((len(late),))],
        compiler_params=params,
        cost_estimate=cost(samples * atoms_here * width * width * 20),
    )(core_at, *map(in_vmem, operands), *map(in_hbm, late))

    operands = (*tiles, near, far, opened)
    first = 3 + len(tiles)
    near, far, opened, held = pl.pallas_call(
        functools.partial(select_kernel, blocks),
        in_specs=[IN_SMEM] * 3 + [IN_VMEM] * len(operands),
        out_specs=[IN_VMEM] * 4,
        out_shape=[
            sent,
            sent,
            pltpu.VMEM((atoms_here, width), BF16),
            pltpu.VMEM((groups * cols, lanes), BF16),
        ],
        input_output_aliases={first: 0, first + 1: 1, first + 2: 2},
        compiler_params=params,
    )(at, pair_at, core_at, *map(in_vmem, operands))

    down = [(2 * i, 2 * (i - 1)) for i in range(1, blocks)] + [(0, 1)]
    up = [(2 * i + 1, 2 * (i + 1) + 1) for i in range(blocks - 1)] + [(2 * blocks - 1, 2 * blocks - 2)]
    cycle = down + up
    first = lax.ppermute(near, ("atoms", "samp"), cycle)
    second = lax.ppermute(far, ("atoms", "samp"), [(target, source) for source, target in cycle])

    margin = -(-EDGE // Q_WIN) * Q_WIN
    inside = margin - Q_WIN + K_WIN - EDGE
    expanded = heads * tok_here
    operands = (query, keys, values, gate, opened, trans, w_out)
    inner, picks, hots, beside_edges = pl.pallas_call(
        functools.partial(inner_kernel, heads, blocks),
        in_specs=[IN_SMEM] + [IN_VMEM] * (2 + len(operands)),
        out_specs=[IN_VMEM] * 4,
        out_shape=[
            pltpu.VMEM((samples, atoms_here - 2 * margin, width), BF16),
            pltpu.VMEM((2, margin // Q_WIN, heads * Q_WIN, expanded), BF16),
            pltpu.VMEM((2, EDGE, EDGE), BF16),
            pltpu.VMEM((2, inside, expanded), BF16),
        ],
        scratch_shapes=[
            pltpu.VMEM((atoms_here, expanded), BF16),
            pltpu.VMEM(wide, BF16),
        ],
        compiler_params=params,
        cost_estimate=cost(samples * atoms_here * width * width * 12),
    )(at, atom_counts, *map(in_vmem, (*operands, held)))

    operands += (inner, picks, hots, beside_edges, w_key, w_value, first, second)
    return pl.pallas_call(
        functools.partial(outer_kernel, heads, blocks),
        in_specs=[IN_SMEM] * 2 + [IN_VMEM] * len(operands),
        out_specs=IN_HBM,
        out_shape=pltpu.HBM(wide, BF16),
        scratch_shapes=[
            pltpu.VMEM(wide, BF16),
            pltpu.VMEM((2, samples, margin, width), BF16),
            pltpu.SemaphoreType.DMA((3,)),
        ],
        compiler_params=params,
        cost_estimate=cost(samples * atoms_here * width * width * 4),
    )(at, core_at, *map(in_vmem, operands))


def solution(mesh):
    return jax.shard_map(
        shards,
        mesh=mesh,
        in_specs=(
            P(("groups", "pair", "samp"), "atoms", None),
            P(("groups", "atoms"), None),
            P(("groups", "pair"), "atoms", None),
            P("groups", None),
        )
        + (P(),) * 15,
        out_specs=P(("groups", "pair", "samp"), "atoms", None),
        check_vma=False,
    )
```

```python
import functools
import math

import jax
import jax.numpy as jnp
from jax import lax
from jax.experimental import pallas as pl
from jax.experimental.pallas import tpu as pltpu
from jax.sharding import PartitionSpec as P

Q_WIN = 32
K_WIN = 128
EDGE = 48
GROUP = 32

EPSILON = 1e-05
MASKED = -1e30
LOG2E = math.log2(math.e)
BF16 = jnp.bfloat16
F32 = jnp.float32
LAST = (((1,), (1,)), ((), ()))
VMEM_LIMIT = 32 << 20
IN_VMEM = pl.BlockSpec(memory_space=pltpu.VMEM)
IN_HBM = pl.BlockSpec(memory_space=pltpu.HBM)
IN_SMEM = pl.BlockSpec(memory_space=pltpu.SMEM)


def dot(a, b):
    return jnp.dot(a, b, preferred_element_type=F32)


def iota(shape, dim):
    return lax.broadcasted_iota(jnp.int32, shape, dim)


def twice(matrix):
    blank = jnp.zeros_like(matrix)
    return jnp.concatenate(
        [jnp.concatenate([matrix, blank], 1), jnp.concatenate([blank, matrix], 1)], 0
    )


def side_by_side(rows):
    half = rows.shape[0] // 2
    return jnp.concatenate([rows[:half], rows[half:]], 1)


def centring(width):
    same = iota((width, width), 0) == iota((width, width), 1)
    return jnp.where(same, 1.0 - 1.0 / width, -1.0 / width).astype(BF16)


def averaging(width):
    return jnp.full((width, width), 1.0 / width, BF16)


def mean_square(centred):
    return jnp.mean(centred * centred, axis=-1, keepdims=True)


def layer_norm(rows):
    width = rows.shape[1]
    both = dot(side_by_side(rows), twice(centring(width)))
    centred = jnp.concatenate([both[:, :width], both[:, width:]], 0)
    return centred * lax.rsqrt(mean_square(centred) + EPSILON)


def sigmoid(values):
    return 0.5 * jnp.tanh(0.5 * values) + 0.5


def attn_norm(cond, single, ada):
    width = single.shape[-1]
    mixed = dot(cond, ada)
    return (sigmoid(mixed[:, :width])[None] * single + mixed[None, :, width:]).astype(BF16)


def pair_kernel(core_ref, w_pair_hbm, pair_hbm, tile_ref, w_pair_ref, pair_ref, pair_sem, sem):
    rows, cols, width = pair_ref.shape
    heads = w_pair_ref.shape[0]
    group = GROUP
    lanes = heads * group
    half = group // 2
    row_start = core_ref[0] * rows

    def pair_copy(i):
        source = pair_hbm.at[pl.ds(row_start + i * group, group)]
        return pltpu.make_async_copy(source, pair_ref.at[pl.ds(i * group, group)], pair_sem.at[i])

    w_pair_copy = pltpu.make_async_copy(w_pair_hbm, w_pair_ref, sem)
    w_pair_copy.start()
    for i in range(rows // group):
        pair_copy(i).start()
    w_pair_copy.wait()
    w_pair = w_pair_ref[...].astype(F32)
    spread = jnp.concatenate(
        [jnp.broadcast_to(w_pair[h : h + 1], (group, width)) for h in range(heads)], 0
    )
    mix = twice(spread.T.astype(BF16))
    centre = twice(centring(width))
    slot = iota((cols, lanes), 1) % group

    chunks = []
    for chunk in range(rows // group):
        pair_copy(chunk).wait()
        pair = pair_ref[chunk * group : (chunk + 1) * group].reshape(group * cols, width)
        chunks.append(dot(side_by_side(pair), centre).astype(BF16))
    mixes = [dot(centred, mix).reshape(half, cols, 2 * lanes) for centred in chunks]
    average = twice(averaging(width))
    averages = [
        dot(centred * centred, average).reshape(half, cols, 2 * lanes) for centred in chunks
    ]
    for chunk, (mixed, variance) in enumerate(zip(mixes, averages)):
        total = jnp.zeros((cols, lanes), F32)
        spread_out = jnp.zeros((cols, lanes), F32)
        for i in range(group):
            side = slice(i // half * lanes, (i // half + 1) * lanes)
            total = jnp.where(slot == i, mixed[i % half, :, side], total)
            spread_out = jnp.where(slot == i, variance[i % half, :, side], spread_out)
        tile_ref[chunk] = (total * lax.rsqrt(spread_out + EPSILON)).astype(BF16)


def beside(first, second):
    return jnp.concatenate([first[...], second[...]], 1)


def project_kernel(
    core_ref,
    single_ref,
    cond_ref,
    ada_attn_scale,
    ada_attn_shift,
    w_key,
    w_value,
    w_query,
    w_gate,
    *refs,
):
    late_hbm, refs = refs[:7], refs[7:]
    query_ref, key_ref, value_ref, gate_ref, open_ref, trans_ref, near_ref, far_ref = refs[:8]
    late_refs, sem = refs[8:15], refs[15]
    ada_trans_scale, ada_trans_shift, attn_gate, trans_gate, w_swish, w_linear, w_down = late_refs
    samples, atoms_here, width = single_ref.shape
    copies = [
        pltpu.make_async_copy(source, target, sem.at[i])
        for i, (source, target) in enumerate(zip(late_hbm, late_refs))
    ]
    for copy in copies:
        copy.start()

    cond = layer_norm(cond_ref[...]).astype(BF16)
    single = layer_norm(single_ref[...].reshape(-1, width)).reshape(samples, atoms_here, width)
    normed = attn_norm(cond, single, beside(ada_attn_scale, ada_attn_shift))
    down = core_ref[0] == 0
    for sample in range(samples):
        cut = slice(sample * EDGE, (sample + 1) * EDGE)
        head, tail = normed[sample, :EDGE], normed[sample, atoms_here - EDGE :]
        near_ref[cut, :] = jnp.where(down, head, tail)
        far_ref[cut, :] = jnp.where(down, tail, head)
    normed = normed.reshape(-1, width)
    both = dot(normed, beside(w_key, w_value)).astype(BF16).reshape(samples, -1, 2 * width)
    key_ref[...] = both[:, :, :width]
    value_ref[...] = both[:, :, width:]
    both = dot(normed, beside(w_query, w_gate)).reshape(samples, -1, 2 * width)
    query_ref[...] = both[:, :, :width].astype(BF16)
    gate_ref[...] = sigmoid(both[:, :, width:]).astype(BF16)

    for copy in copies:
        copy.wait()
    gates = dot(cond, beside(attn_gate, trans_gate))
    open_ref[...] = sigmoid(gates[:, :width]).astype(BF16)
    normed = attn_norm(cond, single, beside(ada_trans_scale, ada_trans_shift)).reshape(-1, width)
    swish = dot(normed, w_swish[...])
    hidden = (swish * sigmoid(swish) * dot(normed, w_linear[...])).astype(BF16)
    down = dot(hidden, w_down[...]).reshape(samples, -1, width)
    trans_ref[...] = (sigmoid(gates[:, width:])[None] * down).astype(BF16)


def tile_of(refs, place, row_block):
    if len(refs) == 1:
        return refs[0][row_block]
    pair_at, core_at = place
    owners = 2
    mine, theirs, across, diagonal = [ref[...] for ref in refs]
    near = jnp.where(row_block % owners == core_at, mine, theirs)
    far = jnp.where(row_block % owners == core_at, across, diagonal)
    return jnp.where(row_block // owners == pair_at, near, far)


def shifted(values, lanes):
    return pltpu.roll(values, lanes % values.shape[1], 1)


def unpacked(rows, side):
    half = EDGE // 2
    whole, packed = rows[:EDGE], rows[EDGE:].astype(F32)
    if side == 0:
        part = jnp.concatenate([packed, shifted(packed, -GROUP // 2)], 0).astype(BF16)
        return jnp.concatenate([whole, part], 1)
    part = jnp.concatenate([shifted(packed, GROUP // 2), packed], 0).astype(BF16)
    return jnp.concatenate([part, whole], 1)


def select_kernel(blocks, at_ref, pair_ref, core_ref, *refs):
    *tile_refs, _, __, ___, near_ref, far_ref, ____, held_ref = refs
    groups, cols, lanes = tile_refs[0].shape[-3:]
    device_at, place = at_ref[0], (pair_ref[0], core_ref[0])
    half = EDGE // 2
    for send_ref, core in ((near_ref, 1), (far_ref, 0)):
        above = core_ref[0] == core
        beside = jnp.where(above, device_at + 1, device_at - 1)
        tile = tile_of(tile_refs, place, jnp.clip(beside, 0, blocks - 1))
        tile = jnp.where(above, tile[:, cols - EDGE :], tile[:, :EDGE])
        whole = jnp.where(above, tile[0], tile[1])
        part = jnp.where(above, tile[1], tile[0]).astype(F32)
        first, last = part[:half], part[half:]
        first = jnp.where(above, first, shifted(first, -GROUP // 2))
        last = jnp.where(above, shifted(last, GROUP // 2), last)
        low = iota((half, lanes), 1) % GROUP < GROUP // 2
        packed = jnp.where(low, first, last).astype(BF16)
        send_ref[send_ref.shape[0] - EDGE - half :, :] = jnp.concatenate([whole, packed], 0)
    held_ref[...] = tile_of(tile_refs, place, device_at).reshape(groups * cols, lanes)


def bounds(counts_ref, block, token):
    tok_here = counts_ref.shape[1]
    counts = counts_ref[pl.ds(block, 1), :].astype(F32).astype(BF16)
    counts = jnp.broadcast_to(counts, (8, tok_here))
    before = iota((tok_here, token.shape[1]), 0)
    first = dot(counts, (before < token).astype(BF16))[:1]
    last = dot(counts, (before <= token).astype(BF16))[:1]
    return first.astype(jnp.int32), last.astype(jnp.int32)


def one_hot(reach, offset, count):
    first, last = reach
    position = iota((count, first.shape[1]), 0) + offset
    return ((first <= position) & (position < last)).astype(F32).astype(BF16)


def expand(hot, tile, groups):
    tile = tile.reshape(groups, -1, tile.shape[-1])
    tile = jnp.concatenate([tile[part] for part in range(groups)], 1)
    return dot(hot, tile).astype(BF16)


def head_mask(heads, lanes):
    rows = heads * Q_WIN
    lane_head = iota((rows, lanes), 1) // GROUP % heads
    row_head = iota((rows, lanes), 0) // Q_WIN
    return (lane_head == row_head).astype(F32).astype(BF16)


def picks_of(heads, reach, starts):
    same_head = head_mask(heads, reach[0].shape[1])
    return [
        jnp.concatenate([one_hot(reach, start, Q_WIN)] * heads, 0) * same_head for start in starts
    ]


def attend(heads, windows, query_ref, gate_ref, gated_ref, paired=0):
    samples, _, width = query_ref.shape
    head_dim = width // heads
    rows = heads * Q_WIN
    own_head = iota((rows, width), 1) // head_dim == iota((rows, width), 0) // Q_WIN
    own_head = own_head.astype(F32).astype(BF16)
    channel_head = iota((Q_WIN, 2 * width), 1) % width // head_dim
    ones = jnp.ones((K_WIN, width), BF16)
    scaling = LOG2E / math.sqrt(head_dim)

    biases = []
    for _, _, near, pick, mask in windows:
        bias = lax.dot_general(pick, near, LAST, preferred_element_type=F32) * LOG2E
        biases.append(bias if mask is None else jnp.where(mask, bias, MASKED))
    units = [(sample, i) for i in range(len(windows)) for sample in range(samples)]
    scores = []
    for first in range(0, len(units), 2):
        couple = units[first : first + 2]
        queries, keys = [], []
        for sample, i in couple:
            query = query_ref[sample, pl.ds(windows[i][0], Q_WIN), :]
            queries.append(jnp.concatenate([query] * heads, 0) * own_head)
            keys.append(windows[i][1][sample][0])
        if len(couple) == 2:
            blank = jnp.zeros_like(keys[0])
            keys = [jnp.concatenate([keys[0], blank], 1), jnp.concatenate([blank, keys[1]], 1)]
        product = lax.dot_general(
            jnp.concatenate(queries, 1),
            jnp.concatenate(keys, 0),
            LAST,
            preferred_element_type=F32,
        )
        for j, (_, i) in enumerate(couple):
            scores.append(product[:, j * K_WIN : (j + 1) * K_WIN] * scaling + biases[i])
    tops = [jnp.max(score, axis=-1, keepdims=True) for score in scores]
    raised = [jnp.exp2(score - top) for score, top in zip(scores, tops)]

    def by_head(parts, like):
        picked = jnp.broadcast_to(parts[:Q_WIN], (Q_WIN, like.shape[1]))
        for head in range(1, heads):
            part = parts[head * Q_WIN : (head + 1) * Q_WIN]
            picked = jnp.where(like == head, part, picked)
        return picked

    mixes = []
    for first in range(0, len(units), 2):
        couple = units[first : first + 2]
        values = [windows[i][1][sample][1] for sample, i in couple]
        weights = [weight.astype(BF16) for weight in raised[first : first + 2]]
        if paired and first // 2 % paired == 0 and len(couple) == 2:
            blank = jnp.zeros_like(values[0])
            values = [
                jnp.concatenate([values[0], blank], 1),
                jnp.concatenate([blank, values[1]], 1),
            ]
            both = dot(jnp.concatenate(weights, 1), jnp.concatenate(values, 0))
            for j in range(2):
                total = jnp.sum(raised[first + j], axis=-1, keepdims=True)
                narrow = channel_head[:, :width]
                attended = by_head(both[:, j * width : (j + 1) * width], narrow)
                mixes.append((attended, by_head(total, narrow)))
        else:
            for value, weight in zip(values, weights):
                picked = by_head(dot(weight, jnp.concatenate([value, ones], 1)), channel_head)
                mixes.append((picked[:, :width], picked[:, width:]))
    for (sample, i), (attended, total) in zip(units, mixes):
        attended = attended * pl.reciprocal(total, approx=True)
        at = pl.ds(windows[i][0], Q_WIN)
        gate = gate_ref[sample, at, :].astype(F32)
        gated_ref[sample, at, :] = (gate * attended).astype(BF16)


def close(sample, cut, gated_ref, open_ref, trans_ref, w_out_ref):
    mixed = dot(gated_ref[sample, cut, :], w_out_ref[...])
    opened, trans = open_ref[cut, :].astype(F32), trans_ref[sample, cut, :].astype(F32)
    return (opened * mixed + trans).astype(BF16)


def row_tokens(heads, tok_here):
    lane = iota((tok_here, heads * tok_here), 1)
    return lane // (heads * GROUP) * GROUP + lane % GROUP


def outer_starts(atoms_here):
    skip = -(-EDGE // Q_WIN)
    return [
        [side * (atoms_here - skip * Q_WIN) + i * Q_WIN for i in range(skip)] for side in range(2)
    ]


def inner_kernel(
    heads,
    blocks,
    at_ref,
    counts_ref,
    query_ref,
    key_ref,
    value_ref,
    gate_ref,
    open_ref,
    trans_ref,
    w_out_ref,
    held_ref,
    out_ref,
    pick_ref,
    hot_ref,
    side_ref,
    near_ref,
    gated_ref,
):
    samples, atoms_here, width = query_ref.shape
    tok_here = counts_ref.shape[1]
    device_at = at_ref[0]
    hot = one_hot(
        bounds(counts_ref, device_at, iota((tok_here, tok_here), 1)), 0, atoms_here
    )
    near_ref[...] = expand(hot, held_ref[...], tok_here // GROUP)
    reach = bounds(counts_ref, device_at, row_tokens(heads, tok_here))
    skip = -(-EDGE // Q_WIN)
    starts = [window * Q_WIN for window in range(skip, atoms_here // Q_WIN - skip)]
    windows = []
    for start, pick in zip(starts, picks_of(heads, reach, starts)):
        cut = slice(start - EDGE, start - EDGE + K_WIN)
        parts = [(key_ref[i, cut, :], value_ref[i, cut, :]) for i in range(samples)]
        windows.append((start, parts, near_ref[cut, :], pick, None))
    attend(heads, windows, query_ref, gate_ref, gated_ref, paired=2)

    cut = slice(starts[0], starts[-1] + Q_WIN)
    for sample in range(samples):
        out_ref[sample] = close(sample, cut, gated_ref, open_ref, trans_ref, w_out_ref)

    inside = side_ref.shape[1]
    sides = (
        (jnp.maximum(device_at - 1, 0), atoms_here - EDGE, tok_here - EDGE, 0),
        (jnp.minimum(device_at + 1, blocks - 1), 0, 0, atoms_here - inside),
    )
    for side, (block, offset, token, own_start) in enumerate(sides):
        nearest = bounds(counts_ref, block, iota((tok_here, EDGE), 1) + token)
        hot_ref[side] = one_hot(nearest, offset, EDGE)
        side_ref[side] = near_ref[own_start : own_start + inside, :]
        for i, pick in enumerate(picks_of(heads, reach, outer_starts(atoms_here)[side])):
            pick_ref[side, i] = pick


def outer_kernel(
    heads,
    blocks,
    at_ref,
    core_ref,
    query_ref,
    own_key_ref,
    own_value_ref,
    gate_ref,
    open_ref,
    trans_ref,
    w_out_ref,
    inner_ref,
    pick_ref,
    hot_ref,
    side_ref,
    w_key,
    w_value,
    first_ref,
    second_ref,
    out_hbm,
    gated_ref,
    out_ref,
    sem,
):
    samples, atoms_here, width = query_ref.shape
    device_at = at_ref[0]
    ends = atoms_here * blocks
    starts = outer_starts(atoms_here)
    margin = len(starts[0]) * Q_WIN
    inside = side_ref.shape[1]

    whole = pltpu.make_async_copy(
        inner_ref, out_hbm.at[:, pl.ds(margin, atoms_here - 2 * margin)], sem.at[0]
    )
    whole.start()

    down = core_ref[0] == 0
    first, second = first_ref[...], second_ref[...]
    arrived = (jnp.where(down, second, first), jnp.where(down, first, second))
    count = samples * EDGE
    edges = jnp.concatenate([rows[:count] for rows in arrived], 0)
    edges = dot(edges, beside(w_key, w_value)).astype(BF16).reshape(2, samples, EDGE, 2 * width)

    def joined(side, edge, own):
        return jnp.concatenate([own, edge] if side else [edge, own], 0)

    windows = []
    for side in range(2):
        own = slice(side * (atoms_here - inside), side * (atoms_here - inside) + inside)
        parts = [
            (
                joined(side, edges[side, i, :, :width], own_key_ref[i, own, :]),
                joined(side, edges[side, i, :, width:], own_value_ref[i, own, :]),
            )
            for i in range(samples)
        ]
        near = dot(hot_ref[side], unpacked(arrived[side][count:], side)).astype(BF16)
        near = joined(side, near, side_ref[side])
        for i, start in enumerate(starts[side]):
            cut = slice(i * Q_WIN, i * Q_WIN + K_WIN)
            key_at = iota((heads * Q_WIN, K_WIN), 1) + (device_at * atoms_here + start - EDGE)
            mask = (key_at >= 0) & (key_at < ends)
            pieces = [(keys[cut], values[cut]) for keys, values in parts]
            windows.append((start, pieces, near[cut], pick_ref[side, i], mask))
    attend(heads, windows, query_ref, gate_ref, gated_ref)
    copies = []
    for side in range(2):
        cut = slice(starts[side][0], starts[side][0] + margin)
        for sample in range(samples):
            out_ref[side, sample] = close(sample, cut, gated_ref, open_ref, trans_ref, w_out_ref)
        target = out_hbm.at[:, pl.ds(starts[side][0], margin)]
        copies.append(pltpu.make_async_copy(out_ref.at[side], target, sem.at[1 + side]))
        copies[-1].start()
    for copy in copies:
        copy.wait()
    whole.wait()


def shards(
    atom_single,
    atom_cond,
    pair_cond,
    atom_counts,
    ada_attn_scale,
    ada_attn_shift,
    w_query,
    w_key,
    w_value,
    w_gate,
    w_out,
    attn_gate,
    w_pair,
    ada_trans_scale,
    ada_trans_shift,
    w_swish,
    w_linear,
    w_down,
    trans_gate,
):
    device_at = lax.axis_index("atoms")
    blocks = lax.axis_size("atoms")
    samples, atoms_here, width = atom_single.shape
    tok_here = atom_counts.shape[1]
    heads = w_pair.shape[1]
    groups = tok_here // GROUP
    pairs = lax.axis_size("pair")
    assert pair_cond.shape[0] == lax.axis_size("samp") * tok_here
    assert groups == 2 and tok_here - EDGE == GROUP // 2
    at = device_at.astype(jnp.int32).reshape(1)
    pair_at = lax.axis_index("pair").astype(jnp.int32).reshape(1)
    core_at = lax.axis_index("samp").astype(jnp.int32).reshape(1)
    in_hbm = lambda array: pltpu.with_memory_space_constraint(array, pltpu.HBM)
    in_vmem = lambda array: pltpu.with_memory_space_constraint(array, pltpu.VMEM)

    cols = pair_cond.shape[1]
    lanes = heads * GROUP
    wide = (samples, atoms_here, width)
    params = pltpu.CompilerParams(vmem_limit_bytes=VMEM_LIMIT)

    def cost(products):
        return pl.CostEstimate(flops=2 * products, bytes_accessed=4 << 20, transcendentals=0)

    sent = pltpu.VMEM((samples * EDGE + EDGE + EDGE // 2, lanes), BF16)
    own = pl.pallas_call(
        pair_kernel,
        in_specs=[IN_SMEM] + [IN_HBM] * 2,
        out_specs=IN_VMEM,
        out_shape=pltpu.VMEM((groups, cols, lanes), BF16),
        scratch_shapes=[
            pltpu.VMEM((heads, width), BF16),
            pltpu.VMEM((tok_here, cols, width), BF16),
            pltpu.SemaphoreType.DMA((groups,)),
            pltpu.SemaphoreType.DMA,
        ],
        compiler_params=params,
        cost_estimate=cost(tok_here * cols * width * width * 2),
    )(core_at, *map(in_hbm, (w_pair.T, pair_cond)))
    if pairs == 2:
        swapped = [(0, 1), (1, 0)]
        across = lax.ppermute(own, "pair", swapped)
        diagonal = lax.ppermute(own, ("pair", "samp"), [(0, 3), (1, 2), (2, 1), (3, 0)])
        tiles = (own, lax.ppermute(own, "samp", swapped), across, diagonal)
    else:
        tiles = (lax.all_gather(own, ("pair", "samp")),)

    operands = (
        atom_single,
        atom_cond,
        ada_attn_scale,
        ada_attn_shift,
        w_key,
        w_value,
        w_query,
        w_gate,
    )
    late = (ada_trans_scale, ada_trans_shift, attn_gate, trans_gate, w_swish, w_linear, w_down)
    query, keys, values, gate, opened, trans, near, far = pl.pallas_call(
        project_kernel,
        in_specs=[IN_SMEM] + [IN_VMEM] * len(operands) + [IN_HBM] * len(late),
        out_specs=[IN_VMEM] * 8,
        out_shape=[pltpu.VMEM(wide, BF16)] * 4
        + [pltpu.VMEM((atoms_here, width), BF16), pltpu.VMEM(wide, BF16), sent, sent],
        scratch_shapes=[pltpu.VMEM(weight.shape, BF16) for weight in late]
        + [pltpu.SemaphoreType.DMA((len(late),))],
        compiler_params=params,
        cost_estimate=cost(samples * atoms_here * width * width * 20),
    )(core_at, *map(in_vmem, operands), *map(in_hbm, late))

    operands = (*tiles, near, far, opened)
    first = 3 + len(tiles)
    near, far, opened, held = pl.pallas_call(
        functools.partial(select_kernel, blocks),
        in_specs=[IN_SMEM] * 3 + [IN_VMEM] * len(operands),
        out_specs=[IN_VMEM] * 4,
        out_shape=[
            sent,
            sent,
            pltpu.VMEM((atoms_here, width), BF16),
            pltpu.VMEM((groups * cols, lanes), BF16),
        ],
        input_output_aliases={first: 0, first + 1: 1, first + 2: 2},
        compiler_params=params,
    )(at, pair_at, core_at, *map(in_vmem, operands))

    down = [(2 * i, 2 * (i - 1)) for i in range(1, blocks)] + [(0, 1)]
    up = [(2 * i + 1, 2 * (i + 1) + 1) for i in range(blocks - 1)] + [(2 * blocks - 1, 2 * blocks - 2)]
    cycle = down + up
    first = lax.ppermute(near, ("atoms", "samp"), cycle)
    second = lax.ppermute(far, ("atoms", "samp"), [(target, source) for source, target in cycle])

    margin = -(-EDGE // Q_WIN) * Q_WIN
    inside = margin - Q_WIN + K_WIN - EDGE
    expanded = heads * tok_here
    operands = (query, keys, values, gate, opened, trans, w_out)
    inner, picks, hots, beside_edges = pl.pallas_call(
        functools.partial(inner_kernel, heads, blocks),
        in_specs=[IN_SMEM] + [IN_VMEM] * (2 + len(operands)),
        out_specs=[IN_VMEM] * 4,
        out_shape=[
            pltpu.VMEM((samples, atoms_here - 2 * margin, width), BF16),
            pltpu.VMEM((2, margin // Q_WIN, heads * Q_WIN, expanded), BF16),
            pltpu.VMEM((2, EDGE, EDGE), BF16),
            pltpu.VMEM((2, inside, expanded), BF16),
        ],
        scratch_shapes=[
            pltpu.VMEM((atoms_here, expanded), BF16),
            pltpu.VMEM(wide, BF16),
        ],
        compiler_params=params,
        cost_estimate=cost(samples * atoms_here * width * width * 12),
    )(at, atom_counts, *map(in_vmem, (*operands, held)))

    operands += (inner, picks, hots, beside_edges, w_key, w_value, first, second)
    return pl.pallas_call(
        functools.partial(outer_kernel, heads, blocks),
        in_specs=[IN_SMEM] * 2 + [IN_VMEM] * len(operands),
        out_specs=IN_HBM,
        out_shape=pltpu.HBM(wide, BF16),
        scratch_shapes=[
            pltpu.VMEM(wide, BF16),
            pltpu.VMEM((2, samples, margin, width), BF16),
            pltpu.SemaphoreType.DMA((3,)),
        ],
        compiler_params=params,
        cost_estimate=cost(samples * atoms_here * width * width * 4),
    )(at, core_at, *map(in_vmem, operands))


def solution(mesh):
    return jax.shard_map(
        shards,
        mesh=mesh,
        in_specs=(
            P(("groups", "pair", "samp"), "atoms", None),
            P(("groups", "atoms"), None),
            P(("groups", "pair"), "atoms", None),
            P("groups", None),
        )
        + (P(),) * 15,
        out_specs=P(("groups", "pair", "samp"), "atoms", None),
        check_vma=False,
    )
```

```python
import functools
import math

import jax
import jax.numpy as jnp
from jax import lax
from jax.experimental import pallas as pl
from jax.experimental.pallas import tpu as pltpu
from jax.sharding import PartitionSpec as P

Q_WIN = 32
K_WIN = 128
EDGE = 48
GROUP = 32

EPSILON = 1e-05
MASKED = -1e30
LOG2E = math.log2(math.e)
BF16 = jnp.bfloat16
F32 = jnp.float32
LAST = (((1,), (1,)), ((), ()))
VMEM_LIMIT = 32 << 20
IN_VMEM = pl.BlockSpec(memory_space=pltpu.VMEM)
IN_HBM = pl.BlockSpec(memory_space=pltpu.HBM)
IN_SMEM = pl.BlockSpec(memory_space=pltpu.SMEM)


def dot(a, b):
    return jnp.dot(a, b, preferred_element_type=F32)


def iota(shape, dim):
    return lax.broadcasted_iota(jnp.int32, shape, dim)


def twice(matrix):
    blank = jnp.zeros_like(matrix)
    return jnp.concatenate(
        [jnp.concatenate([matrix, blank], 1), jnp.concatenate([blank, matrix], 1)], 0
    )


def side_by_side(rows):
    half = rows.shape[0] // 2
    return jnp.concatenate([rows[:half], rows[half:]], 1)


def centring(width):
    same = iota((width, width), 0) == iota((width, width), 1)
    return jnp.where(same, 1.0 - 1.0 / width, -1.0 / width).astype(BF16)


def averaging(width):
    return jnp.full((width, width), 1.0 / width, BF16)


def mean_square(centred):
    return jnp.mean(centred * centred, axis=-1, keepdims=True)


def layer_norm(rows):
    width = rows.shape[1]
    both = dot(side_by_side(rows), twice(centring(width)))
    centred = jnp.concatenate([both[:, :width], both[:, width:]], 0)
    return centred * lax.rsqrt(mean_square(centred) + EPSILON)


def sigmoid(values):
    return 0.5 * jnp.tanh(0.5 * values) + 0.5


def attn_norm(cond, single, ada):
    width = single.shape[-1]
    mixed = dot(cond, ada)
    return (sigmoid(mixed[:, :width])[None] * single + mixed[None, :, width:]).astype(BF16)


def pair_kernel(core_ref, w_pair_hbm, pair_hbm, tile_ref, w_pair_ref, pair_ref, pair_sem, sem):
    rows, cols, width = pair_ref.shape
    heads = w_pair_ref.shape[0]
    group = GROUP
    lanes = heads * group
    half = group // 2
    row_start = core_ref[0] * rows

    def pair_copy(i):
        source = pair_hbm.at[pl.ds(row_start + i * group, group)]
        return pltpu.make_async_copy(source, pair_ref.at[pl.ds(i * group, group)], pair_sem.at[i])

    w_pair_copy = pltpu.make_async_copy(w_pair_hbm, w_pair_ref, sem)
    w_pair_copy.start()
    for i in range(rows // group):
        pair_copy(i).start()
    w_pair_copy.wait()
    w_pair = w_pair_ref[...].astype(F32)
    spread = jnp.concatenate(
        [jnp.broadcast_to(w_pair[h : h + 1], (group, width)) for h in range(heads)], 0
    )
    mix = twice(spread.T.astype(BF16))
    centre = twice(centring(width))
    slot = iota((cols, lanes), 1) % group

    chunks = []
    for chunk in range(rows // group):
        pair_copy(chunk).wait()
        pair = pair_ref[chunk * group : (chunk + 1) * group].reshape(group * cols, width)
        chunks.append(dot(side_by_side(pair), centre).astype(BF16))
    mixes = [dot(centred, mix).reshape(half, cols, 2 * lanes) for centred in chunks]
    squares = chunks[0][:, :width] * chunks[0][:, :width]
    average = dot(side_by_side(squares), twice(averaging(width)))
    average = jnp.concatenate([average[:, :width], average[:, width:]], 0)
    for chunk, (centred, mixed) in enumerate(zip(chunks, mixes)):
        variances = [average.reshape(half, cols, width)] if chunk == 0 else []
        for part in range(len(variances), 2):
            rows_of = centred[:, part * width : (part + 1) * width].astype(F32)
            variances.append(mean_square(rows_of).reshape(half, cols, 1))
        total = jnp.zeros((cols, lanes), F32)
        spread_out = jnp.zeros((cols, lanes), F32)
        for i in range(group):
            side = slice(i // half * lanes, (i // half + 1) * lanes)
            total = jnp.where(slot == i, mixed[i % half, :, side], total)
            spread_out = jnp.where(slot == i, variances[i // half][i % half], spread_out)
        tile_ref[chunk] = (total * lax.rsqrt(spread_out + EPSILON)).astype(BF16)


def beside(first, second):
    return jnp.concatenate([first[...], second[...]], 1)


def project_kernel(
    core_ref,
    single_ref,
    cond_ref,
    ada_attn_scale,
    ada_attn_shift,
    w_key,
    w_value,
    w_query,
    w_gate,
    *refs,
):
    late_hbm, refs = refs[:7], refs[7:]
    query_ref, key_ref, value_ref, gate_ref, open_ref, trans_ref, near_ref, far_ref = refs[:8]
    late_refs, sem = refs[8:15], refs[15]
    ada_trans_scale, ada_trans_shift, attn_gate, trans_gate, w_swish, w_linear, w_down = late_refs
    samples, atoms_here, width = single_ref.shape
    copies = [
        pltpu.make_async_copy(source, target, sem.at[i])
        for i, (source, target) in enumerate(zip(late_hbm, late_refs))
    ]
    for copy in copies:
        copy.start()

    cond = layer_norm(cond_ref[...]).astype(BF16)
    single = layer_norm(single_ref[...].reshape(-1, width)).reshape(samples, atoms_here, width)
    normed = attn_norm(cond, single, beside(ada_attn_scale, ada_attn_shift))
    down = core_ref[0] == 0
    for sample in range(samples):
        cut = slice(sample * EDGE, (sample + 1) * EDGE)
        head, tail = normed[sample, :EDGE], normed[sample, atoms_here - EDGE :]
        near_ref[cut, :] = jnp.where(down, head, tail)
        far_ref[cut, :] = jnp.where(down, tail, head)
    for copy in copies:
        copy.wait()
    normed = normed.reshape(-1, width)
    both = dot(normed, beside(w_key, w_value)).astype(BF16).reshape(samples, -1, 2 * width)
    key_ref[...] = both[:, :, :width]
    value_ref[...] = both[:, :, width:]
    both = dot(normed, beside(w_query, w_gate)).reshape(samples, -1, 2 * width)
    query_ref[...] = both[:, :, :width].astype(BF16)
    gate_ref[...] = sigmoid(both[:, :, width:]).astype(BF16)

    gates = dot(cond, beside(attn_gate, trans_gate))
    open_ref[...] = sigmoid(gates[:, :width]).astype(BF16)
    normed = attn_norm(cond, single, beside(ada_trans_scale, ada_trans_shift)).reshape(-1, width)
    swish = dot(normed, w_swish[...])
    hidden = (swish * sigmoid(swish) * dot(normed, w_linear[...])).astype(BF16)
    down = dot(hidden, w_down[...]).reshape(samples, -1, width)
    trans_ref[...] = (sigmoid(gates[:, width:])[None] * down).astype(BF16)


def tile_of(refs, place, row_block):
    if len(refs) == 1:
        return refs[0][row_block]
    pair_at, core_at = place
    owners = 2
    mine, theirs, across, diagonal = [ref[...] for ref in refs]
    near = jnp.where(row_block % owners == core_at, mine, theirs)
    far = jnp.where(row_block % owners == core_at, across, diagonal)
    return jnp.where(row_block // owners == pair_at, near, far)


def shifted(values, lanes):
    return pltpu.roll(values, lanes % values.shape[1], 1)


def unpacked(rows, side):
    half = EDGE // 2
    whole, packed = rows[:EDGE], rows[EDGE:].astype(F32)
    if side == 0:
        part = jnp.concatenate([packed, shifted(packed, -GROUP // 2)], 0).astype(BF16)
        return jnp.concatenate([whole, part], 1)
    part = jnp.concatenate([shifted(packed, GROUP // 2), packed], 0).astype(BF16)
    return jnp.concatenate([part, whole], 1)


def select_kernel(blocks, at_ref, pair_ref, core_ref, *refs):
    *tile_refs, _, __, ___, near_ref, far_ref, ____, held_ref = refs
    groups, cols, lanes = tile_refs[0].shape[-3:]
    device_at, place = at_ref[0], (pair_ref[0], core_ref[0])
    half = EDGE // 2
    for send_ref, core in ((near_ref, 1), (far_ref, 0)):
        above = core_ref[0] == core
        beside = jnp.where(above, device_at + 1, device_at - 1)
        tile = tile_of(tile_refs, place, jnp.clip(beside, 0, blocks - 1))
        tile = jnp.where(above, tile[:, cols - EDGE :], tile[:, :EDGE])
        whole = jnp.where(above, tile[0], tile[1])
        part = jnp.where(above, tile[1], tile[0]).astype(F32)
        first, last = part[:half], part[half:]
        first = jnp.where(above, first, shifted(first, -GROUP // 2))
        last = jnp.where(above, shifted(last, GROUP // 2), last)
        low = iota((half, lanes), 1) % GROUP < GROUP // 2
        packed = jnp.where(low, first, last).astype(BF16)
        send_ref[send_ref.shape[0] - EDGE - half :, :] = jnp.concatenate([whole, packed], 0)
    held_ref[...] = tile_of(tile_refs, place, device_at).reshape(groups * cols, lanes)


def bounds(counts_ref, block, token):
    tok_here = counts_ref.shape[1]
    counts = counts_ref[pl.ds(block, 1), :].astype(F32).astype(BF16)
    counts = jnp.broadcast_to(counts, (8, tok_here))
    before = iota((tok_here, token.shape[1]), 0)
    first = dot(counts, (before < token).astype(BF16))[:1]
    last = dot(counts, (before <= token).astype(BF16))[:1]
    return first.astype(jnp.int32), last.astype(jnp.int32)


def one_hot(reach, offset, count):
    first, last = reach
    position = iota((count, first.shape[1]), 0) + offset
    return ((first <= position) & (position < last)).astype(F32).astype(BF16)


def expand(hot, tile, groups):
    tile = tile.reshape(groups, -1, tile.shape[-1])
    tile = jnp.concatenate([tile[part] for part in range(groups)], 1)
    return dot(hot, tile).astype(BF16)


def head_mask(heads, lanes):
    rows = heads * Q_WIN
    lane_head = iota((rows, lanes), 1) // GROUP % heads
    row_head = iota((rows, lanes), 0) // Q_WIN
    return (lane_head == row_head).astype(F32).astype(BF16)


def picks_of(heads, reach, starts):
    same_head = head_mask(heads, reach[0].shape[1])
    return [
        jnp.concatenate([one_hot(reach, start, Q_WIN)] * heads, 0) * same_head for start in starts
    ]


def attend(heads, windows, query_ref, gate_ref, gated_ref, paired=0):
    samples, _, width = query_ref.shape
    head_dim = width // heads
    rows = heads * Q_WIN
    own_head = iota((rows, width), 1) // head_dim == iota((rows, width), 0) // Q_WIN
    own_head = own_head.astype(F32).astype(BF16)
    channel_head = iota((Q_WIN, 2 * width), 1) % width // head_dim
    ones = jnp.ones((K_WIN, width), BF16)
    scaling = LOG2E / math.sqrt(head_dim)

    biases = []
    for _, _, near, pick, mask in windows:
        bias = lax.dot_general(pick, near, LAST, preferred_element_type=F32) * LOG2E
        biases.append(bias if mask is None else jnp.where(mask, bias, MASKED))
    units = [(sample, i) for i in range(len(windows)) for sample in range(samples)]
    scores = []
    for first in range(0, len(units), 2):
        couple = units[first : first + 2]
        queries, keys = [], []
        for sample, i in couple:
            query = query_ref[sample, pl.ds(windows[i][0], Q_WIN), :]
            queries.append(jnp.concatenate([query] * heads, 0) * own_head)
            keys.append(windows[i][1][sample][0])
        if len(couple) == 2:
            blank = jnp.zeros_like(keys[0])
            keys = [jnp.concatenate([keys[0], blank], 1), jnp.concatenate([blank, keys[1]], 1)]
        product = lax.dot_general(
            jnp.concatenate(queries, 1),
            jnp.concatenate(keys, 0),
            LAST,
            preferred_element_type=F32,
        )
        for j, (_, i) in enumerate(couple):
            scores.append(product[:, j * K_WIN : (j + 1) * K_WIN] * scaling + biases[i])
    tops = [jnp.max(score, axis=-1, keepdims=True) for score in scores]
    raised = [jnp.exp2(score - top) for score, top in zip(scores, tops)]

    def by_head(parts, like):
        picked = jnp.broadcast_to(parts[:Q_WIN], (Q_WIN, like.shape[1]))
        for head in range(1, heads):
            part = parts[head * Q_WIN : (head + 1) * Q_WIN]
            picked = jnp.where(like == head, part, picked)
        return picked

    mixes = []
    for first in range(0, len(units), 2):
        couple = units[first : first + 2]
        values = [windows[i][1][sample][1] for sample, i in couple]
        weights = [weight.astype(BF16) for weight in raised[first : first + 2]]
        if paired and first // 2 % paired == 0 and len(couple) == 2:
            blank = jnp.zeros_like(values[0])
            values = [
                jnp.concatenate([values[0], blank], 1),
                jnp.concatenate([blank, values[1]], 1),
            ]
            both = dot(jnp.concatenate(weights, 1), jnp.concatenate(values, 0))
            for j in range(2):
                total = jnp.sum(raised[first + j], axis=-1, keepdims=True)
                narrow = channel_head[:, :width]
                attended = by_head(both[:, j * width : (j + 1) * width], narrow)
                mixes.append((attended, by_head(total, narrow)))
        else:
            for value, weight in zip(values, weights):
                picked = by_head(dot(weight, jnp.concatenate([value, ones], 1)), channel_head)
                mixes.append((picked[:, :width], picked[:, width:]))
    for (sample, i), (attended, total) in zip(units, mixes):
        attended = attended * pl.reciprocal(total, approx=True)
        at = pl.ds(windows[i][0], Q_WIN)
        gate = gate_ref[sample, at, :].astype(F32)
        gated_ref[sample, at, :] = (gate * attended).astype(BF16)


def close(sample, cut, gated_ref, open_ref, trans_ref, w_out_ref):
    mixed = dot(gated_ref[sample, cut, :], w_out_ref[...])
    opened, trans = open_ref[cut, :].astype(F32), trans_ref[sample, cut, :].astype(F32)
    return (opened * mixed + trans).astype(BF16)


def row_tokens(heads, tok_here):
    lane = iota((tok_here, heads * tok_here), 1)
    return lane // (heads * GROUP) * GROUP + lane % GROUP


def outer_starts(atoms_here):
    skip = -(-EDGE // Q_WIN)
    return [
        [side * (atoms_here - skip * Q_WIN) + i * Q_WIN for i in range(skip)] for side in range(2)
    ]


def inner_kernel(
    heads,
    blocks,
    at_ref,
    counts_ref,
    query_ref,
    key_ref,
    value_ref,
    gate_ref,
    open_ref,
    trans_ref,
    w_out_ref,
    held_ref,
    out_ref,
    pick_ref,
    hot_ref,
    side_ref,
    near_ref,
    gated_ref,
):
    samples, atoms_here, width = query_ref.shape
    tok_here = counts_ref.shape[1]
    device_at = at_ref[0]
    hot = one_hot(
        bounds(counts_ref, device_at, iota((tok_here, tok_here), 1)), 0, atoms_here
    )
    near_ref[...] = expand(hot, held_ref[...], tok_here // GROUP)
    reach = bounds(counts_ref, device_at, row_tokens(heads, tok_here))
    skip = -(-EDGE // Q_WIN)
    starts = [window * Q_WIN for window in range(skip, atoms_here // Q_WIN - skip)]
    windows = []
    for start, pick in zip(starts, picks_of(heads, reach, starts)):
        cut = slice(start - EDGE, start - EDGE + K_WIN)
        parts = [(key_ref[i, cut, :], value_ref[i, cut, :]) for i in range(samples)]
        windows.append((start, parts, near_ref[cut, :], pick, None))
    attend(heads, windows, query_ref, gate_ref, gated_ref, paired=2)

    cut = slice(starts[0], starts[-1] + Q_WIN)
    for sample in range(samples):
        out_ref[sample] = close(sample, cut, gated_ref, open_ref, trans_ref, w_out_ref)

    inside = side_ref.shape[1]
    sides = (
        (jnp.maximum(device_at - 1, 0), atoms_here - EDGE, tok_here - EDGE, 0),
        (jnp.minimum(device_at + 1, blocks - 1), 0, 0, atoms_here - inside),
    )
    for side, (block, offset, token, own_start) in enumerate(sides):
        nearest = bounds(counts_ref, block, iota((tok_here, EDGE), 1) + token)
        hot_ref[side] = one_hot(nearest, offset, EDGE)
        side_ref[side] = near_ref[own_start : own_start + inside, :]
        for i, pick in enumerate(picks_of(heads, reach, outer_starts(atoms_here)[side])):
            pick_ref[side, i] = pick


def outer_kernel(
    heads,
    blocks,
    at_ref,
    core_ref,
    query_ref,
    own_key_ref,
    own_value_ref,
    gate_ref,
    open_ref,
    trans_ref,
    w_out_ref,
    inner_ref,
    pick_ref,
    hot_ref,
    side_ref,
    w_key,
    w_value,
    first_ref,
    second_ref,
    out_hbm,
    gated_ref,
    out_ref,
    sem,
):
    samples, atoms_here, width = query_ref.shape
    device_at = at_ref[0]
    ends = atoms_here * blocks
    starts = outer_starts(atoms_here)
    margin = len(starts[0]) * Q_WIN
    inside = side_ref.shape[1]

    whole = pltpu.make_async_copy(
        inner_ref, out_hbm.at[:, pl.ds(margin, atoms_here - 2 * margin)], sem.at[0]
    )
    whole.start()

    down = core_ref[0] == 0
    first, second = first_ref[...], second_ref[...]
    arrived = (jnp.where(down, second, first), jnp.where(down, first, second))
    count = samples * EDGE
    edges = jnp.concatenate([rows[:count] for rows in arrived], 0)
    edges = dot(edges, beside(w_key, w_value)).astype(BF16).reshape(2, samples, EDGE, 2 * width)

    def joined(side, edge, own):
        return jnp.concatenate([own, edge] if side else [edge, own], 0)

    windows = []
    for side in range(2):
        own = slice(side * (atoms_here - inside), side * (atoms_here - inside) + inside)
        parts = [
            (
                joined(side, edges[side, i, :, :width], own_key_ref[i, own, :]),
                joined(side, edges[side, i, :, width:], own_value_ref[i, own, :]),
            )
            for i in range(samples)
        ]
        near = dot(hot_ref[side], unpacked(arrived[side][count:], side)).astype(BF16)
        near = joined(side, near, side_ref[side])
        for i, start in enumerate(starts[side]):
            cut = slice(i * Q_WIN, i * Q_WIN + K_WIN)
            key_at = iota((heads * Q_WIN, K_WIN), 1) + (device_at * atoms_here + start - EDGE)
            mask = (key_at >= 0) & (key_at < ends)
            pieces = [(keys[cut], values[cut]) for keys, values in parts]
            windows.append((start, pieces, near[cut], pick_ref[side, i], mask))
    attend(heads, windows, query_ref, gate_ref, gated_ref)
    copies = []
    for side in range(2):
        cut = slice(starts[side][0], starts[side][0] + margin)
        for sample in range(samples):
            out_ref[side, sample] = close(sample, cut, gated_ref, open_ref, trans_ref, w_out_ref)
        target = out_hbm.at[:, pl.ds(starts[side][0], margin)]
        copies.append(pltpu.make_async_copy(out_ref.at[side], target, sem.at[1 + side]))
        copies[-1].start()
    for copy in copies:
        copy.wait()
    whole.wait()


def shards(
    atom_single,
    atom_cond,
    pair_cond,
    atom_counts,
    ada_attn_scale,
    ada_attn_shift,
    w_query,
    w_key,
    w_value,
    w_gate,
    w_out,
    attn_gate,
    w_pair,
    ada_trans_scale,
    ada_trans_shift,
    w_swish,
    w_linear,
    w_down,
    trans_gate,
):
    device_at = lax.axis_index("atoms")
    blocks = lax.axis_size("atoms")
    samples, atoms_here, width = atom_single.shape
    tok_here = atom_counts.shape[1]
    heads = w_pair.shape[1]
    groups = tok_here // GROUP
    pairs = lax.axis_size("pair")
    assert pair_cond.shape[0] == lax.axis_size("samp") * tok_here
    assert groups == 2 and tok_here - EDGE == GROUP // 2
    at = device_at.astype(jnp.int32).reshape(1)
    pair_at = lax.axis_index("pair").astype(jnp.int32).reshape(1)
    core_at = lax.axis_index("samp").astype(jnp.int32).reshape(1)
    in_hbm = lambda array: pltpu.with_memory_space_constraint(array, pltpu.HBM)
    in_vmem = lambda array: pltpu.with_memory_space_constraint(array, pltpu.VMEM)

    cols = pair_cond.shape[1]
    lanes = heads * GROUP
    wide = (samples, atoms_here, width)
    params = pltpu.CompilerParams(vmem_limit_bytes=VMEM_LIMIT)

    def cost(products):
        return pl.CostEstimate(flops=2 * products, bytes_accessed=4 << 20, transcendentals=0)

    sent = pltpu.VMEM((samples * EDGE + EDGE + EDGE // 2, lanes), BF16)
    own = pl.pallas_call(
        pair_kernel,
        in_specs=[IN_SMEM] + [IN_HBM] * 2,
        out_specs=IN_VMEM,
        out_shape=pltpu.VMEM((groups, cols, lanes), BF16),
        scratch_shapes=[
            pltpu.VMEM((heads, width), BF16),
            pltpu.VMEM((tok_here, cols, width), BF16),
            pltpu.SemaphoreType.DMA((groups,)),
            pltpu.SemaphoreType.DMA,
        ],
        compiler_params=params,
        cost_estimate=cost(tok_here * cols * width * width * 2),
    )(core_at, *map(in_hbm, (w_pair.T, pair_cond)))
    if pairs == 2:
        swapped = [(0, 1), (1, 0)]
        across = lax.ppermute(own, "pair", swapped)
        diagonal = lax.ppermute(own, ("pair", "samp"), [(0, 3), (1, 2), (2, 1), (3, 0)])
        tiles = (own, lax.ppermute(own, "samp", swapped), across, diagonal)
    else:
        tiles = (lax.all_gather(own, ("pair", "samp")),)

    operands = (
        atom_single,
        atom_cond,
        ada_attn_scale,
        ada_attn_shift,
        w_key,
        w_value,
        w_query,
        w_gate,
    )
    late = (ada_trans_scale, ada_trans_shift, attn_gate, trans_gate, w_swish, w_linear, w_down)
    query, keys, values, gate, opened, trans, near, far = pl.pallas_call(
        project_kernel,
        in_specs=[IN_SMEM] + [IN_VMEM] * len(operands) + [IN_HBM] * len(late),
        out_specs=[IN_VMEM] * 8,
        out_shape=[pltpu.VMEM(wide, BF16)] * 4
        + [pltpu.VMEM((atoms_here, width), BF16), pltpu.VMEM(wide, BF16), sent, sent],
        scratch_shapes=[pltpu.VMEM(weight.shape, BF16) for weight in late]
        + [pltpu.SemaphoreType.DMA((len(late),))],
        compiler_params=params,
        cost_estimate=cost(samples * atoms_here * width * width * 20),
    )(core_at, *map(in_vmem, operands), *map(in_hbm, late))

    operands = (*tiles, near, far, opened)
    first = 3 + len(tiles)
    near, far, opened, held = pl.pallas_call(
        functools.partial(select_kernel, blocks),
        in_specs=[IN_SMEM] * 3 + [IN_VMEM] * len(operands),
        out_specs=[IN_VMEM] * 4,
        out_shape=[
            sent,
            sent,
            pltpu.VMEM((atoms_here, width), BF16),
            pltpu.VMEM((groups * cols, lanes), BF16),
        ],
        input_output_aliases={first: 0, first + 1: 1, first + 2: 2},
        compiler_params=params,
    )(at, pair_at, core_at, *map(in_vmem, operands))

    down = [(2 * i, 2 * (i - 1)) for i in range(1, blocks)] + [(0, 1)]
    up = [(2 * i + 1, 2 * (i + 1) + 1) for i in range(blocks - 1)] + [(2 * blocks - 1, 2 * blocks - 2)]
    cycle = down + up
    first = lax.ppermute(near, ("atoms", "samp"), cycle)
    second = lax.ppermute(far, ("atoms", "samp"), [(target, source) for source, target in cycle])

    margin = -(-EDGE // Q_WIN) * Q_WIN
    inside = margin - Q_WIN + K_WIN - EDGE
    expanded = heads * tok_here
    operands = (query, keys, values, gate, opened, trans, w_out)
    inner, picks, hots, beside_edges = pl.pallas_call(
        functools.partial(inner_kernel, heads, blocks),
        in_specs=[IN_SMEM] + [IN_VMEM] * (2 + len(operands)),
        out_specs=[IN_VMEM] * 4,
        out_shape=[
            pltpu.VMEM((samples, atoms_here - 2 * margin, width), BF16),
            pltpu.VMEM((2, margin // Q_WIN, heads * Q_WIN, expanded), BF16),
            pltpu.VMEM((2, EDGE, EDGE), BF16),
            pltpu.VMEM((2, inside, expanded), BF16),
        ],
        scratch_shapes=[
            pltpu.VMEM((atoms_here, expanded), BF16),
            pltpu.VMEM(wide, BF16),
        ],
        compiler_params=params,
        cost_estimate=cost(samples * atoms_here * width * width * 12),
    )(at, atom_counts, *map(in_vmem, (*operands, held)))

    operands += (inner, picks, hots, beside_edges, w_key, w_value, first, second)
    return pl.pallas_call(
        functools.partial(outer_kernel, heads, blocks),
        in_specs=[IN_SMEM] * 2 + [IN_VMEM] * len(operands),
        out_specs=IN_HBM,
        out_shape=pltpu.HBM(wide, BF16),
        scratch_shapes=[
            pltpu.VMEM(wide, BF16),
            pltpu.VMEM((2, samples, margin, width), BF16),
            pltpu.SemaphoreType.DMA((3,)),
        ],
        compiler_params=params,
        cost_estimate=cost(samples * atoms_here * width * width * 4),
    )(at, core_at, *map(in_vmem, operands))


def solution(mesh):
    return jax.shard_map(
        shards,
        mesh=mesh,
        in_specs=(
            P(("groups", "pair", "samp"), "atoms", None),
            P(("groups", "atoms"), None),
            P(("groups", "pair"), "atoms", None),
            P("groups", None),
        )
        + (P(),) * 15,
        out_specs=P(("groups", "pair", "samp"), "atoms", None),
        check_vma=False,
    )
```

```python
import functools
import math

import jax
import jax.numpy as jnp
from jax import lax
from jax.experimental import pallas as pl
from jax.experimental.pallas import tpu as pltpu
from jax.sharding import PartitionSpec as P

Q_WIN = 32
K_WIN = 128
EDGE = 48
GROUP = 32

EPSILON = 1e-05
MASKED = -1e30
LOG2E = math.log2(math.e)
BF16 = jnp.bfloat16
F32 = jnp.float32
LAST = (((1,), (1,)), ((), ()))
VMEM_LIMIT = 32 << 20
IN_VMEM = pl.BlockSpec(memory_space=pltpu.VMEM)
IN_HBM = pl.BlockSpec(memory_space=pltpu.HBM)
IN_SMEM = pl.BlockSpec(memory_space=pltpu.SMEM)


def dot(a, b):
    return jnp.dot(a, b, preferred_element_type=F32)


def iota(shape, dim):
    return lax.broadcasted_iota(jnp.int32, shape, dim)


def twice(matrix):
    blank = jnp.zeros_like(matrix)
    return jnp.concatenate(
        [jnp.concatenate([matrix, blank], 1), jnp.concatenate([blank, matrix], 1)], 0
    )


def side_by_side(rows):
    half = rows.shape[0] // 2
    return jnp.concatenate([rows[:half], rows[half:]], 1)


def centring(width):
    same = iota((width, width), 0) == iota((width, width), 1)
    return jnp.where(same, 1.0 - 1.0 / width, -1.0 / width).astype(BF16)


def averaging(width):
    return jnp.full((width, width), 1.0 / width, BF16)


def mean_square(centred):
    return jnp.mean(centred * centred, axis=-1, keepdims=True)


def layer_norm(rows):
    width = rows.shape[1]
    both = dot(side_by_side(rows), twice(centring(width)))
    centred = jnp.concatenate([both[:, :width], both[:, width:]], 0)
    return centred * lax.rsqrt(mean_square(centred) + EPSILON)


def sigmoid(values):
    return 0.5 * jnp.tanh(0.5 * values) + 0.5


def attn_norm(cond, single, ada):
    width = single.shape[-1]
    mixed = dot(cond, ada)
    return (sigmoid(mixed[:, :width])[None] * single + mixed[None, :, width:]).astype(BF16)


def pair_kernel(core_ref, w_pair_hbm, pair_hbm, tile_ref, w_pair_ref, pair_ref, pair_sem, sem):
    rows, cols, width = pair_ref.shape
    heads = w_pair_ref.shape[0]
    group = GROUP
    lanes = heads * group
    half = group // 2
    row_start = core_ref[0] * rows

    def pair_copy(i):
        source = pair_hbm.at[pl.ds(row_start + i * group, group)]
        return pltpu.make_async_copy(source, pair_ref.at[pl.ds(i * group, group)], pair_sem.at[i])

    w_pair_copy = pltpu.make_async_copy(w_pair_hbm, w_pair_ref, sem)
    w_pair_copy.start()
    for i in range(rows // group):
        pair_copy(i).start()
    w_pair_copy.wait()
    w_pair = w_pair_ref[...].astype(F32)
    spread = jnp.concatenate(
        [jnp.broadcast_to(w_pair[h : h + 1], (group, width)) for h in range(heads)], 0
    )
    mix = twice(spread.T.astype(BF16))
    centre = twice(centring(width))
    slot = iota((cols, lanes), 1) % group

    for chunk in range(rows // group):
        pair_copy(chunk).wait()
        pair = pair_ref[chunk * group : (chunk + 1) * group].reshape(group * cols, width)
        centred = dot(side_by_side(pair), centre).astype(BF16)
        mixed = dot(centred, mix).reshape(half, cols, 2 * lanes)
        variances = []
        if chunk == 0:
            squares = side_by_side(centred[:, :width] * centred[:, :width])
            average = dot(squares, twice(averaging(width)))
            average = jnp.concatenate([average[:, :width], average[:, width:]], 0)
            variances.append(average.reshape(half, cols, width))
        for part in range(len(variances), 2):
            rows_of = centred[:, part * width : (part + 1) * width].astype(F32)
            variances.append(mean_square(rows_of).reshape(half, cols, 1))
        total = jnp.zeros((cols, lanes), F32)
        spread_out = jnp.zeros((cols, lanes), F32)
        for i in range(group):
            side = slice(i // half * lanes, (i // half + 1) * lanes)
            total = jnp.where(slot == i, mixed[i % half, :, side], total)
            spread_out = jnp.where(slot == i, variances[i // half][i % half], spread_out)
        tile_ref[chunk] = (total * lax.rsqrt(spread_out + EPSILON)).astype(BF16)


def beside(first, second):
    return jnp.concatenate([first[...], second[...]], 1)


def project_kernel(
    core_ref,
    single_ref,
    cond_ref,
    ada_attn_scale,
    ada_attn_shift,
    w_key,
    w_value,
    w_query,
    w_gate,
    *refs,
):
    late_hbm, refs = refs[:7], refs[7:]
    query_ref, key_ref, value_ref, gate_ref, open_ref, trans_ref, near_ref, far_ref = refs[:8]
    late_refs, sem = refs[8:15], refs[15]
    ada_trans_scale, ada_trans_shift, attn_gate, trans_gate, w_swish, w_linear, w_down = late_refs
    samples, atoms_here, width = single_ref.shape
    copies = [
        pltpu.make_async_copy(source, target, sem.at[i])
        for i, (source, target) in enumerate(zip(late_hbm, late_refs))
    ]
    for copy in copies:
        copy.start()

    cond = layer_norm(cond_ref[...]).astype(BF16)
    single = layer_norm(single_ref[...].reshape(-1, width)).reshape(samples, atoms_here, width)
    normed = attn_norm(cond, single, beside(ada_attn_scale, ada_attn_shift))
    down = core_ref[0] == 0
    for sample in range(samples):
        cut = slice(sample * EDGE, (sample + 1) * EDGE)
        head, tail = normed[sample, :EDGE], normed[sample, atoms_here - EDGE :]
        near_ref[cut, :] = jnp.where(down, head, tail)
        far_ref[cut, :] = jnp.where(down, tail, head)
    for copy in copies:
        copy.wait()
    normed = normed.reshape(-1, width)
    both = dot(normed, beside(w_key, w_value)).astype(BF16).reshape(samples, -1, 2 * width)
    key_ref[...] = both[:, :, :width]
    value_ref[...] = both[:, :, width:]
    both = dot(normed, beside(w_query, w_gate)).reshape(samples, -1, 2 * width)
    query_ref[...] = both[:, :, :width].astype(BF16)
    gate_ref[...] = sigmoid(both[:, :, width:]).astype(BF16)

    gates = dot(cond, beside(attn_gate, trans_gate))
    open_ref[...] = sigmoid(gates[:, :width]).astype(BF16)
    normed = attn_norm(cond, single, beside(ada_trans_scale, ada_trans_shift)).reshape(-1, width)
    swish = dot(normed, w_swish[...])
    hidden = (swish * sigmoid(swish) * dot(normed, w_linear[...])).astype(BF16)
    down = dot(hidden, w_down[...]).reshape(samples, -1, width)
    trans_ref[...] = (sigmoid(gates[:, width:])[None] * down).astype(BF16)


def tile_of(refs, place, row_block):
    if len(refs) == 1:
        return refs[0][row_block]
    pair_at, core_at = place
    owners = 2
    mine, theirs, across, diagonal = [ref[...] for ref in refs]
    near = jnp.where(row_block % owners == core_at, mine, theirs)
    far = jnp.where(row_block % owners == core_at, across, diagonal)
    return jnp.where(row_block // owners == pair_at, near, far)


def shifted(values, lanes):
    return pltpu.roll(values, lanes % values.shape[1], 1)


def unpacked(rows, side):
    half = EDGE // 2
    whole, packed = rows[:EDGE], rows[EDGE:].astype(F32)
    if side == 0:
        part = jnp.concatenate([packed, shifted(packed, -GROUP // 2)], 0).astype(BF16)
        return jnp.concatenate([whole, part], 1)
    part = jnp.concatenate([shifted(packed, GROUP // 2), packed], 0).astype(BF16)
    return jnp.concatenate([part, whole], 1)


def select_kernel(blocks, at_ref, pair_ref, core_ref, *refs):
    *tile_refs, _, __, ___, near_ref, far_ref, ____, held_ref = refs
    groups, cols, lanes = tile_refs[0].shape[-3:]
    device_at, place = at_ref[0], (pair_ref[0], core_ref[0])
    half = EDGE // 2
    for send_ref, core in ((near_ref, 1), (far_ref, 0)):
        above = core_ref[0] == core
        beside = jnp.where(above, device_at + 1, device_at - 1)
        tile = tile_of(tile_refs, place, jnp.clip(beside, 0, blocks - 1))
        tile = jnp.where(above, tile[:, cols - EDGE :], tile[:, :EDGE])
        whole = jnp.where(above, tile[0], tile[1])
        part = jnp.where(above, tile[1], tile[0]).astype(F32)
        first, last = part[:half], part[half:]
        first = jnp.where(above, first, shifted(first, -GROUP // 2))
        last = jnp.where(above, shifted(last, GROUP // 2), last)
        low = iota((half, lanes), 1) % GROUP < GROUP // 2
        packed = jnp.where(low, first, last).astype(BF16)
        send_ref[send_ref.shape[0] - EDGE - half :, :] = jnp.concatenate([whole, packed], 0)
    held_ref[...] = tile_of(tile_refs, place, device_at).reshape(groups * cols, lanes)


def bounds(counts_ref, block, token):
    tok_here = counts_ref.shape[1]
    counts = counts_ref[pl.ds(block, 1), :].astype(F32).astype(BF16)
    counts = jnp.broadcast_to(counts, (8, tok_here))
    before = iota((tok_here, token.shape[1]), 0)
    first = dot(counts, (before < token).astype(BF16))[:1]
    last = dot(counts, (before <= token).astype(BF16))[:1]
    return first.astype(jnp.int32), last.astype(jnp.int32)


def one_hot(reach, offset, count):
    first, last = reach
    position = iota((count, first.shape[1]), 0) + offset
    return ((first <= position) & (position < last)).astype(F32).astype(BF16)


def expand(hot, tile, groups):
    tile = tile.reshape(groups, -1, tile.shape[-1])
    tile = jnp.concatenate([tile[part] for part in range(groups)], 1)
    return dot(hot, tile).astype(BF16)


def head_mask(heads, lanes):
    rows = heads * Q_WIN
    lane_head = iota((rows, lanes), 1) // GROUP % heads
    row_head = iota((rows, lanes), 0) // Q_WIN
    return (lane_head == row_head).astype(F32).astype(BF16)


def picks_of(heads, reach, starts):
    same_head = head_mask(heads, reach[0].shape[1])
    return [
        jnp.concatenate([one_hot(reach, start, Q_WIN)] * heads, 0) * same_head for start in starts
    ]


def attend(heads, windows, query_ref, gate_ref, gated_ref, paired=0):
    samples, _, width = query_ref.shape
    head_dim = width // heads
    rows = heads * Q_WIN
    own_head = iota((rows, width), 1) // head_dim == iota((rows, width), 0) // Q_WIN
    own_head = own_head.astype(F32).astype(BF16)
    channel_head = iota((Q_WIN, 2 * width), 1) % width // head_dim
    ones = jnp.ones((K_WIN, width), BF16)
    scaling = LOG2E / math.sqrt(head_dim)

    biases = []
    for _, _, near, pick, mask in windows:
        bias = lax.dot_general(pick, near, LAST, preferred_element_type=F32) * LOG2E
        biases.append(bias if mask is None else jnp.where(mask, bias, MASKED))
    units = [(sample, i) for i in range(len(windows)) for sample in range(samples)]
    scores = []
    for first in range(0, len(units), 2):
        couple = units[first : first + 2]
        queries, keys = [], []
        for sample, i in couple:
            query = query_ref[sample, pl.ds(windows[i][0], Q_WIN), :]
            queries.append(jnp.concatenate([query] * heads, 0) * own_head)
            keys.append(windows[i][1][sample][0])
        if len(couple) == 2:
            blank = jnp.zeros_like(keys[0])
            keys = [jnp.concatenate([keys[0], blank], 1), jnp.concatenate([blank, keys[1]], 1)]
        product = lax.dot_general(
            jnp.concatenate(queries, 1),
            jnp.concatenate(keys, 0),
            LAST,
            preferred_element_type=F32,
        )
        for j, (_, i) in enumerate(couple):
            scores.append(product[:, j * K_WIN : (j + 1) * K_WIN] * scaling + biases[i])
    tops = [jnp.max(score, axis=-1, keepdims=True) for score in scores]
    raised = [jnp.exp2(score - top) for score, top in zip(scores, tops)]

    def by_head(parts, like):
        picked = jnp.broadcast_to(parts[:Q_WIN], (Q_WIN, like.shape[1]))
        for head in range(1, heads):
            part = parts[head * Q_WIN : (head + 1) * Q_WIN]
            picked = jnp.where(like == head, part, picked)
        return picked

    mixes = []
    for first in range(0, len(units), 2):
        couple = units[first : first + 2]
        values = [windows[i][1][sample][1] for sample, i in couple]
        weights = [weight.astype(BF16) for weight in raised[first : first + 2]]
        if paired and first // 2 % paired == 0 and len(couple) == 2:
            blank = jnp.zeros_like(values[0])
            values = [
                jnp.concatenate([values[0], blank], 1),
                jnp.concatenate([blank, values[1]], 1),
            ]
            both = dot(jnp.concatenate(weights, 1), jnp.concatenate(values, 0))
            for j in range(2):
                total = jnp.sum(raised[first + j], axis=-1, keepdims=True)
                narrow = channel_head[:, :width]
                attended = by_head(both[:, j * width : (j + 1) * width], narrow)
                mixes.append((attended, by_head(total, narrow)))
        else:
            for value, weight in zip(values, weights):
                picked = by_head(dot(weight, jnp.concatenate([value, ones], 1)), channel_head)
                mixes.append((picked[:, :width], picked[:, width:]))
    for (sample, i), (attended, total) in zip(units, mixes):
        attended = attended * pl.reciprocal(total, approx=True)
        at = pl.ds(windows[i][0], Q_WIN)
        gate = gate_ref[sample, at, :].astype(F32)
        gated_ref[sample, at, :] = (gate * attended).astype(BF16)


def close(sample, cut, gated_ref, open_ref, trans_ref, w_out_ref):
    mixed = dot(gated_ref[sample, cut, :], w_out_ref[...])
    opened, trans = open_ref[cut, :].astype(F32), trans_ref[sample, cut, :].astype(F32)
    return (opened * mixed + trans).astype(BF16)


def row_tokens(heads, tok_here):
    lane = iota((tok_here, heads * tok_here), 1)
    return lane // (heads * GROUP) * GROUP + lane % GROUP


def outer_starts(atoms_here):
    skip = -(-EDGE // Q_WIN)
    return [
        [side * (atoms_here - skip * Q_WIN) + i * Q_WIN for i in range(skip)] for side in range(2)
    ]


def inner_kernel(
    heads,
    blocks,
    at_ref,
    counts_ref,
    query_ref,
    key_ref,
    value_ref,
    gate_ref,
    open_ref,
    trans_ref,
    w_out_ref,
    held_ref,
    out_ref,
    pick_ref,
    hot_ref,
    side_ref,
    near_ref,
    gated_ref,
):
    samples, atoms_here, width = query_ref.shape
    tok_here = counts_ref.shape[1]
    device_at = at_ref[0]
    hot = one_hot(
        bounds(counts_ref, device_at, iota((tok_here, tok_here), 1)), 0, atoms_here
    )
    near_ref[...] = expand(hot, held_ref[...], tok_here // GROUP)
    reach = bounds(counts_ref, device_at, row_tokens(heads, tok_here))
    skip = -(-EDGE // Q_WIN)
    starts = [window * Q_WIN for window in range(skip, atoms_here // Q_WIN - skip)]
    windows = []
    for start, pick in zip(starts, picks_of(heads, reach, starts)):
        cut = slice(start - EDGE, start - EDGE + K_WIN)
        parts = [(key_ref[i, cut, :], value_ref[i, cut, :]) for i in range(samples)]
        windows.append((start, parts, near_ref[cut, :], pick, None))
    attend(heads, windows, query_ref, gate_ref, gated_ref, paired=2)

    cut = slice(starts[0], starts[-1] + Q_WIN)
    for sample in range(samples):
        out_ref[sample] = close(sample, cut, gated_ref, open_ref, trans_ref, w_out_ref)

    inside = side_ref.shape[1]
    sides = (
        (jnp.maximum(device_at - 1, 0), atoms_here - EDGE, tok_here - EDGE, 0),
        (jnp.minimum(device_at + 1, blocks - 1), 0, 0, atoms_here - inside),
    )
    for side, (block, offset, token, own_start) in enumerate(sides):
        nearest = bounds(counts_ref, block, iota((tok_here, EDGE), 1) + token)
        hot_ref[side] = one_hot(nearest, offset, EDGE)
        side_ref[side] = near_ref[own_start : own_start + inside, :]
        for i, pick in enumerate(picks_of(heads, reach, outer_starts(atoms_here)[side])):
            pick_ref[side, i] = pick


def outer_kernel(
    heads,
    blocks,
    at_ref,
    core_ref,
    query_ref,
    own_key_ref,
    own_value_ref,
    gate_ref,
    open_ref,
    trans_ref,
    w_out_ref,
    inner_ref,
    pick_ref,
    hot_ref,
    side_ref,
    w_key,
    w_value,
    first_ref,
    second_ref,
    out_hbm,
    gated_ref,
    out_ref,
    sem,
):
    samples, atoms_here, width = query_ref.shape
    device_at = at_ref[0]
    ends = atoms_here * blocks
    starts = outer_starts(atoms_here)
    margin = len(starts[0]) * Q_WIN
    inside = side_ref.shape[1]

    whole = pltpu.make_async_copy(
        inner_ref, out_hbm.at[:, pl.ds(margin, atoms_here - 2 * margin)], sem.at[0]
    )
    whole.start()

    down = core_ref[0] == 0
    first, second = first_ref[...], second_ref[...]
    arrived = (jnp.where(down, second, first), jnp.where(down, first, second))
    count = samples * EDGE
    edges = jnp.concatenate([rows[:count] for rows in arrived], 0)
    edges = dot(edges, beside(w_key, w_value)).astype(BF16).reshape(2, samples, EDGE, 2 * width)

    def joined(side, edge, own):
        return jnp.concatenate([own, edge] if side else [edge, own], 0)

    windows = []
    for side in range(2):
        own = slice(side * (atoms_here - inside), side * (atoms_here - inside) + inside)
        parts = [
            (
                joined(side, edges[side, i, :, :width], own_key_ref[i, own, :]),
                joined(side, edges[side, i, :, width:], own_value_ref[i, own, :]),
            )
            for i in range(samples)
        ]
        near = dot(hot_ref[side], unpacked(arrived[side][count:], side)).astype(BF16)
        near = joined(side, near, side_ref[side])
        for i, start in enumerate(starts[side]):
            cut = slice(i * Q_WIN, i * Q_WIN + K_WIN)
            key_at = iota((heads * Q_WIN, K_WIN), 1) + (device_at * atoms_here + start - EDGE)
            mask = (key_at >= 0) & (key_at < ends)
            pieces = [(keys[cut], values[cut]) for keys, values in parts]
            windows.append((start, pieces, near[cut], pick_ref[side, i], mask))
    attend(heads, windows, query_ref, gate_ref, gated_ref)
    copies = []
    for side in range(2):
        cut = slice(starts[side][0], starts[side][0] + margin)
        for sample in range(samples):
            out_ref[side, sample] = close(sample, cut, gated_ref, open_ref, trans_ref, w_out_ref)
        target = out_hbm.at[:, pl.ds(starts[side][0], margin)]
        copies.append(pltpu.make_async_copy(out_ref.at[side], target, sem.at[1 + side]))
        copies[-1].start()
    for copy in copies:
        copy.wait()
    whole.wait()


def shards(
    atom_single,
    atom_cond,
    pair_cond,
    atom_counts,
    ada_attn_scale,
    ada_attn_shift,
    w_query,
    w_key,
    w_value,
    w_gate,
    w_out,
    attn_gate,
    w_pair,
    ada_trans_scale,
    ada_trans_shift,
    w_swish,
    w_linear,
    w_down,
    trans_gate,
):
    device_at = lax.axis_index("atoms")
    blocks = lax.axis_size("atoms")
    samples, atoms_here, width = atom_single.shape
    tok_here = atom_counts.shape[1]
    heads = w_pair.shape[1]
    groups = tok_here // GROUP
    pairs = lax.axis_size("pair")
    assert pair_cond.shape[0] == lax.axis_size("samp") * tok_here
    assert groups == 2 and tok_here - EDGE == GROUP // 2
    at = device_at.astype(jnp.int32).reshape(1)
    pair_at = lax.axis_index("pair").astype(jnp.int32).reshape(1)
    core_at = lax.axis_index("samp").astype(jnp.int32).reshape(1)
    in_hbm = lambda array: pltpu.with_memory_space_constraint(array, pltpu.HBM)
    in_vmem = lambda array: pltpu.with_memory_space_constraint(array, pltpu.VMEM)

    cols = pair_cond.shape[1]
    lanes = heads * GROUP
    wide = (samples, atoms_here, width)
    params = pltpu.CompilerParams(vmem_limit_bytes=VMEM_LIMIT)

    def cost(products):
        return pl.CostEstimate(flops=2 * products, bytes_accessed=4 << 20, transcendentals=0)

    sent = pltpu.VMEM((samples * EDGE + EDGE + EDGE // 2, lanes), BF16)
    own = pl.pallas_call(
        pair_kernel,
        in_specs=[IN_SMEM] + [IN_HBM] * 2,
        out_specs=IN_VMEM,
        out_shape=pltpu.VMEM((groups, cols, lanes), BF16),
        scratch_shapes=[
            pltpu.VMEM((heads, width), BF16),
            pltpu.VMEM((tok_here, cols, width), BF16),
            pltpu.SemaphoreType.DMA((groups,)),
            pltpu.SemaphoreType.DMA,
        ],
        compiler_params=params,
        cost_estimate=cost(tok_here * cols * width * width * 2),
    )(core_at, *map(in_hbm, (w_pair.T, pair_cond)))
    if pairs == 2:
        swapped = [(0, 1), (1, 0)]
        across = lax.ppermute(own, "pair", swapped)
        diagonal = lax.ppermute(own, ("pair", "samp"), [(0, 3), (1, 2), (2, 1), (3, 0)])
        tiles = (own, lax.ppermute(own, "samp", swapped), across, diagonal)
    else:
        tiles = (lax.all_gather(own, ("pair", "samp")),)

    operands = (
        atom_single,
        atom_cond,
        ada_attn_scale,
        ada_attn_shift,
        w_key,
        w_value,
        w_query,
        w_gate,
    )
    late = (ada_trans_scale, ada_trans_shift, attn_gate, trans_gate, w_swish, w_linear, w_down)
    query, keys, values, gate, opened, trans, near, far = pl.pallas_call(
        project_kernel,
        in_specs=[IN_SMEM] + [IN_VMEM] * len(operands) + [IN_HBM] * len(late),
        out_specs=[IN_VMEM] * 8,
        out_shape=[pltpu.VMEM(wide, BF16)] * 4
        + [pltpu.VMEM((atoms_here, width), BF16), pltpu.VMEM(wide, BF16), sent, sent],
        scratch_shapes=[pltpu.VMEM(weight.shape, BF16) for weight in late]
        + [pltpu.SemaphoreType.DMA((len(late),))],
        compiler_params=params,
        cost_estimate=cost(samples * atoms_here * width * width * 20),
    )(core_at, *map(in_vmem, operands), *map(in_hbm, late))

    operands = (*tiles, near, far, opened)
    first = 3 + len(tiles)
    near, far, opened, held = pl.pallas_call(
        functools.partial(select_kernel, blocks),
        in_specs=[IN_SMEM] * 3 + [IN_VMEM] * len(operands),
        out_specs=[IN_VMEM] * 4,
        out_shape=[
            sent,
            sent,
            pltpu.VMEM((atoms_here, width), BF16),
            pltpu.VMEM((groups * cols, lanes), BF16),
        ],
        input_output_aliases={first: 0, first + 1: 1, first + 2: 2},
        compiler_params=params,
    )(at, pair_at, core_at, *map(in_vmem, operands))

    down = [(2 * i, 2 * (i - 1)) for i in range(1, blocks)] + [(0, 1)]
    up = [(2 * i + 1, 2 * (i + 1) + 1) for i in range(blocks - 1)] + [(2 * blocks - 1, 2 * blocks - 2)]
    cycle = down + up
    first = lax.ppermute(near, ("atoms", "samp"), cycle)
    second = lax.ppermute(far, ("atoms", "samp"), [(target, source) for source, target in cycle])

    margin = -(-EDGE // Q_WIN) * Q_WIN
    inside = margin - Q_WIN + K_WIN - EDGE
    expanded = heads * tok_here
    operands = (query, keys, values, gate, opened, trans, w_out)
    inner, picks, hots, beside_edges = pl.pallas_call(
        functools.partial(inner_kernel, heads, blocks),
        in_specs=[IN_SMEM] + [IN_VMEM] * (2 + len(operands)),
        out_specs=[IN_VMEM] * 4,
        out_shape=[
            pltpu.VMEM((samples, atoms_here - 2 * margin, width), BF16),
            pltpu.VMEM((2, margin // Q_WIN, heads * Q_WIN, expanded), BF16),
            pltpu.VMEM((2, EDGE, EDGE), BF16),
            pltpu.VMEM((2, inside, expanded), BF16),
        ],
        scratch_shapes=[
            pltpu.VMEM((atoms_here, expanded), BF16),
            pltpu.VMEM(wide, BF16),
        ],
        compiler_params=params,
        cost_estimate=cost(samples * atoms_here * width * width * 12),
    )(at, atom_counts, *map(in_vmem, (*operands, held)))

    operands += (inner, picks, hots, beside_edges, w_key, w_value, first, second)
    return pl.pallas_call(
        functools.partial(outer_kernel, heads, blocks),
        in_specs=[IN_SMEM] * 2 + [IN_VMEM] * len(operands),
        out_specs=IN_HBM,
        out_shape=pltpu.HBM(wide, BF16),
        scratch_shapes=[
            pltpu.VMEM(wide, BF16),
            pltpu.VMEM((2, samples, margin, width), BF16),
            pltpu.SemaphoreType.DMA((3,)),
        ],
        compiler_params=params,
        cost_estimate=cost(samples * atoms_here * width * width * 4),
    )(at, core_at, *map(in_vmem, operands))


def solution(mesh):
    return jax.shard_map(
        shards,
        mesh=mesh,
        in_specs=(
            P(("groups", "pair", "samp"), "atoms", None),
            P(("groups", "atoms"), None),
            P(("groups", "pair"), "atoms", None),
            P("groups", None),
        )
        + (P(),) * 15,
        out_specs=P(("groups", "pair", "samp"), "atoms", None),
        check_vma=False,
    )
```

```python
import functools
import math

import jax
import jax.numpy as jnp
from jax import lax
from jax.experimental import pallas as pl
from jax.experimental.pallas import tpu as pltpu
from jax.sharding import PartitionSpec as P

Q_WIN = 32
K_WIN = 128
EDGE = 48
GROUP = 32

EPSILON = 1e-05
MASKED = -1e30
LOG2E = math.log2(math.e)
BF16 = jnp.bfloat16
F32 = jnp.float32
LAST = (((1,), (1,)), ((), ()))
VMEM_LIMIT = 32 << 20
IN_VMEM = pl.BlockSpec(memory_space=pltpu.VMEM)
IN_HBM = pl.BlockSpec(memory_space=pltpu.HBM)
IN_SMEM = pl.BlockSpec(memory_space=pltpu.SMEM)


def dot(a, b):
    return jnp.dot(a, b, preferred_element_type=F32)


def iota(shape, dim):
    return lax.broadcasted_iota(jnp.int32, shape, dim)


def twice(matrix):
    blank = jnp.zeros_like(matrix)
    return jnp.concatenate(
        [jnp.concatenate([matrix, blank], 1), jnp.concatenate([blank, matrix], 1)], 0
    )


def side_by_side(rows):
    half = rows.shape[0] // 2
    return jnp.concatenate([rows[:half], rows[half:]], 1)


def centring(width):
    same = iota((width, width), 0) == iota((width, width), 1)
    return jnp.where(same, 1.0 - 1.0 / width, -1.0 / width).astype(BF16)


def mean_square(centred):
    return jnp.mean(centred * centred, axis=-1, keepdims=True)


def layer_norm(rows):
    width = rows.shape[1]
    both = dot(side_by_side(rows), twice(centring(width)))
    centred = jnp.concatenate([both[:, :width], both[:, width:]], 0)
    return centred * lax.rsqrt(mean_square(centred) + EPSILON)


def sigmoid(values):
    return 0.5 * jnp.tanh(0.5 * values) + 0.5


def attn_norm(cond, single, ada):
    width = single.shape[-1]
    mixed = dot(cond, ada)
    return (sigmoid(mixed[:, :width])[None] * single + mixed[None, :, width:]).astype(BF16)


def pair_kernel(core_ref, w_pair_hbm, pair_hbm, tile_ref, w_pair_ref, pair_ref, pair_sem, sem):
    rows, cols, width = pair_ref.shape
    heads = w_pair_ref.shape[0]
    group = GROUP
    lanes = heads * group
    half = group // 2
    row_start = core_ref[0] * rows

    def pair_copy(i):
        source = pair_hbm.at[pl.ds(row_start + i * group, group)]
        return pltpu.make_async_copy(source, pair_ref.at[pl.ds(i * group, group)], pair_sem.at[i])

    w_pair_copy = pltpu.make_async_copy(w_pair_hbm, w_pair_ref, sem)
    w_pair_copy.start()
    for i in range(rows // group):
        pair_copy(i).start()
    w_pair_copy.wait()
    w_pair = w_pair_ref[...].astype(F32)
    spread = jnp.concatenate(
        [jnp.broadcast_to(w_pair[h : h + 1], (group, width)) for h in range(heads)], 0
    )
    weight = spread.T.astype(BF16)
    low = iota((width, lanes), 1) % group < half
    blank = jnp.zeros_like(weight)

    def shared(columns):
        return jnp.concatenate([jnp.where(low, columns, blank), jnp.where(low, blank, columns)], 0)

    mix = shared(weight)
    average = shared(jnp.full((width, lanes), 1.0 / width, BF16))
    centre = twice(centring(width))
    slot = iota((cols, lanes), 1) % half

    chunks = []
    for chunk in range(rows // group):
        pair_copy(chunk).wait()
        pair = pair_ref[chunk * group : (chunk + 1) * group].reshape(group * cols, width)
        chunks.append(dot(side_by_side(pair), centre).astype(BF16))
    mixes = [dot(centred, mix).reshape(half, cols, lanes) for centred in chunks]
    variances = [dot(centred * centred, average).reshape(half, cols, lanes) for centred in chunks]
    for chunk, (mixed, variance) in enumerate(zip(mixes, variances)):
        total, spread_out = mixed[0], variance[0]
        for i in range(1, half):
            total = jnp.where(slot == i, mixed[i], total)
            spread_out = jnp.where(slot == i, variance[i], spread_out)
        tile_ref[chunk] = (total * lax.rsqrt(spread_out + EPSILON)).astype(BF16)


def beside(first, second):
    return jnp.concatenate([first[...], second[...]], 1)


def project_kernel(
    core_ref,
    single_ref,
    cond_ref,
    ada_attn_scale,
    ada_attn_shift,
    w_key,
    w_value,
    w_query,
    w_gate,
    *refs,
):
    late_hbm, refs = refs[:7], refs[7:]
    query_ref, key_ref, value_ref, gate_ref, open_ref, trans_ref, near_ref, far_ref = refs[:8]
    late_refs, sem = refs[8:15], refs[15]
    ada_trans_scale, ada_trans_shift, attn_gate, trans_gate, w_swish, w_linear, w_down = late_refs
    samples, atoms_here, width = single_ref.shape
    copies = [
        pltpu.make_async_copy(source, target, sem.at[i])
        for i, (source, target) in enumerate(zip(late_hbm, late_refs))
    ]
    for copy in copies:
        copy.start()

    cond = layer_norm(cond_ref[...]).astype(BF16)
    single = layer_norm(single_ref[...].reshape(-1, width)).reshape(samples, atoms_here, width)
    normed = attn_norm(cond, single, beside(ada_attn_scale, ada_attn_shift))
    down = core_ref[0] == 0
    for sample in range(samples):
        cut = slice(sample * EDGE, (sample + 1) * EDGE)
        head, tail = normed[sample, :EDGE], normed[sample, atoms_here - EDGE :]
        near_ref[cut, :] = jnp.where(down, head, tail)
        far_ref[cut, :] = jnp.where(down, tail, head)
    for copy in copies:
        copy.wait()
    normed = normed.reshape(-1, width)
    both = dot(normed, beside(w_key, w_value)).astype(BF16).reshape(samples, -1, 2 * width)
    key_ref[...] = both[:, :, :width]
    value_ref[...] = both[:, :, width:]
    both = dot(normed, beside(w_query, w_gate)).reshape(samples, -1, 2 * width)
    query_ref[...] = both[:, :, :width].astype(BF16)
    gate_ref[...] = sigmoid(both[:, :, width:]).astype(BF16)

    gates = dot(cond, beside(attn_gate, trans_gate))
    open_ref[...] = sigmoid(gates[:, :width]).astype(BF16)
    normed = attn_norm(cond, single, beside(ada_trans_scale, ada_trans_shift)).reshape(-1, width)
    swish = dot(normed, w_swish[...])
    hidden = (swish * sigmoid(swish) * dot(normed, w_linear[...])).astype(BF16)
    down = dot(hidden, w_down[...]).reshape(samples, -1, width)
    trans_ref[...] = (sigmoid(gates[:, width:])[None] * down).astype(BF16)


def tile_of(refs, place, row_block):
    if len(refs) == 1:
        return refs[0][row_block]
    pair_at, core_at = place
    owners = 2
    mine, theirs, across, diagonal = [ref[...] for ref in refs]
    near = jnp.where(row_block % owners == core_at, mine, theirs)
    far = jnp.where(row_block % owners == core_at, across, diagonal)
    return jnp.where(row_block // owners == pair_at, near, far)


def shifted(values, lanes):
    return pltpu.roll(values, lanes % values.shape[1], 1)


def unpacked(rows, side):
    half = EDGE // 2
    whole, packed = rows[:EDGE], rows[EDGE:].astype(F32)
    if side == 0:
        part = jnp.concatenate([packed, shifted(packed, -GROUP // 2)], 0).astype(BF16)
        return jnp.concatenate([whole, part], 1)
    part = jnp.concatenate([shifted(packed, GROUP // 2), packed], 0).astype(BF16)
    return jnp.concatenate([part, whole], 1)


def select_kernel(blocks, at_ref, pair_ref, core_ref, *refs):
    *tile_refs, _, __, ___, near_ref, far_ref, ____, held_ref = refs
    groups, cols, lanes = tile_refs[0].shape[-3:]
    device_at, place = at_ref[0], (pair_ref[0], core_ref[0])
    half = EDGE // 2
    for send_ref, core in ((near_ref, 1), (far_ref, 0)):
        above = core_ref[0] == core
        beside = jnp.where(above, device_at + 1, device_at - 1)
        tile = tile_of(tile_refs, place, jnp.clip(beside, 0, blocks - 1))
        tile = jnp.where(above, tile[:, cols - EDGE :], tile[:, :EDGE])
        whole = jnp.where(above, tile[0], tile[1])
        part = jnp.where(above, tile[1], tile[0]).astype(F32)
        first, last = part[:half], part[half:]
        first = jnp.where(above, first, shifted(first, -GROUP // 2))
        last = jnp.where(above, shifted(last, GROUP // 2), last)
        low = iota((half, lanes), 1) % GROUP < GROUP // 2
        packed = jnp.where(low, first, last).astype(BF16)
        send_ref[send_ref.shape[0] - EDGE - half :, :] = jnp.concatenate([whole, packed], 0)
    held_ref[...] = tile_of(tile_refs, place, device_at).reshape(groups * cols, lanes)


def bounds(counts_ref, block, token):
    tok_here = counts_ref.shape[1]
    counts = counts_ref[pl.ds(block, 1), :].astype(F32).astype(BF16)
    counts = jnp.broadcast_to(counts, (8, tok_here))
    before = iota((tok_here, token.shape[1]), 0)
    first = dot(counts, (before < token).astype(BF16))[:1]
    last = dot(counts, (before <= token).astype(BF16))[:1]
    return first.astype(jnp.int32), last.astype(jnp.int32)


def one_hot(reach, offset, count):
    first, last = reach
    position = iota((count, first.shape[1]), 0) + offset
    return ((first <= position) & (position < last)).astype(F32).astype(BF16)


def expand(hot, tile, groups):
    tile = tile.reshape(groups, -1, tile.shape[-1])
    tile = jnp.concatenate([tile[part] for part in range(groups)], 1)
    return dot(hot, tile).astype(BF16)


def head_mask(heads, lanes):
    rows = heads * Q_WIN
    lane_head = iota((rows, lanes), 1) // GROUP % heads
    row_head = iota((rows, lanes), 0) // Q_WIN
    return (lane_head == row_head).astype(F32).astype(BF16)


def picks_of(heads, reach, starts):
    same_head = head_mask(heads, reach[0].shape[1])
    return [
        jnp.concatenate([one_hot(reach, start, Q_WIN)] * heads, 0) * same_head for start in starts
    ]


def attend(heads, windows, query_ref, gate_ref, gated_ref, paired=0):
    samples, _, width = query_ref.shape
    head_dim = width // heads
    rows = heads * Q_WIN
    own_head = iota((rows, width), 1) // head_dim == iota((rows, width), 0) // Q_WIN
    own_head = own_head.astype(F32).astype(BF16)
    channel_head = iota((Q_WIN, 2 * width), 1) % width // head_dim
    ones = jnp.ones((K_WIN, width), BF16)
    scaling = LOG2E / math.sqrt(head_dim)

    biases = []
    for _, _, near, pick, mask in windows:
        bias = lax.dot_general(pick, near, LAST, preferred_element_type=F32) * LOG2E
        biases.append(bias if mask is None else jnp.where(mask, bias, MASKED))
    units = [(sample, i) for i in range(len(windows)) for sample in range(samples)]
    scores = []
    for first in range(0, len(units), 2):
        couple = units[first : first + 2]
        queries, keys = [], []
        for sample, i in couple:
            query = query_ref[sample, pl.ds(windows[i][0], Q_WIN), :]
            queries.append(jnp.concatenate([query] * heads, 0) * own_head)
            keys.append(windows[i][1][sample][0])
        if len(couple) == 2:
            blank = jnp.zeros_like(keys[0])
            keys = [jnp.concatenate([keys[0], blank], 1), jnp.concatenate([blank, keys[1]], 1)]
        product = lax.dot_general(
            jnp.concatenate(queries, 1),
            jnp.concatenate(keys, 0),
            LAST,
            preferred_element_type=F32,
        )
        for j, (_, i) in enumerate(couple):
            scores.append(product[:, j * K_WIN : (j + 1) * K_WIN] * scaling + biases[i])
    tops = [jnp.max(score, axis=-1, keepdims=True) for score in scores]
    raised = [jnp.exp2(score - top) for score, top in zip(scores, tops)]

    def by_head(parts, like):
        picked = jnp.broadcast_to(parts[:Q_WIN], (Q_WIN, like.shape[1]))
        for head in range(1, heads):
            part = parts[head * Q_WIN : (head + 1) * Q_WIN]
            picked = jnp.where(like == head, part, picked)
        return picked

    mixes = []
    for first in range(0, len(units), 2):
        couple = units[first : first + 2]
        values = [windows[i][1][sample][1] for sample, i in couple]
        weights = [weight.astype(BF16) for weight in raised[first : first + 2]]
        if paired and first // 2 % paired == 0 and len(couple) == 2:
            blank = jnp.zeros_like(values[0])
            values = [
                jnp.concatenate([values[0], blank], 1),
                jnp.concatenate([blank, values[1]], 1),
            ]
            both = dot(jnp.concatenate(weights, 1), jnp.concatenate(values, 0))
            for j in range(2):
                total = jnp.sum(raised[first + j], axis=-1, keepdims=True)
                narrow = channel_head[:, :width]
                attended = by_head(both[:, j * width : (j + 1) * width], narrow)
                mixes.append((attended, by_head(total, narrow)))
        else:
            for value, weight in zip(values, weights):
                picked = by_head(dot(weight, jnp.concatenate([value, ones], 1)), channel_head)
                mixes.append((picked[:, :width], picked[:, width:]))
    for (sample, i), (attended, total) in zip(units, mixes):
        attended = attended * pl.reciprocal(total, approx=True)
        at = pl.ds(windows[i][0], Q_WIN)
        gate = gate_ref[sample, at, :].astype(F32)
        gated_ref[sample, at, :] = (gate * attended).astype(BF16)


def close(sample, cut, gated_ref, open_ref, trans_ref, w_out_ref):
    mixed = dot(gated_ref[sample, cut, :], w_out_ref[...])
    opened, trans = open_ref[cut, :].astype(F32), trans_ref[sample, cut, :].astype(F32)
    return (opened * mixed + trans).astype(BF16)


def row_tokens(heads, tok_here):
    lane = iota((tok_here, heads * tok_here), 1)
    return lane // (heads * GROUP) * GROUP + lane % GROUP


def outer_starts(atoms_here):
    skip = -(-EDGE // Q_WIN)
    return [
        [side * (atoms_here - skip * Q_WIN) + i * Q_WIN for i in range(skip)] for side in range(2)
    ]


def inner_kernel(
    heads,
    blocks,
    at_ref,
    counts_ref,
    query_ref,
    key_ref,
    value_ref,
    gate_ref,
    open_ref,
    trans_ref,
    w_out_ref,
    held_ref,
    out_ref,
    pick_ref,
    hot_ref,
    side_ref,
    near_ref,
    gated_ref,
):
    samples, atoms_here, width = query_ref.shape
    tok_here = counts_ref.shape[1]
    device_at = at_ref[0]
    hot = one_hot(
        bounds(counts_ref, device_at, iota((tok_here, tok_here), 1)), 0, atoms_here
    )
    near_ref[...] = expand(hot, held_ref[...], tok_here // GROUP)
    reach = bounds(counts_ref, device_at, row_tokens(heads, tok_here))
    skip = -(-EDGE // Q_WIN)
    starts = [window * Q_WIN for window in range(skip, atoms_here // Q_WIN - skip)]
    windows = []
    for start, pick in zip(starts, picks_of(heads, reach, starts)):
        cut = slice(start - EDGE, start - EDGE + K_WIN)
        parts = [(key_ref[i, cut, :], value_ref[i, cut, :]) for i in range(samples)]
        windows.append((start, parts, near_ref[cut, :], pick, None))
    attend(heads, windows, query_ref, gate_ref, gated_ref, paired=2)

    cut = slice(starts[0], starts[-1] + Q_WIN)
    for sample in range(samples):
        out_ref[sample] = close(sample, cut, gated_ref, open_ref, trans_ref, w_out_ref)

    inside = side_ref.shape[1]
    sides = (
        (jnp.maximum(device_at - 1, 0), atoms_here - EDGE, tok_here - EDGE, 0),
        (jnp.minimum(device_at + 1, blocks - 1), 0, 0, atoms_here - inside),
    )
    for side, (block, offset, token, own_start) in enumerate(sides):
        nearest = bounds(counts_ref, block, iota((tok_here, EDGE), 1) + token)
        hot_ref[side] = one_hot(nearest, offset, EDGE)
        side_ref[side] = near_ref[own_start : own_start + inside, :]
        for i, pick in enumerate(picks_of(heads, reach, outer_starts(atoms_here)[side])):
            pick_ref[side, i] = pick


def outer_kernel(
    heads,
    blocks,
    at_ref,
    core_ref,
    query_ref,
    own_key_ref,
    own_value_ref,
    gate_ref,
    open_ref,
    trans_ref,
    w_out_ref,
    inner_ref,
    pick_ref,
    hot_ref,
    side_ref,
    w_key,
    w_value,
    first_ref,
    second_ref,
    out_hbm,
    gated_ref,
    out_ref,
    sem,
):
    samples, atoms_here, width = query_ref.shape
    device_at = at_ref[0]
    ends = atoms_here * blocks
    starts = outer_starts(atoms_here)
    margin = len(starts[0]) * Q_WIN
    inside = side_ref.shape[1]

    whole = pltpu.make_async_copy(
        inner_ref, out_hbm.at[:, pl.ds(margin, atoms_here - 2 * margin)], sem.at[0]
    )
    whole.start()

    down = core_ref[0] == 0
    first, second = first_ref[...], second_ref[...]
    arrived = (jnp.where(down, second, first), jnp.where(down, first, second))
    count = samples * EDGE
    edges = jnp.concatenate([rows[:count] for rows in arrived], 0)
    edges = dot(edges, beside(w_key, w_value)).astype(BF16).reshape(2, samples, EDGE, 2 * width)

    def joined(side, edge, own):
        return jnp.concatenate([own, edge] if side else [edge, own], 0)

    windows = []
    for side in range(2):
        own = slice(side * (atoms_here - inside), side * (atoms_here - inside) + inside)
        parts = [
            (
                joined(side, edges[side, i, :, :width], own_key_ref[i, own, :]),
                joined(side, edges[side, i, :, width:], own_value_ref[i, own, :]),
            )
            for i in range(samples)
        ]
        near = dot(hot_ref[side], unpacked(arrived[side][count:], side)).astype(BF16)
        near = joined(side, near, side_ref[side])
        for i, start in enumerate(starts[side]):
            cut = slice(i * Q_WIN, i * Q_WIN + K_WIN)
            key_at = iota((heads * Q_WIN, K_WIN), 1) + (device_at * atoms_here + start - EDGE)
            mask = (key_at >= 0) & (key_at < ends)
            pieces = [(keys[cut], values[cut]) for keys, values in parts]
            windows.append((start, pieces, near[cut], pick_ref[side, i], mask))
    attend(heads, windows, query_ref, gate_ref, gated_ref)
    copies = []
    for side in range(2):
        cut = slice(starts[side][0], starts[side][0] + margin)
        for sample in range(samples):
            out_ref[side, sample] = close(sample, cut, gated_ref, open_ref, trans_ref, w_out_ref)
        target = out_hbm.at[:, pl.ds(starts[side][0], margin)]
        copies.append(pltpu.make_async_copy(out_ref.at[side], target, sem.at[1 + side]))
        copies[-1].start()
    for copy in copies:
        copy.wait()
    whole.wait()


def shards(
    atom_single,
    atom_cond,
    pair_cond,
    atom_counts,
    ada_attn_scale,
    ada_attn_shift,
    w_query,
    w_key,
    w_value,
    w_gate,
    w_out,
    attn_gate,
    w_pair,
    ada_trans_scale,
    ada_trans_shift,
    w_swish,
    w_linear,
    w_down,
    trans_gate,
):
    device_at = lax.axis_index("atoms")
    blocks = lax.axis_size("atoms")
    samples, atoms_here, width = atom_single.shape
    tok_here = atom_counts.shape[1]
    heads = w_pair.shape[1]
    groups = tok_here // GROUP
    pairs = lax.axis_size("pair")
    assert pair_cond.shape[0] == lax.axis_size("samp") * tok_here
    assert groups == 2 and tok_here - EDGE == GROUP // 2
    at = device_at.astype(jnp.int32).reshape(1)
    pair_at = lax.axis_index("pair").astype(jnp.int32).reshape(1)
    core_at = lax.axis_index("samp").astype(jnp.int32).reshape(1)
    in_hbm = lambda array: pltpu.with_memory_space_constraint(array, pltpu.HBM)
    in_vmem = lambda array: pltpu.with_memory_space_constraint(array, pltpu.VMEM)

    cols = pair_cond.shape[1]
    lanes = heads * GROUP
    wide = (samples, atoms_here, width)
    params = pltpu.CompilerParams(vmem_limit_bytes=VMEM_LIMIT)

    def cost(products):
        return pl.CostEstimate(flops=2 * products, bytes_accessed=4 << 20, transcendentals=0)

    sent = pltpu.VMEM((samples * EDGE + EDGE + EDGE // 2, lanes), BF16)
    own = pl.pallas_call(
        pair_kernel,
        in_specs=[IN_SMEM] + [IN_HBM] * 2,
        out_specs=IN_VMEM,
        out_shape=pltpu.VMEM((groups, cols, lanes), BF16),
        scratch_shapes=[
            pltpu.VMEM((heads, width), BF16),
            pltpu.VMEM((tok_here, cols, width), BF16),
            pltpu.SemaphoreType.DMA((groups,)),
            pltpu.SemaphoreType.DMA,
        ],
        compiler_params=params,
        cost_estimate=cost(tok_here * cols * width * width * 2),
    )(core_at, *map(in_hbm, (w_pair.T, pair_cond)))
    if pairs == 2:
        swapped = [(0, 1), (1, 0)]
        across = lax.ppermute(own, "pair", swapped)
        diagonal = lax.ppermute(own, ("pair", "samp"), [(0, 3), (1, 2), (2, 1), (3, 0)])
        tiles = (own, lax.ppermute(own, "samp", swapped), across, diagonal)
    else:
        tiles = (lax.all_gather(own, ("pair", "samp")),)

    operands = (
        atom_single,
        atom_cond,
        ada_attn_scale,
        ada_attn_shift,
        w_key,
        w_value,
        w_query,
        w_gate,
    )
    late = (ada_trans_scale, ada_trans_shift, attn_gate, trans_gate, w_swish, w_linear, w_down)
    query, keys, values, gate, opened, trans, near, far = pl.pallas_call(
        project_kernel,
        in_specs=[IN_SMEM] + [IN_VMEM] * len(operands) + [IN_HBM] * len(late),
        out_specs=[IN_VMEM] * 8,
        out_shape=[pltpu.VMEM(wide, BF16)] * 4
        + [pltpu.VMEM((atoms_here, width), BF16), pltpu.VMEM(wide, BF16), sent, sent],
        scratch_shapes=[pltpu.VMEM(weight.shape, BF16) for weight in late]
        + [pltpu.SemaphoreType.DMA((len(late),))],
        compiler_params=params,
        cost_estimate=cost(samples * atoms_here * width * width * 20),
    )(core_at, *map(in_vmem, operands), *map(in_hbm, late))

    operands = (*tiles, near, far, opened)
    first = 3 + len(tiles)
    near, far, opened, held = pl.pallas_call(
        functools.partial(select_kernel, blocks),
        in_specs=[IN_SMEM] * 3 + [IN_VMEM] * len(operands),
        out_specs=[IN_VMEM] * 4,
        out_shape=[
            sent,
            sent,
            pltpu.VMEM((atoms_here, width), BF16),
            pltpu.VMEM((groups * cols, lanes), BF16),
        ],
        input_output_aliases={first: 0, first + 1: 1, first + 2: 2},
        compiler_params=params,
    )(at, pair_at, core_at, *map(in_vmem, operands))

    down = [(2 * i, 2 * (i - 1)) for i in range(1, blocks)] + [(0, 1)]
    up = [(2 * i + 1, 2 * (i + 1) + 1) for i in range(blocks - 1)] + [(2 * blocks - 1, 2 * blocks - 2)]
    cycle = down + up
    first = lax.ppermute(near, ("atoms", "samp"), cycle)
    second = lax.ppermute(far, ("atoms", "samp"), [(target, source) for source, target in cycle])

    margin = -(-EDGE // Q_WIN) * Q_WIN
    inside = margin - Q_WIN + K_WIN - EDGE
    expanded = heads * tok_here
    operands = (query, keys, values, gate, opened, trans, w_out)
    inner, picks, hots, beside_edges = pl.pallas_call(
        functools.partial(inner_kernel, heads, blocks),
        in_specs=[IN_SMEM] + [IN_VMEM] * (2 + len(operands)),
        out_specs=[IN_VMEM] * 4,
        out_shape=[
            pltpu.VMEM((samples, atoms_here - 2 * margin, width), BF16),
            pltpu.VMEM((2, margin // Q_WIN, heads * Q_WIN, expanded), BF16),
            pltpu.VMEM((2, EDGE, EDGE), BF16),
            pltpu.VMEM((2, inside, expanded), BF16),
        ],
        scratch_shapes=[
            pltpu.VMEM((atoms_here, expanded), BF16),
            pltpu.VMEM(wide, BF16),
        ],
        compiler_params=params,
        cost_estimate=cost(samples * atoms_here * width * width * 12),
    )(at, atom_counts, *map(in_vmem, (*operands, held)))

    operands += (inner, picks, hots, beside_edges, w_key, w_value, first, second)
    return pl.pallas_call(
        functools.partial(outer_kernel, heads, blocks),
        in_specs=[IN_SMEM] * 2 + [IN_VMEM] * len(operands),
        out_specs=IN_HBM,
        out_shape=pltpu.HBM(wide, BF16),
        scratch_shapes=[
            pltpu.VMEM(wide, BF16),
            pltpu.VMEM((2, samples, margin, width), BF16),
            pltpu.SemaphoreType.DMA((3,)),
        ],
        compiler_params=params,
        cost_estimate=cost(samples * atoms_here * width * width * 4),
    )(at, core_at, *map(in_vmem, operands))


def solution(mesh):
    return jax.shard_map(
        shards,
        mesh=mesh,
        in_specs=(
            P(("groups", "pair", "samp"), "atoms", None),
            P(("groups", "atoms"), None),
            P(("groups", "pair"), "atoms", None),
            P("groups", None),
        )
        + (P(),) * 15,
        out_specs=P(("groups", "pair", "samp"), "atoms", None),
        check_vma=False,
    )
```

```python
import functools
import math

import jax
import jax.numpy as jnp
from jax import lax
from jax.experimental import pallas as pl
from jax.experimental.pallas import tpu as pltpu
from jax.sharding import PartitionSpec as P

Q_WIN = 32
K_WIN = 128
EDGE = 48
GROUP = 32

EPSILON = 1e-05
MASKED = -1e30
LOG2E = math.log2(math.e)
BF16 = jnp.bfloat16
F32 = jnp.float32
LAST = (((1,), (1,)), ((), ()))
VMEM_LIMIT = 32 << 20
IN_VMEM = pl.BlockSpec(memory_space=pltpu.VMEM)
IN_HBM = pl.BlockSpec(memory_space=pltpu.HBM)
IN_SMEM = pl.BlockSpec(memory_space=pltpu.SMEM)


def dot(a, b):
    return jnp.dot(a, b, preferred_element_type=F32)


def iota(shape, dim):
    return lax.broadcasted_iota(jnp.int32, shape, dim)


def twice(matrix):
    blank = jnp.zeros_like(matrix)
    return jnp.concatenate(
        [jnp.concatenate([matrix, blank], 1), jnp.concatenate([blank, matrix], 1)], 0
    )


def side_by_side(rows):
    half = rows.shape[0] // 2
    return jnp.concatenate([rows[:half], rows[half:]], 1)


def centring(width):
    same = iota((width, width), 0) == iota((width, width), 1)
    return jnp.where(same, 1.0 - 1.0 / width, -1.0 / width).astype(BF16)


def averaging(width):
    return jnp.full((width, width), 1.0 / width, BF16)


def mean_square(centred):
    return jnp.mean(centred * centred, axis=-1, keepdims=True)


def layer_norm(rows):
    width = rows.shape[1]
    both = dot(side_by_side(rows), twice(centring(width)))
    centred = jnp.concatenate([both[:, :width], both[:, width:]], 0)
    return centred * lax.rsqrt(mean_square(centred) + EPSILON)


def sigmoid(values):
    return 0.5 * jnp.tanh(0.5 * values) + 0.5


def attn_norm(cond, single, ada):
    width = single.shape[-1]
    mixed = dot(cond, ada)
    return (sigmoid(mixed[:, :width])[None] * single + mixed[None, :, width:]).astype(BF16)


def pair_kernel(core_ref, w_pair_hbm, pair_hbm, tile_ref, w_pair_ref, pair_ref, pair_sem, sem):
    rows, cols, width = pair_ref.shape
    heads = w_pair_ref.shape[0]
    group = GROUP
    lanes = heads * group
    half = group // 2
    row_start = core_ref[0] * rows

    def pair_copy(i):
        source = pair_hbm.at[pl.ds(row_start + i * group, group)]
        return pltpu.make_async_copy(source, pair_ref.at[pl.ds(i * group, group)], pair_sem.at[i])

    w_pair_copy = pltpu.make_async_copy(w_pair_hbm, w_pair_ref, sem)
    w_pair_copy.start()
    for i in range(rows // group):
        pair_copy(i).start()
    w_pair_copy.wait()
    w_pair = w_pair_ref[...].astype(F32)
    spread = jnp.concatenate(
        [jnp.broadcast_to(w_pair[h : h + 1], (group, width)) for h in range(heads)], 0
    )
    weight = spread.T.astype(BF16)
    low = iota((width, lanes), 1) % group < half
    blank = jnp.zeros_like(weight)
    mix = jnp.concatenate([jnp.where(low, weight, blank), jnp.where(low, blank, weight)], 0)
    centre = twice(centring(width))
    slot = iota((cols, lanes), 1) % group

    chunks = []
    for chunk in range(rows // group):
        pair_copy(chunk).wait()
        pair = pair_ref[chunk * group : (chunk + 1) * group].reshape(group * cols, width)
        chunks.append(dot(side_by_side(pair), centre).astype(BF16))
    mixes = [dot(centred, mix).reshape(half, cols, lanes) for centred in chunks]
    squares = chunks[0][:, :width] * chunks[0][:, :width]
    average = dot(side_by_side(squares), twice(averaging(width)))
    average = jnp.concatenate([average[:, :width], average[:, width:]], 0)
    for chunk, (centred, mixed) in enumerate(zip(chunks, mixes)):
        variances = [average.reshape(half, cols, width)] if chunk == 0 else []
        for part in range(len(variances), 2):
            rows_of = centred[:, part * width : (part + 1) * width].astype(F32)
            variances.append(mean_square(rows_of).reshape(half, cols, 1))
        total = mixed[0]
        for i in range(1, half):
            total = jnp.where(slot % half == i, mixed[i], total)
        spread_out = jnp.zeros((cols, lanes), F32)
        for i in range(group):
            spread_out = jnp.where(slot == i, variances[i // half][i % half], spread_out)
        tile_ref[chunk] = (total * lax.rsqrt(spread_out + EPSILON)).astype(BF16)


def beside(first, second):
    return jnp.concatenate([first[...], second[...]], 1)


def project_kernel(
    core_ref,
    single_ref,
    cond_ref,
    ada_attn_scale,
    ada_attn_shift,
    w_key,
    w_value,
    w_query,
    w_gate,
    *refs,
):
    late_hbm, refs = refs[:7], refs[7:]
    query_ref, key_ref, value_ref, gate_ref, open_ref, trans_ref, near_ref, far_ref = refs[:8]
    late_refs, sem = refs[8:15], refs[15]
    ada_trans_scale, ada_trans_shift, attn_gate, trans_gate, w_swish, w_linear, w_down = late_refs
    samples, atoms_here, width = single_ref.shape
    copies = [
        pltpu.make_async_copy(source, target, sem.at[i])
        for i, (source, target) in enumerate(zip(late_hbm, late_refs))
    ]
    for copy in copies:
        copy.start()

    cond = layer_norm(cond_ref[...]).astype(BF16)
    single = layer_norm(single_ref[...].reshape(-1, width)).reshape(samples, atoms_here, width)
    normed = attn_norm(cond, single, beside(ada_attn_scale, ada_attn_shift))
    down = core_ref[0] == 0
    for sample in range(samples):
        cut = slice(sample * EDGE, (sample + 1) * EDGE)
        head, tail = normed[sample, :EDGE], normed[sample, atoms_here - EDGE :]
        near_ref[cut, :] = jnp.where(down, head, tail)
        far_ref[cut, :] = jnp.where(down, tail, head)
    for copy in copies:
        copy.wait()
    normed = normed.reshape(-1, width)
    both = dot(normed, beside(w_key, w_value)).astype(BF16).reshape(samples, -1, 2 * width)
    key_ref[...] = both[:, :, :width]
    value_ref[...] = both[:, :, width:]
    both = dot(normed, beside(w_query, w_gate)).reshape(samples, -1, 2 * width)
    query_ref[...] = both[:, :, :width].astype(BF16)
    gate_ref[...] = sigmoid(both[:, :, width:]).astype(BF16)

    gates = dot(cond, beside(attn_gate, trans_gate))
    open_ref[...] = sigmoid(gates[:, :width]).astype(BF16)
    normed = attn_norm(cond, single, beside(ada_trans_scale, ada_trans_shift)).reshape(-1, width)
    swish = dot(normed, w_swish[...])
    hidden = (swish * sigmoid(swish) * dot(normed, w_linear[...])).astype(BF16)
    down = dot(hidden, w_down[...]).reshape(samples, -1, width)
    trans_ref[...] = (sigmoid(gates[:, width:])[None] * down).astype(BF16)


def tile_of(refs, place, row_block):
    if len(refs) == 1:
        return refs[0][row_block]
    pair_at, core_at = place
    owners = 2
    mine, theirs, across, diagonal = [ref[...] for ref in refs]
    near = jnp.where(row_block % owners == core_at, mine, theirs)
    far = jnp.where(row_block % owners == core_at, across, diagonal)
    return jnp.where(row_block // owners == pair_at, near, far)


def shifted(values, lanes):
    return pltpu.roll(values, lanes % values.shape[1], 1)


def unpacked(rows, side):
    half = EDGE // 2
    whole, packed = rows[:EDGE], rows[EDGE:].astype(F32)
    if side == 0:
        part = jnp.concatenate([packed, shifted(packed, -GROUP // 2)], 0).astype(BF16)
        return jnp.concatenate([whole, part], 1)
    part = jnp.concatenate([shifted(packed, GROUP // 2), packed], 0).astype(BF16)
    return jnp.concatenate([part, whole], 1)


def select_kernel(blocks, at_ref, pair_ref, core_ref, *refs):
    *tile_refs, _, __, ___, near_ref, far_ref, ____, held_ref = refs
    groups, cols, lanes = tile_refs[0].shape[-3:]
    device_at, place = at_ref[0], (pair_ref[0], core_ref[0])
    half = EDGE // 2
    for send_ref, core in ((near_ref, 1), (far_ref, 0)):
        above = core_ref[0] == core
        beside = jnp.where(above, device_at + 1, device_at - 1)
        tile = tile_of(tile_refs, place, jnp.clip(beside, 0, blocks - 1))
        tile = jnp.where(above, tile[:, cols - EDGE :], tile[:, :EDGE])
        whole = jnp.where(above, tile[0], tile[1])
        part = jnp.where(above, tile[1], tile[0]).astype(F32)
        first, last = part[:half], part[half:]
        first = jnp.where(above, first, shifted(first, -GROUP // 2))
        last = jnp.where(above, shifted(last, GROUP // 2), last)
        low = iota((half, lanes), 1) % GROUP < GROUP // 2
        packed = jnp.where(low, first, last).astype(BF16)
        send_ref[send_ref.shape[0] - EDGE - half :, :] = jnp.concatenate([whole, packed], 0)
    held_ref[...] = tile_of(tile_refs, place, device_at).reshape(groups * cols, lanes)


def bounds(counts_ref, block, token):
    tok_here = counts_ref.shape[1]
    counts = counts_ref[pl.ds(block, 1), :].astype(F32).astype(BF16)
    counts = jnp.broadcast_to(counts, (8, tok_here))
    before = iota((tok_here, token.shape[1]), 0)
    first = dot(counts, (before < token).astype(BF16))[:1]
    last = dot(counts, (before <= token).astype(BF16))[:1]
    return first.astype(jnp.int32), last.astype(jnp.int32)


def one_hot(reach, offset, count):
    first, last = reach
    position = iota((count, first.shape[1]), 0) + offset
    return ((first <= position) & (position < last)).astype(F32).astype(BF16)


def expand(hot, tile, groups):
    tile = tile.reshape(groups, -1, tile.shape[-1])
    tile = jnp.concatenate([tile[part] for part in range(groups)], 1)
    return dot(hot, tile).astype(BF16)


def head_mask(heads, lanes):
    rows = heads * Q_WIN
    lane_head = iota((rows, lanes), 1) // GROUP % heads
    row_head = iota((rows, lanes), 0) // Q_WIN
    return (lane_head == row_head).astype(F32).astype(BF16)


def picks_of(heads, reach, starts):
    same_head = head_mask(heads, reach[0].shape[1])
    return [
        jnp.concatenate([one_hot(reach, start, Q_WIN)] * heads, 0) * same_head for start in starts
    ]


def attend(heads, windows, query_ref, gate_ref, gated_ref, paired=0):
    samples, _, width = query_ref.shape
    head_dim = width // heads
    rows = heads * Q_WIN
    own_head = iota((rows, width), 1) // head_dim == iota((rows, width), 0) // Q_WIN
    own_head = own_head.astype(F32).astype(BF16)
    channel_head = iota((Q_WIN, 2 * width), 1) % width // head_dim
    ones = jnp.ones((K_WIN, width), BF16)
    scaling = LOG2E / math.sqrt(head_dim)

    biases = []
    for _, _, near, pick, mask in windows:
        bias = lax.dot_general(pick, near, LAST, preferred_element_type=F32) * LOG2E
        biases.append(bias if mask is None else jnp.where(mask, bias, MASKED))
    units = [(sample, i) for i in range(len(windows)) for sample in range(samples)]
    scores = []
    for first in range(0, len(units), 2):
        couple = units[first : first + 2]
        queries, keys = [], []
        for sample, i in couple:
            query = query_ref[sample, pl.ds(windows[i][0], Q_WIN), :]
            queries.append(jnp.concatenate([query] * heads, 0) * own_head)
            keys.append(windows[i][1][sample][0])
        if len(couple) == 2:
            blank = jnp.zeros_like(keys[0])
            keys = [jnp.concatenate([keys[0], blank], 1), jnp.concatenate([blank, keys[1]], 1)]
        product = lax.dot_general(
            jnp.concatenate(queries, 1),
            jnp.concatenate(keys, 0),
            LAST,
            preferred_element_type=F32,
        )
        for j, (_, i) in enumerate(couple):
            scores.append(product[:, j * K_WIN : (j + 1) * K_WIN] * scaling + biases[i])
    tops = [jnp.max(score, axis=-1, keepdims=True) for score in scores]
    raised = [jnp.exp2(score - top) for score, top in zip(scores, tops)]

    def by_head(parts, like):
        picked = jnp.broadcast_to(parts[:Q_WIN], (Q_WIN, like.shape[1]))
        for head in range(1, heads):
            part = parts[head * Q_WIN : (head + 1) * Q_WIN]
            picked = jnp.where(like == head, part, picked)
        return picked

    mixes = []
    for first in range(0, len(units), 2):
        couple = units[first : first + 2]
        values = [windows[i][1][sample][1] for sample, i in couple]
        weights = [weight.astype(BF16) for weight in raised[first : first + 2]]
        if paired and first // 2 % paired == 0 and len(couple) == 2:
            blank = jnp.zeros_like(values[0])
            values = [
                jnp.concatenate([values[0], blank], 1),
                jnp.concatenate([blank, values[1]], 1),
            ]
            both = dot(jnp.concatenate(weights, 1), jnp.concatenate(values, 0))
            for j in range(2):
                total = jnp.sum(raised[first + j], axis=-1, keepdims=True)
                narrow = channel_head[:, :width]
                attended = by_head(both[:, j * width : (j + 1) * width], narrow)
                mixes.append((attended, by_head(total, narrow)))
        else:
            for value, weight in zip(values, weights):
                picked = by_head(dot(weight, jnp.concatenate([value, ones], 1)), channel_head)
                mixes.append((picked[:, :width], picked[:, width:]))
    for (sample, i), (attended, total) in zip(units, mixes):
        attended = attended * pl.reciprocal(total, approx=True)
        at = pl.ds(windows[i][0], Q_WIN)
        gate = gate_ref[sample, at, :].astype(F32)
        gated_ref[sample, at, :] = (gate * attended).astype(BF16)


def close(sample, cut, gated_ref, open_ref, trans_ref, w_out_ref):
    mixed = dot(gated_ref[sample, cut, :], w_out_ref[...])
    opened, trans = open_ref[cut, :].astype(F32), trans_ref[sample, cut, :].astype(F32)
    return (opened * mixed + trans).astype(BF16)


def row_tokens(heads, tok_here):
    lane = iota((tok_here, heads * tok_here), 1)
    return lane // (heads * GROUP) * GROUP + lane % GROUP


def outer_starts(atoms_here):
    skip = -(-EDGE // Q_WIN)
    return [
        [side * (atoms_here - skip * Q_WIN) + i * Q_WIN for i in range(skip)] for side in range(2)
    ]


def inner_kernel(
    heads,
    blocks,
    at_ref,
    counts_ref,
    query_ref,
    key_ref,
    value_ref,
    gate_ref,
    open_ref,
    trans_ref,
    w_out_ref,
    held_ref,
    out_ref,
    pick_ref,
    hot_ref,
    side_ref,
    near_ref,
    gated_ref,
):
    samples, atoms_here, width = query_ref.shape
    tok_here = counts_ref.shape[1]
    device_at = at_ref[0]
    hot = one_hot(
        bounds(counts_ref, device_at, iota((tok_here, tok_here), 1)), 0, atoms_here
    )
    near_ref[...] = expand(hot, held_ref[...], tok_here // GROUP)
    reach = bounds(counts_ref, device_at, row_tokens(heads, tok_here))
    skip = -(-EDGE // Q_WIN)
    starts = [window * Q_WIN for window in range(skip, atoms_here // Q_WIN - skip)]
    windows = []
    for start, pick in zip(starts, picks_of(heads, reach, starts)):
        cut = slice(start - EDGE, start - EDGE + K_WIN)
        parts = [(key_ref[i, cut, :], value_ref[i, cut, :]) for i in range(samples)]
        windows.append((start, parts, near_ref[cut, :], pick, None))
    attend(heads, windows, query_ref, gate_ref, gated_ref, paired=2)

    cut = slice(starts[0], starts[-1] + Q_WIN)
    for sample in range(samples):
        out_ref[sample] = close(sample, cut, gated_ref, open_ref, trans_ref, w_out_ref)

    inside = side_ref.shape[1]
    sides = (
        (jnp.maximum(device_at - 1, 0), atoms_here - EDGE, tok_here - EDGE, 0),
        (jnp.minimum(device_at + 1, blocks - 1), 0, 0, atoms_here - inside),
    )
    for side, (block, offset, token, own_start) in enumerate(sides):
        nearest = bounds(counts_ref, block, iota((tok_here, EDGE), 1) + token)
        hot_ref[side] = one_hot(nearest, offset, EDGE)
        side_ref[side] = near_ref[own_start : own_start + inside, :]
        for i, pick in enumerate(picks_of(heads, reach, outer_starts(atoms_here)[side])):
            pick_ref[side, i] = pick


def outer_kernel(
    heads,
    blocks,
    at_ref,
    core_ref,
    query_ref,
    own_key_ref,
    own_value_ref,
    gate_ref,
    open_ref,
    trans_ref,
    w_out_ref,
    inner_ref,
    pick_ref,
    hot_ref,
    side_ref,
    w_key,
    w_value,
    first_ref,
    second_ref,
    out_hbm,
    gated_ref,
    out_ref,
    sem,
):
    samples, atoms_here, width = query_ref.shape
    device_at = at_ref[0]
    ends = atoms_here * blocks
    starts = outer_starts(atoms_here)
    margin = len(starts[0]) * Q_WIN
    inside = side_ref.shape[1]

    whole = pltpu.make_async_copy(
        inner_ref, out_hbm.at[:, pl.ds(margin, atoms_here - 2 * margin)], sem.at[0]
    )
    whole.start()

    down = core_ref[0] == 0
    first, second = first_ref[...], second_ref[...]
    arrived = (jnp.where(down, second, first), jnp.where(down, first, second))
    count = samples * EDGE
    edges = jnp.concatenate([rows[:count] for rows in arrived], 0)
    edges = dot(edges, beside(w_key, w_value)).astype(BF16).reshape(2, samples, EDGE, 2 * width)

    def joined(side, edge, own):
        return jnp.concatenate([own, edge] if side else [edge, own], 0)

    windows = []
    for side in range(2):
        own = slice(side * (atoms_here - inside), side * (atoms_here - inside) + inside)
        parts = [
            (
                joined(side, edges[side, i, :, :width], own_key_ref[i, own, :]),
                joined(side, edges[side, i, :, width:], own_value_ref[i, own, :]),
            )
            for i in range(samples)
        ]
        near = dot(hot_ref[side], unpacked(arrived[side][count:], side)).astype(BF16)
        near = joined(side, near, side_ref[side])
        for i, start in enumerate(starts[side]):
            cut = slice(i * Q_WIN, i * Q_WIN + K_WIN)
            key_at = iota((heads * Q_WIN, K_WIN), 1) + (device_at * atoms_here + start - EDGE)
            mask = (key_at >= 0) & (key_at < ends)
            pieces = [(keys[cut], values[cut]) for keys, values in parts]
            windows.append((start, pieces, near[cut], pick_ref[side, i], mask))
    attend(heads, windows, query_ref, gate_ref, gated_ref)
    copies = []
    for side in range(2):
        cut = slice(starts[side][0], starts[side][0] + margin)
        for sample in range(samples):
            out_ref[side, sample] = close(sample, cut, gated_ref, open_ref, trans_ref, w_out_ref)
        target = out_hbm.at[:, pl.ds(starts[side][0], margin)]
        copies.append(pltpu.make_async_copy(out_ref.at[side], target, sem.at[1 + side]))
        copies[-1].start()
    for copy in copies:
        copy.wait()
    whole.wait()


def shards(
    atom_single,
    atom_cond,
    pair_cond,
    atom_counts,
    ada_attn_scale,
    ada_attn_shift,
    w_query,
    w_key,
    w_value,
    w_gate,
    w_out,
    attn_gate,
    w_pair,
    ada_trans_scale,
    ada_trans_shift,
    w_swish,
    w_linear,
    w_down,
    trans_gate,
):
    device_at = lax.axis_index("atoms")
    blocks = lax.axis_size("atoms")
    samples, atoms_here, width = atom_single.shape
    tok_here = atom_counts.shape[1]
    heads = w_pair.shape[1]
    groups = tok_here // GROUP
    pairs = lax.axis_size("pair")
    assert pair_cond.shape[0] == lax.axis_size("samp") * tok_here
    assert groups == 2 and tok_here - EDGE == GROUP // 2
    at = device_at.astype(jnp.int32).reshape(1)
    pair_at = lax.axis_index("pair").astype(jnp.int32).reshape(1)
    core_at = lax.axis_index("samp").astype(jnp.int32).reshape(1)
    in_hbm = lambda array: pltpu.with_memory_space_constraint(array, pltpu.HBM)
    in_vmem = lambda array: pltpu.with_memory_space_constraint(array, pltpu.VMEM)

    cols = pair_cond.shape[1]
    lanes = heads * GROUP
    wide = (samples, atoms_here, width)
    params = pltpu.CompilerParams(vmem_limit_bytes=VMEM_LIMIT)

    def cost(products):
        return pl.CostEstimate(flops=2 * products, bytes_accessed=4 << 20, transcendentals=0)

    sent = pltpu.VMEM((samples * EDGE + EDGE + EDGE // 2, lanes), BF16)
    own = pl.pallas_call(
        pair_kernel,
        in_specs=[IN_SMEM] + [IN_HBM] * 2,
        out_specs=IN_VMEM,
        out_shape=pltpu.VMEM((groups, cols, lanes), BF16),
        scratch_shapes=[
            pltpu.VMEM((heads, width), BF16),
            pltpu.VMEM((tok_here, cols, width), BF16),
            pltpu.SemaphoreType.DMA((groups,)),
            pltpu.SemaphoreType.DMA,
        ],
        compiler_params=params,
        cost_estimate=cost(tok_here * cols * width * width * 2),
    )(core_at, *map(in_hbm, (w_pair.T, pair_cond)))
    if pairs == 2:
        swapped = [(0, 1), (1, 0)]
        across = lax.ppermute(own, "pair", swapped)
        diagonal = lax.ppermute(own, ("pair", "samp"), [(0, 3), (1, 2), (2, 1), (3, 0)])
        tiles = (own, lax.ppermute(own, "samp", swapped), across, diagonal)
    else:
        tiles = (lax.all_gather(own, ("pair", "samp")),)

    operands = (
        atom_single,
        atom_cond,
        ada_attn_scale,
        ada_attn_shift,
        w_key,
        w_value,
        w_query,
        w_gate,
    )
    late = (ada_trans_scale, ada_trans_shift, attn_gate, trans_gate, w_swish, w_linear, w_down)
    query, keys, values, gate, opened, trans, near, far = pl.pallas_call(
        project_kernel,
        in_specs=[IN_SMEM] + [IN_VMEM] * len(operands) + [IN_HBM] * len(late),
        out_specs=[IN_VMEM] * 8,
        out_shape=[pltpu.VMEM(wide, BF16)] * 4
        + [pltpu.VMEM((atoms_here, width), BF16), pltpu.VMEM(wide, BF16), sent, sent],
        scratch_shapes=[pltpu.VMEM(weight.shape, BF16) for weight in late]
        + [pltpu.SemaphoreType.DMA((len(late),))],
        compiler_params=params,
        cost_estimate=cost(samples * atoms_here * width * width * 20),
    )(core_at, *map(in_vmem, operands), *map(in_hbm, late))

    operands = (*tiles, near, far, opened)
    first = 3 + len(tiles)
    near, far, opened, held = pl.pallas_call(
        functools.partial(select_kernel, blocks),
        in_specs=[IN_SMEM] * 3 + [IN_VMEM] * len(operands),
        out_specs=[IN_VMEM] * 4,
        out_shape=[
            sent,
            sent,
            pltpu.VMEM((atoms_here, width), BF16),
            pltpu.VMEM((groups * cols, lanes), BF16),
        ],
        input_output_aliases={first: 0, first + 1: 1, first + 2: 2},
        compiler_params=params,
    )(at, pair_at, core_at, *map(in_vmem, operands))

    down = [(2 * i, 2 * (i - 1)) for i in range(1, blocks)] + [(0, 1)]
    up = [(2 * i + 1, 2 * (i + 1) + 1) for i in range(blocks - 1)] + [(2 * blocks - 1, 2 * blocks - 2)]
    cycle = down + up
    first = lax.ppermute(near, ("atoms", "samp"), cycle)
    second = lax.ppermute(far, ("atoms", "samp"), [(target, source) for source, target in cycle])

    margin = -(-EDGE // Q_WIN) * Q_WIN
    inside = margin - Q_WIN + K_WIN - EDGE
    expanded = heads * tok_here
    operands = (query, keys, values, gate, opened, trans, w_out)
    inner, picks, hots, beside_edges = pl.pallas_call(
        functools.partial(inner_kernel, heads, blocks),
        in_specs=[IN_SMEM] + [IN_VMEM] * (2 + len(operands)),
        out_specs=[IN_VMEM] * 4,
        out_shape=[
            pltpu.VMEM((samples, atoms_here - 2 * margin, width), BF16),
            pltpu.VMEM((2, margin // Q_WIN, heads * Q_WIN, expanded), BF16),
            pltpu.VMEM((2, EDGE, EDGE), BF16),
            pltpu.VMEM((2, inside, expanded), BF16),
        ],
        scratch_shapes=[
            pltpu.VMEM((atoms_here, expanded), BF16),
            pltpu.VMEM(wide, BF16),
        ],
        compiler_params=params,
        cost_estimate=cost(samples * atoms_here * width * width * 12),
    )(at, atom_counts, *map(in_vmem, (*operands, held)))

    operands += (inner, picks, hots, beside_edges, w_key, w_value, first, second)
    return pl.pallas_call(
        functools.partial(outer_kernel, heads, blocks),
        in_specs=[IN_SMEM] * 2 + [IN_VMEM] * len(operands),
        out_specs=IN_HBM,
        out_shape=pltpu.HBM(wide, BF16),
        scratch_shapes=[
            pltpu.VMEM(wide, BF16),
            pltpu.VMEM((2, samples, margin, width), BF16),
            pltpu.SemaphoreType.DMA((3,)),
        ],
        compiler_params=params,
        cost_estimate=cost(samples * atoms_here * width * width * 4),
    )(at, core_at, *map(in_vmem, operands))


def solution(mesh):
    return jax.shard_map(
        shards,
        mesh=mesh,
        in_specs=(
            P(("groups", "pair", "samp"), "atoms", None),
            P(("groups", "atoms"), None),
            P(("groups", "pair"), "atoms", None),
            P("groups", None),
        )
        + (P(),) * 15,
        out_specs=P(("groups", "pair", "samp"), "atoms", None),
        check_vma=False,
    )
```

```python
import functools
import math

import jax
import jax.numpy as jnp
from jax import lax
from jax.experimental import pallas as pl
from jax.experimental.pallas import tpu as pltpu
from jax.sharding import PartitionSpec as P

Q_WIN = 32
K_WIN = 128
EDGE = 48
GROUP = 32

EPSILON = 1e-05
MASKED = -1e30
LOG2E = math.log2(math.e)
BF16 = jnp.bfloat16
F32 = jnp.float32
LAST = (((1,), (1,)), ((), ()))
VMEM_LIMIT = 32 << 20
IN_VMEM = pl.BlockSpec(memory_space=pltpu.VMEM)
IN_HBM = pl.BlockSpec(memory_space=pltpu.HBM)
IN_SMEM = pl.BlockSpec(memory_space=pltpu.SMEM)


def dot(a, b):
    return jnp.dot(a, b, preferred_element_type=F32)


def iota(shape, dim):
    return lax.broadcasted_iota(jnp.int32, shape, dim)


def twice(matrix):
    blank = jnp.zeros_like(matrix)
    return jnp.concatenate(
        [jnp.concatenate([matrix, blank], 1), jnp.concatenate([blank, matrix], 1)], 0
    )


def side_by_side(rows):
    half = rows.shape[0] // 2
    return jnp.concatenate([rows[:half], rows[half:]], 1)


def centring(width):
    same = iota((width, width), 0) == iota((width, width), 1)
    return jnp.where(same, 1.0 - 1.0 / width, -1.0 / width).astype(BF16)


def averaging(width):
    return jnp.full((width, width), 1.0 / width, BF16)


def mean_square(centred):
    return jnp.mean(centred * centred, axis=-1, keepdims=True)


def layer_norm(rows):
    width = rows.shape[1]
    both = dot(side_by_side(rows), twice(centring(width)))
    centred = jnp.concatenate([both[:, :width], both[:, width:]], 0)
    return centred * lax.rsqrt(mean_square(centred) + EPSILON)


def sigmoid(values):
    return 0.5 * jnp.tanh(0.5 * values) + 0.5


def attn_norm(cond, single, ada):
    width = single.shape[-1]
    mixed = dot(cond, ada)
    return (sigmoid(mixed[:, :width])[None] * single + mixed[None, :, width:]).astype(BF16)


def pair_kernel(core_ref, w_pair_hbm, pair_hbm, tile_ref, w_pair_ref, pair_ref, pair_sem, sem):
    rows, cols, width = pair_ref.shape
    heads = w_pair_ref.shape[0]
    group = GROUP
    lanes = heads * group
    half = group // 2
    row_start = core_ref[0] * rows

    def pair_copy(i):
        source = pair_hbm.at[pl.ds(row_start + i * group, group)]
        return pltpu.make_async_copy(source, pair_ref.at[pl.ds(i * group, group)], pair_sem.at[i])

    w_pair_copy = pltpu.make_async_copy(w_pair_hbm, w_pair_ref, sem)
    w_pair_copy.start()
    for i in range(rows // group):
        pair_copy(i).start()
    w_pair_copy.wait()
    w_pair = w_pair_ref[...].astype(F32)
    spread = jnp.concatenate(
        [jnp.broadcast_to(w_pair[h : h + 1], (group, width)) for h in range(heads)], 0
    )
    mix = twice(spread.T.astype(BF16))
    centre = twice(centring(width))
    slot = iota((cols, lanes), 1) % group

    chunks = []
    for chunk in range(rows // group):
        pair_copy(chunk).wait()
        pair = pair_ref[chunk * group : (chunk + 1) * group].reshape(group * cols, width)
        chunks.append(dot(side_by_side(pair), centre).astype(BF16))
    mixes = [dot(centred, mix).reshape(half, cols, 2 * lanes) for centred in chunks]
    squares = chunks[0][:, :width] * chunks[0][:, :width]
    average = dot(side_by_side(squares), twice(averaging(width)))
    average = jnp.concatenate([average[:, :width], average[:, width:]], 0)
    for chunk, (centred, mixed) in enumerate(zip(chunks, mixes)):
        variances = [average.reshape(half, cols, width)] if chunk == 0 else []
        for part in range(len(variances), 2):
            rows_of = centred[:, part * width : (part + 1) * width].astype(F32)
            variances.append(mean_square(rows_of).reshape(half, cols, 1))
        total = jnp.zeros((cols, lanes), F32)
        spread_out = jnp.zeros((cols, lanes), F32)
        for i in range(group):
            side = slice(i // half * lanes, (i // half + 1) * lanes)
            total = jnp.where(slot == i, mixed[i % half, :, side], total)
            spread_out = jnp.where(slot == i, variances[i // half][i % half], spread_out)
        tile_ref[chunk] = (total * lax.rsqrt(spread_out + EPSILON)).astype(BF16)


def beside(first, second):
    return jnp.concatenate([first[...], second[...]], 1)


def project_kernel(
    core_ref,
    single_ref,
    cond_ref,
    ada_attn_scale,
    ada_attn_shift,
    w_key,
    w_value,
    w_query,
    w_gate,
    *refs,
):
    late_hbm, refs = refs[:7], refs[7:]
    query_ref, key_ref, value_ref, gate_ref, open_ref, trans_ref, near_ref, far_ref = refs[:8]
    late_refs, sem = refs[8:15], refs[15]
    ada_trans_scale, ada_trans_shift, attn_gate, trans_gate, w_swish, w_linear, w_down = late_refs
    samples, atoms_here, width = single_ref.shape
    copies = [
        pltpu.make_async_copy(source, target, sem.at[i])
        for i, (source, target) in enumerate(zip(late_hbm, late_refs))
    ]
    for copy in copies:
        copy.start()

    cond = layer_norm(cond_ref[...]).astype(BF16)
    single = layer_norm(single_ref[...].reshape(-1, width)).reshape(samples, atoms_here, width)
    normed = attn_norm(cond, single, beside(ada_attn_scale, ada_attn_shift))
    down = core_ref[0] == 0
    for sample in range(samples):
        cut = slice(sample * EDGE, (sample + 1) * EDGE)
        head, tail = normed[sample, :EDGE], normed[sample, atoms_here - EDGE :]
        near_ref[cut, :] = jnp.where(down, head, tail)
        far_ref[cut, :] = jnp.where(down, tail, head)
    for copy in copies:
        copy.wait()
    normed = normed.reshape(-1, width)
    both = dot(normed, beside(w_key, w_value)).astype(BF16).reshape(samples, -1, 2 * width)
    key_ref[...] = both[:, :, :width]
    value_ref[...] = both[:, :, width:]
    both = dot(normed, beside(w_query, w_gate)).reshape(samples, -1, 2 * width)
    query_ref[...] = both[:, :, :width].astype(BF16)
    gate_ref[...] = sigmoid(both[:, :, width:]).astype(BF16)

    gates = dot(cond, beside(attn_gate, trans_gate))
    open_ref[...] = sigmoid(gates[:, :width]).astype(BF16)
    normed = attn_norm(cond, single, beside(ada_trans_scale, ada_trans_shift)).reshape(-1, width)
    swish = dot(normed, w_swish[...])
    hidden = (swish * sigmoid(swish) * dot(normed, w_linear[...])).astype(BF16)
    down = dot(hidden, w_down[...]).reshape(samples, -1, width)
    trans_ref[...] = (sigmoid(gates[:, width:])[None] * down).astype(BF16)


def tile_of(refs, place, row_block):
    if len(refs) == 1:
        return refs[0][row_block]
    pair_at, core_at = place
    owners = 2
    mine, theirs, across, diagonal = [ref[...] for ref in refs]
    near = jnp.where(row_block % owners == core_at, mine, theirs)
    far = jnp.where(row_block % owners == core_at, across, diagonal)
    return jnp.where(row_block // owners == pair_at, near, far)


def shifted(values, lanes):
    return pltpu.roll(values, lanes % values.shape[1], 1)


def unpacked(rows, side):
    half = EDGE // 2
    whole, packed = rows[:EDGE], rows[EDGE:].astype(F32)
    if side == 0:
        part = jnp.concatenate([packed, shifted(packed, -GROUP // 2)], 0).astype(BF16)
        return jnp.concatenate([whole, part], 1)
    part = jnp.concatenate([shifted(packed, GROUP // 2), packed], 0).astype(BF16)
    return jnp.concatenate([part, whole], 1)


def select_kernel(blocks, at_ref, pair_ref, core_ref, *refs):
    *tile_refs, _, __, ___, near_ref, far_ref, ____, held_ref = refs
    groups, cols, lanes = tile_refs[0].shape[-3:]
    device_at, place = at_ref[0], (pair_ref[0], core_ref[0])
    half = EDGE // 2
    for send_ref, core in ((near_ref, 1), (far_ref, 0)):
        above = core_ref[0] == core
        beside = jnp.where(above, device_at + 1, device_at - 1)
        tile = tile_of(tile_refs, place, jnp.clip(beside, 0, blocks - 1))
        tile = jnp.where(above, tile[:, cols - EDGE :], tile[:, :EDGE])
        whole = jnp.where(above, tile[0], tile[1])
        part = jnp.where(above, tile[1], tile[0]).astype(F32)
        first, last = part[:half], part[half:]
        first = jnp.where(above, first, shifted(first, -GROUP // 2))
        last = jnp.where(above, shifted(last, GROUP // 2), last)
        low = iota((half, lanes), 1) % GROUP < GROUP // 2
        packed = jnp.where(low, first, last).astype(BF16)
        send_ref[send_ref.shape[0] - EDGE - half :, :] = jnp.concatenate([whole, packed], 0)
    held_ref[...] = tile_of(tile_refs, place, device_at).reshape(groups * cols, lanes)


def bounds(counts_ref, block, token):
    tok_here = counts_ref.shape[1]
    counts = counts_ref[pl.ds(block, 1), :].astype(F32).astype(BF16)
    counts = jnp.broadcast_to(counts, (8, tok_here))
    before = iota((tok_here, token.shape[1]), 0)
    first = dot(counts, (before < token).astype(BF16))[:1]
    last = dot(counts, (before <= token).astype(BF16))[:1]
    return first.astype(jnp.int32), last.astype(jnp.int32)


def one_hot(reach, offset, count):
    first, last = reach
    position = iota((count, first.shape[1]), 0) + offset
    return ((first <= position) & (position < last)).astype(F32).astype(BF16)


def expand(hot, tile, groups):
    tile = tile.reshape(groups, -1, tile.shape[-1])
    tile = jnp.concatenate([tile[part] for part in range(groups)], 1)
    return dot(hot, tile).astype(BF16)


def head_mask(heads, lanes):
    rows = heads * Q_WIN
    lane_head = iota((rows, lanes), 1) // GROUP % heads
    row_head = iota((rows, lanes), 0) // Q_WIN
    return (lane_head == row_head).astype(F32).astype(BF16)


def picks_of(heads, reach, starts):
    same_head = head_mask(heads, reach[0].shape[1])
    return [
        jnp.concatenate([one_hot(reach, start, Q_WIN)] * heads, 0) * same_head for start in starts
    ]


def attend(heads, windows, query_ref, gate_ref, gated_ref, paired=0):
    samples, _, width = query_ref.shape
    head_dim = width // heads
    rows = heads * Q_WIN
    own_head = iota((rows, width), 1) // head_dim == iota((rows, width), 0) // Q_WIN
    own_head = own_head.astype(F32).astype(BF16)
    channel_head = iota((Q_WIN, 2 * width), 1) % width // head_dim
    ones = jnp.ones((K_WIN, width), BF16)
    scaling = LOG2E / math.sqrt(head_dim)

    biases = []
    for _, _, near, pick, mask in windows:
        bias = lax.dot_general(pick, near, LAST, preferred_element_type=F32) * LOG2E
        biases.append(bias if mask is None else jnp.where(mask, bias, MASKED))
    units = [(sample, i) for i in range(len(windows)) for sample in range(samples)]
    scores = []
    for first in range(0, len(units), 2):
        couple = units[first : first + 2]
        queries, keys = [], []
        for sample, i in couple:
            query = query_ref[sample, pl.ds(windows[i][0], Q_WIN), :]
            queries.append(jnp.concatenate([query] * heads, 0) * own_head)
            keys.append(windows[i][1][sample][0])
        if len(couple) == 2:
            blank = jnp.zeros_like(keys[0])
            keys = [jnp.concatenate([keys[0], blank], 1), jnp.concatenate([blank, keys[1]], 1)]
        product = lax.dot_general(
            jnp.concatenate(queries, 1),
            jnp.concatenate(keys, 0),
            LAST,
            preferred_element_type=F32,
        )
        for j, (_, i) in enumerate(couple):
            scores.append(product[:, j * K_WIN : (j + 1) * K_WIN] * scaling + biases[i])
    tops = [jnp.max(score, axis=-1, keepdims=True) for score in scores]
    raised = [jnp.exp2(score - top) for score, top in zip(scores, tops)]

    def by_head(parts, like):
        picked = jnp.broadcast_to(parts[:Q_WIN], (Q_WIN, like.shape[1]))
        for head in range(1, heads):
            part = parts[head * Q_WIN : (head + 1) * Q_WIN]
            picked = jnp.where(like == head, part, picked)
        return picked

    mixes = []
    for first in range(0, len(units), 2):
        couple = units[first : first + 2]
        values = [windows[i][1][sample][1] for sample, i in couple]
        weights = [weight.astype(BF16) for weight in raised[first : first + 2]]
        if paired and first // 2 % paired == 0 and len(couple) == 2:
            blank = jnp.zeros_like(values[0])
            values = [
                jnp.concatenate([values[0], blank], 1),
                jnp.concatenate([blank, values[1]], 1),
            ]
            both = dot(jnp.concatenate(weights, 1), jnp.concatenate(values, 0))
            for j in range(2):
                total = jnp.sum(raised[first + j], axis=-1, keepdims=True)
                narrow = channel_head[:, :width]
                attended = by_head(both[:, j * width : (j + 1) * width], narrow)
                mixes.append((attended, by_head(total, narrow)))
        else:
            for value, weight in zip(values, weights):
                picked = by_head(dot(weight, jnp.concatenate([value, ones], 1)), channel_head)
                mixes.append((picked[:, :width], picked[:, width:]))
    for (sample, i), (attended, total) in zip(units, mixes):
        attended = attended * pl.reciprocal(total, approx=True)
        at = pl.ds(windows[i][0], Q_WIN)
        gate = gate_ref[sample, at, :].astype(F32)
        gated_ref[sample, at, :] = (gate * attended).astype(BF16)


def close(sample, cut, gated_ref, open_ref, trans_ref, w_out_ref):
    mixed = dot(gated_ref[sample, cut, :], w_out_ref[...])
    opened, trans = open_ref[cut, :].astype(F32), trans_ref[sample, cut, :].astype(F32)
    return (opened * mixed + trans).astype(BF16)


def row_tokens(heads, tok_here):
    lane = iota((tok_here, heads * tok_here), 1)
    return lane // (heads * GROUP) * GROUP + lane % GROUP


def outer_starts(atoms_here):
    skip = -(-EDGE // Q_WIN)
    return [
        [side * (atoms_here - skip * Q_WIN) + i * Q_WIN for i in range(skip)] for side in range(2)
    ]


def inner_kernel(
    heads,
    blocks,
    at_ref,
    counts_ref,
    query_ref,
    key_ref,
    value_ref,
    gate_ref,
    open_ref,
    trans_ref,
    w_out_ref,
    held_ref,
    out_ref,
    pick_ref,
    hot_ref,
    side_ref,
    near_ref,
    gated_ref,
):
    samples, atoms_here, width = query_ref.shape
    tok_here = counts_ref.shape[1]
    device_at = at_ref[0]
    hot = one_hot(
        bounds(counts_ref, device_at, iota((tok_here, tok_here), 1)), 0, atoms_here
    )
    near_ref[...] = expand(hot, held_ref[...], tok_here // GROUP)
    reach = bounds(counts_ref, device_at, row_tokens(heads, tok_here))
    skip = -(-EDGE // Q_WIN)
    starts = [window * Q_WIN for window in range(skip, atoms_here // Q_WIN - skip)]
    windows = []
    for start, pick in zip(starts, picks_of(heads, reach, starts)):
        cut = slice(start - EDGE, start - EDGE + K_WIN)
        parts = [(key_ref[i, cut, :], value_ref[i, cut, :]) for i in range(samples)]
        windows.append((start, parts, near_ref[cut, :], pick, None))
    attend(heads, windows, query_ref, gate_ref, gated_ref, paired=2)

    cut = slice(starts[0], starts[-1] + Q_WIN)
    for sample in range(samples):
        out_ref[sample] = close(sample, cut, gated_ref, open_ref, trans_ref, w_out_ref)

    inside = side_ref.shape[1]
    sides = (
        (jnp.maximum(device_at - 1, 0), atoms_here - EDGE, tok_here - EDGE, 0),
        (jnp.minimum(device_at + 1, blocks - 1), 0, 0, atoms_here - inside),
    )
    for side, (block, offset, token, own_start) in enumerate(sides):
        nearest = bounds(counts_ref, block, iota((tok_here, EDGE), 1) + token)
        hot_ref[side] = one_hot(nearest, offset, EDGE)
        side_ref[side] = near_ref[own_start : own_start + inside, :]
        for i, pick in enumerate(picks_of(heads, reach, outer_starts(atoms_here)[side])):
            pick_ref[side, i] = pick


def outer_kernel(
    heads,
    blocks,
    at_ref,
    core_ref,
    query_ref,
    own_key_ref,
    own_value_ref,
    gate_ref,
    open_ref,
    trans_ref,
    w_out_ref,
    inner_ref,
    pick_ref,
    hot_ref,
    side_ref,
    w_key,
    w_value,
    first_ref,
    second_ref,
    out_hbm,
    gated_ref,
    out_ref,
    sem,
):
    samples, atoms_here, width = query_ref.shape
    device_at = at_ref[0]
    ends = atoms_here * blocks
    starts = outer_starts(atoms_here)
    margin = len(starts[0]) * Q_WIN
    inside = side_ref.shape[1]

    whole = pltpu.make_async_copy(
        inner_ref, out_hbm.at[:, pl.ds(margin, atoms_here - 2 * margin)], sem.at[0]
    )
    whole.start()

    down = core_ref[0] == 0
    first, second = first_ref[...], second_ref[...]
    arrived = (jnp.where(down, second, first), jnp.where(down, first, second))
    count = samples * EDGE
    edges = jnp.concatenate([rows[:count] for rows in arrived], 0)
    edges = dot(edges, beside(w_key, w_value)).astype(BF16).reshape(2, samples, EDGE, 2 * width)

    def joined(side, edge, own):
        return jnp.concatenate([own, edge] if side else [edge, own], 0)

    windows = []
    for side in range(2):
        own = slice(side * (atoms_here - inside), side * (atoms_here - inside) + inside)
        parts = [
            (
                joined(side, edges[side, i, :, :width], own_key_ref[i, own, :]),
                joined(side, edges[side, i, :, width:], own_value_ref[i, own, :]),
            )
            for i in range(samples)
        ]
        near = dot(hot_ref[side], unpacked(arrived[side][count:], side)).astype(BF16)
        near = joined(side, near, side_ref[side])
        for i, start in enumerate(starts[side]):
            cut = slice(i * Q_WIN, i * Q_WIN + K_WIN)
            key_at = iota((heads * Q_WIN, K_WIN), 1) + (device_at * atoms_here + start - EDGE)
            mask = (key_at >= 0) & (key_at < ends)
            pieces = [(keys[cut], values[cut]) for keys, values in parts]
            windows.append((start, pieces, near[cut], pick_ref[side, i], mask))
    attend(heads, windows, query_ref, gate_ref, gated_ref, paired=2)
    copies = []
    for side in range(2):
        cut = slice(starts[side][0], starts[side][0] + margin)
        for sample in range(samples):
            out_ref[side, sample] = close(sample, cut, gated_ref, open_ref, trans_ref, w_out_ref)
        target = out_hbm.at[:, pl.ds(starts[side][0], margin)]
        copies.append(pltpu.make_async_copy(out_ref.at[side], target, sem.at[1 + side]))
        copies[-1].start()
    for copy in copies:
        copy.wait()
    whole.wait()


def shards(
    atom_single,
    atom_cond,
    pair_cond,
    atom_counts,
    ada_attn_scale,
    ada_attn_shift,
    w_query,
    w_key,
    w_value,
    w_gate,
    w_out,
    attn_gate,
    w_pair,
    ada_trans_scale,
    ada_trans_shift,
    w_swish,
    w_linear,
    w_down,
    trans_gate,
):
    device_at = lax.axis_index("atoms")
    blocks = lax.axis_size("atoms")
    samples, atoms_here, width = atom_single.shape
    tok_here = atom_counts.shape[1]
    heads = w_pair.shape[1]
    groups = tok_here // GROUP
    pairs = lax.axis_size("pair")
    assert pair_cond.shape[0] == lax.axis_size("samp") * tok_here
    assert groups == 2 and tok_here - EDGE == GROUP // 2
    at = device_at.astype(jnp.int32).reshape(1)
    pair_at = lax.axis_index("pair").astype(jnp.int32).reshape(1)
    core_at = lax.axis_index("samp").astype(jnp.int32).reshape(1)
    in_hbm = lambda array: pltpu.with_memory_space_constraint(array, pltpu.HBM)
    in_vmem = lambda array: pltpu.with_memory_space_constraint(array, pltpu.VMEM)

    cols = pair_cond.shape[1]
    lanes = heads * GROUP
    wide = (samples, atoms_here, width)
    params = pltpu.CompilerParams(vmem_limit_bytes=VMEM_LIMIT)

    def cost(products):
        return pl.CostEstimate(flops=2 * products, bytes_accessed=4 << 20, transcendentals=0)

    sent = pltpu.VMEM((samples * EDGE + EDGE + EDGE // 2, lanes), BF16)
    own = pl.pallas_call(
        pair_kernel,
        in_specs=[IN_SMEM] + [IN_HBM] * 2,
        out_specs=IN_VMEM,
        out_shape=pltpu.VMEM((groups, cols, lanes), BF16),
        scratch_shapes=[
            pltpu.VMEM((heads, width), BF16),
            pltpu.VMEM((tok_here, cols, width), BF16),
            pltpu.SemaphoreType.DMA((groups,)),
            pltpu.SemaphoreType.DMA,
        ],
        compiler_params=params,
        cost_estimate=cost(tok_here * cols * width * width * 2),
    )(core_at, *map(in_hbm, (w_pair.T, pair_cond)))
    if pairs == 2:
        swapped = [(0, 1), (1, 0)]
        across = lax.ppermute(own, "pair", swapped)
        diagonal = lax.ppermute(own, ("pair", "samp"), [(0, 3), (1, 2), (2, 1), (3, 0)])
        tiles = (own, lax.ppermute(own, "samp", swapped), across, diagonal)
    else:
        tiles = (lax.all_gather(own, ("pair", "samp")),)

    operands = (
        atom_single,
        atom_cond,
        ada_attn_scale,
        ada_attn_shift,
        w_key,
        w_value,
        w_query,
        w_gate,
    )
    late = (ada_trans_scale, ada_trans_shift, attn_gate, trans_gate, w_swish, w_linear, w_down)
    query, keys, values, gate, opened, trans, near, far = pl.pallas_call(
        project_kernel,
        in_specs=[IN_SMEM] + [IN_VMEM] * len(operands) + [IN_HBM] * len(late),
        out_specs=[IN_VMEM] * 8,
        out_shape=[pltpu.VMEM(wide, BF16)] * 4
        + [pltpu.VMEM((atoms_here, width), BF16), pltpu.VMEM(wide, BF16), sent, sent],
        scratch_shapes=[pltpu.VMEM(weight.shape, BF16) for weight in late]
        + [pltpu.SemaphoreType.DMA((len(late),))],
        compiler_params=params,
        cost_estimate=cost(samples * atoms_here * width * width * 20),
    )(core_at, *map(in_vmem, operands), *map(in_hbm, late))

    operands = (*tiles, near, far, opened)
    first = 3 + len(tiles)
    near, far, opened, held = pl.pallas_call(
        functools.partial(select_kernel, blocks),
        in_specs=[IN_SMEM] * 3 + [IN_VMEM] * len(operands),
        out_specs=[IN_VMEM] * 4,
        out_shape=[
            sent,
            sent,
            pltpu.VMEM((atoms_here, width), BF16),
            pltpu.VMEM((groups * cols, lanes), BF16),
        ],
        input_output_aliases={first: 0, first + 1: 1, first + 2: 2},
        compiler_params=params,
    )(at, pair_at, core_at, *map(in_vmem, operands))

    down = [(2 * i, 2 * (i - 1)) for i in range(1, blocks)] + [(0, 1)]
    up = [(2 * i + 1, 2 * (i + 1) + 1) for i in range(blocks - 1)] + [(2 * blocks - 1, 2 * blocks - 2)]
    cycle = down + up
    first = lax.ppermute(near, ("atoms", "samp"), cycle)
    second = lax.ppermute(far, ("atoms", "samp"), [(target, source) for source, target in cycle])

    margin = -(-EDGE // Q_WIN) * Q_WIN
    inside = margin - Q_WIN + K_WIN - EDGE
    expanded = heads * tok_here
    operands = (query, keys, values, gate, opened, trans, w_out)
    inner, picks, hots, beside_edges = pl.pallas_call(
        functools.partial(inner_kernel, heads, blocks),
        in_specs=[IN_SMEM] + [IN_VMEM] * (2 + len(operands)),
        out_specs=[IN_VMEM] * 4,
        out_shape=[
            pltpu.VMEM((samples, atoms_here - 2 * margin, width), BF16),
            pltpu.VMEM((2, margin // Q_WIN, heads * Q_WIN, expanded), BF16),
            pltpu.VMEM((2, EDGE, EDGE), BF16),
            pltpu.VMEM((2, inside, expanded), BF16),
        ],
        scratch_shapes=[
            pltpu.VMEM((atoms_here, expanded), BF16),
            pltpu.VMEM(wide, BF16),
        ],
        compiler_params=params,
        cost_estimate=cost(samples * atoms_here * width * width * 12),
    )(at, atom_counts, *map(in_vmem, (*operands, held)))

    operands += (inner, picks, hots, beside_edges, w_key, w_value, first, second)
    return pl.pallas_call(
        functools.partial(outer_kernel, heads, blocks),
        in_specs=[IN_SMEM] * 2 + [IN_VMEM] * len(operands),
        out_specs=IN_HBM,
        out_shape=pltpu.HBM(wide, BF16),
        scratch_shapes=[
            pltpu.VMEM(wide, BF16),
            pltpu.VMEM((2, samples, margin, width), BF16),
            pltpu.SemaphoreType.DMA((3,)),
        ],
        compiler_params=params,
        cost_estimate=cost(samples * atoms_here * width * width * 4),
    )(at, core_at, *map(in_vmem, operands))


def solution(mesh):
    return jax.shard_map(
        shards,
        mesh=mesh,
        in_specs=(
            P(("groups", "pair", "samp"), "atoms", None),
            P(("groups", "atoms"), None),
            P(("groups", "pair"), "atoms", None),
            P("groups", None),
        )
        + (P(),) * 15,
        out_specs=P(("groups", "pair", "samp"), "atoms", None),
        check_vma=False,
    )
```
